32 devices in a mesh: seq: 8 (over z, x), batch: 4 (over y, core).
Axes of the slice: x: 2, y: 2, z: 4, core: 2. Of those that a mesh axis runs over, the one named last changes fastest.
Arguments:
- tokens: bfloat16 [8, 2048, 1024], P('batch', 'seq'), may hold values from -6 to 6
- cotangent: bfloat16 [8, 2048, 1024], P('batch', 'seq'), may hold values from -6 to 6
- lengths: int32 [8], P('batch'), may hold values from 128 to 2048, as said below
- span_order: int32 [8, 2], replicated, may hold values from 0 to 15, as said below
- attn_gain: bfloat16 [1024], P('seq'), may hold values from 0.5 to 1.5
- query_heads: bfloat16 [1024, 96], P('seq'), may hold values from -0.375 to 0.375
- query_dims: bfloat16 [1024, 384], P('seq'), may hold values from -0.375 to 0.375
- key_heads: bfloat16 [1024, 32], P('seq'), may hold values from -0.25 to 0.25
- key_dims: bfloat16 [1024, 128], P('seq'), may hold values from -0.1875 to 0.1875
- value_heads: bfloat16 [1024, 32], P('seq'), may hold values from -0.375 to 0.375
- value_dims: bfloat16 [1024, 128], P('seq'), may hold values from -0.1875 to 0.1875
- out_proj: bfloat16 [1024, 1024], P('seq'), may hold values from -1.5 to 1.5
- ffn_gain: bfloat16 [1024], P('seq'), may hold values from 0.5 to 1.5
- gate_proj: bfloat16 [1024, 2816], P('seq'), may hold values from -0.1875 to 0.1875
- up_proj: bfloat16 [1024, 2816], P('seq'), may hold values from -0.1875 to 0.1875
- down_proj: bfloat16 [2816, 1024], P('seq'), may hold values from -0.109375 to 0.109375
Outputs:
- output: bfloat16 [8, 2048, 1024], P('batch', 'seq')
- input_grad: float32 [8, 2048, 1024], P('batch', 'seq')
- attn_gain_grad: float32 [1024], P('seq')
- query_heads_grad: float32 [1024, 96], P('seq')
- query_dims_grad: float32 [1024, 384], P('seq')
- key_heads_grad: float32 [1024, 32], P('seq')
- key_dims_grad: float32 [1024, 128], P('seq')
- value_heads_grad: float32 [1024, 32], P('seq')
- value_dims_grad: float32 [1024, 128], P('seq')
- out_proj_grad: float32 [1024, 1024], P('seq')
- ffn_gain_grad: float32 [1024], P('seq')
- gate_proj_grad: float32 [1024, 2816], P('seq')
- up_proj_grad: float32 [1024, 2816], P('seq')
- down_proj_grad: float32 [2816, 1024], P('seq')
The draws below stay inside these ranges and needn't reach their ends.
Inputs may be any that keep to these rules, and one draw needn't show every extreme that they name: `lengths`: in each aligned block of 2 rows (the rows of one index of batch) at least one row has length 2048. `span_order`: the two entries of each row add up to 15 and the first is the smaller; every span number appears once.
All inputs are finite; a program needn't handle non-finite values.
Results may differ from the reference program's by a relative error of at most 0.017.
The reference program's roundings to bfloat16 on the way count: a program that leaves them out, or rounds other values in their place, can miss the bound.
Values may be sent and summed in bfloat16 or wider, within the bound.
A program may use at most 320 MiB of HBM per device.

```python
import math
import jax
import jax.numpy as jnp
from jax import lax

D = 1024
HEADS = 16
HDIM = 64
QRANK = 6
KVRANK = 2
FF = 2816
ROWS_DEV = 2
MINLEN = 128
SLOTS = 2048
NCHUNK = 16
SPAN = 128
ROWS = 8


def draw_lengths(key, part):
    levels = (SLOTS // MINLEN).bit_length()
    first, second, third, fourth = jax.random.split(key, 4)
    power = jnp.minimum(jax.random.randint(first, (ROWS,), 0, levels), jax.random.randint(second, (ROWS,), 0, levels))
    base = jnp.left_shift(jnp.full((ROWS,), MINLEN, jnp.int32), power.astype(jnp.int32))
    extra = jax.random.randint(third, (ROWS,), 0, 1 << 20) % base
    ragged = jnp.minimum(base + extra, SLOTS)
    chosen = jax.random.randint(fourth, (ROWS // ROWS_DEV,), 0, ROWS_DEV)
    is_full = jnp.arange(ROWS) % ROWS_DEV == jnp.repeat(chosen, ROWS_DEV)
    return jnp.where(is_full, SLOTS, ragged).astype(jnp.int32)


def draw_span_order(key, part):
    half = NCHUNK // 2
    picked = jax.random.permutation(key, half).astype(jnp.int32)
    return jnp.stack([picked, NCHUNK - 1 - picked], 1).astype(jnp.int32)


def steps_of(rng, extent, shards, low, top_value):
    loudness, own = 1.0, jax.random.fold_in(rng, 6)
    for position, parts in shards:
        heights = jnp.exp(jax.random.uniform(jax.random.fold_in(own, position), (parts,), jnp.float32, low / len(shards), top_value / len(shards)))
        loudness = loudness * jnp.repeat(heights, extent[position] // parts).reshape([-1 if axis == position else 1 for axis in range(len(extent))])
    return loudness


def centred(key, dims, deviation, limit, shards=(), kind=jnp.bfloat16):
    values = jax.random.normal(key, dims, jnp.float32) * deviation
    if len(shards) > 0:
        values = steps_of(key, dims, shards, -0.22, 0.18) * values
    return jnp.clip(values, min=-limit, max=limit).astype(kind)


def setup_inputs(seed: int = 0) -> dict:
    streams_of = jax.random.split(jax.random.key(seed), 17)
    return {
        "tokens": centred(streams_of[0], (ROWS, SLOTS, D), 1.0, 6.0, ((0, 4), (1, 8))),
        "cotangent": centred(streams_of[1], (ROWS, SLOTS, D), 1.0, 6.0, ((0, 4), (1, 8))),
        "lengths": draw_lengths(jax.random.fold_in(streams_of[16], 71), 0),
        "span_order": draw_span_order(jax.random.fold_in(streams_of[16], 71), 0),
        "attn_gain": jnp.clip(1.0 + 0.1 * jax.random.normal(streams_of[4], (D,), jnp.float32), 0.5, 1.5).astype(jnp.bfloat16),
        "query_heads": centred(streams_of[5], (D, QRANK * HEADS), (D // 4) ** -0.5, 0.375, ((0, 8),)),
        "query_dims": centred(streams_of[6], (D, QRANK * HDIM), (D // 4) ** -0.5, 0.375, ((0, 8),)),
        "key_heads": centred(streams_of[7], (D, KVRANK * HEADS), (D // 2) ** -0.5, 0.25, ((0, 8),)),
        "key_dims": centred(streams_of[8], (D, KVRANK * HDIM), D ** -0.5, 0.1875, ((0, 8),)),
        "value_heads": centred(streams_of[9], (D, KVRANK * HEADS), (D // 4) ** -0.5, 0.375, ((0, 8),)),
        "value_dims": centred(streams_of[10], (D, KVRANK * HDIM), D ** -0.5, 0.1875, ((0, 8),)),
        "out_proj": centred(streams_of[11], (D, D), (D // 64) ** -0.5, 1.5, ((0, 8),)),
        "ffn_gain": jnp.clip(1.0 + 0.1 * jax.random.normal(streams_of[12], (D,), jnp.float32), 0.5, 1.5).astype(jnp.bfloat16),
        "gate_proj": centred(streams_of[13], (D, FF), D ** -0.5, 0.1875, ((0, 8),)),
        "up_proj": centred(streams_of[14], (D, FF), D ** -0.5, 0.1875, ((0, 8),)),
        "down_proj": centred(streams_of[15], (FF, D), FF ** -0.5, 0.109375, ((0, 8),)),
    }


EPSILON = 1e-06
NEG_LARGE = -1e+30
HIGH = lax.Precision.HIGHEST

@jax.custom_vjp
def low(v):
    return lax.optimization_barrier(v.astype(jnp.bfloat16)).astype(jnp.float32)

@jax.custom_vjp
def low_back(v):
    return v

def low_keep(v):
    return (low(v), None)

def low_pass(kept, grad):
    return (grad,)

def back_keep(v):
    return (v, None)

def back_low(kept, grad):
    return (low(grad),)
low.defvjp(low_keep, low_pass)
low_back.defvjp(back_keep, back_low)

def matmul(left, right):
    return jnp.dot(left, right, precision=HIGH)

def rms_norm(values, gain):
    return values * lax.rsqrt(lax.optimization_barrier(jnp.mean(values * values, -1, keepdims=True)) + EPSILON) * gain

def rotation(positions):
    half = HDIM // 2
    index = jnp.arange(half).astype(jnp.float32)
    inverse = jnp.exp(index * (-math.log(10000.0) / half))
    angles = positions.astype(jnp.float32)[:, None] * inverse[None, :]
    return (jnp.cos(angles), jnp.sin(angles))

def rotate(vectors, cosine, sine):
    half = HDIM // 2
    first = vectors[..., :half]
    second = vectors[..., half:]
    cos_b = cosine[:, None, :]
    sin_b = sine[:, None, :]
    return jnp.concatenate([first * cos_b - second * sin_b, second * cos_b + first * sin_b], -1)

def reference(tokens, cotangent, lengths, span_order, attn_gain, query_heads, query_dims, key_heads, key_dims, value_heads, value_dims, out_proj, ffn_gain, gate_proj, up_proj, down_proj):
    positions = (span_order.reshape(-1)[:, None] * SPAN + jnp.arange(SPAN, dtype=jnp.int32)[None, :]).reshape(-1).astype(jnp.int32)
    cosine, sine = rotation(positions)
    block = math.gcd(SLOTS, 512)
    nblocks = SLOTS // block

    def forward(inputs, params):
        gain1, w_qh, w_qd, w_kh, w_kd, w_vh, w_vd, w_out, gain2, w_gate, w_up, w_down = params

        def one_row(pair):
            row_x, length = pair
            normed = low(rms_norm(row_x, gain1))
            q_heads = low_back(matmul(normed, w_qh)).reshape(SLOTS, QRANK, HEADS)
            q_dims = low_back(matmul(normed, w_qd)).reshape(SLOTS, QRANK, HDIM)
            q_rot = rotate(q_dims, cosine, sine)
            queries = low(jnp.einsum('trh,trd->thd', q_heads, q_rot, precision=HIGH) / QRANK)
            k_heads = low(low_back(matmul(normed, w_kh))).reshape(SLOTS, KVRANK, HEADS)
            k_dims = low(rotate(low_back(matmul(normed, w_kd)).reshape(SLOTS, KVRANK, HDIM), cosine, sine))
            v_heads = low(low_back(matmul(normed, w_vh))).reshape(SLOTS, KVRANK, HEADS)
            v_dims = low(low_back(matmul(normed, w_vd))).reshape(SLOTS, KVRANK, HDIM)
            keys = low(jnp.einsum('krh,krd->khd', k_heads, k_dims, precision=HIGH) / KVRANK)
            values = low(jnp.einsum('krh,krd->khd', v_heads, v_dims, precision=HIGH) / KVRANK)
            key_live = positions < length

            def attend(args):
                query_block, query_pos = args
                raw = jnp.einsum('qhd,khd->hqk', query_block, keys, precision=HIGH) * 0.125
                valid = (positions[None, :] <= query_pos[:, None]) & key_live[None, :]
                scores = low_back(jnp.where(valid[None], raw, NEG_LARGE))
                probs = jax.nn.softmax(scores, axis=-1)
                mixed = jnp.einsum('hqk,khd->qhd', low(probs), values, precision=HIGH)
                return low(low_back(mixed))
            mixed = lax.map(jax.checkpoint(attend), (queries.reshape(nblocks, block, HEADS, HDIM), positions.reshape(nblocks, block)))
            heads_out = mixed.reshape(SLOTS, D)
            resid = row_x + low_back(matmul(heads_out, w_out))
            normed2 = low(rms_norm(resid, gain2))
            gate = low_back(matmul(normed2, w_gate))
            up = low_back(matmul(normed2, w_up))
            hidden = low(jax.nn.silu(gate) * up)
            return resid + matmul(hidden, w_down)
        return lax.map(jax.checkpoint(one_row), (inputs, lengths))
    params = tuple((weight.astype(jnp.float32) for weight in (attn_gain, query_heads, query_dims, key_heads, key_dims, value_heads, value_dims, out_proj, ffn_gain, gate_proj, up_proj, down_proj)))
    result, pullback = jax.vjp(forward, tokens.astype(jnp.float32), params)
    input_grad, grads = pullback(cotangent.astype(jnp.float32))
    return (result.astype(jnp.bfloat16), input_grad, grads[0], grads[1], grads[2], grads[3], grads[4], grads[5], grads[6], grads[7], grads[8], grads[9], grads[10], grads[11])
```

```python
import functools
import math

import jax
import jax.numpy as jnp
from jax import lax
from jax.experimental import pallas as pl
from jax.experimental.pallas import tpu as pltpu
from jax.sharding import PartitionSpec as P


MESH = pl.DeviceIdType.MESH
NZ, NX = 4, 2

class Place:
    def __init__(self):
        self.seq = lax.axis_index("seq")
        self.batch = lax.axis_index("batch")
        self.z = self.seq // 2
        self.x = lax.rem(self.seq, 2)
        self.y = self.batch // 2
        self.c = lax.rem(self.batch, 2)
        self.up = (jnp.minimum(self.seq + 2, 7), self.batch)
        self.down = (jnp.maximum(self.seq - 2, 0), self.batch)
        self.xp = (self.seq + 1 - 2 * self.x, self.batch)
        self.yp = (self.seq, lax.rem(self.batch + 2, 4))
        self.cp = (self.seq, self.batch + 1 - 2 * self.c)

def greet(me):
    bar = pltpu.get_barrier_semaphore()
    def sig(d):
        pl.semaphore_signal(bar, inc=1, device_id=d, device_id_type=MESH)
    pl.when(me.z < NZ - 1)(lambda: sig(me.up))
    pl.when(me.z > 0)(lambda: sig(me.down))
    sig(me.xp); sig(me.yp); sig(me.cp)
    ends = (me.z == 0) | (me.z == NZ - 1)
    pl.semaphore_wait(bar, jnp.where(ends, 4, 5))

def piece(ref, spec, y, c):
    flow, axis, size = spec
    part = (2 * y + c, size // 4) if flow == "P" else (c, size // 2)
    start = pl.multiple_of(part[0] * part[1], part[1])
    idx = [slice(None)] * 2
    idx[axis] = pl.ds(start, part[1])
    return ref.at[tuple(idx)]

def gather_kernel(specs, order, *refs):
    n = len(specs)
    ins, outs = refs[:n], refs[n:2 * n]
    zs, zr, xs, xr, ys, yr, cs, cr, ls = refs[2 * n:]
    me = Place()
    greet(me)
    sends = []
    def remote(cond, src, dst, ss, rs, dev):
        cp = lambda: pltpu.make_async_remote_copy(src_ref=src, dst_ref=dst, send_sem=ss, recv_sem=rs, device_id=dev, device_id_type=MESH)
        if cond is None:
            cp().start()
        else:
            pl.when(cond)(lambda: cp().start())
        sends.append((cond, cp))
    def recv(src, dst, rs, dev):
        pltpu.make_async_remote_copy(src_ref=dst, dst_ref=dst, send_sem=rs, recv_sem=rs, device_id=dev, device_id_type=MESH).wait_recv()
    def view(a, shard, y, c):
        return piece(outs[a].at[shard], specs[a], y, c)
    own = [piece(ins[a], specs[a], me.y, me.c) for a in range(n)]
    for a in order:
        dst = view(a, me.seq, me.y, me.c)
        remote(me.z < NZ - 1, own[a], dst, zs.at[a, 0, 0], zr.at[a, 0, 0], me.up)
        remote(me.z > 0, own[a], dst, zs.at[a, 1, 0], zr.at[a, 1, 0], me.down)
        remote(None, own[a], dst, xs.at[a, me.z], xr.at[a, me.z], me.xp)
    for a in range(n):
        pltpu.make_async_copy(ins[a], outs[a].at[me.seq], ls.at[a]).start()
    def onward(a, shard, cond, wave):
        v = view(a, shard, me.y, me.c)
        if specs[a][0] == "P":
            remote(cond, v, v, ys.at[a, shard], yr.at[a, shard], me.yp)
        remote(cond, v, v, cs.at[a, 0, shard], cr.at[a, 0, shard], me.cp)
    def zstep(a, k):
        for d, (cond, zz, frm, fwd_ok, to) in enumerate((
            (me.z - k >= 0, me.z - k, me.down, me.z < NZ - 1, me.up),
            (me.z + k < NZ, me.z + k, me.up, me.z > 0, me.down))):
            zz = jnp.clip(zz, 0, NZ - 1)
            shard = 2 * zz + me.x
            v = view(a, shard, me.y, me.c)
            pl.when(cond)(lambda: recv(v, v, zr.at[a, d, k - 1], frm))
            if k < NZ - 1:
                remote(cond & fwd_ok, v, v, zs.at[a, d, k], zr.at[a, d, k], to)
            remote(cond, v, v, xs.at[a, zz], xr.at[a, zz], me.xp)
            onward(a, shard, cond, 0)
    def xstep(a, k):
        alts = ((None, me.z),) if k == 0 else ((me.z - k >= 0, me.z - k), (me.z + k < NZ, me.z + k))
        for cond, zz in alts:
            zz = jnp.clip(zz, 0, NZ - 1)
            shard = 2 * zz + 1 - me.x
            v = view(a, shard, me.y, me.c)
            if cond is None:
                recv(v, v, xr.at[a, zz], me.xp)
            else:
                pl.when(cond)(lambda: recv(v, v, xr.at[a, zz], me.xp))
            onward(a, shard, cond, 1)
    def ystep(a, cond, shard):
        v = view(a, shard, 1 - me.y, me.c)
        def go():
            recv(v, v, yr.at[a, shard], me.yp)
        if cond is None: go()
        else: pl.when(cond)(go)
        remote(cond, v, v, cs.at[a, 1, shard], cr.at[a, 1, shard], me.cp)
    def ysteps(a, k, which):
        if specs[a][0] != "P": return
        if which == "z":
            for cond, zz in ((me.z - k >= 0, me.z - k), (me.z + k < NZ, me.z + k)):
                ystep(a, cond, 2 * jnp.clip(zz, 0, NZ - 1) + me.x)
        elif k == 0:
            ystep(a, None, 2 * me.z + 1 - me.x)
        else:
            for cond, zz in ((me.z - k >= 0, me.z - k), (me.z + k < NZ, me.z + k)):
                ystep(a, cond, 2 * jnp.clip(zz, 0, NZ - 1) + 1 - me.x)
    for k in range(1, NZ + 2):
        for a in order:
            if k < NZ: zstep(a, k)
            if k - 1 < NZ: xstep(a, k - 1)
        for a in order:
            if 1 <= k - 1 < NZ: ysteps(a, k - 1, "z")
            if 0 <= k - 2 < NZ: ysteps(a, k - 2, "x")
    for a in range(n):
        for k in range(1, NZ):
            for cond, zz in ((me.z - k >= 0, me.z - k), (me.z + k < NZ, me.z + k)):
                shard = 2 * jnp.clip(zz, 0, NZ - 1) + me.x
                for w in range(2 if specs[a][0] == "P" else 1):
                    v = view(a, shard, me.y if w == 0 else 1 - me.y, 1 - me.c)
                    pl.when(cond)(lambda: recv(v, v, cr.at[a, w, shard], me.cp))
        for zz in range(NZ):
            shard = 2 * zz + 1 - me.x
            for w in range(2 if specs[a][0] == "P" else 1):
                v = view(a, shard, me.y if w == 0 else 1 - me.y, 1 - me.c)
                recv(v, v, cr.at[a, w, shard], me.cp)
        pltpu.make_async_copy(ins[a], outs[a].at[me.seq], ls.at[a]).wait()
    for cond, cp in sends:
        if cond is None: cp().wait_send()
        else: pl.when(cond)(lambda: cp().wait_send())

def gather_weights(arrays, specs, order, cid):
    n = len(arrays)
    DMA = pltpu.SemaphoreType.DMA
    return pl.pallas_call(
        functools.partial(gather_kernel, specs, order),
        out_shape=[jax.ShapeDtypeStruct((8, *a.shape), a.dtype) for a in arrays],
        in_specs=[pl.BlockSpec(memory_space=pl.ANY)] * n,
        out_specs=[pl.BlockSpec(memory_space=pl.ANY)] * n,
        scratch_shapes=[DMA((n, 2, 3)), DMA((n, 2, 3)), DMA((n, 4)), DMA((n, 4)), DMA((n, 8)), DMA((n, 8)), DMA((n, 2, 8)), DMA((n, 2, 8)), DMA((n,))],
        compiler_params=pltpu.CompilerParams(collective_id=cid, has_side_effects=True),
        name="gather_weights",
    )(*arrays)

class Unit:
    def __init__(self, arr, row, col, flow, axis):
        self.arr, self.row, self.col, self.flow, self.axis = arr, row, col, flow, axis
        self.shape = (row[1], col[1])
        h = list(self.shape); h[axis] //= 2
        self.half = tuple(h)
        q = list(h)
        if flow == "P": q[axis] //= 2
        self.piece = tuple(q)

def rect(unit, ref, part, nparts):
    start = [unit.row[0], unit.col[0]]
    size = list(unit.shape)
    size[unit.axis] //= nparts
    idx = []
    for d in range(2):
        if d == unit.axis:
            off = part * size[d] + start[d]
            idx.append(pl.ds(pl.multiple_of(off, 16 if d == 0 else 128), size[d]))
        else:
            idx.append(pl.ds(start[d], size[d]))
    return ref.at[tuple(idx)]

def reduce_kernel(units, narr, *refs):
    ins, outs = refs[:narr], refs[narr:2 * narr]
    nu = len(units)
    pos = 2 * narr
    A, RC, RY, RX, RZ, RF = [refs[pos + i * nu: pos + (i + 1) * nu] for i in range(6)]
    pos += 6 * nu
    ls, cs, cr, ys, yr, xs, xr, zs, zr, fs, fr, os_ = refs[pos:]
    me = Place()
    greet(me)
    def remote(src, dst, ss, rs, dev):
        return pltpu.make_async_remote_copy(src_ref=src, dst_ref=dst, send_sem=ss, recv_sem=rs, device_id=dev, device_id_type=MESH)
    def shard_at(i):
        zz = lax.rem(me.z + 1 + i // 2, NZ)
        xx = lax.rem(1 - me.x + lax.rem(i, 2), 2)
        return zz, xx, 2 * zz + xx
    def sub(u, ref, y):
        if u.flow == "R":
            return ref
        n = u.piece[u.axis]
        idx = [slice(None)] * 2
        idx[u.axis] = pl.ds(pl.multiple_of(y * n, n), n)
        return ref.at[tuple(idx)]
    def core_copy(k, i):
        u = units[k]; zz, xx, s = shard_at(i)
        return remote(rect(u, ins[u.arr].at[s], 1 - me.c, 2), RC[k].at[s], cs.at[k, s], cr.at[k, s], me.cp)
    def local_copy(k, i):
        u = units[k]; zz, xx, s = shard_at(i)
        return pltpu.make_async_copy(rect(u, ins[u.arr].at[s], me.c, 2), A[k].at[s], ls.at[k, s])
    def y_copy(k, i):
        u = units[k]; zz, xx, s = shard_at(i)
        return remote(sub(u, A[k].at[s], 1 - me.y), RY[k].at[s], ys.at[k, s], yr.at[k, s], me.yp)
    def x_copy(k, zz):
        u = units[k]
        return remote(sub(u, A[k].at[2 * zz + 1 - me.x], me.y), RX[k].at[zz], xs.at[k, zz], xr.at[k, zz], me.xp)
    def z_copy(k, d, zz):
        u = units[k]
        return remote(sub(u, A[k].at[2 * zz + me.x], me.y), RZ[k].at[d, zz], zs.at[k, d, zz], zr.at[k, d, zz], me.up if d == 0 else me.down)
    def add(dst, src):
        dst[...] = dst[...] + src[...]
    def start_core(k):
        def body(i, c):
            core_copy(k, i).start()
            local_copy(k, i).start()
            return c
        lax.fori_loop(0, 8, body, 0)
    def core_stage(k):
        u = units[k]
        def body(i, c):
            zz, xx, s = shard_at(i)
            local_copy(k, i).wait()
            core_copy(k, i).wait_recv()
            add(A[k].at[s], RC[k].at[s])
            if u.flow == "P":
                y_copy(k, i).start()
            else:
                @pl.when(xx != me.x)
                def _(): x_copy(k, zz).start()
            return c
        lax.fori_loop(0, 8, body, 0)
    def y_stage(k):
        u = units[k]
        def body(i, c):
            zz, xx, s = shard_at(i)
            y_copy(k, i).wait_recv()
            add(sub(u, A[k].at[s], me.y), RY[k].at[s])
            @pl.when(xx != me.x)
            def _(): x_copy(k, zz).start()
            return c
        lax.fori_loop(0, 8, body, 0)
    def x_stage(k):
        u = units[k]
        def body(i, c):
            zz = lax.rem(me.z + 1 + i, NZ)
            x_copy(k, zz).wait_recv()
            add(sub(u, A[k].at[2 * zz + me.x], me.y), RX[k].at[zz])
            @pl.when((me.z == 0) & (zz > 0))
            def _(): z_copy(k, 0, zz).start()
            @pl.when((me.z == NZ - 1) & (zz < NZ - 1))
            def _(): z_copy(k, 1, zz).start()
            return c
        lax.fori_loop(0, NZ, body, 0)
    def z_stage(k):
        u = units[k]
        def body(i, c):
            up, down = NZ - 1 - i, i
            @pl.when((up > me.z) & (me.z > 0))
            def _():
                z_copy(k, 0, up).wait_recv()
                add(sub(u, A[k].at[2 * up + me.x], me.y), RZ[k].at[0, up])
                z_copy(k, 0, up).start()
            @pl.when((down < me.z) & (me.z < NZ - 1))
            def _():
                z_copy(k, 1, down).wait_recv()
                add(sub(u, A[k].at[2 * down + me.x], me.y), RZ[k].at[1, down])
                z_copy(k, 1, down).start()
            return c
        lax.fori_loop(0, NZ, body, 0)
    def fin_y(k):
        u = units[k]; mine = sub(u, A[k].at[me.seq], me.y)
        if u.flow == "P":
            dst = rect(u, outs[u.arr], 2 * me.c + me.y, 4)
            return remote(mine, dst, fs.at[k, 0], fr.at[k, 0], me.yp)
        return remote(mine, RF[k], fs.at[k, 0], fr.at[k, 0], me.yp)
    def fin_c(k, w):
        u = units[k]
        if u.flow == "P":
            if w == 0:
                return remote(sub(u, A[k].at[me.seq], me.y), rect(u, outs[u.arr], 2 * me.c + me.y, 4), fs.at[k, 1], fr.at[k, 1], me.cp)
            v = rect(u, outs[u.arr], 2 * me.c + 1 - me.y, 4)
            return remote(v, v, fs.at[k, 2], fr.at[k, 2], me.cp)
        v = rect(u, outs[u.arr], me.c, 2)
        return remote(RF[k], v, fs.at[k, 1], fr.at[k, 1], me.cp)
    def out_copy(k):
        u = units[k]
        if u.flow == "P":
            return pltpu.make_async_copy(sub(u, A[k].at[me.seq], me.y), rect(u, outs[u.arr], 2 * me.c + me.y, 4), os_.at[k])
        return pltpu.make_async_copy(RF[k], rect(u, outs[u.arr], me.c, 2), os_.at[k])
    def own_stage(k):
        u = units[k]
        @pl.when(me.z > 0)
        def _():
            z_copy(k, 0, me.z).wait_recv()
            add(sub(u, A[k].at[me.seq], me.y), RZ[k].at[0, me.z])
        @pl.when(me.z < NZ - 1)
        def _():
            z_copy(k, 1, me.z).wait_recv()
            add(sub(u, A[k].at[me.seq], me.y), RZ[k].at[1, me.z])
        fin_y(k).start()
        if u.flow == "P":
            out_copy(k).start()
            fin_c(k, 0).start()
    def last_stage(k):
        u = units[k]
        fin_y(k).wait_recv()
        if u.flow == "P":
            fin_c(k, 1).start()
        else:
            add(RF[k], A[k].at[me.seq])
            out_copy(k).start()
            fin_c(k, 0).start()
    def end_stage(k):
        u = units[k]
        fin_c(k, 0).wait_recv()
        fin_c(k, 0).wait_send()
        if u.flow == "P":
            fin_c(k, 1).wait_recv()
            fin_c(k, 1).wait_send()
        out_copy(k).wait()
        fin_y(k).wait_send()
        def body(i, c):
            core_copy(k, i).wait_send()
            if u.flow == "P": y_copy(k, i).wait_send()
            return c
        lax.fori_loop(0, 8, body, 0)
        def body(zz, c):
            x_copy(k, zz).wait_send()
            @pl.when((zz > me.z))
            def _(): z_copy(k, 0, zz).wait_send()
            @pl.when((zz < me.z))
            def _(): z_copy(k, 1, zz).wait_send()
            return c
        lax.fori_loop(0, NZ, body, 0)
    for k in range(nu): start_core(k)
    for k in range(nu): core_stage(k)
    Ps = [k for k in range(nu) if units[k].flow == "P"]
    Rs = [k for k in range(nu) if units[k].flow == "R"]
    for i in range(max(len(Ps), len(Rs))):
        if i < len(Ps): y_stage(Ps[i])
        if i < len(Rs): x_stage(Rs[i]);
        if i < len(Rs): z_stage(Rs[i])
    for k in Rs: own_stage(k)
    for k in Ps:
        x_stage(k); z_stage(k)
    for k in Rs: last_stage(k)
    for k in Ps: own_stage(k)
    for k in Ps: last_stage(k)
    for k in range(nu): end_stage(k)

def reduce_weights(arrays, units, cid):
    narr, nu = len(arrays), len(units)
    DMA = pltpu.SemaphoreType.DMA
    bf = jnp.bfloat16
    V = pltpu.VMEM
    scratch = ([V((8, *u.half), bf) for u in units] + [V((8, *u.half), bf) for u in units]
        + [V((8, *u.piece) if u.flow == "P" else (16, 128), bf) for u in units] + [V((4, *u.piece), bf) for u in units]
        + [V((2, 4, *u.piece), bf) for u in units] + [V(u.piece if u.flow == "R" else (16, 128), bf) for u in units]
        + [DMA((nu, 8))] * 5 + [DMA((nu, 4))] * 2 + [DMA((nu, 2, 4))] * 2 + [DMA((nu, 3))] * 2 + [DMA((nu,))])
    return pl.pallas_call(
        functools.partial(reduce_kernel, units, narr),
        out_shape=[jax.ShapeDtypeStruct(a.shape[1:], a.dtype) for a in arrays],
        in_specs=[pl.BlockSpec(memory_space=pl.ANY)] * narr,
        out_specs=[pl.BlockSpec(memory_space=pl.ANY)] * narr,
        scratch_shapes=scratch,
        compiler_params=pltpu.CompilerParams(collective_id=cid, has_side_effects=True, vmem_limit_bytes=58 << 20),
        name="reduce_weights",
    )(*arrays)

def gather_rows_kernel(src, out, zs, zr, xs, xr, ls):
    me = Place()
    greet(me)
    rows = src.shape[0]
    def remote(s, b, ss, rs, dev):
        v = out.at[s, b]
        return pltpu.make_async_remote_copy(src_ref=v, dst_ref=v, send_sem=ss, recv_sem=rs, device_id=dev, device_id_type=MESH)
    def first(b, ss, rs, dev):
        return pltpu.make_async_remote_copy(src_ref=src.at[b], dst_ref=out.at[me.seq, b], send_sem=ss, recv_sem=rs, device_id=dev, device_id_type=MESH)
    sends = []
    def start(cond, mk):
        pl.when(cond)(lambda: mk().start())
        sends.append((cond, mk))
    for b in range(rows):
        start(me.z < NZ - 1, functools.partial(first, b, zs.at[b, 0, 0], zr.at[b, 0, 0], me.up))
        start(me.z > 0, functools.partial(first, b, zs.at[b, 1, 0], zr.at[b, 1, 0], me.down))
        start(me.z >= 0, functools.partial(first, b, xs.at[b, me.z], xr.at[b, me.z], me.xp))
    for b in range(rows):
        pltpu.make_async_copy(src.at[b], out.at[me.seq, b], ls.at[b]).start()
    for k in range(1, NZ):
        for b in range(rows):
            for d, (cond, zz, fwd, to) in enumerate((
                (me.z - k >= 0, me.z - k, me.z < NZ - 1, me.up),
                (me.z + k < NZ, me.z + k, me.z > 0, me.down))):
                zz = jnp.clip(zz, 0, NZ - 1)
                s = 2 * zz + me.x
                pl.when(cond)(lambda: remote(s, b, zr.at[b, d, k - 1], zr.at[b, d, k - 1], to).wait_recv())
                if k < NZ - 1:
                    start(cond & fwd, functools.partial(remote, s, b, zs.at[b, d, k], zr.at[b, d, k], to))
                start(cond, functools.partial(remote, s, b, xs.at[b, zz], xr.at[b, zz], me.xp))
    for b in range(rows):
        for zz in range(NZ):
            remote(2 * zz + 1 - me.x, b, xs.at[b, zz], xr.at[b, zz], me.xp).wait_recv()
        pltpu.make_async_copy(src.at[b], out.at[me.seq, b], ls.at[b]).wait()
    for cond, mk in sends:
        pl.when(cond)(lambda: mk().wait_send())

def gather_rows(a, cid):
    DMA = pltpu.SemaphoreType.DMA
    r = a.shape[0]
    return pl.pallas_call(
        gather_rows_kernel,
        out_shape=jax.ShapeDtypeStruct((8, *a.shape), a.dtype),
        in_specs=[pl.BlockSpec(memory_space=pl.ANY)],
        out_specs=pl.BlockSpec(memory_space=pl.ANY),
        scratch_shapes=[DMA((r, 2, 3)), DMA((r, 2, 3)), DMA((r, 4)), DMA((r, 4)), DMA((r,))],
        compiler_params=pltpu.CompilerParams(collective_id=cid, has_side_effects=True),
        name="gather_rows",
    )(a)

def reduce_rows_kernel(src, out, A, RX, RZ, xs, xr, zs, zr, ls):
    me = Place()
    greet(me)
    rows = src.shape[1]
    def remote(s, d, ss, rs, dev):
        return pltpu.make_async_remote_copy(src_ref=s, dst_ref=d, send_sem=ss, recv_sem=rs, device_id=dev, device_id_type=MESH)
    def local(b, zz):
        return pltpu.make_async_copy(src.at[2 * zz + me.x, b], A.at[b, zz], ls.at[b, zz])
    def x_copy(b, zz):
        return remote(src.at[2 * zz + 1 - me.x, b], RX.at[b, zz], xs.at[b, zz], xr.at[b, zz], me.xp)
    def z_copy(b, d, zz):
        return remote(A.at[b, zz], RZ.at[b, d, zz], zs.at[b, d, zz], zr.at[b, d, zz], me.up if d == 0 else me.down)
    def add(dst, more):
        dst[...] = dst[...] + more[...]
    def turn(i):
        return lax.rem(me.z + 1 + i, NZ)
    def begin(i, c):
        for b in range(rows):
            x_copy(b, turn(i)).start()
            local(b, turn(i)).start()
        return c
    lax.fori_loop(0, NZ, begin, 0)
    for b in range(rows):
        def arrive(i, c):
            zz = turn(i)
            local(b, zz).wait()
            x_copy(b, zz).wait_recv()
            add(A.at[b, zz], RX.at[b, zz])
            pl.when((me.z == 0) & (zz > 0))(lambda: z_copy(b, 0, zz).start())
            pl.when((me.z == NZ - 1) & (zz < NZ - 1))(lambda: z_copy(b, 1, zz).start())
            return c
        lax.fori_loop(0, NZ, arrive, 0)
    for b in range(rows):
        def pass_on(i, c):
            up, down = NZ - 1 - i, i
            @pl.when((up > me.z) & (me.z > 0))
            def _():
                z_copy(b, 0, up).wait_recv()
                add(A.at[b, up], RZ.at[b, 0, up])
                z_copy(b, 0, up).start()
            @pl.when((down < me.z) & (me.z < NZ - 1))
            def _():
                z_copy(b, 1, down).wait_recv()
                add(A.at[b, down], RZ.at[b, 1, down])
                z_copy(b, 1, down).start()
            return c
        lax.fori_loop(0, NZ, pass_on, 0)
    for b in range(rows):
        @pl.when(me.z > 0)
        def _():
            z_copy(b, 0, me.z).wait_recv()
            add(A.at[b, me.z], RZ.at[b, 0, me.z])
        @pl.when(me.z < NZ - 1)
        def _():
            z_copy(b, 1, me.z).wait_recv()
            add(A.at[b, me.z], RZ.at[b, 1, me.z])
        out[b] = A[b, me.z]
        def sent(zz, c):
            x_copy(b, zz).wait_send()
            pl.when(zz > me.z)(lambda: z_copy(b, 0, zz).wait_send())
            pl.when(zz < me.z)(lambda: z_copy(b, 1, zz).wait_send())
            return c
        lax.fori_loop(0, NZ, sent, 0)

def reduce_rows(a, cid):
    DMA = pltpu.SemaphoreType.DMA
    shape = a.shape[1:]
    r = shape[0]
    V = pltpu.VMEM
    return pl.pallas_call(
        reduce_rows_kernel,
        out_shape=jax.ShapeDtypeStruct(shape, a.dtype),
        in_specs=[pl.BlockSpec(memory_space=pl.ANY)],
        out_specs=pl.BlockSpec(memory_space=pltpu.VMEM),
        scratch_shapes=[V((r, 4, *shape[1:]), a.dtype), V((r, 4, *shape[1:]), a.dtype), V((r, 2, 4, *shape[1:]), a.dtype),
                        DMA((r, 4)), DMA((r, 4)), DMA((r, 2, 4)), DMA((r, 2, 4)), DMA((r, 4))],
        compiler_params=pltpu.CompilerParams(collective_id=cid, has_side_effects=True, vmem_limit_bytes=32 << 20),
        name="reduce_rows",
    )(a)
F32, BF16 = jnp.float32, jnp.bfloat16
NEG = -1e30

def nn(a, b):
    return lax.dot_general(a, b, (((1,), (0,)), ((), ())), preferred_element_type=F32)

def nt(a, b):
    return lax.dot_general(a, b, (((1,), (1,)), ((), ())), preferred_element_type=F32)

def expand(heads, dims, base):
    parts = []
    for h in range(2):
        parts.append((heads[base + h:base + h + 1] * dims[0] + heads[base + 2 + h:base + 3 + h] * dims[1]) * 0.5)
    return jnp.concatenate(parts, 0)

def queries(qh, qr):
    parts = []
    for h in range(2):
        total = qh[h:h + 1] * qr[0:64]
        for r in range(1, 6):
            total = total + qh[2 * r + h:2 * r + h + 1] * qr[64 * r:64 * r + 64]
        parts.append(total)
    return jnp.concatenate(parts, 0) / 6.0

def lanes_below(shape, n):
    return lax.broadcasted_iota(jnp.int32, shape, 1) < n

def stack_heads(part):
    first = lanes_below(part.shape, 64)
    zero = jnp.zeros_like(part)
    return jnp.concatenate([jnp.where(first, part, zero), jnp.where(first, zero, part)], 0)

def unstack_heads(part):
    n = part.shape[0] // 2
    return jnp.where(lanes_below((n, 128), 64), part[:n], part[n:])

def causal_bias(n2, span):
    row = lax.broadcasted_iota(jnp.int32, (n2, span), 0) % span
    col = lax.broadcasted_iota(jnp.int32, (n2, span), 1)
    return jnp.where(col <= row, 0.0, NEG)

def pair_factors(heads, dims, cond, base, at):
    hl, hs = heads
    dl, ds = dims
    low = expand(hl, (dl[at:at + 64].astype(F32), dl[at + 64:at + 128].astype(F32)), base).astype(BF16)
    sel = expand(hs, (ds[at:at + 64].astype(F32), ds[at + 64:at + 128].astype(F32)), base)
    left = jnp.where(cond > 0.5, sel, 0.0).astype(BF16)
    right = jnp.where(cond > 0.5, 0.0, sel).astype(BF16)
    return low, jnp.concatenate([left, right], 0)

def attend_kernel(span, chunk, qh_ref, qr_ref, hl_ref, hs_ref, dl_ref, ds_ref, cond_ref, bl_ref, bs_ref, o_ref, lse_ref, s1, s2):
    p = pl.program_id(1)
    n2 = 2 * span
    nk = dl_ref.shape[-1]
    qt = queries(qh_ref[0, 0], qr_ref[0])
    q = (qt.T.astype(BF16) * BF16(0.125)) if False else (qt.astype(BF16).astype(F32).T * 0.125).astype(BF16)
    qlo, qhi = stack_heads(q[:span]), stack_heads(q[span:])
    qboth = jnp.concatenate([qlo, qhi], 1)
    heads = (hl_ref[0, 0], hs_ref[0, 0])
    dims = (dl_ref[0], ds_ref[0])
    cond = cond_ref[...]
    klo, ksel = pair_factors(heads, dims, cond, 0, 0)
    vlo, vsel = pair_factors(heads, dims, cond, 4, 128)
    tri = causal_bias(n2, span)
    width = min(128, chunk)
    mlo = jnp.full((n2, width), NEG, F32)
    mhi = jnp.full((n2, width), NEG, F32)
    s3 = nn(qlo, klo[:, :span]) + bl_ref[0][:, :span] + tri
    m3 = jnp.max(s3, -1, keepdims=True)
    for c in range(0, nk, chunk):
        sl = slice(c, c + chunk)
        a = nn(qhi, klo[:, sl]) + bl_ref[0][:, sl]
        s1[:, sl] = a
        b = nn(qboth, ksel[:, sl]) + bs_ref[0][:, sl]
        if c == 0:
            b = jnp.concatenate([b[:, :span] + tri, b[:, span:]], 1)
        s2[:, sl] = b
        for i in range(0, chunk, width):
            on = cond[:, c + i:c + i + width] > 0.5
            ai, bi = a[:, i:i + width], b[:, i:i + width]
            mlo = jnp.maximum(mlo, jnp.where(on, bi, NEG))
            mhi = jnp.maximum(mhi, jnp.maximum(ai, jnp.where(on, NEG, bi)))
    mlo = jnp.maximum(jnp.max(mlo, -1, keepdims=True), m3)
    mhi = jnp.max(mhi, -1, keepdims=True)
    e3 = jnp.exp(s3 - mlo)
    tlo = jnp.zeros((n2, width), F32)
    thi = jnp.zeros((n2, width), F32)
    o3 = nt(e3.astype(BF16), vlo[:, :span])
    o1 = jnp.zeros((n2, 128), F32)
    o2 = jnp.zeros((n2, 256), F32)
    for c in range(0, nk, chunk):
        sl = slice(c, c + chunk)
        on = cond[:, sl] > 0.5
        a = jnp.exp(s1[:, sl] - mhi)
        b = jnp.exp(s2[:, sl] - jnp.where(on, mlo, mhi))
        blo = jnp.where(on, b, 0.0)
        bhi = a + jnp.where(on, 0.0, b)
        for i in range(0, chunk, width):
            tlo = tlo + blo[:, i:i + width]
            thi = thi + bhi[:, i:i + width]
        o1 = o1 + nt(a.astype(BF16), vlo[:, sl])
        o2 = o2 + nt(b.astype(BF16), vsel[:, sl])
    llo = jnp.sum(tlo, -1, keepdims=True) + jnp.sum(e3, -1, keepdims=True)
    lhi = jnp.sum(thi, -1, keepdims=True)
    olo = unstack_heads((o2[:, :128] + o3) / llo)
    ohi = unstack_heads((o2[:, 128:] + o1) / lhi)
    o_ref[0] = jnp.concatenate([olo, ohi], 0).astype(BF16)
    lane = lax.broadcasted_iota(jnp.int32, (span, 128), 1)
    tlo = mlo + jnp.log(llo)
    thi = mhi + jnp.log(lhi)
    old = jnp.where(p == 0, 0.0, lse_ref[0])
    new = []
    for k, t in enumerate((tlo, thi)):
        part = old[k * span:(k + 1) * span]
        part = jnp.where(lane == 2 * p, t[:span], part)
        new.append(jnp.where(lane == 2 * p + 1, t[span:], part))
    lse_ref[0] = jnp.concatenate(new, 0)

def attend(qh, qr, hl, hs, dl, ds, cond, bl, bs):
    rows, pairs, _, nq = qh.shape
    nk = dl.shape[-1]
    span = nq // 2
    chunk = min(512, nk)
    full = lambda *s: pl.BlockSpec((1, *s), lambda b, p: (b, *([0] * len(s))))
    pairb = lambda *s: pl.BlockSpec((1, 1, *s), lambda b, p: (b, p, *([0] * len(s))))
    return pl.pallas_call(
        functools.partial(attend_kernel, span, chunk),
        grid=(rows, pairs),
        out_shape=[jax.ShapeDtypeStruct((rows, nq, pairs * 128), BF16), jax.ShapeDtypeStruct((rows, nq, 128), F32)],
        in_specs=[pairb(12, nq), full(384, nq), pairb(8, nk), pairb(8, nk), full(256, nk), full(256, nk),
                  pl.BlockSpec((1, nk), lambda b, p: (0, 0)), full(1, nk), full(1, nk)],
        out_specs=[pl.BlockSpec((1, nq, 128), lambda b, p: (b, 0, p)), full(nq, 128)],
        scratch_shapes=[pltpu.VMEM((nq, nk), F32), pltpu.VMEM((nq, nk), F32)],
        compiler_params=pltpu.CompilerParams(vmem_limit_bytes=56 << 20),
        name="attend",
    )(qh, qr, hl, hs, dl, ds, cond, bl, bs)

def attend_back_kernel(span, chunk, qh_ref, qr_ref, hl_ref, hs_ref, dl_ref, ds_ref, cond_ref, bl_ref, bs_ref, lse_ref, o_ref, g_ref,
                       dqh_ref, dqr_ref, dhl_ref, dhs_ref, ddl_ref, dds_ref):
    p = pl.program_id(1)
    n2 = 2 * span
    nk = dl_ref.shape[-1]
    qh, qr = qh_ref[0, 0], qr_ref[0]
    qt = (queries(qh, qr).astype(BF16).astype(F32)) * 0.125
    q = qt.T.astype(BF16)
    qlo, qhi = stack_heads(q[:span]), stack_heads(q[span:])
    qboth = jnp.concatenate([qlo, qhi], 1)
    g = g_ref[0]
    glo, ghi = stack_heads(g[:span]), stack_heads(g[span:])
    gboth = jnp.concatenate([glo, ghi], 1)
    gt = g.astype(F32).T
    first = lax.broadcasted_iota(jnp.int32, (128, span), 0) < 64
    def stack_lanes(part):
        return jnp.concatenate([jnp.where(first, part, 0.0), jnp.where(first, 0.0, part)], 1).astype(BF16)
    qtlo, qthi = stack_lanes(qt[:, :span]), stack_lanes(qt[:, span:])
    gtlo, gthi = stack_lanes(gt[:, :span]), stack_lanes(gt[:, span:])
    qtboth = jnp.concatenate([qtlo, qthi], 0)
    gtboth = jnp.concatenate([gtlo, gthi], 0)
    prod = g.astype(F32) * o_ref[0].astype(F32)
    flane = lanes_below((n2, 128), 64)
    d0 = jnp.sum(jnp.where(flane, prod, 0.0), -1, keepdims=True)
    d1 = jnp.sum(jnp.where(flane, 0.0, prod), -1, keepdims=True)
    lane = lax.broadcasted_iota(jnp.int32, (n2, 128), 1)
    lse = lse_ref[0]
    l0 = jnp.sum(jnp.where(lane == 2 * p, lse, 0.0), -1, keepdims=True)
    l1 = jnp.sum(jnp.where(lane == 2 * p + 1, lse, 0.0), -1, keepdims=True)
    dello, delhi = jnp.concatenate([d0[:span], d1[:span]], 0), jnp.concatenate([d0[span:], d1[span:]], 0)
    lselo, lsehi = jnp.concatenate([l0[:span], l1[:span]], 0), jnp.concatenate([l0[span:], l1[span:]], 0)
    heads = (hl_ref[0, 0], hs_ref[0, 0])
    dims = (dl_ref[0], ds_ref[0])
    cond = cond_ref[...]
    klo, ksel = pair_factors(heads, dims, cond, 0, 0)
    vlo, vsel = pair_factors(heads, dims, cond, 4, 128)
    tri = causal_bias(n2, span)

    @pl.when(p == 0)
    def _():
        dqr_ref[...] = jnp.zeros_like(dqr_ref)
        ddl_ref[...] = jnp.zeros_like(ddl_ref)
        dds_ref[...] = jnp.zeros_like(dds_ref)

    def put(dkt, h_ref, d_ref, hd_ref, dd_ref, base, at, sl):
        for r in range(2):
            dim = d_ref[0, at + 64 * r:at + 64 * r + 64, sl].astype(F32)
            total = None
            for h in range(2):
                part = dkt[64 * h:64 * h + 64]
                j = base + 2 * r + h
                hd_ref[0, 0, j:j + 1, sl] = jnp.sum(part * dim, 0, keepdims=True) * 0.5
                term = part * h_ref[0, 0, j:j + 1, sl]
                total = term if total is None else total + term
            dd_ref[0, at + 64 * r:at + 64 * r + 64, sl] += total * 0.5

    s3 = nn(qlo, klo[:, :span]) + bl_ref[0][:, :span] + tri
    p3 = jnp.exp(s3 - lselo)
    dp3 = nn(glo, vlo[:, :span])
    ds3 = (p3 * (dp3 - dello)).astype(BF16)
    p3 = p3.astype(BF16)
    dq3 = nt(ds3, klo[:, :span])
    dk3 = nn(qtlo, ds3)
    dv3 = nn(gtlo, p3)
    dq1 = jnp.zeros((n2, 128), F32)
    dq2 = jnp.zeros((n2, 256), F32)
    for c in range(0, nk, chunk):
        sl = slice(c, c + chunk)
        pa = jnp.exp(nn(qhi, klo[:, sl]) + bl_ref[0][:, sl] - lsehi)
        dpa = nn(ghi, vlo[:, sl])
        dsa = (pa * (dpa - delhi)).astype(BF16)
        pa = pa.astype(BF16)
        dq1 = dq1 + nt(dsa, klo[:, sl])
        dk = nn(qthi, dsa)
        dv = nn(gthi, pa)
        if c == 0:
            dk = jnp.concatenate([dk[:, :span] + dk3, dk[:, span:]], 1)
            dv = jnp.concatenate([dv[:, :span] + dv3, dv[:, span:]], 1)
        put(dk, hl_ref, dl_ref, dhl_ref, ddl_ref, 0, 0, sl)
        put(dv, hl_ref, dl_ref, dhl_ref, ddl_ref, 4, 128, sl)
    for c in range(0, nk, chunk):
        sl = slice(c, c + chunk)
        on = cond[:, sl] > 0.5
        s = nn(qboth, ksel[:, sl]) + bs_ref[0][:, sl]
        if c == 0:
            s = jnp.concatenate([s[:, :span] + tri, s[:, span:]], 1)
        pb = jnp.exp(s - jnp.where(on, lselo, lsehi))
        dpb = nn(gboth, vsel[:, sl])
        dsb = (pb * (dpb - jnp.where(on, dello, delhi))).astype(BF16)
        pb = pb.astype(BF16)
        dq2 = dq2 + nt(dsb, ksel[:, sl])
        dk = nn(qtboth, dsb)
        dv = nn(gtboth, pb)
        dk = jnp.where(on, dk[:128], dk[128:])
        dv = jnp.where(on, dv[:128], dv[128:])
        put(dk, hs_ref, ds_ref, dhs_ref, dds_ref, 0, 0, sl)
        put(dv, hs_ref, ds_ref, dhs_ref, dds_ref, 4, 128, sl)
    dqlo = unstack_heads(dq2[:, :128] + dq3)
    dqhi = unstack_heads(dq2[:, 128:] + dq1)
    dqt = (jnp.concatenate([dqlo, dqhi], 0) * (0.125 / 6.0)).T
    for r in range(6):
        total = None
        for h in range(2):
            part = dqt[64 * h:64 * h + 64]
            j = 2 * r + h
            dqh_ref[0, 0, j:j + 1, :] = jnp.sum(part * qr[64 * r:64 * r + 64], 0, keepdims=True)
            term = part * qh[j:j + 1]
            total = term if total is None else total + term
        dqr_ref[0, 64 * r:64 * r + 64, :] += total

def attend_back(qh, qr, hl, hs, dl, ds, cond, bl, bs, lse, o, g):
    rows, pairs, _, nq = qh.shape
    nk = dl.shape[-1]
    span = nq // 2
    chunk = min(512, nk)
    full = lambda *s: pl.BlockSpec((1, *s), lambda b, p: (b, *([0] * len(s))))
    pairb = lambda *s: pl.BlockSpec((1, 1, *s), lambda b, p: (b, p, *([0] * len(s))))
    tok = pl.BlockSpec((1, nq, 128), lambda b, p: (b, 0, p))
    sd = jax.ShapeDtypeStruct
    return pl.pallas_call(
        functools.partial(attend_back_kernel, span, chunk),
        grid=(rows, pairs),
        out_shape=[sd((rows, pairs, 12, nq), F32), sd((rows, 384, nq), F32), sd((rows, pairs, 8, nk), F32), sd((rows, pairs, 8, nk), F32),
                   sd((rows, 256, nk), F32), sd((rows, 256, nk), F32)],
        in_specs=[pairb(12, nq), full(384, nq), pairb(8, nk), pairb(8, nk), full(256, nk), full(256, nk),
                  pl.BlockSpec((1, nk), lambda b, p: (0, 0)), full(1, nk), full(1, nk), full(nq, 128), tok, tok],
        out_specs=[pairb(12, nq), full(384, nq), pairb(8, nk), pairb(8, nk), full(256, nk), full(256, nk)],
        compiler_params=pltpu.CompilerParams(vmem_limit_bytes=56 << 20),
        name="attend_back",
    )(qh, qr, hl, hs, dl, ds, cond, bl, bs, lse, o, g)

HEADS, HDIM, QRANK, KVRANK = 16, 64, 6, 2
PAIRS = HEADS // 2
EPSILON = 1e-06


def rms_forward(values, gain):
    scale = lax.rsqrt(jnp.mean(values * values, -1, keepdims=True) + EPSILON)
    unit = values * scale
    return (unit * gain, unit, scale)


def rms_backward(grad_out, unit, scale, gain):
    scaled = grad_out * gain
    grad_in = scale * (scaled - unit * jnp.mean(scaled * unit, -1, keepdims=True))
    return (grad_in, jnp.sum(grad_out * unit, 0))


def rotation(positions):
    half = HDIM // 2
    index = jnp.arange(half).astype(F32)
    inverse = jnp.exp(index * (-math.log(10000.0) / half))
    angles = inverse[:, None] * positions.astype(F32)[None, :]
    return (jnp.cos(angles), jnp.sin(angles))


def rotate(u, cosine, sine):
    rows, depth, slots = u.shape
    v = u.reshape(rows, depth // HDIM, HDIM, slots)
    a, b = v[:, :, :HDIM // 2], v[:, :, HDIM // 2:]
    return jnp.concatenate([a * cosine - b * sine, b * cosine + a * sine], 2).reshape(u.shape)


def dot(a, b, ca, cb):
    return lax.dot_general(a, b, ((ca, cb), ((), ())), preferred_element_type=F32)


def pair_rows(a, ranks):
    rows, _, n = a.shape
    return a.reshape(rows, ranks, PAIRS, 2, n).transpose(0, 2, 1, 3, 4).reshape(rows, PAIRS, ranks * 2, n)


def unpair_rows(a, ranks):
    rows, _, _, n = a.shape
    return a.reshape(rows, PAIRS, ranks, 2, n).transpose(0, 2, 1, 3, 4).reshape(rows, ranks * HEADS, n)


GATHER_SPECS = [("R", 0, 128), ("P", 0, 128), ("P", 0, 128), ("R", 0, 128), ("P", 1, 1024)]
REDUCE_UNITS = [
    Unit(4, (0, 176), (0, 1024), "P", 1), Unit(3, (0, 128), (0, 1408), "R", 0),
    Unit(4, (176, 176), (0, 1024), "P", 1), Unit(3, (0, 128), (1408, 1408), "R", 0),
    Unit(2, (0, 128), (0, 1408), "P", 0), Unit(1, (0, 128), (0, 1024), "R", 0),
    Unit(2, (0, 128), (1408, 1408), "P", 0), Unit(0, (0, 128), (0, 896), "R", 0)]


def gather_all(near, arrays):
    if near:
        return gather_weights(arrays, GATHER_SPECS, [0, 2, 4, 3, 1], 0)
    return [lax.all_gather(a, "seq", axis=0) for a in arrays]


def reduce_all(near, arrays):
    if near:
        return reduce_weights(arrays, REDUCE_UNITS, 1)
    out = []
    for a in arrays:
        own = lax.psum_scatter(a.astype(F32), "seq", scatter_dimension=0, tiled=True)[0]
        out.append(lax.psum(own.astype(BF16), "batch"))
    return out


def per_device(near, tokens, cotangent, lengths, span_order, attn_gain, query_heads, query_dims, key_heads, key_dims,
               value_heads, value_dims, out_proj, ffn_gain, gate_proj, up_proj, down_proj):
    rows, slots, width = tokens.shape
    span = slots // 2
    count = rows * slots
    nseq = span_order.shape[0]
    nk = nseq * span
    me = lax.axis_index("seq")
    small = jnp.concatenate([query_heads, query_dims, key_dims, value_dims, key_heads, value_heads, attn_gain[:, None], ffn_gain[:, None]], 1)
    small = jnp.pad(small, ((0, 0), (0, 896 - small.shape[1])))
    parts = gather_all(near, [small, out_proj, gate_proj, up_proj, down_proj])
    small, w_out, w_gate, w_up, w_down = [p.reshape(-1, p.shape[-1]) for p in parts]
    w_qkv = small[:, :800]
    gain_one = small[:, 800].astype(F32)
    gain_two = small[:, 801].astype(F32)

    offsets = jnp.arange(span, dtype=jnp.int32)
    spans = jnp.concatenate([span_order, span_order], 0)
    spans = lax.dynamic_slice_in_dim(spans, me, nseq, 0)
    local_pos = (spans[0][:, None] * span + offsets[None, :]).reshape(-1)
    cosine, sine = rotation(local_pos)
    chosen = spans[:, 0] < spans[0, 0]
    low_pos = (spans[:, 0][:, None] * span + offsets[None, :]).reshape(1, nk)
    sel_pos = (jnp.where(chosen, spans[:, 0], spans[:, 1])[:, None] * span + offsets[None, :]).reshape(1, nk)
    cond = jnp.repeat(chosen.astype(F32), span).reshape(1, nk)
    low_bias = jnp.where(low_pos < lengths[:, None], 0.0, NEG)[:, None, :]
    sel_bias = jnp.where(sel_pos < lengths[:, None], 0.0, NEG)[:, None, :]

    flat = tokens.reshape(count, width).astype(F32)
    normed_full, unit_one, scale_one = rms_forward(flat, gain_one)
    normed = normed_full.astype(BF16)
    by_row = normed.reshape(rows, slots, width)
    factors = jnp.stack([dot(w_qkv, by_row[b], (0,), (1,)) for b in range(rows)])
    qh = factors[:, :96]
    qr = rotate(factors[:, 96:480], cosine, sine)
    own = jnp.concatenate([rotate(factors[:, 480:608], cosine, sine), factors[:, 608:800]], 1).astype(BF16)
    shared = gather_rows(own, 2) if near else lax.all_gather(own, "seq", axis=0)
    shared = lax.dynamic_slice_in_dim(jnp.concatenate([shared, shared], 0), me, nseq, 0)
    low, high = shared[..., :span], shared[..., span:]
    sel = jnp.where(chosen[:, None, None, None], low, high)
    low = low.transpose(1, 2, 0, 3).reshape(rows, 320, nk)
    sel = sel.transpose(1, 2, 0, 3).reshape(rows, 320, nk)
    att = (pair_rows(qh, QRANK), qr, pair_rows(low[:, 256:].astype(F32), 4), pair_rows(sel[:, 256:].astype(F32), 4),
           low[:, :256], sel[:, :256], cond, low_bias, sel_bias)
    heads_out, lse = attend(*att)
    heads_flat = heads_out.reshape(count, width)

    resid = flat + dot(heads_flat, w_out, (1,), (0,))
    normed_two_full, unit_two, scale_two = rms_forward(resid, gain_two)
    normed_two = normed_two_full.astype(BF16)
    gate = dot(normed_two, w_gate, (1,), (0,))
    up_part = dot(normed_two, w_up, (1,), (0,))
    sigma = jax.nn.sigmoid(gate)
    hidden = (gate * sigma * up_part).astype(BF16)
    output = (resid + dot(hidden, w_down, (1,), (0,))).astype(BF16).reshape(rows, slots, width)

    grad_out = cotangent.reshape(count, width)
    down_grad = dot(hidden, grad_out, (0,), (0,)).astype(BF16)
    d_hidden = dot(grad_out, w_down, (1,), (1,))
    d_gate = (d_hidden * up_part * sigma * (1.0 + gate * (1.0 - sigma))).astype(BF16)
    d_up = (d_hidden * gate * sigma).astype(BF16)
    gate_grad = dot(normed_two, d_gate, (0,), (0,)).astype(BF16)
    up_grad = dot(normed_two, d_up, (0,), (0,)).astype(BF16)
    d_normed_two = dot(d_gate, w_gate, (1,), (1,)) + dot(d_up, w_up, (1,), (1,))
    d_mid, gain_two_grad = rms_backward(d_normed_two, unit_two, scale_two, gain_two)
    d_resid = grad_out.astype(F32) + d_mid
    d_attn = d_resid.astype(BF16)
    out_grad = dot(heads_flat, d_attn, (0,), (0,)).astype(BF16)
    d_heads = dot(d_attn, w_out, (1,), (1,)).astype(BF16).reshape(rows, slots, width)

    dqh, dqr, dhl, dhs, ddl, dds = attend_back(*att, lse, heads_out, d_heads)
    from_low = jnp.concatenate([ddl, unpair_rows(dhl, 4)], 1).reshape(rows, 320, nseq, span)
    from_sel = jnp.concatenate([dds, unpair_rows(dhs, 4)], 1).reshape(rows, 320, nseq, span)
    pick = chosen[None, None, :, None]
    both = jnp.concatenate([from_low + jnp.where(pick, from_sel, 0.0), jnp.where(pick, 0.0, from_sel)], -1)
    both = both.astype(BF16) if near else both
    both = both.transpose(2, 0, 1, 3)
    both = lax.dynamic_slice_in_dim(jnp.concatenate([both, both], 0), lax.rem(nseq - me, nseq), nseq, 0)
    mine = (reduce_rows(both, 3) if near else lax.psum_scatter(both, "seq", scatter_dimension=0, tiled=True)[0]).astype(F32)
    turned = jnp.concatenate([unpair_rows(dqh, QRANK), rotate(dqr, cosine, -sine), rotate(mine[:, :128], cosine, -sine), mine[:, 128:]], 1).astype(BF16)
    small_grad = dot(by_row, turned, (0, 1), (0, 2))
    d_normed = dot(turned, w_qkv, (1,), (1,)).reshape(count, width)
    d_first, gain_one_grad = rms_backward(d_normed, unit_one, scale_one, gain_one)
    input_grad = (d_resid + d_first).reshape(rows, slots, width)
    small_grad = jnp.concatenate([small_grad, gain_one_grad[:, None], gain_two_grad[:, None], jnp.zeros((width, 94), F32)], 1).astype(BF16)

    grads = [g.reshape(nseq, -1, g.shape[-1]) for g in (small_grad, out_grad, gate_grad, up_grad, down_grad)]
    small_sum, out_sum, gate_sum, up_sum, down_sum = [g.astype(F32) for g in reduce_all(near, grads)]
    return (output, input_grad, small_sum[:, 800], small_sum[:, :96], small_sum[:, 96:480], small_sum[:, 736:768], small_sum[:, 480:608],
            small_sum[:, 768:800], small_sum[:, 608:736], out_sum, small_sum[:, 801], gate_sum, up_sum, down_sum)


def solution(mesh):
    near = mesh.shape["seq"] == 8 and mesh.shape["batch"] == 4
    by_slot = P("batch", "seq", None)
    line, table = P("seq"), P("seq", None)
    return jax.shard_map(
        functools.partial(per_device, near),
        mesh=mesh,
        in_specs=(by_slot, by_slot, P("batch"), P(), line, *([table] * 7), line, *([table] * 3)),
        out_specs=(by_slot, by_slot, line, *([table] * 7), line, *([table] * 3)),
        check_vma=False,
    )
```

```python
import functools
import math

import jax
import jax.numpy as jnp
from jax import lax
from jax.experimental import pallas as pl
from jax.experimental.pallas import tpu as pltpu
from jax.sharding import PartitionSpec as P


MESH = pl.DeviceIdType.MESH
NZ, NX = 4, 2

class Place:
    def __init__(self):
        self.seq = lax.axis_index("seq")
        self.batch = lax.axis_index("batch")
        self.z = self.seq // 2
        self.x = lax.rem(self.seq, 2)
        self.y = self.batch // 2
        self.c = lax.rem(self.batch, 2)
        self.up = (jnp.minimum(self.seq + 2, 7), self.batch)
        self.down = (jnp.maximum(self.seq - 2, 0), self.batch)
        self.xp = (self.seq + 1 - 2 * self.x, self.batch)
        self.yp = (self.seq, lax.rem(self.batch + 2, 4))
        self.cp = (self.seq, self.batch + 1 - 2 * self.c)

    def along(self, k):
        return (2 * lax.rem(self.z + k, NZ) + self.x, self.batch)

def greet(me):
    bar = pltpu.get_barrier_semaphore()
    def sig(d):
        pl.semaphore_signal(bar, inc=1, device_id=d, device_id_type=MESH)
    for k in range(1, NZ):
        sig(me.along(k))
    sig(me.xp); sig(me.yp); sig(me.cp)
    pl.semaphore_wait(bar, NZ + 2)

def piece(ref, spec, y, c):
    flow, axis, size = spec
    part = (2 * y + c, size // 4) if flow == "P" else (c, size // 2)
    start = pl.multiple_of(part[0] * part[1], part[1])
    idx = [slice(None)] * 2
    idx[axis] = pl.ds(start, part[1])
    return ref.at[tuple(idx)]

def gather_kernel(specs, order, *refs):
    n = len(specs)
    ins, outs = refs[:n], refs[n:2 * n]
    zs, zr, xs, xr, ys, yr, cs, cr, ls = refs[2 * n:]
    me = Place()
    greet(me)
    sends = []
    def remote(cond, src, dst, ss, rs, dev):
        cp = lambda: pltpu.make_async_remote_copy(src_ref=src, dst_ref=dst, send_sem=ss, recv_sem=rs, device_id=dev, device_id_type=MESH)
        if cond is None:
            cp().start()
        else:
            pl.when(cond)(lambda: cp().start())
        sends.append((cond, cp))
    def recv(src, dst, rs, dev):
        pltpu.make_async_remote_copy(src_ref=dst, dst_ref=dst, send_sem=rs, recv_sem=rs, device_id=dev, device_id_type=MESH).wait_recv()
    def view(a, shard, y, c):
        return piece(outs[a].at[shard], specs[a], y, c)
    own = [piece(ins[a], specs[a], me.y, me.c) for a in range(n)]
    for a in order:
        dst = view(a, me.seq, me.y, me.c)
        remote(me.z < NZ - 1, own[a], dst, zs.at[a, 0, 0], zr.at[a, 0, 0], me.up)
        remote(me.z > 0, own[a], dst, zs.at[a, 1, 0], zr.at[a, 1, 0], me.down)
        remote(None, own[a], dst, xs.at[a, me.z], xr.at[a, me.z], me.xp)
    for a in range(n):
        pltpu.make_async_copy(ins[a], outs[a].at[me.seq], ls.at[a]).start()
    def onward(a, shard, cond, wave):
        v = view(a, shard, me.y, me.c)
        if specs[a][0] == "P":
            remote(cond, v, v, ys.at[a, shard], yr.at[a, shard], me.yp)
        remote(cond, v, v, cs.at[a, 0, shard], cr.at[a, 0, shard], me.cp)
    def zstep(a, k):
        for d, (cond, zz, frm, fwd_ok, to) in enumerate((
            (me.z - k >= 0, me.z - k, me.down, me.z < NZ - 1, me.up),
            (me.z + k < NZ, me.z + k, me.up, me.z > 0, me.down))):
            zz = jnp.clip(zz, 0, NZ - 1)
            shard = 2 * zz + me.x
            v = view(a, shard, me.y, me.c)
            pl.when(cond)(lambda: recv(v, v, zr.at[a, d, k - 1], frm))
            if k < NZ - 1:
                remote(cond & fwd_ok, v, v, zs.at[a, d, k], zr.at[a, d, k], to)
            remote(cond, v, v, xs.at[a, zz], xr.at[a, zz], me.xp)
            onward(a, shard, cond, 0)
    def xstep(a, k):
        alts = ((None, me.z),) if k == 0 else ((me.z - k >= 0, me.z - k), (me.z + k < NZ, me.z + k))
        for cond, zz in alts:
            zz = jnp.clip(zz, 0, NZ - 1)
            shard = 2 * zz + 1 - me.x
            v = view(a, shard, me.y, me.c)
            if cond is None:
                recv(v, v, xr.at[a, zz], me.xp)
            else:
                pl.when(cond)(lambda: recv(v, v, xr.at[a, zz], me.xp))
            onward(a, shard, cond, 1)
    def ystep(a, cond, shard):
        v = view(a, shard, 1 - me.y, me.c)
        def go():
            recv(v, v, yr.at[a, shard], me.yp)
        if cond is None: go()
        else: pl.when(cond)(go)
        remote(cond, v, v, cs.at[a, 1, shard], cr.at[a, 1, shard], me.cp)
    def ysteps(a, k, which):
        if specs[a][0] != "P": return
        if which == "z":
            for cond, zz in ((me.z - k >= 0, me.z - k), (me.z + k < NZ, me.z + k)):
                ystep(a, cond, 2 * jnp.clip(zz, 0, NZ - 1) + me.x)
        elif k == 0:
            ystep(a, None, 2 * me.z + 1 - me.x)
        else:
            for cond, zz in ((me.z - k >= 0, me.z - k), (me.z + k < NZ, me.z + k)):
                ystep(a, cond, 2 * jnp.clip(zz, 0, NZ - 1) + 1 - me.x)
    for k in range(1, NZ + 2):
        for a in order:
            if k < NZ: zstep(a, k)
            if k - 1 < NZ: xstep(a, k - 1)
        for a in order:
            if 1 <= k - 1 < NZ: ysteps(a, k - 1, "z")
            if 0 <= k - 2 < NZ: ysteps(a, k - 2, "x")
    for a in range(n):
        for k in range(1, NZ):
            for cond, zz in ((me.z - k >= 0, me.z - k), (me.z + k < NZ, me.z + k)):
                shard = 2 * jnp.clip(zz, 0, NZ - 1) + me.x
                for w in range(2 if specs[a][0] == "P" else 1):
                    v = view(a, shard, me.y if w == 0 else 1 - me.y, 1 - me.c)
                    pl.when(cond)(lambda: recv(v, v, cr.at[a, w, shard], me.cp))
        for zz in range(NZ):
            shard = 2 * zz + 1 - me.x
            for w in range(2 if specs[a][0] == "P" else 1):
                v = view(a, shard, me.y if w == 0 else 1 - me.y, 1 - me.c)
                recv(v, v, cr.at[a, w, shard], me.cp)
        pltpu.make_async_copy(ins[a], outs[a].at[me.seq], ls.at[a]).wait()
    for cond, cp in sends:
        if cond is None: cp().wait_send()
        else: pl.when(cond)(lambda: cp().wait_send())

def gather_weights(arrays, specs, order, cid):
    n = len(arrays)
    DMA = pltpu.SemaphoreType.DMA
    return pl.pallas_call(
        functools.partial(gather_kernel, specs, order),
        out_shape=[jax.ShapeDtypeStruct((8, *a.shape), a.dtype) for a in arrays],
        in_specs=[pl.BlockSpec(memory_space=pl.ANY)] * n,
        out_specs=[pl.BlockSpec(memory_space=pl.ANY)] * n,
        scratch_shapes=[DMA((n, 2, 3)), DMA((n, 2, 3)), DMA((n, 4)), DMA((n, 4)), DMA((n, 8)), DMA((n, 8)), DMA((n, 2, 8)), DMA((n, 2, 8)), DMA((n,))],
        compiler_params=pltpu.CompilerParams(collective_id=cid, has_side_effects=True),
        name="gather_weights",
    )(*arrays)

class Unit:
    def __init__(self, arr, row, col, flow, axis):
        self.arr, self.row, self.col, self.flow, self.axis = arr, row, col, flow, axis
        self.shape = (row[1], col[1])
        h = list(self.shape); h[axis] //= 2
        self.half = tuple(h)
        q = list(h)
        if flow == "P": q[axis] //= 2
        self.piece = tuple(q)

def rect(unit, ref, part, nparts):
    start = [unit.row[0], unit.col[0]]
    size = list(unit.shape)
    size[unit.axis] //= nparts
    idx = []
    for d in range(2):
        if d == unit.axis:
            off = part * size[d] + start[d]
            idx.append(pl.ds(pl.multiple_of(off, 16 if d == 0 else 128), size[d]))
        else:
            idx.append(pl.ds(start[d], size[d]))
    return ref.at[tuple(idx)]

class Reduce:
    def __init__(self, me, units, ins, outs, scratch):
        self.me, self.units, self.ins, self.outs = me, units, ins, outs
        nu = len(units)
        self.A, self.RC, self.RY, self.RX, self.RZ, self.RF = [scratch[i * nu:(i + 1) * nu] for i in range(6)]
        self.ls, self.cs, self.cr, self.ys, self.yr, self.xs, self.xr, self.zs, self.zr, self.fs, self.fr, self.os_ = scratch[6 * nu:]

    def shard_at(self, i):
        me = self.me
        zz = lax.rem(me.z + 1 + lax.rem(i, NZ), NZ)
        xx = jnp.where(i < NZ, 1 - me.x, me.x)
        return zz, xx, 2 * zz + xx

    def sub(self, u, ref, y):
        if u.flow == "R":
            return ref
        n = u.piece[u.axis]
        idx = [slice(None)] * 2
        idx[u.axis] = pl.ds(pl.multiple_of(y * n, n), n)
        return ref.at[tuple(idx)]

    def remote(self, src, dst, ss, rs, dev):
        return pltpu.make_async_remote_copy(src_ref=src, dst_ref=dst, send_sem=ss, recv_sem=rs, device_id=dev, device_id_type=MESH)

    def core_copy(self, k, i):
        u = self.units[k]; zz, xx, s = self.shard_at(i)
        return self.remote(rect(u, self.ins[u.arr].at[s], 1 - self.me.c, 2), self.RC[k].at[s], self.cs.at[k, s], self.cr.at[k, s], self.me.cp)

    def local_copy(self, k, i):
        u = self.units[k]; zz, xx, s = self.shard_at(i)
        return pltpu.make_async_copy(rect(u, self.ins[u.arr].at[s], self.me.c, 2), self.A[k].at[s], self.ls.at[k, s])

    def y_copy(self, k, i):
        u = self.units[k]; zz, xx, s = self.shard_at(i)
        return self.remote(self.sub(u, self.A[k].at[s], 1 - self.me.y), self.RY[k].at[s], self.ys.at[k, s], self.yr.at[k, s], self.me.yp)

    def x_copy(self, k, zz):
        u, me = self.units[k], self.me
        return self.remote(self.sub(u, self.A[k].at[2 * zz + 1 - me.x], me.y), self.RX[k].at[zz], self.xs.at[k, zz], self.xr.at[k, zz], me.xp)

    def z_copy(self, k, zz):
        u, me = self.units[k], self.me
        return self.remote(self.mine(k, zz), self.RZ[k].at[me.z], self.zs.at[k, zz], self.zr.at[k, me.z], (2 * zz + me.x, me.batch))

    def z_recv(self, k, zz):
        u, me = self.units[k], self.me
        return self.remote(self.RZ[k].at[zz], self.RZ[k].at[zz], self.zs.at[k, zz], self.zr.at[k, zz], (2 * zz + me.x, me.batch))

    def mine(self, k, zz):
        return self.sub(self.units[k], self.A[k].at[2 * zz + self.me.x], self.me.y)

    @staticmethod
    def add(dst, src):
        dst[...] = dst[...] + src[...]

    def begin(self, k, i):
        self.core_copy(k, i).start()
        self.local_copy(k, i).start()

    def core(self, k, i):
        u = self.units[k]; zz, xx, s = self.shard_at(i)
        self.local_copy(k, i).wait()
        self.core_copy(k, i).wait_recv()
        self.add(self.A[k].at[s], self.RC[k].at[s])
        if u.flow == "P":
            self.y_copy(k, i).start()
        else:
            pl.when(i < NZ)(lambda: self.x_copy(k, zz).start())

    def y(self, k, i):
        u = self.units[k]; zz, xx, s = self.shard_at(i)
        self.y_copy(k, i).wait_recv()
        self.add(self.sub(u, self.A[k].at[s], self.me.y), self.RY[k].at[s])
        pl.when(i < NZ)(lambda: self.x_copy(k, zz).start())

    def x(self, k, i):
        me = self.me
        zz = lax.rem(me.z + 1 + i, NZ)
        self.x_copy(k, zz).wait_recv()
        self.add(self.mine(k, zz), self.RX[k].at[zz])
        pl.when(zz != me.z)(lambda: self.z_copy(k, zz).start())

    def fin_y(self, k):
        u, me = self.units[k], self.me
        mine = self.mine(k, me.z)
        dst = rect(u, self.outs[u.arr], 2 * me.c + me.y, 4) if u.flow == "P" else self.RF[k]
        return self.remote(mine, dst, self.fs.at[k, 0], self.fr.at[k, 0], me.yp)

    def fin_c(self, k, w):
        u, me = self.units[k], self.me
        if u.flow == "P":
            if w == 0:
                return self.remote(self.mine(k, me.z), rect(u, self.outs[u.arr], 2 * me.c + me.y, 4), self.fs.at[k, 1], self.fr.at[k, 1], me.cp)
            v = rect(u, self.outs[u.arr], 2 * me.c + 1 - me.y, 4)
            return self.remote(v, v, self.fs.at[k, 2], self.fr.at[k, 2], me.cp)
        return self.remote(self.RF[k], rect(u, self.outs[u.arr], me.c, 2), self.fs.at[k, 1], self.fr.at[k, 1], me.cp)

    def out_copy(self, k):
        u, me = self.units[k], self.me
        if u.flow == "P":
            return pltpu.make_async_copy(self.mine(k, me.z), rect(u, self.outs[u.arr], 2 * me.c + me.y, 4), self.os_.at[k])
        return pltpu.make_async_copy(self.RF[k], rect(u, self.outs[u.arr], me.c, 2), self.os_.at[k])

    def own(self, k, i):
        me = self.me
        def body(i, c):
            zz = lax.rem(me.z + i, NZ)
            self.z_recv(k, zz).wait_recv()
            self.add(self.mine(k, me.z), self.RZ[k].at[zz])
            return c
        lax.fori_loop(1, NZ, body, 0)
        self.fin_y(k).start()
        if self.units[k].flow == "P":
            self.out_copy(k).start()
            self.fin_c(k, 0).start()

    def last(self, k, i):
        self.fin_y(k).wait_recv()
        if self.units[k].flow == "P":
            self.fin_c(k, 1).start()
        else:
            self.add(self.RF[k], self.mine(k, self.me.z))
            self.out_copy(k).start()
            self.fin_c(k, 0).start()

    def end(self, k, i):
        me = self.me
        flow = self.units[k].flow
        for w in range(2 if flow == "P" else 1):
            self.fin_c(k, w).wait_recv()
            self.fin_c(k, w).wait_send()
        self.out_copy(k).wait()
        self.fin_y(k).wait_send()
        def body(i, c):
            self.core_copy(k, i).wait_send()
            if flow == "P": self.y_copy(k, i).wait_send()
            return c
        lax.fori_loop(0, 8, body, 0)
        def body(zz, c):
            self.x_copy(k, zz).wait_send()
            pl.when(zz != me.z)(lambda: self.z_copy(k, zz).wait_send())
            return c
        lax.fori_loop(0, NZ, body, 0)

    def run(self, plan):
        for step, k, first, n in plan:
            fn = getattr(self, step)
            if n == 1:
                fn(k, first)
            else:
                def body(i, c):
                    fn(k, i)
                    return c
                lax.fori_loop(first, first + n, body, 0)

def reduce_kernel(units, narr, plan, *refs):
    me = Place()
    greet(me)
    red = Reduce(me, units, refs[:narr], refs[narr:2 * narr], refs[2 * narr:])
    red.run(plan)

def reduce_scratch(units):
    nu = len(units)
    DMA = pltpu.SemaphoreType.DMA
    bf = jnp.bfloat16
    V = pltpu.VMEM
    return ([V((8, *u.half), bf) for u in units] + [V((8, *u.half), bf) for u in units]
        + [V((8, *u.piece) if u.flow == "P" else (16, 128), bf) for u in units] + [V((4, *u.piece), bf) for u in units]
        + [V((4, *u.piece), bf) for u in units] + [V(u.piece if u.flow == "R" else (16, 128), bf) for u in units]
        + [DMA((nu, 8))] * 5 + [DMA((nu, 4))] * 4 + [DMA((nu, 3))] * 2 + [DMA((nu,))])

def reduce_weights(arrays, units, plan, cid):
    narr = len(arrays)
    return pl.pallas_call(
        functools.partial(reduce_kernel, units, narr, plan),
        out_shape=[jax.ShapeDtypeStruct(a.shape[1:], a.dtype) for a in arrays],
        in_specs=[pl.BlockSpec(memory_space=pl.ANY)] * narr,
        out_specs=[pl.BlockSpec(memory_space=pl.ANY)] * narr,
        scratch_shapes=reduce_scratch(units),
        compiler_params=pltpu.CompilerParams(collective_id=cid, has_side_effects=True, vmem_limit_bytes=58 << 20),
        name="reduce_weights",
    )(*arrays)

def gather_rows_kernel(src, out, zs, zr, xs, xr, ls):
    me = Place()
    greet(me)
    rows = src.shape[0]
    def remote(s, b, ss, rs, dev):
        v = out.at[s, b]
        return pltpu.make_async_remote_copy(src_ref=v, dst_ref=v, send_sem=ss, recv_sem=rs, device_id=dev, device_id_type=MESH)
    def first(b, ss, rs, dev):
        return pltpu.make_async_remote_copy(src_ref=src.at[b], dst_ref=out.at[me.seq, b], send_sem=ss, recv_sem=rs, device_id=dev, device_id_type=MESH)
    sends = []
    def start(cond, mk):
        pl.when(cond)(lambda: mk().start())
        sends.append((cond, mk))
    for b in range(rows):
        start(me.z < NZ - 1, functools.partial(first, b, zs.at[b, 0, 0], zr.at[b, 0, 0], me.up))
        start(me.z > 0, functools.partial(first, b, zs.at[b, 1, 0], zr.at[b, 1, 0], me.down))
        start(me.z >= 0, functools.partial(first, b, xs.at[b, me.z], xr.at[b, me.z], me.xp))
    for b in range(rows):
        pltpu.make_async_copy(src.at[b], out.at[me.seq, b], ls.at[b]).start()
    for k in range(1, NZ):
        for b in range(rows):
            for d, (cond, zz, fwd, to) in enumerate((
                (me.z - k >= 0, me.z - k, me.z < NZ - 1, me.up),
                (me.z + k < NZ, me.z + k, me.z > 0, me.down))):
                zz = jnp.clip(zz, 0, NZ - 1)
                s = 2 * zz + me.x
                pl.when(cond)(lambda: remote(s, b, zr.at[b, d, k - 1], zr.at[b, d, k - 1], to).wait_recv())
                if k < NZ - 1:
                    start(cond & fwd, functools.partial(remote, s, b, zs.at[b, d, k], zr.at[b, d, k], to))
                start(cond, functools.partial(remote, s, b, xs.at[b, zz], xr.at[b, zz], me.xp))
    for b in range(rows):
        for zz in range(NZ):
            remote(2 * zz + 1 - me.x, b, xs.at[b, zz], xr.at[b, zz], me.xp).wait_recv()
        pltpu.make_async_copy(src.at[b], out.at[me.seq, b], ls.at[b]).wait()
    for cond, mk in sends:
        pl.when(cond)(lambda: mk().wait_send())

def gather_rows(a, cid):
    DMA = pltpu.SemaphoreType.DMA
    r = a.shape[0]
    return pl.pallas_call(
        gather_rows_kernel,
        out_shape=jax.ShapeDtypeStruct((8, *a.shape), a.dtype),
        in_specs=[pl.BlockSpec(memory_space=pl.ANY)],
        out_specs=pl.BlockSpec(memory_space=pl.ANY),
        scratch_shapes=[DMA((r, 2, 3)), DMA((r, 2, 3)), DMA((r, 4)), DMA((r, 4)), DMA((r,))],
        compiler_params=pltpu.CompilerParams(collective_id=cid, has_side_effects=True),
        name="gather_rows",
    )(a)

def reduce_rows_kernel(src, out, A, RX, RZ, xs, xr, zs, zr, ls):
    me = Place()
    greet(me)
    rows = src.shape[1]
    def remote(s, d, ss, rs, dev):
        return pltpu.make_async_remote_copy(src_ref=s, dst_ref=d, send_sem=ss, recv_sem=rs, device_id=dev, device_id_type=MESH)
    def local(b, zz):
        return pltpu.make_async_copy(src.at[2 * zz + me.x, b], A.at[b, zz], ls.at[b, zz])
    def x_copy(b, zz):
        return remote(src.at[2 * zz + 1 - me.x, b], RX.at[b, zz], xs.at[b, zz], xr.at[b, zz], me.xp)
    def z_copy(b, d, zz):
        return remote(A.at[b, zz], RZ.at[b, d, zz], zs.at[b, d, zz], zr.at[b, d, zz], me.up if d == 0 else me.down)
    def add(dst, more):
        dst[...] = dst[...] + more[...]
    def turn(i):
        return lax.rem(me.z + 1 + i, NZ)
    def begin(i, c):
        for b in range(rows):
            x_copy(b, turn(i)).start()
            local(b, turn(i)).start()
        return c
    lax.fori_loop(0, NZ, begin, 0)
    for b in range(rows):
        def arrive(i, c):
            zz = turn(i)
            local(b, zz).wait()
            x_copy(b, zz).wait_recv()
            add(A.at[b, zz], RX.at[b, zz])
            pl.when((me.z == 0) & (zz > 0))(lambda: z_copy(b, 0, zz).start())
            pl.when((me.z == NZ - 1) & (zz < NZ - 1))(lambda: z_copy(b, 1, zz).start())
            return c
        lax.fori_loop(0, NZ, arrive, 0)
    for b in range(rows):
        def pass_on(i, c):
            up, down = NZ - 1 - i, i
            @pl.when((up > me.z) & (me.z > 0))
            def _():
                z_copy(b, 0, up).wait_recv()
                add(A.at[b, up], RZ.at[b, 0, up])
                z_copy(b, 0, up).start()
            @pl.when((down < me.z) & (me.z < NZ - 1))
            def _():
                z_copy(b, 1, down).wait_recv()
                add(A.at[b, down], RZ.at[b, 1, down])
                z_copy(b, 1, down).start()
            return c
        lax.fori_loop(0, NZ, pass_on, 0)
    for b in range(rows):
        @pl.when(me.z > 0)
        def _():
            z_copy(b, 0, me.z).wait_recv()
            add(A.at[b, me.z], RZ.at[b, 0, me.z])
        @pl.when(me.z < NZ - 1)
        def _():
            z_copy(b, 1, me.z).wait_recv()
            add(A.at[b, me.z], RZ.at[b, 1, me.z])
        out[b] = A[b, me.z]
        def sent(zz, c):
            x_copy(b, zz).wait_send()
            pl.when(zz > me.z)(lambda: z_copy(b, 0, zz).wait_send())
            pl.when(zz < me.z)(lambda: z_copy(b, 1, zz).wait_send())
            return c
        lax.fori_loop(0, NZ, sent, 0)

def reduce_rows(a, cid):
    DMA = pltpu.SemaphoreType.DMA
    shape = a.shape[1:]
    r = shape[0]
    V = pltpu.VMEM
    return pl.pallas_call(
        reduce_rows_kernel,
        out_shape=jax.ShapeDtypeStruct(shape, a.dtype),
        in_specs=[pl.BlockSpec(memory_space=pl.ANY)],
        out_specs=pl.BlockSpec(memory_space=pltpu.VMEM),
        scratch_shapes=[V((r, 4, *shape[1:]), a.dtype), V((r, 4, *shape[1:]), a.dtype), V((r, 2, 4, *shape[1:]), a.dtype),
                        DMA((r, 4)), DMA((r, 4)), DMA((r, 2, 4)), DMA((r, 2, 4)), DMA((r, 4))],
        compiler_params=pltpu.CompilerParams(collective_id=cid, has_side_effects=True, vmem_limit_bytes=32 << 20),
        name="reduce_rows",
    )(a)
F32, BF16 = jnp.float32, jnp.bfloat16
NEG = -1e30

def nn(a, b):
    return lax.dot_general(a, b, (((1,), (0,)), ((), ())), preferred_element_type=F32)

def nt(a, b):
    return lax.dot_general(a, b, (((1,), (1,)), ((), ())), preferred_element_type=F32)

def expand(heads, dims, base):
    parts = []
    for h in range(2):
        parts.append((heads[base + h:base + h + 1] * dims[0] + heads[base + 2 + h:base + 3 + h] * dims[1]) * 0.5)
    return jnp.concatenate(parts, 0)

def queries(qh, qr):
    parts = []
    for h in range(2):
        total = qh[h:h + 1] * qr[0:64]
        for r in range(1, 6):
            total = total + qh[2 * r + h:2 * r + h + 1] * qr[64 * r:64 * r + 64]
        parts.append(total)
    return jnp.concatenate(parts, 0) / 6.0

def lanes_below(shape, n):
    return lax.broadcasted_iota(jnp.int32, shape, 1) < n

def stack_heads(part):
    first = lanes_below(part.shape, 64)
    zero = jnp.zeros_like(part)
    return jnp.concatenate([jnp.where(first, part, zero), jnp.where(first, zero, part)], 0)

def unstack_heads(part):
    n = part.shape[0] // 2
    return jnp.where(lanes_below((n, 128), 64), part[:n], part[n:])

def causal_bias(n2, span):
    row = lax.broadcasted_iota(jnp.int32, (n2, span), 0) % span
    col = lax.broadcasted_iota(jnp.int32, (n2, span), 1)
    return jnp.where(col <= row, 0.0, NEG)

def pair_factors(heads, dims, cond, base, at):
    hl, hs = heads
    dl, ds = dims
    low = expand(hl, (dl[at:at + 64].astype(F32), dl[at + 64:at + 128].astype(F32)), base).astype(BF16)
    sel = expand(hs, (ds[at:at + 64].astype(F32), ds[at + 64:at + 128].astype(F32)), base)
    left = jnp.where(cond > 0.5, sel, 0.0).astype(BF16)
    right = jnp.where(cond > 0.5, 0.0, sel).astype(BF16)
    return low, jnp.concatenate([left, right], 0)

def attend_kernel(span, chunk, qh_ref, qr_ref, hl_ref, hs_ref, dl_ref, ds_ref, cond_ref, bl_ref, bs_ref, o_ref, lse_ref, s1, s2):
    p = pl.program_id(1)
    n2 = 2 * span
    nk = dl_ref.shape[-1]
    qt = queries(qh_ref[0, 0], qr_ref[0])
    q = (qt.T.astype(BF16) * BF16(0.125)) if False else (qt.astype(BF16).astype(F32).T * 0.125).astype(BF16)
    qlo, qhi = stack_heads(q[:span]), stack_heads(q[span:])
    qboth = jnp.concatenate([qlo, qhi], 1)
    heads = (hl_ref[0, 0], hs_ref[0, 0])
    dims = (dl_ref[0], ds_ref[0])
    cond = cond_ref[...]
    klo, ksel = pair_factors(heads, dims, cond, 0, 0)
    vlo, vsel = pair_factors(heads, dims, cond, 4, 128)
    tri = causal_bias(n2, span)
    width = min(128, chunk)
    mlo = jnp.full((n2, width), NEG, F32)
    mhi = jnp.full((n2, width), NEG, F32)
    s3 = nn(qlo, klo[:, :span]) + bl_ref[0][:, :span] + tri
    m3 = jnp.max(s3, -1, keepdims=True)
    for c in range(0, nk, chunk):
        sl = slice(c, c + chunk)
        a = nn(qhi, klo[:, sl]) + bl_ref[0][:, sl]
        s1[:, sl] = a
        b = nn(qboth, ksel[:, sl]) + bs_ref[0][:, sl]
        if c == 0:
            b = jnp.concatenate([b[:, :span] + tri, b[:, span:]], 1)
        s2[:, sl] = b
        for i in range(0, chunk, width):
            on = cond[:, c + i:c + i + width] > 0.5
            ai, bi = a[:, i:i + width], b[:, i:i + width]
            mlo = jnp.maximum(mlo, jnp.where(on, bi, NEG))
            mhi = jnp.maximum(mhi, jnp.maximum(ai, jnp.where(on, NEG, bi)))
    mlo = jnp.maximum(jnp.max(mlo, -1, keepdims=True), m3)
    mhi = jnp.max(mhi, -1, keepdims=True)
    e3 = jnp.exp(s3 - mlo)
    tlo = jnp.zeros((n2, width), F32)
    thi = jnp.zeros((n2, width), F32)
    o3 = nt(e3.astype(BF16), vlo[:, :span])
    o1 = jnp.zeros((n2, 128), F32)
    o2 = jnp.zeros((n2, 256), F32)
    for c in range(0, nk, chunk):
        sl = slice(c, c + chunk)
        on = cond[:, sl] > 0.5
        a = jnp.exp(s1[:, sl] - mhi)
        b = jnp.exp(s2[:, sl] - jnp.where(on, mlo, mhi))
        blo = jnp.where(on, b, 0.0)
        bhi = a + jnp.where(on, 0.0, b)
        for i in range(0, chunk, width):
            tlo = tlo + blo[:, i:i + width]
            thi = thi + bhi[:, i:i + width]
        o1 = o1 + nt(a.astype(BF16), vlo[:, sl])
        o2 = o2 + nt(b.astype(BF16), vsel[:, sl])
    llo = jnp.sum(tlo, -1, keepdims=True) + jnp.sum(e3, -1, keepdims=True)
    lhi = jnp.sum(thi, -1, keepdims=True)
    olo = unstack_heads((o2[:, :128] + o3) / llo)
    ohi = unstack_heads((o2[:, 128:] + o1) / lhi)
    o_ref[0] = jnp.concatenate([olo, ohi], 0).astype(BF16)
    lane = lax.broadcasted_iota(jnp.int32, (span, 128), 1)
    tlo = mlo + jnp.log(llo)
    thi = mhi + jnp.log(lhi)
    old = jnp.where(p == 0, 0.0, lse_ref[0])
    new = []
    for k, t in enumerate((tlo, thi)):
        part = old[k * span:(k + 1) * span]
        part = jnp.where(lane == 2 * p, t[:span], part)
        new.append(jnp.where(lane == 2 * p + 1, t[span:], part))
    lse_ref[0] = jnp.concatenate(new, 0)

def attend(qh, qr, hl, hs, dl, ds, cond, bl, bs):
    rows, pairs, _, nq = qh.shape
    nk = dl.shape[-1]
    span = nq // 2
    chunk = min(512, nk)
    full = lambda *s: pl.BlockSpec((1, *s), lambda b, p: (b, *([0] * len(s))))
    pairb = lambda *s: pl.BlockSpec((1, 1, *s), lambda b, p: (b, p, *([0] * len(s))))
    return pl.pallas_call(
        functools.partial(attend_kernel, span, chunk),
        grid=(rows, pairs),
        out_shape=[jax.ShapeDtypeStruct((rows, nq, pairs * 128), BF16), jax.ShapeDtypeStruct((rows, nq, 128), F32)],
        in_specs=[pairb(12, nq), full(384, nq), pairb(8, nk), pairb(8, nk), full(256, nk), full(256, nk),
                  pl.BlockSpec((1, nk), lambda b, p: (0, 0)), full(1, nk), full(1, nk)],
        out_specs=[pl.BlockSpec((1, nq, 128), lambda b, p: (b, 0, p)), full(nq, 128)],
        scratch_shapes=[pltpu.VMEM((nq, nk), F32), pltpu.VMEM((nq, nk), F32)],
        compiler_params=pltpu.CompilerParams(vmem_limit_bytes=56 << 20),
        name="attend",
    )(qh, qr, hl, hs, dl, ds, cond, bl, bs)

def attend_back_kernel(span, chunk, qh_ref, qr_ref, hl_ref, hs_ref, dl_ref, ds_ref, cond_ref, bl_ref, bs_ref, lse_ref, o_ref, g_ref,
                       dqh_ref, dqr_ref, dhl_ref, dhs_ref, ddl_ref, dds_ref):
    p = pl.program_id(1)
    @pl.when(p == 0)
    def _():
        dqr_ref[...] = jnp.zeros_like(dqr_ref)
        ddl_ref[...] = jnp.zeros_like(ddl_ref)
        dds_ref[...] = jnp.zeros_like(dds_ref)
    pair_back(span, chunk, p, qh_ref, qr_ref, Pair(hl_ref, 0, 0), Pair(hs_ref, 0, 0), dl_ref, ds_ref, cond_ref, bl_ref, bs_ref, lse_ref, o_ref, g_ref,
              dqh_ref, dqr_ref, Pair(dhl_ref, 0, 0), Pair(dhs_ref, 0, 0), ddl_ref, dds_ref)

class Pair:
    def __init__(self, ref, *at):
        self.ref, self.at = ref, at

    def all(self):
        return self.ref[self.at]

    def row(self, j, sl):
        return self.ref[(*self.at, slice(j, j + 1), sl)]

    def put(self, j, sl, value):
        self.ref[(*self.at, slice(j, j + 1), sl)] = value

def pair_back(span, chunk, p, qh_ref, qr_ref, hl, hs, dl_ref, ds_ref, cond_ref, bl_ref, bs_ref, lse_ref, o_ref, g_ref,
              dqh_ref, dqr_ref, dhl, dhs, ddl_ref, dds_ref):
    n2 = 2 * span
    nk = dl_ref.shape[-1]
    qh, qr = qh_ref[0, 0], qr_ref[0]
    qt = (queries(qh, qr).astype(BF16).astype(F32)) * 0.125
    q = qt.T.astype(BF16)
    qlo, qhi = stack_heads(q[:span]), stack_heads(q[span:])
    qboth = jnp.concatenate([qlo, qhi], 1)
    g = g_ref[0]
    glo, ghi = stack_heads(g[:span]), stack_heads(g[span:])
    gboth = jnp.concatenate([glo, ghi], 1)
    gt = g.astype(F32).T
    first = lax.broadcasted_iota(jnp.int32, (128, span), 0) < 64
    def stack_lanes(part):
        return jnp.concatenate([jnp.where(first, part, 0.0), jnp.where(first, 0.0, part)], 1).astype(BF16)
    qtlo, qthi = stack_lanes(qt[:, :span]), stack_lanes(qt[:, span:])
    gtlo, gthi = stack_lanes(gt[:, :span]), stack_lanes(gt[:, span:])
    qtboth = jnp.concatenate([qtlo, qthi], 0)
    gtboth = jnp.concatenate([gtlo, gthi], 0)
    prod = g.astype(F32) * o_ref[0].astype(F32)
    flane = lanes_below((n2, 128), 64)
    d0 = jnp.sum(jnp.where(flane, prod, 0.0), -1, keepdims=True)
    d1 = jnp.sum(jnp.where(flane, 0.0, prod), -1, keepdims=True)
    lane = lax.broadcasted_iota(jnp.int32, (n2, 128), 1)
    lse = lse_ref[0]
    l0 = jnp.sum(jnp.where(lane == 2 * p, lse, 0.0), -1, keepdims=True)
    l1 = jnp.sum(jnp.where(lane == 2 * p + 1, lse, 0.0), -1, keepdims=True)
    dello, delhi = jnp.concatenate([d0[:span], d1[:span]], 0), jnp.concatenate([d0[span:], d1[span:]], 0)
    lselo, lsehi = jnp.concatenate([l0[:span], l1[:span]], 0), jnp.concatenate([l0[span:], l1[span:]], 0)
    heads = (hl.all(), hs.all())
    dims = (dl_ref[0], ds_ref[0])
    cond = cond_ref[...]
    klo, ksel = pair_factors(heads, dims, cond, 0, 0)
    vlo, vsel = pair_factors(heads, dims, cond, 4, 128)
    tri = causal_bias(n2, span)

    def put(dkt, h, d_ref, hd, dd_ref, base, at, sl):
        for r in range(2):
            dim = d_ref[0, at + 64 * r:at + 64 * r + 64, sl].astype(F32)
            total = None
            for k in range(2):
                part = dkt[64 * k:64 * k + 64]
                j = base + 2 * r + k
                hd.put(j, sl, jnp.sum(part * dim, 0, keepdims=True) * 0.5)
                term = part * h.row(j, sl)
                total = term if total is None else total + term
            dd_ref[0, at + 64 * r:at + 64 * r + 64, sl] += total * 0.5

    s3 = nn(qlo, klo[:, :span]) + bl_ref[0][:, :span] + tri
    p3 = jnp.exp(s3 - lselo)
    dp3 = nn(glo, vlo[:, :span])
    ds3 = (p3 * (dp3 - dello)).astype(BF16)
    p3 = p3.astype(BF16)
    dq3 = nt(ds3, klo[:, :span])
    dk3 = nn(qtlo, ds3)
    dv3 = nn(gtlo, p3)
    dq1 = jnp.zeros((n2, 128), F32)
    dq2 = jnp.zeros((n2, 256), F32)
    for c in range(0, nk, chunk):
        sl = slice(c, c + chunk)
        pa = jnp.exp(nn(qhi, klo[:, sl]) + bl_ref[0][:, sl] - lsehi)
        dpa = nn(ghi, vlo[:, sl])
        dsa = (pa * (dpa - delhi)).astype(BF16)
        pa = pa.astype(BF16)
        dq1 = dq1 + nt(dsa, klo[:, sl])
        dk = nn(qthi, dsa)
        dv = nn(gthi, pa)
        if c == 0:
            dk = jnp.concatenate([dk[:, :span] + dk3, dk[:, span:]], 1)
            dv = jnp.concatenate([dv[:, :span] + dv3, dv[:, span:]], 1)
        put(dk, hl, dl_ref, dhl, ddl_ref, 0, 0, sl)
        put(dv, hl, dl_ref, dhl, ddl_ref, 4, 128, sl)
    for c in range(0, nk, chunk):
        sl = slice(c, c + chunk)
        on = cond[:, sl] > 0.5
        s = nn(qboth, ksel[:, sl]) + bs_ref[0][:, sl]
        if c == 0:
            s = jnp.concatenate([s[:, :span] + tri, s[:, span:]], 1)
        pb = jnp.exp(s - jnp.where(on, lselo, lsehi))
        dpb = nn(gboth, vsel[:, sl])
        dsb = (pb * (dpb - jnp.where(on, dello, delhi))).astype(BF16)
        pb = pb.astype(BF16)
        dq2 = dq2 + nt(dsb, ksel[:, sl])
        dk = nn(qtboth, dsb)
        dv = nn(gtboth, pb)
        dk = jnp.where(on, dk[:128], dk[128:])
        dv = jnp.where(on, dv[:128], dv[128:])
        put(dk, hs, ds_ref, dhs, dds_ref, 0, 0, sl)
        put(dv, hs, ds_ref, dhs, dds_ref, 4, 128, sl)
    dqlo = unstack_heads(dq2[:, :128] + dq3)
    dqhi = unstack_heads(dq2[:, 128:] + dq1)
    dqt = (jnp.concatenate([dqlo, dqhi], 0) * (0.125 / 6.0)).T
    for r in range(6):
        total = None
        for h in range(2):
            part = dqt[64 * h:64 * h + 64]
            j = 2 * r + h
            dqh_ref[0, 0, j:j + 1, :] = jnp.sum(part * qr[64 * r:64 * r + 64], 0, keepdims=True)
            term = part * qh[j:j + 1]
            total = term if total is None else total + term
        dqr_ref[0, 64 * r:64 * r + 64, :] += total

def attend_back(qh, qr, hl, hs, dl, ds, cond, bl, bs, lse, o, g):
    rows, pairs, _, nq = qh.shape
    nk = dl.shape[-1]
    span = nq // 2
    chunk = min(512, nk)
    full = lambda *s: pl.BlockSpec((1, *s), lambda b, p: (b, *([0] * len(s))))
    pairb = lambda *s: pl.BlockSpec((1, 1, *s), lambda b, p: (b, p, *([0] * len(s))))
    tok = pl.BlockSpec((1, nq, 128), lambda b, p: (b, 0, p))
    sd = jax.ShapeDtypeStruct
    return pl.pallas_call(
        functools.partial(attend_back_kernel, span, chunk),
        grid=(rows, pairs),
        out_shape=[sd((rows, pairs, 12, nq), F32), sd((rows, 384, nq), F32), sd((rows, pairs, 8, nk), F32), sd((rows, pairs, 8, nk), F32),
                   sd((rows, 256, nk), F32), sd((rows, 256, nk), F32)],
        in_specs=[pairb(12, nq), full(384, nq), pairb(8, nk), pairb(8, nk), full(256, nk), full(256, nk),
                  pl.BlockSpec((1, nk), lambda b, p: (0, 0)), full(1, nk), full(1, nk), full(nq, 128), tok, tok],
        out_specs=[pairb(12, nq), full(384, nq), pairb(8, nk), pairb(8, nk), full(256, nk), full(256, nk)],
        compiler_params=pltpu.CompilerParams(vmem_limit_bytes=56 << 20),
        name="attend_back",
    )(qh, qr, hl, hs, dl, ds, cond, bl, bs, lse, o, g)

class Rows:
    def __init__(self, me, pack, out, RX, RZ, xs, xr, zs, zr):
        self.me, self.pack, self.out, self.RX, self.RZ = me, pack, out, RX, RZ
        self.xs, self.xr, self.zs, self.zr = xs, xr, zs, zr

    def remote(self, src, dst, ss, rs, dev):
        return pltpu.make_async_remote_copy(src_ref=src, dst_ref=dst, send_sem=ss, recv_sem=rs, device_id=dev, device_id_type=MESH)

    def x_copy(self, b, zz):
        return self.remote(self.pack.at[b, 2 * zz + 1 - self.me.x], self.RX.at[b, zz], self.xs.at[b, zz], self.xr.at[b, zz], self.me.xp)

    def z_copy(self, b, zz):
        me = self.me
        return self.remote(self.mine(b, zz), self.RZ.at[b, me.z], self.zs.at[b, zz], self.zr.at[b, me.z], (2 * zz + me.x, me.batch))

    def z_recv(self, b, zz):
        me = self.me
        return self.remote(self.RZ.at[b, zz], self.RZ.at[b, zz], self.zs.at[b, zz], self.zr.at[b, zz], (2 * zz + me.x, me.batch))

    def mine(self, b, zz):
        return self.pack.at[b, 2 * zz + self.me.x]

    @staticmethod
    def add(dst, src):
        dst[...] = dst[...] + src[...]

    def begin(self, b):
        def body(i, c):
            self.x_copy(b, lax.rem(self.me.z + 1 + i, NZ)).start()
            return c
        lax.fori_loop(0, NZ, body, 0)

    def x(self, b):
        me = self.me
        def body(i, c):
            zz = lax.rem(me.z + 1 + i, NZ)
            self.x_copy(b, zz).wait_recv()
            self.add(self.mine(b, zz), self.RX.at[b, zz])
            pl.when(zz != me.z)(lambda: self.z_copy(b, zz).start())
            return c
        lax.fori_loop(0, NZ, body, 0)

    def own(self, b):
        me = self.me
        def body(i, c):
            zz = lax.rem(me.z + i, NZ)
            self.z_recv(b, zz).wait_recv()
            self.add(self.mine(b, me.z), self.RZ.at[b, zz])
            return c
        lax.fori_loop(1, NZ, body, 0)
        self.out[b] = self.pack[b, me.seq]

    def end(self, b):
        me = self.me
        def sent(zz, c):
            self.x_copy(b, zz).wait_send()
            pl.when(zz != me.z)(lambda: self.z_copy(b, zz).wait_send())
            return c
        lax.fori_loop(0, NZ, sent, 0)

def lay_out(me, shared_ref, b, span, cond_ref, dl, ds, hl, hs):
    n = shared_ref.shape[0]
    for i in range(n):
        j = lax.rem(me.seq + i, n)
        sl = slice(i * span, (i + 1) * span)
        on = cond_ref[:, sl] > 0.5
        low = shared_ref[j, b, :256, :span].astype(F32)
        high = shared_ref[j, b, :256, span:].astype(F32)
        dl[0, :, sl] = low.astype(BF16)
        ds[0, :, sl] = jnp.where(on, low, high).astype(BF16)
        low = shared_ref[j, b, 256:, :span].astype(F32)
        high = shared_ref[j, b, 256:, span:].astype(F32)
        hl[:, :, sl] = low.reshape(PAIRS, 8, span)
        hs[:, :, sl] = jnp.where(on, low, high).reshape(PAIRS, 8, span)

def pack_up(me, b, span, cond_ref, pack, ddl, dds, dhl, dhs):
    n = pack.shape[1]
    for i in range(n):
        j = lax.rem(me.seq + i, n)
        sl = slice(i * span, (i + 1) * span)
        on = cond_ref[:, sl] > 0.5
        for at, lo, se in ((0, ddl[0, :, sl], dds[0, :, sl]), (256, dhl[:, :, sl].reshape(64, span), dhs[:, :, sl].reshape(64, span))):
            rows = slice(at, at + lo.shape[0])
            pack[b, j, rows, :span] = (lo + jnp.where(on, se, 0.0)).astype(BF16)
            pack[b, j, rows, span:] = jnp.where(on, 0.0, se).astype(BF16)

def back_kernel(span, chunk, units, narr, plan, qh_ref, qr_ref, shared_ref, cond_ref, bl_ref, bs_ref, lse_ref, o_ref, g_ref, *refs):
    ins = refs[:narr]
    dqh_ref, dqr_ref, mine_ref = refs[narr:narr + 3]
    outs = refs[narr + 3:2 * narr + 3]
    dl, ds, hl, hs, ddl, dds, dhl, dhs, pack, RX, RZ, xs, xr, zs, zr = refs[2 * narr + 3:2 * narr + 18]
    me = Place()
    b, p = pl.program_id(0), pl.program_id(1)
    step = b * PAIRS + p
    red = Reduce(me, units, ins, outs, refs[2 * narr + 18:])
    row = Rows(me, pack, mine_ref, RX, RZ, xs, xr, zs, zr)

    @pl.when(step == 0)
    def _():
        greet(me)
        red.run(plan["first"])

    @pl.when(p == 0)
    def _():
        lay_out(me, shared_ref, b, span, cond_ref, dl, ds, hl, hs)
        dqr_ref[...] = jnp.zeros_like(dqr_ref)
        ddl[...] = jnp.zeros_like(ddl)
        dds[...] = jnp.zeros_like(dds)

    pair_back(span, chunk, p, qh_ref, qr_ref, Pair(hl, p), Pair(hs, p), dl, ds, cond_ref, bl_ref, bs_ref, lse_ref, o_ref, g_ref, dqh_ref, dqr_ref, Pair(dhl, p), Pair(dhs, p), ddl, dds)

    @pl.when(p == PAIRS - 1)
    def _():
        pack_up(me, b, span, cond_ref, pack, ddl, dds, dhl, dhs)
        row.begin(b)

    def act(items):
        for it in items:
            if it[0] == "row":
                getattr(row, it[1])(it[2])
            else:
                red.run([it])
    for s, items in plan["steps"].items():
        pl.when(step == s)(functools.partial(act, items))

def attend_back_reduce(qh, qr, shared, cond, bl, bs, lse, o, g, grads, units, plan, cid):
    rows, pairs, _, nq = qh.shape
    n = shared.shape[0]
    span = nq // 2
    nk = n * span
    narr, nu = len(grads), len(units)
    full = lambda *s: pl.BlockSpec((1, *s), lambda b, p: (b, *([0] * len(s))))
    pairb = lambda *s: pl.BlockSpec((1, 1, *s), lambda b, p: (b, p, *([0] * len(s))))
    tok = pl.BlockSpec((1, nq, 128), lambda b, p: (b, 0, p))
    sd = jax.ShapeDtypeStruct
    DMA = pltpu.SemaphoreType.DMA
    V = pltpu.VMEM
    whole = pl.BlockSpec(memory_space=pltpu.VMEM)
    far = pl.BlockSpec(memory_space=pl.ANY)
    part = shared.shape[2:]
    scratch = [V((1, 256, nk), BF16)] * 2 + [V((PAIRS, 8, nk), F32)] * 2 + [V((1, 256, nk), F32)] * 2 + [V((PAIRS, 8, nk), F32)] * 2
    scratch += [V((rows, n, *part), BF16), V((rows, NZ, *part), BF16), V((rows, NZ, *part), BF16)] + [DMA((rows, NZ))] * 4
    return pl.pallas_call(
        functools.partial(back_kernel, span, min(512, nk), units, narr, plan),
        grid=(rows, pairs),
        out_shape=[sd((rows, pairs, 12, nq), F32), sd((rows, 384, nq), F32), sd((rows, *part), BF16)] + [sd(a.shape[1:], BF16) for a in grads],
        in_specs=[pairb(12, nq), full(384, nq), whole, pl.BlockSpec((1, nk), lambda b, p: (0, 0)), full(1, nk), full(1, nk), full(nq, 128), tok, tok] + [far] * narr,
        out_specs=[pairb(12, nq), full(384, nq), whole] + [far] * narr,
        scratch_shapes=scratch + reduce_scratch(units),
        compiler_params=pltpu.CompilerParams(collective_id=cid, has_side_effects=True, vmem_limit_bytes=60 << 20),
        name="attend_back_reduce",
    )(qh, qr, shared, cond, bl, bs, lse, o, g, *grads)

HEADS, HDIM, QRANK, KVRANK = 16, 64, 6, 2
PAIRS = HEADS // 2
EPSILON = 1e-06


def rms_forward(values, gain):
    scale = lax.rsqrt(jnp.mean(values * values, -1, keepdims=True) + EPSILON)
    unit = values * scale
    return (unit * gain, unit, scale)


def rms_backward(grad_out, unit, scale, gain):
    scaled = grad_out * gain
    grad_in = scale * (scaled - unit * jnp.mean(scaled * unit, -1, keepdims=True))
    return (grad_in, jnp.sum(grad_out * unit, 0))


def rotation(positions):
    half = HDIM // 2
    index = jnp.arange(half).astype(F32)
    inverse = jnp.exp(index * (-math.log(10000.0) / half))
    angles = inverse[:, None] * positions.astype(F32)[None, :]
    return (jnp.cos(angles), jnp.sin(angles))


def rotate(u, cosine, sine):
    rows, depth, slots = u.shape
    v = u.reshape(rows, depth // HDIM, HDIM, slots)
    a, b = v[:, :, :HDIM // 2], v[:, :, HDIM // 2:]
    return jnp.concatenate([a * cosine - b * sine, b * cosine + a * sine], 2).reshape(u.shape)


def dot(a, b, ca, cb):
    return lax.dot_general(a, b, ((ca, cb), ((), ())), preferred_element_type=F32)


def pair_columns(a, ranks):
    return a.reshape(-1, ranks, PAIRS, 2).transpose(0, 2, 1, 3).reshape(a.shape)


def head_columns(a, ranks):
    return a.reshape(-1, PAIRS, ranks, 2).transpose(0, 2, 1, 3).reshape(a.shape)


GATHER_SPECS = [("R", 0, 128), ("P", 0, 128), ("P", 0, 128), ("R", 0, 128), ("P", 1, 1024)]
REDUCE_UNITS = [
    Unit(3, (0, 176), (0, 1024), "P", 1), Unit(2, (0, 128), (0, 1408), "R", 0),
    Unit(3, (176, 176), (0, 1024), "P", 1), Unit(2, (0, 128), (1408, 1408), "R", 0),
    Unit(1, (0, 128), (0, 1408), "P", 0), Unit(1, (0, 128), (1408, 1408), "P", 0),
    Unit(0, (0, 128), (0, 1024), "P", 0)]
REDUCE_PLAN = {
    "first": [("begin", 0, 0, 8), ("begin", 1, 0, 8), ("begin", 2, 0, 8), ("begin", 3, 0, 8), ("begin", 4, 0, 8), ("begin", 5, 0, 8), ("begin", 6, 0, 8), ("core", 0, 0, 4), ("core", 0, 4, 4), ("core", 1, 0, 4)],
    "steps": {
        0: [("core", 1, 4, 4)],
        1: [("core", 3, 0, 4), ("core", 2, 0, 4), ("x", 1, 0, 4)],
        2: [("core", 4, 4, 4)],
        3: [("core", 2, 4, 4), ("y", 2, 0, 4)],
        4: [("core", 3, 4, 4), ("x", 3, 0, 4)],
        5: [("core", 5, 4, 4), ("y", 2, 4, 4), ("core", 4, 0, 4), ("core", 5, 0, 4), ("y", 0, 0, 4), ("core", 6, 4, 4)],
        6: [("x", 2, 0, 4)],
        7: [("y", 0, 4, 4)],
        8: [("x", 0, 0, 4)],
        9: [("y", 4, 0, 4), ("row", "x", 0), ("y", 5, 0, 4), ("core", 6, 0, 4)],
        10: [("y", 6, 4, 4), ("y", 4, 4, 4), ("y", 5, 4, 4)],
        11: [("x", 4, 0, 4)],
        13: [("y", 6, 0, 4), ("own", 0, 0, 1), ("x", 5, 0, 4), ("own", 3, 0, 1)],
        15: [("own", 1, 0, 1), ("own", 4, 0, 1), ("own", 2, 0, 1), ("x", 6, 0, 4), ("own", 5, 0, 1), ("last", 3, 0, 1), ("row", "x", 1), ("own", 6, 0, 1), ("row", "own", 0), ("last", 1, 0, 1), ("last", 6, 0, 1), ("last", 2, 0, 1), ("last", 5, 0, 1), ("last", 4, 0, 1), ("last", 0, 0, 1), ("row", "own", 1), ("end", 0, 0, 1), ("end", 1, 0, 1), ("end", 2, 0, 1), ("end", 3, 0, 1), ("end", 4, 0, 1), ("end", 5, 0, 1), ("end", 6, 0, 1), ("row", "end", 0), ("row", "end", 1)],
    }}
SMALL_UNITS = [Unit(0, (0, 128), (0, 896), "P", 0)]
SMALL_PLAN = [("begin", 0, 0, 8), ("core", 0, 0, 8), ("y", 0, 0, 8), ("x", 0, 0, 4), ("own", 0, 0, 1), ("last", 0, 0, 1), ("end", 0, 0, 1)]


def gather_all(near, arrays):
    if near:
        return gather_weights(arrays, GATHER_SPECS, [0, 2, 4, 3, 1], 0)
    return [lax.all_gather(a, "seq", axis=0) for a in arrays]


def reduce_far(arrays):
    out = []
    for a in arrays:
        own = lax.psum_scatter(a.astype(F32), "seq", scatter_dimension=0, tiled=True)[0]
        out.append(lax.psum(own.astype(BF16), "batch"))
    return out


def per_device(near, tokens, cotangent, lengths, span_order, attn_gain, query_heads, query_dims, key_heads, key_dims,
               value_heads, value_dims, out_proj, ffn_gain, gate_proj, up_proj, down_proj):
    rows, slots, width = tokens.shape
    span = slots // 2
    count = rows * slots
    nseq = span_order.shape[0]
    nk = nseq * span
    me = lax.axis_index("seq")
    key_value_heads = pair_columns(jnp.concatenate([key_heads, value_heads], 1), 4)
    small = jnp.concatenate([pair_columns(query_heads, QRANK), query_dims, key_dims, value_dims, key_value_heads, attn_gain[:, None], ffn_gain[:, None]], 1)
    small = jnp.pad(small, ((0, 0), (0, 896 - small.shape[1])))
    parts = gather_all(near, [small, out_proj, gate_proj, up_proj, down_proj])
    small, w_out, w_gate, w_up, w_down = [p.reshape(-1, p.shape[-1]) for p in parts]
    w_qkv = small[:, :800]
    gain_one = small[:, 800].astype(F32)
    gain_two = small[:, 801].astype(F32)

    offsets = jnp.arange(span, dtype=jnp.int32)
    spans = jnp.concatenate([span_order, span_order], 0)
    spans = lax.dynamic_slice_in_dim(spans, me, nseq, 0)
    local_pos = (spans[0][:, None] * span + offsets[None, :]).reshape(-1)
    cosine, sine = rotation(local_pos)
    chosen = spans[:, 0] < spans[0, 0]
    low_pos = (spans[:, 0][:, None] * span + offsets[None, :]).reshape(1, nk)
    sel_pos = (jnp.where(chosen, spans[:, 0], spans[:, 1])[:, None] * span + offsets[None, :]).reshape(1, nk)
    cond = jnp.repeat(chosen.astype(F32), span).reshape(1, nk)
    low_bias = jnp.where(low_pos < lengths[:, None], 0.0, NEG)[:, None, :]
    sel_bias = jnp.where(sel_pos < lengths[:, None], 0.0, NEG)[:, None, :]

    flat = tokens.reshape(count, width).astype(F32)
    normed_full, unit_one, scale_one = rms_forward(flat, gain_one)
    normed = normed_full.astype(BF16)
    by_row = normed.reshape(rows, slots, width)
    factors = jnp.stack([dot(w_qkv, by_row[b], (0,), (1,)) for b in range(rows)])
    qh = factors[:, :96]
    qr = rotate(factors[:, 96:480], cosine, sine)
    own = jnp.concatenate([rotate(factors[:, 480:608], cosine, sine), factors[:, 608:800]], 1).astype(BF16)
    shared = gather_rows(own, 2) if near else lax.all_gather(own, "seq", axis=0)
    turned = lax.dynamic_slice_in_dim(jnp.concatenate([shared, shared], 0), me, nseq, 0)
    low, high = turned[..., :span], turned[..., span:]
    sel = jnp.where(chosen[:, None, None, None], low, high)
    low = low.transpose(1, 2, 0, 3).reshape(rows, 320, nk)
    sel = sel.transpose(1, 2, 0, 3).reshape(rows, 320, nk)
    qh = qh.reshape(rows, PAIRS, 12, slots)
    in_pairs = lambda a: a[:, 256:].astype(F32).reshape(rows, PAIRS, 8, nk)
    factors = (in_pairs(low), in_pairs(sel), low[:, :256], sel[:, :256])
    masks = (cond, low_bias, sel_bias)
    heads_out, lse = attend(qh, qr, *factors, *masks)
    heads_flat = heads_out.reshape(count, width)

    resid = flat + dot(heads_flat, w_out, (1,), (0,))
    normed_two_full, unit_two, scale_two = rms_forward(resid, gain_two)
    normed_two = normed_two_full.astype(BF16)
    gate = dot(normed_two, w_gate, (1,), (0,))
    up_part = dot(normed_two, w_up, (1,), (0,))
    sigma = jax.nn.sigmoid(gate)
    hidden = (gate * sigma * up_part).astype(BF16)
    output = (resid + dot(hidden, w_down, (1,), (0,))).astype(BF16).reshape(rows, slots, width)

    grad_out = cotangent.reshape(count, width)
    down_grad = dot(hidden, grad_out, (0,), (0,)).astype(BF16)
    d_hidden = dot(grad_out, w_down, (1,), (1,))
    d_gate = (d_hidden * up_part * sigma * (1.0 + gate * (1.0 - sigma))).astype(BF16)
    d_up = (d_hidden * gate * sigma).astype(BF16)
    gate_grad = dot(normed_two, d_gate, (0,), (0,)).astype(BF16)
    up_grad = dot(normed_two, d_up, (0,), (0,)).astype(BF16)
    d_normed_two = dot(d_gate, w_gate, (1,), (1,)) + dot(d_up, w_up, (1,), (1,))
    d_mid, gain_two_grad = rms_backward(d_normed_two, unit_two, scale_two, gain_two)
    d_resid = grad_out.astype(F32) + d_mid
    d_attn = d_resid.astype(BF16)
    out_grad = dot(heads_flat, d_attn, (0,), (0,)).astype(BF16)
    d_heads = dot(d_attn, w_out, (1,), (1,)).astype(BF16).reshape(rows, slots, width)

    grads = [g.reshape(nseq, -1, g.shape[-1]) for g in (out_grad, gate_grad, up_grad, down_grad)]
    if near:
        dqh, dqr, mine, *sums = attend_back_reduce(qh, qr, shared, *masks, lse, heads_out, d_heads, grads, REDUCE_UNITS, REDUCE_PLAN, 1)
    else:
        dqh, dqr, dhl, dhs, ddl, dds = attend_back(qh, qr, *factors, *masks, lse, heads_out, d_heads)
        from_low = jnp.concatenate([ddl, dhl.reshape(rows, 64, nk)], 1).reshape(rows, 320, nseq, span)
        from_sel = jnp.concatenate([dds, dhs.reshape(rows, 64, nk)], 1).reshape(rows, 320, nseq, span)
        pick = chosen[None, None, :, None]
        both = jnp.concatenate([from_low + jnp.where(pick, from_sel, 0.0), jnp.where(pick, 0.0, from_sel)], -1).transpose(2, 0, 1, 3)
        both = lax.dynamic_slice_in_dim(jnp.concatenate([both, both], 0), lax.rem(nseq - me, nseq), nseq, 0)
        mine = lax.psum_scatter(both, "seq", scatter_dimension=0, tiled=True)[0]
        sums = reduce_far(grads)
    mine = mine.astype(F32)
    turned = jnp.concatenate([dqh.reshape(rows, 96, slots), rotate(dqr, cosine, -sine), rotate(mine[:, :128], cosine, -sine), mine[:, 128:]], 1).astype(BF16)
    small_grad = dot(by_row, turned, (0, 1), (0, 2))
    d_normed = dot(turned, w_qkv, (1,), (1,)).reshape(count, width)
    d_first, gain_one_grad = rms_backward(d_normed, unit_one, scale_one, gain_one)
    input_grad = (d_resid + d_first).reshape(rows, slots, width)
    small_grad = jnp.concatenate([small_grad, gain_one_grad[:, None], gain_two_grad[:, None], jnp.zeros((width, 94), F32)], 1).astype(BF16)

    small_grad = small_grad.reshape(nseq, -1, 896)
    small_sum = reduce_weights([small_grad], SMALL_UNITS, SMALL_PLAN, 3)[0] if near else reduce_far([small_grad])[0]
    small_sum = small_sum.astype(F32)
    out_sum, gate_sum, up_sum, down_sum = [g.astype(F32) for g in sums]
    key_value = head_columns(small_sum[:, 736:800], 4)
    return (output, input_grad, small_sum[:, 800], head_columns(small_sum[:, :96], QRANK), small_sum[:, 96:480], key_value[:, :32], small_sum[:, 480:608],
            key_value[:, 32:], small_sum[:, 608:736], out_sum, small_sum[:, 801], gate_sum, up_sum, down_sum)


def solution(mesh):
    near = mesh.shape["seq"] == 8 and mesh.shape["batch"] == 4
    by_slot = P("batch", "seq", None)
    line, table = P("seq"), P("seq", None)
    return jax.shard_map(
        functools.partial(per_device, near),
        mesh=mesh,
        in_specs=(by_slot, by_slot, P("batch"), P(), line, *([table] * 7), line, *([table] * 3)),
        out_specs=(by_slot, by_slot, line, *([table] * 7), line, *([table] * 3)),
        check_vma=False,
    )
```

```python
import functools
import math

import jax
import jax.numpy as jnp
from jax import lax
from jax.experimental import pallas as pl
from jax.experimental.pallas import tpu as pltpu
from jax.sharding import PartitionSpec as P


MESH = pl.DeviceIdType.MESH
NZ, NX = 4, 2

class Place:
    def __init__(self):
        self.seq = lax.axis_index("seq")
        self.batch = lax.axis_index("batch")
        self.z = self.seq // 2
        self.x = lax.rem(self.seq, 2)
        self.y = self.batch // 2
        self.c = lax.rem(self.batch, 2)
        self.up = (jnp.minimum(self.seq + 2, 7), self.batch)
        self.down = (jnp.maximum(self.seq - 2, 0), self.batch)
        self.xp = (self.seq + 1 - 2 * self.x, self.batch)
        self.yp = (self.seq, lax.rem(self.batch + 2, 4))
        self.cp = (self.seq, self.batch + 1 - 2 * self.c)

    def along(self, k):
        return (2 * lax.rem(self.z + k, NZ) + self.x, self.batch)

def greet(me):
    bar = pltpu.get_barrier_semaphore()
    def sig(d):
        pl.semaphore_signal(bar, inc=1, device_id=d, device_id_type=MESH)
    for k in range(1, NZ):
        sig(me.along(k))
    sig(me.xp); sig(me.yp); sig(me.cp)
    pl.semaphore_wait(bar, NZ + 2)

class Unit:
    def __init__(self, arr, row, col, flow, axis):
        self.arr, self.row, self.col, self.flow, self.axis = arr, row, col, flow, axis
        self.shape = (row[1], col[1])
        h = list(self.shape); h[axis] //= 2
        self.half = tuple(h)
        q = list(h)
        if flow == "P": q[axis] //= 2
        self.piece = tuple(q)

def rect(unit, ref, part, nparts):
    start = [unit.row[0], unit.col[0]]
    size = list(unit.shape)
    size[unit.axis] //= nparts
    idx = []
    for d in range(2):
        if d == unit.axis:
            off = part * size[d] + start[d]
            idx.append(pl.ds(pl.multiple_of(off, 16 if d == 0 else 128), size[d]))
        else:
            idx.append(pl.ds(start[d], size[d]))
    return ref.at[tuple(idx)]

class Reduce:
    def __init__(self, me, units, ins, outs, scratch):
        self.me, self.units, self.ins, self.outs = me, units, ins, outs
        nu = len(units)
        self.A, self.RC, self.RY, self.RX, self.RZ, self.RF = [scratch[i * nu:(i + 1) * nu] for i in range(6)]
        self.ls, self.cs, self.cr, self.ys, self.yr, self.xs, self.xr, self.zs, self.zr, self.fs, self.fr, self.os_ = scratch[6 * nu:]

    def shard_at(self, i):
        me = self.me
        zz = lax.rem(me.z + 1 + lax.rem(i, NZ), NZ)
        xx = jnp.where(i < NZ, 1 - me.x, me.x)
        return zz, xx, 2 * zz + xx

    def sub(self, u, ref, y):
        if u.flow == "R":
            return ref
        n = u.piece[u.axis]
        idx = [slice(None)] * 2
        idx[u.axis] = pl.ds(pl.multiple_of(y * n, n), n)
        return ref.at[tuple(idx)]

    def remote(self, src, dst, ss, rs, dev):
        return pltpu.make_async_remote_copy(src_ref=src, dst_ref=dst, send_sem=ss, recv_sem=rs, device_id=dev, device_id_type=MESH)

    def core_copy(self, k, i):
        u = self.units[k]; zz, xx, s = self.shard_at(i)
        return self.remote(rect(u, self.ins[u.arr].at[s], 1 - self.me.c, 2), self.RC[k].at[s], self.cs.at[k, s], self.cr.at[k, s], self.me.cp)

    def local_copy(self, k, i):
        u = self.units[k]; zz, xx, s = self.shard_at(i)
        return pltpu.make_async_copy(rect(u, self.ins[u.arr].at[s], self.me.c, 2), self.A[k].at[s], self.ls.at[k, s])

    def y_copy(self, k, i):
        u = self.units[k]; zz, xx, s = self.shard_at(i)
        return self.remote(self.sub(u, self.A[k].at[s], 1 - self.me.y), self.RY[k].at[s], self.ys.at[k, s], self.yr.at[k, s], self.me.yp)

    def x_copy(self, k, zz):
        u, me = self.units[k], self.me
        return self.remote(self.sub(u, self.A[k].at[2 * zz + 1 - me.x], me.y), self.RX[k].at[zz], self.xs.at[k, zz], self.xr.at[k, zz], me.xp)

    def z_copy(self, k, zz):
        u, me = self.units[k], self.me
        return self.remote(self.mine(k, zz), self.RZ[k].at[me.z], self.zs.at[k, zz], self.zr.at[k, me.z], (2 * zz + me.x, me.batch))

    def z_recv(self, k, zz):
        u, me = self.units[k], self.me
        return self.remote(self.RZ[k].at[zz], self.RZ[k].at[zz], self.zs.at[k, zz], self.zr.at[k, zz], (2 * zz + me.x, me.batch))

    def mine(self, k, zz):
        return self.sub(self.units[k], self.A[k].at[2 * zz + self.me.x], self.me.y)

    @staticmethod
    def add(dst, src):
        dst[...] = dst[...] + src[...]

    def begin(self, k, i):
        self.core_copy(k, i).start()
        self.local_copy(k, i).start()

    def core(self, k, i):
        u = self.units[k]; zz, xx, s = self.shard_at(i)
        self.local_copy(k, i).wait()
        self.core_copy(k, i).wait_recv()
        self.add(self.A[k].at[s], self.RC[k].at[s])
        if u.flow == "P":
            self.y_copy(k, i).start()
        else:
            pl.when(i < NZ)(lambda: self.x_copy(k, zz).start())

    def y(self, k, i):
        u = self.units[k]; zz, xx, s = self.shard_at(i)
        self.y_copy(k, i).wait_recv()
        self.add(self.sub(u, self.A[k].at[s], self.me.y), self.RY[k].at[s])
        pl.when(i < NZ)(lambda: self.x_copy(k, zz).start())

    def x(self, k, i):
        me = self.me
        zz = lax.rem(me.z + 1 + i, NZ)
        self.x_copy(k, zz).wait_recv()
        self.add(self.mine(k, zz), self.RX[k].at[zz])
        pl.when(zz != me.z)(lambda: self.z_copy(k, zz).start())

    def fin_y(self, k):
        u, me = self.units[k], self.me
        mine = self.mine(k, me.z)
        dst = rect(u, self.outs[u.arr], 2 * me.c + me.y, 4) if u.flow == "P" else self.RF[k]
        return self.remote(mine, dst, self.fs.at[k, 0], self.fr.at[k, 0], me.yp)

    def fin_c(self, k, w):
        u, me = self.units[k], self.me
        if u.flow == "P":
            if w == 0:
                return self.remote(self.mine(k, me.z), rect(u, self.outs[u.arr], 2 * me.c + me.y, 4), self.fs.at[k, 1], self.fr.at[k, 1], me.cp)
            v = rect(u, self.outs[u.arr], 2 * me.c + 1 - me.y, 4)
            return self.remote(v, v, self.fs.at[k, 2], self.fr.at[k, 2], me.cp)
        return self.remote(self.RF[k], rect(u, self.outs[u.arr], me.c, 2), self.fs.at[k, 1], self.fr.at[k, 1], me.cp)

    def out_copy(self, k):
        u, me = self.units[k], self.me
        if u.flow == "P":
            return pltpu.make_async_copy(self.mine(k, me.z), rect(u, self.outs[u.arr], 2 * me.c + me.y, 4), self.os_.at[k])
        return pltpu.make_async_copy(self.RF[k], rect(u, self.outs[u.arr], me.c, 2), self.os_.at[k])

    def own(self, k, i):
        me = self.me
        def body(i, c):
            zz = lax.rem(me.z + i, NZ)
            self.z_recv(k, zz).wait_recv()
            self.add(self.mine(k, me.z), self.RZ[k].at[zz])
            return c
        lax.fori_loop(1, NZ, body, 0)
        self.fin_y(k).start()
        if self.units[k].flow == "P":
            self.out_copy(k).start()
            self.fin_c(k, 0).start()

    def last(self, k, i):
        self.fin_y(k).wait_recv()
        if self.units[k].flow == "P":
            self.fin_c(k, 1).start()
        else:
            self.add(self.RF[k], self.mine(k, self.me.z))
            self.out_copy(k).start()
            self.fin_c(k, 0).start()

    def end(self, k, i):
        me = self.me
        flow = self.units[k].flow
        for w in range(2 if flow == "P" else 1):
            self.fin_c(k, w).wait_recv()
            self.fin_c(k, w).wait_send()
        self.out_copy(k).wait()
        self.fin_y(k).wait_send()
        def body(i, c):
            self.core_copy(k, i).wait_send()
            if flow == "P": self.y_copy(k, i).wait_send()
            return c
        lax.fori_loop(0, 8, body, 0)
        def body(zz, c):
            self.x_copy(k, zz).wait_send()
            pl.when(zz != me.z)(lambda: self.z_copy(k, zz).wait_send())
            return c
        lax.fori_loop(0, NZ, body, 0)

    def run(self, plan):
        for step, k, first, n in plan:
            fn = getattr(self, step)
            if n == 1:
                fn(k, first)
            else:
                def body(i, c):
                    fn(k, i)
                    return c
                lax.fori_loop(first, first + n, body, 0)

def reduce_kernel(units, narr, plan, *refs):
    me = Place()
    greet(me)
    red = Reduce(me, units, refs[:narr], refs[narr:2 * narr], refs[2 * narr:])
    red.run(plan)

def reduce_scratch(units):
    nu = len(units)
    DMA = pltpu.SemaphoreType.DMA
    bf = jnp.bfloat16
    V = pltpu.VMEM
    return ([V((8, *u.half), bf) for u in units] + [V((8, *u.half), bf) for u in units]
        + [V((8, *u.piece) if u.flow == "P" else (16, 128), bf) for u in units] + [V((4, *u.piece), bf) for u in units]
        + [V((4, *u.piece), bf) for u in units] + [V(u.piece if u.flow == "R" else (16, 128), bf) for u in units]
        + [DMA((nu, 8))] * 5 + [DMA((nu, 4))] * 4 + [DMA((nu, 3))] * 2 + [DMA((nu,))])

def reduce_weights(arrays, units, plan, cid):
    narr = len(arrays)
    return pl.pallas_call(
        functools.partial(reduce_kernel, units, narr, plan),
        out_shape=[jax.ShapeDtypeStruct(a.shape[1:], a.dtype) for a in arrays],
        in_specs=[pl.BlockSpec(memory_space=pl.ANY)] * narr,
        out_specs=[pl.BlockSpec(memory_space=pl.ANY)] * narr,
        scratch_shapes=reduce_scratch(units),
        compiler_params=pltpu.CompilerParams(collective_id=cid, has_side_effects=True, vmem_limit_bytes=58 << 20),
        name="reduce_weights",
    )(*arrays)

F32, BF16 = jnp.float32, jnp.bfloat16
NEG = -1e30

def nn(a, b):
    return lax.dot_general(a, b, (((1,), (0,)), ((), ())), preferred_element_type=F32)

def nt(a, b):
    return lax.dot_general(a, b, (((1,), (1,)), ((), ())), preferred_element_type=F32)

def expand(heads, dims, base):
    parts = []
    for h in range(2):
        parts.append((heads[base + h:base + h + 1] * dims[0] + heads[base + 2 + h:base + 3 + h] * dims[1]) * 0.5)
    return jnp.concatenate(parts, 0)

def queries(qh, qr):
    parts = []
    for h in range(2):
        total = qh[h:h + 1] * qr[0:64]
        for r in range(1, 6):
            total = total + qh[2 * r + h:2 * r + h + 1] * qr[64 * r:64 * r + 64]
        parts.append(total)
    return jnp.concatenate(parts, 0) / 6.0

def lanes_below(shape, n):
    return lax.broadcasted_iota(jnp.int32, shape, 1) < n

def stack_heads(part):
    first = lanes_below(part.shape, 64)
    zero = jnp.zeros_like(part)
    return jnp.concatenate([jnp.where(first, part, zero), jnp.where(first, zero, part)], 0)

def unstack_heads(part):
    n = part.shape[0] // 2
    return jnp.where(lanes_below((n, 128), 64), part[:n], part[n:])

def causal_bias(n2, span):
    row = lax.broadcasted_iota(jnp.int32, (n2, span), 0) % span
    col = lax.broadcasted_iota(jnp.int32, (n2, span), 1)
    return jnp.where(col <= row, 0.0, NEG)

def pair_factors(heads, dims, cond, base, at):
    hl, hs = heads
    dl, ds = dims
    low = expand(hl, (dl[at:at + 64].astype(F32), dl[at + 64:at + 128].astype(F32)), base).astype(BF16)
    sel = expand(hs, (ds[at:at + 64].astype(F32), ds[at + 64:at + 128].astype(F32)), base)
    left = jnp.where(cond > 0.5, sel, 0.0).astype(BF16)
    right = jnp.where(cond > 0.5, 0.0, sel).astype(BF16)
    return low, jnp.concatenate([left, right], 0)

def attend_kernel(span, chunk, qh_ref, qr_ref, hl_ref, hs_ref, dl_ref, ds_ref, cond_ref, bl_ref, bs_ref, o_ref, lse_ref, s1, s2):
    pair_forward(span, chunk, pl.program_id(1), qh_ref[0, 0], qr_ref[0], hl_ref[0, 0], hs_ref[0, 0], dl_ref, ds_ref, cond_ref, bl_ref, bs_ref, o_ref, lse_ref, s1, s2)

def pair_forward(span, chunk, p, qh, qr, hl, hs, dl_ref, ds_ref, cond_ref, bl_ref, bs_ref, o_ref, lse_ref, s1, s2):
    n2 = 2 * span
    nk = dl_ref.shape[-1]
    qt = queries(qh, qr)
    q = (qt.astype(BF16).astype(F32).T * 0.125).astype(BF16)
    qlo, qhi = stack_heads(q[:span]), stack_heads(q[span:])
    qboth = jnp.concatenate([qlo, qhi], 1)
    heads = (hl, hs)
    dims = (dl_ref[0], ds_ref[0])
    cond = cond_ref[...]
    klo, ksel = pair_factors(heads, dims, cond, 0, 0)
    vlo, vsel = pair_factors(heads, dims, cond, 4, 128)
    tri = causal_bias(n2, span)
    width = min(128, chunk)
    mlo = jnp.full((n2, width), NEG, F32)
    mhi = jnp.full((n2, width), NEG, F32)
    s3 = nn(qlo, klo[:, :span]) + bl_ref[0][:, :span] + tri
    m3 = jnp.max(s3, -1, keepdims=True)
    for c in range(0, nk, chunk):
        sl = slice(c, c + chunk)
        a = nn(qhi, klo[:, sl]) + bl_ref[0][:, sl]
        s1[:, sl] = a
        b = nn(qboth, ksel[:, sl]) + bs_ref[0][:, sl]
        if c == 0:
            b = jnp.concatenate([b[:, :span] + tri, b[:, span:]], 1)
        s2[:, sl] = b
        for i in range(0, chunk, width):
            on = cond[:, c + i:c + i + width] > 0.5
            ai, bi = a[:, i:i + width], b[:, i:i + width]
            mlo = jnp.maximum(mlo, jnp.where(on, bi, NEG))
            mhi = jnp.maximum(mhi, jnp.maximum(ai, jnp.where(on, NEG, bi)))
    mlo = jnp.maximum(jnp.max(mlo, -1, keepdims=True), m3)
    mhi = jnp.max(mhi, -1, keepdims=True)
    e3 = jnp.exp(s3 - mlo)
    tlo = jnp.zeros((n2, width), F32)
    thi = jnp.zeros((n2, width), F32)
    o3 = nt(e3.astype(BF16), vlo[:, :span])
    o1 = jnp.zeros((n2, 128), F32)
    o2 = jnp.zeros((n2, 256), F32)
    for c in range(0, nk, chunk):
        sl = slice(c, c + chunk)
        on = cond[:, sl] > 0.5
        a = jnp.exp(s1[:, sl] - mhi)
        b = jnp.exp(s2[:, sl] - jnp.where(on, mlo, mhi))
        blo = jnp.where(on, b, 0.0)
        bhi = a + jnp.where(on, 0.0, b)
        for i in range(0, chunk, width):
            tlo = tlo + blo[:, i:i + width]
            thi = thi + bhi[:, i:i + width]
        o1 = o1 + nt(a.astype(BF16), vlo[:, sl])
        o2 = o2 + nt(b.astype(BF16), vsel[:, sl])
    llo = jnp.sum(tlo, -1, keepdims=True) + jnp.sum(e3, -1, keepdims=True)
    lhi = jnp.sum(thi, -1, keepdims=True)
    olo = unstack_heads((o2[:, :128] + o3) / llo)
    ohi = unstack_heads((o2[:, 128:] + o1) / lhi)
    o_ref[0] = jnp.concatenate([olo, ohi], 0).astype(BF16)
    lane = lax.broadcasted_iota(jnp.int32, (span, 128), 1)
    tlo = mlo + jnp.log(llo)
    thi = mhi + jnp.log(lhi)
    old = jnp.where(p == 0, 0.0, lse_ref[0])
    new = []
    for k, t in enumerate((tlo, thi)):
        part = old[k * span:(k + 1) * span]
        part = jnp.where(lane == 2 * p, t[:span], part)
        new.append(jnp.where(lane == 2 * p + 1, t[span:], part))
    lse_ref[0] = jnp.concatenate(new, 0)

def attend(qh, qr, hl, hs, dl, ds, cond, bl, bs):
    rows, pairs, _, nq = qh.shape
    nk = dl.shape[-1]
    span = nq // 2
    chunk = min(512, nk)
    full = lambda *s: pl.BlockSpec((1, *s), lambda b, p: (b, *([0] * len(s))))
    pairb = lambda *s: pl.BlockSpec((1, 1, *s), lambda b, p: (b, p, *([0] * len(s))))
    return pl.pallas_call(
        functools.partial(attend_kernel, span, chunk),
        grid=(rows, pairs),
        out_shape=[jax.ShapeDtypeStruct((rows, nq, pairs * 128), BF16), jax.ShapeDtypeStruct((rows, nq, 128), F32)],
        in_specs=[pairb(12, nq), full(384, nq), pairb(8, nk), pairb(8, nk), full(256, nk), full(256, nk),
                  pl.BlockSpec((1, nk), lambda b, p: (0, 0)), full(1, nk), full(1, nk)],
        out_specs=[pl.BlockSpec((1, nq, 128), lambda b, p: (b, 0, p)), full(nq, 128)],
        scratch_shapes=[pltpu.VMEM((nq, nk), F32), pltpu.VMEM((nq, nk), F32)],
        compiler_params=pltpu.CompilerParams(vmem_limit_bytes=56 << 20),
        name="attend",
    )(qh, qr, hl, hs, dl, ds, cond, bl, bs)

def attend_back_kernel(span, chunk, qh_ref, qr_ref, hl_ref, hs_ref, dl_ref, ds_ref, cond_ref, bl_ref, bs_ref, lse_ref, o_ref, g_ref,
                       dqh_ref, dqr_ref, dhl_ref, dhs_ref, ddl_ref, dds_ref):
    p = pl.program_id(1)
    @pl.when(p == 0)
    def _():
        dqr_ref[...] = jnp.zeros_like(dqr_ref)
        ddl_ref[...] = jnp.zeros_like(ddl_ref)
        dds_ref[...] = jnp.zeros_like(dds_ref)
    pair_back(span, chunk, p, qh_ref, qr_ref, Pair(hl_ref, 0, 0), Pair(hs_ref, 0, 0), dl_ref, ds_ref, cond_ref, bl_ref, bs_ref, lse_ref, o_ref, g_ref,
              dqh_ref, dqr_ref, Pair(dhl_ref, 0, 0), Pair(dhs_ref, 0, 0), ddl_ref, dds_ref)

class Pair:
    def __init__(self, ref, *at):
        self.ref, self.at = ref, at

    def all(self):
        return self.ref[self.at]

    def row(self, j, sl):
        return self.ref[(*self.at, slice(j, j + 1), sl)]

    def put(self, j, sl, value):
        self.ref[(*self.at, slice(j, j + 1), sl)] = value

def pair_back(span, chunk, p, qh_ref, qr_ref, hl, hs, dl_ref, ds_ref, cond_ref, bl_ref, bs_ref, lse_ref, o_ref, g_ref,
              dqh_ref, dqr_ref, dhl, dhs, ddl_ref, dds_ref):
    n2 = 2 * span
    nk = dl_ref.shape[-1]
    qh, qr = qh_ref[0, 0], qr_ref[0]
    qt = (queries(qh, qr).astype(BF16).astype(F32)) * 0.125
    q = qt.T.astype(BF16)
    qlo, qhi = stack_heads(q[:span]), stack_heads(q[span:])
    qboth = jnp.concatenate([qlo, qhi], 1)
    g = g_ref[0]
    glo, ghi = stack_heads(g[:span]), stack_heads(g[span:])
    gboth = jnp.concatenate([glo, ghi], 1)
    gt = g.astype(F32).T
    first = lax.broadcasted_iota(jnp.int32, (128, span), 0) < 64
    def stack_lanes(part):
        return jnp.concatenate([jnp.where(first, part, 0.0), jnp.where(first, 0.0, part)], 1).astype(BF16)
    qtlo, qthi = stack_lanes(qt[:, :span]), stack_lanes(qt[:, span:])
    gtlo, gthi = stack_lanes(gt[:, :span]), stack_lanes(gt[:, span:])
    qtboth = jnp.concatenate([qtlo, qthi], 0)
    gtboth = jnp.concatenate([gtlo, gthi], 0)
    prod = g.astype(F32) * o_ref[0].astype(F32)
    flane = lanes_below((n2, 128), 64)
    d0 = jnp.sum(jnp.where(flane, prod, 0.0), -1, keepdims=True)
    d1 = jnp.sum(jnp.where(flane, 0.0, prod), -1, keepdims=True)
    lane = lax.broadcasted_iota(jnp.int32, (n2, 128), 1)
    lse = lse_ref[0]
    l0 = jnp.sum(jnp.where(lane == 2 * p, lse, 0.0), -1, keepdims=True)
    l1 = jnp.sum(jnp.where(lane == 2 * p + 1, lse, 0.0), -1, keepdims=True)
    dello, delhi = jnp.concatenate([d0[:span], d1[:span]], 0), jnp.concatenate([d0[span:], d1[span:]], 0)
    lselo, lsehi = jnp.concatenate([l0[:span], l1[:span]], 0), jnp.concatenate([l0[span:], l1[span:]], 0)
    heads = (hl.all(), hs.all())
    dims = (dl_ref[0], ds_ref[0])
    cond = cond_ref[...]
    klo, ksel = pair_factors(heads, dims, cond, 0, 0)
    vlo, vsel = pair_factors(heads, dims, cond, 4, 128)
    tri = causal_bias(n2, span)

    def put(dkt, h, d_ref, hd, dd_ref, base, at, sl):
        for r in range(2):
            dim = d_ref[0, at + 64 * r:at + 64 * r + 64, sl].astype(F32)
            total = None
            for k in range(2):
                part = dkt[64 * k:64 * k + 64]
                j = base + 2 * r + k
                hd.put(j, sl, jnp.sum(part * dim, 0, keepdims=True) * 0.5)
                term = part * h.row(j, sl)
                total = term if total is None else total + term
            dd_ref[0, at + 64 * r:at + 64 * r + 64, sl] += total * 0.5

    s3 = nn(qlo, klo[:, :span]) + bl_ref[0][:, :span] + tri
    p3 = jnp.exp(s3 - lselo)
    dp3 = nn(glo, vlo[:, :span])
    ds3 = (p3 * (dp3 - dello)).astype(BF16)
    p3 = p3.astype(BF16)
    dq3 = nt(ds3, klo[:, :span])
    dk3 = nn(qtlo, ds3)
    dv3 = nn(gtlo, p3)
    dq1 = jnp.zeros((n2, 128), F32)
    dq2 = jnp.zeros((n2, 256), F32)
    for c in range(0, nk, chunk):
        sl = slice(c, c + chunk)
        pa = jnp.exp(nn(qhi, klo[:, sl]) + bl_ref[0][:, sl] - lsehi)
        dpa = nn(ghi, vlo[:, sl])
        dsa = (pa * (dpa - delhi)).astype(BF16)
        pa = pa.astype(BF16)
        dq1 = dq1 + nt(dsa, klo[:, sl])
        dk = nn(qthi, dsa)
        dv = nn(gthi, pa)
        if c == 0:
            dk = jnp.concatenate([dk[:, :span] + dk3, dk[:, span:]], 1)
            dv = jnp.concatenate([dv[:, :span] + dv3, dv[:, span:]], 1)
        put(dk, hl, dl_ref, dhl, ddl_ref, 0, 0, sl)
        put(dv, hl, dl_ref, dhl, ddl_ref, 4, 128, sl)
    for c in range(0, nk, chunk):
        sl = slice(c, c + chunk)
        on = cond[:, sl] > 0.5
        s = nn(qboth, ksel[:, sl]) + bs_ref[0][:, sl]
        if c == 0:
            s = jnp.concatenate([s[:, :span] + tri, s[:, span:]], 1)
        pb = jnp.exp(s - jnp.where(on, lselo, lsehi))
        dpb = nn(gboth, vsel[:, sl])
        dsb = (pb * (dpb - jnp.where(on, dello, delhi))).astype(BF16)
        pb = pb.astype(BF16)
        dq2 = dq2 + nt(dsb, ksel[:, sl])
        dk = nn(qtboth, dsb)
        dv = nn(gtboth, pb)
        dk = jnp.where(on, dk[:128], dk[128:])
        dv = jnp.where(on, dv[:128], dv[128:])
        put(dk, hs, ds_ref, dhs, dds_ref, 0, 0, sl)
        put(dv, hs, ds_ref, dhs, dds_ref, 4, 128, sl)
    dqlo = unstack_heads(dq2[:, :128] + dq3)
    dqhi = unstack_heads(dq2[:, 128:] + dq1)
    dqt = (jnp.concatenate([dqlo, dqhi], 0) * (0.125 / 6.0)).T
    for r in range(6):
        total = None
        for h in range(2):
            part = dqt[64 * h:64 * h + 64]
            j = 2 * r + h
            dqh_ref[0, 0, j:j + 1, :] = jnp.sum(part * qr[64 * r:64 * r + 64], 0, keepdims=True)
            term = part * qh[j:j + 1]
            total = term if total is None else total + term
        dqr_ref[0, 64 * r:64 * r + 64, :] += total

def attend_back(qh, qr, hl, hs, dl, ds, cond, bl, bs, lse, o, g):
    rows, pairs, _, nq = qh.shape
    nk = dl.shape[-1]
    span = nq // 2
    chunk = min(512, nk)
    full = lambda *s: pl.BlockSpec((1, *s), lambda b, p: (b, *([0] * len(s))))
    pairb = lambda *s: pl.BlockSpec((1, 1, *s), lambda b, p: (b, p, *([0] * len(s))))
    tok = pl.BlockSpec((1, nq, 128), lambda b, p: (b, 0, p))
    sd = jax.ShapeDtypeStruct
    return pl.pallas_call(
        functools.partial(attend_back_kernel, span, chunk),
        grid=(rows, pairs),
        out_shape=[sd((rows, pairs, 12, nq), F32), sd((rows, 384, nq), F32), sd((rows, pairs, 8, nk), F32), sd((rows, pairs, 8, nk), F32),
                   sd((rows, 256, nk), F32), sd((rows, 256, nk), F32)],
        in_specs=[pairb(12, nq), full(384, nq), pairb(8, nk), pairb(8, nk), full(256, nk), full(256, nk),
                  pl.BlockSpec((1, nk), lambda b, p: (0, 0)), full(1, nk), full(1, nk), full(nq, 128), tok, tok],
        out_specs=[pairb(12, nq), full(384, nq), pairb(8, nk), pairb(8, nk), full(256, nk), full(256, nk)],
        compiler_params=pltpu.CompilerParams(vmem_limit_bytes=56 << 20),
        name="attend_back",
    )(qh, qr, hl, hs, dl, ds, cond, bl, bs, lse, o, g)

class Rows:
    def __init__(self, me, pack, out, RX, RZ, xs, xr, zs, zr):
        self.me, self.pack, self.out, self.RX, self.RZ = me, pack, out, RX, RZ
        self.xs, self.xr, self.zs, self.zr = xs, xr, zs, zr

    def remote(self, src, dst, ss, rs, dev):
        return pltpu.make_async_remote_copy(src_ref=src, dst_ref=dst, send_sem=ss, recv_sem=rs, device_id=dev, device_id_type=MESH)

    def x_copy(self, b, zz):
        return self.remote(self.pack.at[b, 2 * zz + 1 - self.me.x], self.RX.at[b, zz], self.xs.at[b, zz], self.xr.at[b, zz], self.me.xp)

    def z_copy(self, b, zz):
        me = self.me
        return self.remote(self.mine(b, zz), self.RZ.at[b, me.z], self.zs.at[b, zz], self.zr.at[b, me.z], (2 * zz + me.x, me.batch))

    def z_recv(self, b, zz):
        me = self.me
        return self.remote(self.RZ.at[b, zz], self.RZ.at[b, zz], self.zs.at[b, zz], self.zr.at[b, zz], (2 * zz + me.x, me.batch))

    def mine(self, b, zz):
        return self.pack.at[b, 2 * zz + self.me.x]

    @staticmethod
    def add(dst, src):
        dst[...] = dst[...] + src[...]

    def begin(self, b):
        def body(i, c):
            self.x_copy(b, lax.rem(self.me.z + 1 + i, NZ)).start()
            return c
        lax.fori_loop(0, NZ, body, 0)

    def x(self, b):
        me = self.me
        def body(i, c):
            zz = lax.rem(me.z + 1 + i, NZ)
            self.x_copy(b, zz).wait_recv()
            self.add(self.mine(b, zz), self.RX.at[b, zz])
            pl.when(zz != me.z)(lambda: self.z_copy(b, zz).start())
            return c
        lax.fori_loop(0, NZ, body, 0)

    def own(self, b):
        me = self.me
        def body(i, c):
            zz = lax.rem(me.z + i, NZ)
            self.z_recv(b, zz).wait_recv()
            self.add(self.mine(b, me.z), self.RZ.at[b, zz])
            return c
        lax.fori_loop(1, NZ, body, 0)
        self.out[b] = self.pack[b, me.seq]

    def end(self, b):
        me = self.me
        def sent(zz, c):
            self.x_copy(b, zz).wait_send()
            pl.when(zz != me.z)(lambda: self.z_copy(b, zz).wait_send())
            return c
        lax.fori_loop(0, NZ, sent, 0)

def lay_out(me, shared_ref, b, span, cond_ref, dl, ds, hl, hs):
    n = shared_ref.shape[0]
    for i in range(n):
        j = lax.rem(me.seq + i, n)
        sl = slice(i * span, (i + 1) * span)
        on = cond_ref[:, sl] > 0.5
        low = shared_ref[j, b, :256, :span].astype(F32)
        high = shared_ref[j, b, :256, span:].astype(F32)
        dl[0, :, sl] = low.astype(BF16)
        ds[0, :, sl] = jnp.where(on, low, high).astype(BF16)
        low = shared_ref[j, b, 256:, :span].astype(F32)
        high = shared_ref[j, b, 256:, span:].astype(F32)
        hl[:, :, sl] = low.reshape(PAIRS, 8, span)
        hs[:, :, sl] = jnp.where(on, low, high).reshape(PAIRS, 8, span)

def pack_up(me, b, span, cond_ref, pack, ddl, dds, dhl, dhs):
    n = pack.shape[1]
    for i in range(n):
        j = lax.rem(me.seq + i, n)
        sl = slice(i * span, (i + 1) * span)
        on = cond_ref[:, sl] > 0.5
        for at, lo, se in ((0, ddl[0, :, sl], dds[0, :, sl]), (256, dhl[:, :, sl].reshape(64, span), dhs[:, :, sl].reshape(64, span))):
            rows = slice(at, at + lo.shape[0])
            pack[b, j, rows, :span] = (lo + jnp.where(on, se, 0.0)).astype(BF16)
            pack[b, j, rows, span:] = jnp.where(on, 0.0, se).astype(BF16)

def back_kernel(span, chunk, units, narr, plan, qh_ref, qr_ref, shared_ref, cond_ref, bl_ref, bs_ref, lse_ref, o_ref, g_ref, *refs):
    ins = refs[:narr]
    dqh_ref, dqr_ref, mine_ref = refs[narr:narr + 3]
    outs = refs[narr + 3:2 * narr + 3]
    dl, ds, hl, hs, ddl, dds, dhl, dhs, pack, RX, RZ, xs, xr, zs, zr = refs[2 * narr + 3:2 * narr + 18]
    me = Place()
    b, p = pl.program_id(0), pl.program_id(1)
    step = b * PAIRS + p
    red = Reduce(me, units, ins, outs, refs[2 * narr + 18:])
    row = Rows(me, pack, mine_ref, RX, RZ, xs, xr, zs, zr)

    @pl.when(step == 0)
    def _():
        greet(me)
        red.run(plan["first"])

    @pl.when(p == 0)
    def _():
        lay_out(me, shared_ref, b, span, cond_ref, dl, ds, hl, hs)
        dqr_ref[...] = jnp.zeros_like(dqr_ref)
        ddl[...] = jnp.zeros_like(ddl)
        dds[...] = jnp.zeros_like(dds)

    pair_back(span, chunk, p, qh_ref, qr_ref, Pair(hl, p), Pair(hs, p), dl, ds, cond_ref, bl_ref, bs_ref, lse_ref, o_ref, g_ref, dqh_ref, dqr_ref, Pair(dhl, p), Pair(dhs, p), ddl, dds)

    @pl.when(p == PAIRS - 1)
    def _():
        pack_up(me, b, span, cond_ref, pack, ddl, dds, dhl, dhs)
        row.begin(b)

    def act(items):
        for it in items:
            if it[0] == "row":
                getattr(row, it[1])(it[2])
            else:
                red.run([it])
    for s, items in plan["steps"].items():
        pl.when(step == s)(functools.partial(act, items))

def attend_back_reduce(qh, qr, shared, cond, bl, bs, lse, o, g, grads, units, plan, cid):
    rows, pairs, _, nq = qh.shape
    n = shared.shape[0]
    span = nq // 2
    nk = n * span
    narr, nu = len(grads), len(units)
    full = lambda *s: pl.BlockSpec((1, *s), lambda b, p: (b, *([0] * len(s))))
    pairb = lambda *s: pl.BlockSpec((1, 1, *s), lambda b, p: (b, p, *([0] * len(s))))
    tok = pl.BlockSpec((1, nq, 128), lambda b, p: (b, 0, p))
    sd = jax.ShapeDtypeStruct
    DMA = pltpu.SemaphoreType.DMA
    V = pltpu.VMEM
    whole = pl.BlockSpec(memory_space=pltpu.VMEM)
    far = pl.BlockSpec(memory_space=pl.ANY)
    part = shared.shape[2:]
    scratch = [V((1, 256, nk), BF16)] * 2 + [V((PAIRS, 8, nk), F32)] * 2 + [V((1, 256, nk), F32)] * 2 + [V((PAIRS, 8, nk), F32)] * 2
    scratch += [V((rows, n, *part), BF16), V((rows, NZ, *part), BF16), V((rows, NZ, *part), BF16)] + [DMA((rows, NZ))] * 4
    return pl.pallas_call(
        functools.partial(back_kernel, span, min(512, nk), units, narr, plan),
        grid=(rows, pairs),
        out_shape=[sd((rows, pairs, 12, nq), F32), sd((rows, 384, nq), F32), sd((rows, *part), BF16)] + [sd(a.shape[1:], BF16) for a in grads],
        in_specs=[pairb(12, nq), full(384, nq), whole, pl.BlockSpec((1, nk), lambda b, p: (0, 0)), full(1, nk), full(1, nk), full(nq, 128), tok, tok] + [far] * narr,
        out_specs=[pairb(12, nq), full(384, nq), whole] + [far] * narr,
        scratch_shapes=scratch + reduce_scratch(units),
        compiler_params=pltpu.CompilerParams(collective_id=cid, has_side_effects=True, vmem_limit_bytes=60 << 20),
        name="attend_back_reduce",
    )(qh, qr, shared, cond, bl, bs, lse, o, g, *grads)

class Gather:
    def __init__(self, me, units, ins, outs, sems):
        self.me, self.units, self.ins, self.outs = me, units, ins, outs
        self.zs, self.zr, self.xs, self.xr, self.ys, self.yr, self.cs, self.cr, self.ls = sems

    def remote(self, src, dst, ss, rs, dev):
        return pltpu.make_async_remote_copy(src_ref=src, dst_ref=dst, send_sem=ss, recv_sem=rs, device_id=dev, device_id_type=MESH)

    def view(self, k, shard, y, c):
        u = self.units[k]
        return self.part(u, self.outs[u.arr].at[shard], y, c)

    @staticmethod
    def part(u, ref, y, c):
        return rect(u, ref, 2 * c + y, 4) if u.flow == "P" else rect(u, ref, c, 2)

    def first(self, k, ss, rs, dev):
        u, me = self.units[k], self.me
        return self.remote(self.part(u, self.ins[u.arr], me.y, me.c), self.view(k, me.seq, me.y, me.c), ss, rs, dev)

    def onward(self, k, shard, y, ss, rs, dev):
        v = self.view(k, shard, y, self.me.c)
        return self.remote(v, v, ss, rs, dev)

    def zsend(self, k, zz):
        return self.first(k, self.zs.at[k, zz], self.zr.at[k, self.me.z], (2 * zz + self.me.x, self.me.batch))

    def zrecv(self, k, zz):
        me = self.me
        return self.onward(k, 2 * zz + me.x, me.y, self.zs.at[k, zz], self.zr.at[k, zz], (2 * zz + me.x, me.batch))

    def xown(self, k):
        return self.first(k, self.xs.at[k, self.me.z], self.xr.at[k, self.me.z], self.me.xp)

    def xsend(self, k, zz):
        return self.onward(k, 2 * zz + self.me.x, self.me.y, self.xs.at[k, zz], self.xr.at[k, zz], self.me.xp)

    def xrecv(self, k, zz):
        return self.onward(k, 2 * zz + 1 - self.me.x, self.me.y, self.xs.at[k, zz], self.xr.at[k, zz], self.me.xp)

    def ycopy(self, k, shard, mine):
        return self.onward(k, shard, self.me.y if mine else 1 - self.me.y, self.ys.at[k, shard], self.yr.at[k, shard], self.me.yp)

    def ccopy(self, k, w, shard):
        return self.onward(k, shard, self.me.y if w == 0 else 1 - self.me.y, self.cs.at[k, w, shard], self.cr.at[k, w, shard], self.me.cp)

    def crecv(self, k, w, shard):
        v = self.view(k, shard, self.me.y if w == 0 else 1 - self.me.y, 1 - self.me.c)
        return self.remote(v, v, self.cs.at[k, w, shard], self.cr.at[k, w, shard], self.me.cp)

    def local(self, a):
        return pltpu.make_async_copy(self.ins[a], self.outs[a].at[self.me.seq], self.ls.at[a])

    def other(self, i):
        return lax.rem(self.me.z + i, NZ)

    def begin(self, k, i):
        self.zsend(k, self.other(i)).start()
        pl.when(i == 1)(lambda: self.xown(k).start())

    def spread(self, k, shard):
        if self.units[k].flow == "P":
            self.ycopy(k, shard, True).start()
        self.ccopy(k, 0, shard).start()

    def z(self, k, i):
        zz = self.other(i)
        self.zrecv(k, zz).wait_recv()
        self.xsend(k, zz).start()
        self.spread(k, 2 * zz + self.me.x)

    def x(self, k, i):
        zz = self.other(i)
        self.xrecv(k, zz).wait_recv()
        self.spread(k, 2 * zz + 1 - self.me.x)

    def far(self, i):
        return 2 * self.other(i) + jnp.where(i < NZ, self.me.x, 1 - self.me.x)

    def y(self, k, i):
        shard = self.far(i)
        self.ycopy(k, shard, False).wait_recv()
        self.ccopy(k, 1, shard).start()

    def got(self, k, i):
        for w in range(2 if self.units[k].flow == "P" else 1):
            self.crecv(k, w, self.far(i)).wait_recv()

    def sent(self, k, i):
        me = self.me
        pl.when(i < NZ)(lambda: self.zsend(k, self.other(i)).wait_send())
        pl.when(i < NZ)(lambda: self.xsend(k, self.other(i)).wait_send())
        pl.when(i == NZ)(lambda: self.xown(k).wait_send())
        shard = self.far(i)
        self.ccopy(k, 0, shard).wait_send()
        if self.units[k].flow == "P":
            self.ycopy(k, shard, True).wait_send()
            self.ccopy(k, 1, shard).wait_send()

    def run(self, plan):
        for step, k, first, n in plan:
            fn = getattr(self, step)
            def body(i, c):
                fn(k, i)
                return c
            lax.fori_loop(first, first + n, body, 0)

class RowsGather:
    def __init__(self, me, shared, zs, zr, xs, xr):
        self.me, self.shared, self.zs, self.zr, self.xs, self.xr = me, shared, zs, zr, xs, xr

    def copy(self, b, shard, ss, rs, dev):
        v = self.shared.at[shard, b]
        return pltpu.make_async_remote_copy(src_ref=v, dst_ref=v, send_sem=ss, recv_sem=rs, device_id=dev, device_id_type=MESH)

    def zsend(self, b, zz):
        me = self.me
        return self.copy(b, me.seq, self.zs.at[b, zz], self.zr.at[b, me.z], (2 * zz + me.x, me.batch))

    def zrecv(self, b, zz):
        me = self.me
        return self.copy(b, 2 * zz + me.x, self.zs.at[b, zz], self.zr.at[b, zz], (2 * zz + me.x, me.batch))

    def xsend(self, b, zz):
        return self.copy(b, 2 * zz + self.me.x, self.xs.at[b, zz], self.xr.at[b, zz], self.me.xp)

    def xrecv(self, b, zz):
        return self.copy(b, 2 * zz + 1 - self.me.x, self.xs.at[b, zz], self.xr.at[b, zz], self.me.xp)

    def loop(self, first, fn):
        def body(i, c):
            fn(lax.rem(self.me.z + i, NZ))
            return c
        lax.fori_loop(first, NZ, body, 0)

    def begin(self, b):
        self.loop(1, lambda zz: self.zsend(b, zz).start())
        self.xsend(b, self.me.z).start()

    def z(self, b):
        def one(zz):
            self.zrecv(b, zz).wait_recv()
            self.xsend(b, zz).start()
        self.loop(1, one)

    def x(self, b):
        self.loop(0, lambda zz: self.xrecv(b, zz).wait_recv())

    def end(self, b):
        self.loop(1, lambda zz: self.zsend(b, zz).wait_send())
        self.loop(0, lambda zz: self.xsend(b, zz).wait_send())

def turn_rows(u, cosine, sine):
    out = []
    for r in range(0, u.shape[0], 64):
        a, b = u[r:r + 32], u[r + 32:r + 64]
        out += [a * cosine - b * sine, b * cosine + a * sine]
    return jnp.concatenate(out, 0)

def project(me, span, tok_ref, small_ref, cos_ref, sin_ref, normed_ref, qh_ref, qr_ref, shared_ref, b):
    nq = 2 * span
    d = tok_ref.shape[-1]
    gains = small_ref[:, :, 768:896].reshape(d, 128).astype(F32).T
    x = tok_ref[b].astype(F32)
    unit = x * lax.rsqrt(jnp.mean(x * x, -1, keepdims=True) + 1e-6)
    normed = (unit * gains[32:33]).astype(BF16)
    normed_ref[b] = normed
    w = small_ref[...].reshape(d, 896)
    f = nn(normed, w).T
    qh_ref[b] = f[:96].reshape(PAIRS, 12, nq)
    cosine, sine = cos_ref[...], sin_ref[...]
    qr_ref[b] = turn_rows(f[96:480], cosine, sine)
    own = jnp.concatenate([turn_rows(f[480:608], cosine, sine), f[608:800]], 0)
    shared_ref[me.seq, b] = own.astype(BF16)

def forward_kernel(span, chunk, units, narr, plan, tok_ref, cos_ref, sin_ref, cond_ref, bl_ref, bs_ref, *refs):
    ins = refs[:narr]
    normed_ref, qh_ref, qr_ref, shared_out, o_ref, lse_ref = refs[narr:narr + 6]
    outs = refs[narr + 6:2 * narr + 6]
    shared_ref, small, saved, dl, ds, hl, hs, s1, s2, rzs, rzr, rxs, rxr = refs[2 * narr + 6:2 * narr + 19]
    small_out, outs = outs[0], (small, *outs[1:])
    me = Place()
    b, p = pl.program_id(0), pl.program_id(1)
    step = b * PAIRS + p
    gat = Gather(me, units, ins, outs, refs[2 * narr + 19:])
    saves = (pltpu.make_async_copy(small, small_out, saved.at[0]), pltpu.make_async_copy(shared_ref, shared_out, saved.at[1]))
    row = RowsGather(me, shared_ref, rzs, rzr, rxs, rxr)

    def act(items):
        for it in items:
            if it[0] == "row":
                getattr(row, it[1])(it[2])
            elif it[0] == "project":
                for r in range(tok_ref.shape[0]):
                    project(me, span, tok_ref, small, cos_ref, sin_ref, normed_ref, qh_ref, qr_ref, shared_ref, r)
            elif it[0] == "local":
                for a in range(narr):
                    gat.local(a).start()
                gat.local(0).wait()
            elif it[0] == "locals":
                for a in range(1, narr):
                    gat.local(a).wait()
                for save in saves:
                    save.start()
                for save in saves:
                    save.wait()
            else:
                gat.run([it])

    @pl.when(step == 0)
    def _():
        greet(me)
        act(plan["first"])

    @pl.when(p == 0)
    def _():
        lay_out(me, shared_ref, b, span, cond_ref, dl, ds, hl, hs)

    pair_forward(span, chunk, p, qh_ref[b, p], qr_ref[b], hl[p], hs[p], dl, ds, cond_ref, bl_ref, bs_ref, o_ref, lse_ref, s1, s2)

    for s, items in plan["steps"].items():
        pl.when(step == s)(functools.partial(act, items))

def forward(tokens, cosine, sine, cond, bl, bs, weights, units, plan, cid):
    rows, nq, width = tokens.shape
    span = nq // 2
    n = 2 * NZ
    nk = n * span
    narr, nu = len(weights), len(units)
    chunk = min(512, nk)
    whole = pl.BlockSpec(memory_space=pltpu.VMEM)
    far = pl.BlockSpec(memory_space=pl.ANY)
    full = lambda *s: pl.BlockSpec((1, *s), lambda b, p: (b, *([0] * len(s))))
    sd = jax.ShapeDtypeStruct
    DMA = pltpu.SemaphoreType.DMA
    V = pltpu.VMEM
    scratch = [V((n, rows, 320, nq), BF16), V((n, *weights[0].shape), BF16), DMA((2,))] + [V((1, 256, nk), BF16)] * 2 + [V((PAIRS, 8, nk), F32)] * 2 + [V((nq, nk), F32)] * 2 + [DMA((rows, NZ))] * 4
    scratch += [DMA((nu, NZ))] * 4 + [DMA((nu, n))] * 2 + [DMA((nu, 2, n))] * 2 + [DMA((narr,))]
    return pl.pallas_call(
        functools.partial(forward_kernel, span, chunk, units, narr, plan),
        grid=(rows, PAIRS),
        out_shape=[sd((rows, nq, width), BF16), sd((rows, PAIRS, 12, nq), F32), sd((rows, 384, nq), F32), sd((n, rows, 320, nq), BF16),
                   sd((rows, nq, width), BF16), sd((rows, nq, 128), F32)] + [sd((n, *a.shape), a.dtype) for a in weights],
        in_specs=[whole, whole, whole, pl.BlockSpec((1, nk), lambda b, p: (0, 0)), full(1, nk), full(1, nk)] + [far] * narr,
        out_specs=[whole, whole, whole, far, pl.BlockSpec((1, nq, 128), lambda b, p: (b, 0, p)), full(nq, 128)] + [far] * narr,
        scratch_shapes=scratch,
        compiler_params=pltpu.CompilerParams(collective_id=cid, has_side_effects=True, vmem_limit_bytes=56 << 20),
        name="forward",
    )(tokens, cosine, sine, cond, bl, bs, *weights)

HEADS, HDIM, QRANK, KVRANK = 16, 64, 6, 2
PAIRS = HEADS // 2
EPSILON = 1e-06


def rms_forward(values, gain):
    scale = lax.rsqrt(jnp.mean(values * values, -1, keepdims=True) + EPSILON)
    unit = values * scale
    return (unit * gain, unit, scale)


def rms_backward(grad_out, unit, scale, gain):
    scaled = grad_out * gain
    grad_in = scale * (scaled - unit * jnp.mean(scaled * unit, -1, keepdims=True))
    return (grad_in, jnp.sum(grad_out * unit, 0))


def rotation(positions):
    half = HDIM // 2
    index = jnp.arange(half).astype(F32)
    inverse = jnp.exp(index * (-math.log(10000.0) / half))
    angles = inverse[:, None] * positions.astype(F32)[None, :]
    return (jnp.cos(angles), jnp.sin(angles))


def rotate(u, cosine, sine):
    rows, depth, slots = u.shape
    v = u.reshape(rows, depth // HDIM, HDIM, slots)
    a, b = v[:, :, :HDIM // 2], v[:, :, HDIM // 2:]
    return jnp.concatenate([a * cosine - b * sine, b * cosine + a * sine], 2).reshape(u.shape)


def dot(a, b, ca, cb):
    return lax.dot_general(a, b, ((ca, cb), ((), ())), preferred_element_type=F32)


def pair_columns(a, ranks):
    return a.reshape(-1, ranks, PAIRS, 2).transpose(0, 2, 1, 3).reshape(a.shape)


def head_columns(a, ranks):
    return a.reshape(-1, PAIRS, ranks, 2).transpose(0, 2, 1, 3).reshape(a.shape)


GATHER_UNITS = [
    Unit(0, (0, 128), (0, 896), "P", 0), Unit(1, (0, 128), (0, 1024), "P", 0),
    Unit(2, (0, 128), (0, 1408), "P", 0), Unit(2, (0, 128), (1408, 1408), "P", 0),
    Unit(3, (0, 128), (0, 1408), "R", 0), Unit(3, (0, 128), (1408, 1408), "P", 0),
    Unit(4, (0, 176), (0, 1024), "P", 1), Unit(4, (176, 176), (0, 1024), "P", 1)]
GATHER_PLAN = {
    "first": [("local",), ("begin", 0, 1, 3), ("begin", 1, 1, 3), ("z", 0, 1, 3), ("x", 0, 0, 4), ("begin", 3, 1, 3), ("y", 0, 1, 7), ("begin", 7, 1, 3), ("begin", 2, 1, 3), ("z", 1, 1, 3), ("got", 0, 1, 7), ("x", 1, 0, 4), ("begin", 6, 1, 3), ("z", 3, 1, 3), ("project",), ("z", 2, 1, 3), ("x", 3, 0, 4), ("row", "begin", 0), ("row", "begin", 1), ("x", 2, 0, 4), ("z", 7, 1, 3), ("row", "z", 0), ("z", 6, 1, 3), ("row", "x", 0), ("y", 3, 4, 4), ("y", 2, 1, 3), ("begin", 5, 1, 3), ("begin", 4, 1, 3), ("y", 7, 1, 3)],
    "steps": {
        2: [("x", 6, 0, 4), ("y", 1, 1, 3), ("y", 3, 1, 3), ("row", "z", 1)],
        5: [("z", 5, 1, 3), ("y", 1, 4, 4)],
        6: [("x", 7, 0, 4)],
        7: [("y", 2, 4, 4), ("row", "x", 1)],
        10: [("z", 4, 1, 3), ("x", 5, 0, 4)],
        12: [("y", 7, 4, 4), ("y", 6, 1, 3)],
        13: [("y", 6, 4, 4), ("y", 5, 1, 3)],
        14: [("x", 4, 0, 4)],
        15: [("y", 5, 4, 4), ("got", 1, 1, 7), ("got", 2, 1, 7), ("got", 3, 1, 7), ("got", 4, 1, 7), ("got", 5, 1, 7), ("got", 6, 1, 7), ("got", 7, 1, 7), ("locals",), ("sent", 0, 1, 7), ("sent", 1, 1, 7), ("sent", 2, 1, 7), ("sent", 3, 1, 7), ("sent", 4, 1, 7), ("sent", 5, 1, 7), ("sent", 6, 1, 7), ("sent", 7, 1, 7), ("row", "end", 0), ("row", "end", 1)],
    }}
REDUCE_UNITS = [
    Unit(3, (0, 176), (0, 1024), "P", 1), Unit(2, (0, 128), (0, 1408), "R", 0),
    Unit(3, (176, 176), (0, 1024), "P", 1), Unit(2, (0, 128), (1408, 1408), "R", 0),
    Unit(1, (0, 128), (0, 1408), "P", 0), Unit(1, (0, 128), (1408, 1408), "P", 0),
    Unit(0, (0, 128), (0, 1024), "P", 0)]
REDUCE_PLAN = {
    "first": [("begin", 0, 0, 8), ("begin", 1, 0, 8), ("begin", 2, 0, 8), ("begin", 3, 0, 8), ("begin", 4, 0, 8), ("begin", 5, 0, 8), ("begin", 6, 0, 8), ("core", 0, 0, 4), ("core", 0, 4, 4), ("core", 1, 0, 4)],
    "steps": {
        0: [("core", 1, 4, 4)],
        1: [("core", 3, 0, 4), ("core", 2, 0, 4), ("x", 1, 0, 4)],
        2: [("core", 4, 4, 4)],
        3: [("core", 2, 4, 4), ("y", 2, 0, 4)],
        4: [("core", 3, 4, 4), ("x", 3, 0, 4)],
        5: [("core", 5, 4, 4), ("y", 2, 4, 4), ("core", 4, 0, 4), ("core", 5, 0, 4), ("y", 0, 0, 4), ("core", 6, 4, 4)],
        6: [("x", 2, 0, 4)],
        7: [("y", 0, 4, 4)],
        8: [("x", 0, 0, 4)],
        9: [("y", 4, 0, 4), ("row", "x", 0), ("y", 5, 0, 4), ("core", 6, 0, 4)],
        10: [("y", 6, 4, 4), ("y", 4, 4, 4), ("y", 5, 4, 4)],
        11: [("x", 4, 0, 4)],
        13: [("y", 6, 0, 4), ("own", 0, 0, 1), ("x", 5, 0, 4), ("own", 3, 0, 1)],
        15: [("own", 1, 0, 1), ("own", 4, 0, 1), ("own", 2, 0, 1), ("x", 6, 0, 4), ("own", 5, 0, 1), ("last", 3, 0, 1), ("row", "x", 1), ("own", 6, 0, 1), ("row", "own", 0), ("last", 1, 0, 1), ("last", 6, 0, 1), ("last", 2, 0, 1), ("last", 5, 0, 1), ("last", 4, 0, 1), ("last", 0, 0, 1), ("row", "own", 1), ("end", 0, 0, 1), ("end", 1, 0, 1), ("end", 2, 0, 1), ("end", 3, 0, 1), ("end", 4, 0, 1), ("end", 5, 0, 1), ("end", 6, 0, 1), ("row", "end", 0), ("row", "end", 1)],
    }}
SMALL_UNITS = [Unit(0, (0, 128), (0, 896), "P", 0)]
SMALL_PLAN = [("begin", 0, 0, 8), ("core", 0, 0, 8), ("y", 0, 0, 8), ("x", 0, 0, 4), ("own", 0, 0, 1), ("last", 0, 0, 1), ("end", 0, 0, 1)]


def reduce_far(arrays):
    out = []
    for a in arrays:
        own = lax.psum_scatter(a.astype(F32), "seq", scatter_dimension=0, tiled=True)[0]
        out.append(lax.psum(own.astype(BF16), "batch"))
    return out


def per_device(near, tokens, cotangent, lengths, span_order, attn_gain, query_heads, query_dims, key_heads, key_dims,
               value_heads, value_dims, out_proj, ffn_gain, gate_proj, up_proj, down_proj):
    rows, slots, width = tokens.shape
    span = slots // 2
    count = rows * slots
    nseq = span_order.shape[0]
    nk = nseq * span
    me = lax.axis_index("seq")
    key_value_heads = pair_columns(jnp.concatenate([key_heads, value_heads], 1), 4)
    small = jnp.concatenate([pair_columns(query_heads, QRANK), query_dims, key_dims, value_dims, key_value_heads, attn_gain[:, None], ffn_gain[:, None]], 1)
    small = jnp.pad(small, ((0, 0), (0, 896 - small.shape[1])))
    offsets = jnp.arange(span, dtype=jnp.int32)
    spans = jnp.concatenate([span_order, span_order], 0)
    spans = lax.dynamic_slice_in_dim(spans, me, nseq, 0)
    local_pos = (spans[0][:, None] * span + offsets[None, :]).reshape(-1)
    cosine, sine = rotation(local_pos)
    chosen = spans[:, 0] < spans[0, 0]
    low_pos = (spans[:, 0][:, None] * span + offsets[None, :]).reshape(1, nk)
    sel_pos = (jnp.where(chosen, spans[:, 0], spans[:, 1])[:, None] * span + offsets[None, :]).reshape(1, nk)
    cond = jnp.repeat(chosen.astype(F32), span).reshape(1, nk)
    low_bias = jnp.where(low_pos < lengths[:, None], 0.0, NEG)[:, None, :]
    sel_bias = jnp.where(sel_pos < lengths[:, None], 0.0, NEG)[:, None, :]

    masks = (cond, low_bias, sel_bias)
    flat = tokens.reshape(count, width).astype(F32)
    weights = [small, out_proj, gate_proj, up_proj, down_proj]
    if near:
        by_row, qh, qr, shared, heads_out, lse, *parts = forward(tokens, cosine, sine, *masks, weights, GATHER_UNITS, GATHER_PLAN, 0)
    else:
        parts = [lax.all_gather(a, "seq", axis=0) for a in weights]
    small, w_out, w_gate, w_up, w_down = [p.reshape(-1, p.shape[-1]) for p in parts]
    w_qkv = small[:, :800]
    gain_one = small[:, 800].astype(F32)
    gain_two = small[:, 801].astype(F32)
    normed_full, unit_one, scale_one = rms_forward(flat, gain_one)
    if not near:
        by_row = normed_full.astype(BF16).reshape(rows, slots, width)
        factors = jnp.stack([dot(w_qkv, by_row[b], (0,), (1,)) for b in range(rows)])
        qh = factors[:, :96].reshape(rows, PAIRS, 12, slots)
        qr = rotate(factors[:, 96:480], cosine, sine)
        own = jnp.concatenate([rotate(factors[:, 480:608], cosine, sine), factors[:, 608:800]], 1).astype(BF16)
        shared = lax.all_gather(own, "seq", axis=0)
        turned = lax.dynamic_slice_in_dim(jnp.concatenate([shared, shared], 0), me, nseq, 0)
        low, high = turned[..., :span], turned[..., span:]
        sel = jnp.where(chosen[:, None, None, None], low, high)
        low = low.transpose(1, 2, 0, 3).reshape(rows, 320, nk)
        sel = sel.transpose(1, 2, 0, 3).reshape(rows, 320, nk)
        in_pairs = lambda a: a[:, 256:].astype(F32).reshape(rows, PAIRS, 8, nk)
        factors = (in_pairs(low), in_pairs(sel), low[:, :256], sel[:, :256])
        heads_out, lse = attend(qh, qr, *factors, *masks)
    heads_flat = heads_out.reshape(count, width)

    resid = flat + dot(heads_flat, w_out, (1,), (0,))
    normed_two_full, unit_two, scale_two = rms_forward(resid, gain_two)
    normed_two = normed_two_full.astype(BF16)
    gate = dot(normed_two, w_gate, (1,), (0,))
    up_part = dot(normed_two, w_up, (1,), (0,))
    sigma = jax.nn.sigmoid(gate)
    hidden = (gate * sigma * up_part).astype(BF16)
    output = (resid + dot(hidden, w_down, (1,), (0,))).astype(BF16).reshape(rows, slots, width)

    grad_out = cotangent.reshape(count, width)
    down_grad = dot(hidden, grad_out, (0,), (0,)).astype(BF16)
    d_hidden = dot(grad_out, w_down, (1,), (1,))
    d_gate = (d_hidden * up_part * sigma * (1.0 + gate * (1.0 - sigma))).astype(BF16)
    d_up = (d_hidden * gate * sigma).astype(BF16)
    gate_grad = dot(normed_two, d_gate, (0,), (0,)).astype(BF16)
    up_grad = dot(normed_two, d_up, (0,), (0,)).astype(BF16)
    d_normed_two = dot(d_gate, w_gate, (1,), (1,)) + dot(d_up, w_up, (1,), (1,))
    d_mid, gain_two_grad = rms_backward(d_normed_two, unit_two, scale_two, gain_two)
    d_resid = grad_out.astype(F32) + d_mid
    d_attn = d_resid.astype(BF16)
    out_grad = dot(heads_flat, d_attn, (0,), (0,)).astype(BF16)
    d_heads = dot(d_attn, w_out, (1,), (1,)).astype(BF16).reshape(rows, slots, width)

    grads = [g.reshape(nseq, -1, g.shape[-1]) for g in (out_grad, gate_grad, up_grad, down_grad)]
    if near:
        dqh, dqr, mine, *sums = attend_back_reduce(qh, qr, shared, *masks, lse, heads_out, d_heads, grads, REDUCE_UNITS, REDUCE_PLAN, 1)
    else:
        dqh, dqr, dhl, dhs, ddl, dds = attend_back(qh, qr, *factors, *masks, lse, heads_out, d_heads)
        from_low = jnp.concatenate([ddl, dhl.reshape(rows, 64, nk)], 1).reshape(rows, 320, nseq, span)
        from_sel = jnp.concatenate([dds, dhs.reshape(rows, 64, nk)], 1).reshape(rows, 320, nseq, span)
        pick = chosen[None, None, :, None]
        both = jnp.concatenate([from_low + jnp.where(pick, from_sel, 0.0), jnp.where(pick, 0.0, from_sel)], -1).transpose(2, 0, 1, 3)
        both = lax.dynamic_slice_in_dim(jnp.concatenate([both, both], 0), lax.rem(nseq - me, nseq), nseq, 0)
        mine = lax.psum_scatter(both, "seq", scatter_dimension=0, tiled=True)[0]
        sums = reduce_far(grads)
    mine = mine.astype(F32)
    turned = jnp.concatenate([dqh.reshape(rows, 96, slots), rotate(dqr, cosine, -sine), rotate(mine[:, :128], cosine, -sine), mine[:, 128:]], 1).astype(BF16)
    small_grad = dot(by_row, turned, (0, 1), (0, 2))
    d_normed = dot(turned, w_qkv, (1,), (1,)).reshape(count, width)
    d_first, gain_one_grad = rms_backward(d_normed, unit_one, scale_one, gain_one)
    input_grad = (d_resid + d_first).reshape(rows, slots, width)
    small_grad = jnp.concatenate([small_grad, gain_one_grad[:, None], gain_two_grad[:, None], jnp.zeros((width, 94), F32)], 1).astype(BF16)

    small_grad = small_grad.reshape(nseq, -1, 896)
    small_sum = reduce_weights([small_grad], SMALL_UNITS, SMALL_PLAN, 3)[0] if near else reduce_far([small_grad])[0]
    small_sum = small_sum.astype(F32)
    out_sum, gate_sum, up_sum, down_sum = [g.astype(F32) for g in sums]
    key_value = head_columns(small_sum[:, 736:800], 4)
    return (output, input_grad, small_sum[:, 800], head_columns(small_sum[:, :96], QRANK), small_sum[:, 96:480], key_value[:, :32], small_sum[:, 480:608],
            key_value[:, 32:], small_sum[:, 608:736], out_sum, small_sum[:, 801], gate_sum, up_sum, down_sum)


def solution(mesh):
    near = mesh.shape["seq"] == 8 and mesh.shape["batch"] == 4
    by_slot = P("batch", "seq", None)
    line, table = P("seq"), P("seq", None)
    return jax.shard_map(
        functools.partial(per_device, near),
        mesh=mesh,
        in_specs=(by_slot, by_slot, P("batch"), P(), line, *([table] * 7), line, *([table] * 3)),
        out_specs=(by_slot, by_slot, line, *([table] * 7), line, *([table] * 3)),
        check_vma=False,
    )
```

```python
import functools
import math

import jax
import jax.numpy as jnp
from jax import lax
from jax.experimental import pallas as pl
from jax.experimental.pallas import tpu as pltpu
from jax.sharding import PartitionSpec as P


MESH = pl.DeviceIdType.MESH
NZ, NX = 4, 2

class Place:
    def __init__(self):
        self.seq = lax.axis_index("seq")
        self.batch = lax.axis_index("batch")
        self.z = self.seq // 2
        self.x = lax.rem(self.seq, 2)
        self.y = self.batch // 2
        self.c = lax.rem(self.batch, 2)
        self.up = (jnp.minimum(self.seq + 2, 7), self.batch)
        self.down = (jnp.maximum(self.seq - 2, 0), self.batch)
        self.xp = (self.seq + 1 - 2 * self.x, self.batch)
        self.yp = (self.seq, lax.rem(self.batch + 2, 4))
        self.cp = (self.seq, self.batch + 1 - 2 * self.c)

    def along(self, k):
        return (2 * lax.rem(self.z + k, NZ) + self.x, self.batch)

def greet(me):
    bar = pltpu.get_barrier_semaphore()
    def sig(d):
        pl.semaphore_signal(bar, inc=1, device_id=d, device_id_type=MESH)
    for k in range(1, NZ):
        sig(me.along(k))
    sig(me.xp); sig(me.yp); sig(me.cp)
    pl.semaphore_wait(bar, NZ + 2)

class Unit:
    def __init__(self, arr, row, col, flow, axis):
        self.arr, self.row, self.col, self.flow, self.axis = arr, row, col, flow, axis
        self.shape = (row[1], col[1])
        h = list(self.shape); h[axis] //= 2
        self.half = tuple(h)
        q = list(h)
        if flow == "P": q[axis] //= 2
        self.piece = tuple(q)

def rect(unit, ref, part, nparts):
    start = [unit.row[0], unit.col[0]]
    size = list(unit.shape)
    size[unit.axis] //= nparts
    idx = []
    for d in range(2):
        if d == unit.axis:
            off = part * size[d] + start[d]
            idx.append(pl.ds(pl.multiple_of(off, 16 if d == 0 else 128), size[d]))
        else:
            idx.append(pl.ds(start[d], size[d]))
    return ref.at[tuple(idx)]

def shard_of(ref, s, n=8):
    if len(ref.shape) == 3:
        return ref.at[s]
    rows = ref.shape[0] // n
    return ref.at[pl.ds(pl.multiple_of(s * rows, 16), rows)]

class Reduce:
    def __init__(self, me, units, ins, outs, scratch):
        self.me, self.units, self.ins, self.outs = me, units, ins, outs
        nu = len(units)
        self.A, self.RC, self.RY, self.RX, self.RZ, self.RF = [scratch[i * nu:(i + 1) * nu] for i in range(6)]
        self.ls, self.cs, self.cr, self.ys, self.yr, self.xs, self.xr, self.zs, self.zr, self.fs, self.fr, self.os_ = scratch[6 * nu:]

    def shard_at(self, i):
        me = self.me
        zz = lax.rem(me.z + 1 + lax.rem(i, NZ), NZ)
        xx = jnp.where(i < NZ, 1 - me.x, me.x)
        return zz, xx, 2 * zz + xx

    def sub(self, u, ref, y):
        if u.flow == "R":
            return ref
        n = u.piece[u.axis]
        idx = [slice(None)] * 2
        idx[u.axis] = pl.ds(pl.multiple_of(y * n, n), n)
        return ref.at[tuple(idx)]

    def remote(self, src, dst, ss, rs, dev):
        return pltpu.make_async_remote_copy(src_ref=src, dst_ref=dst, send_sem=ss, recv_sem=rs, device_id=dev, device_id_type=MESH)

    def core_copy(self, k, i):
        u = self.units[k]; zz, xx, s = self.shard_at(i)
        return self.remote(rect(u, shard_of(self.ins[u.arr], s), 1 - self.me.c, 2), self.RC[k].at[s], self.cs.at[k, s], self.cr.at[k, s], self.me.cp)

    def local_copy(self, k, i):
        u = self.units[k]; zz, xx, s = self.shard_at(i)
        return pltpu.make_async_copy(rect(u, shard_of(self.ins[u.arr], s), self.me.c, 2), self.A[k].at[s], self.ls.at[k, s])

    def y_copy(self, k, i):
        u = self.units[k]; zz, xx, s = self.shard_at(i)
        return self.remote(self.sub(u, self.A[k].at[s], 1 - self.me.y), self.RY[k].at[s], self.ys.at[k, s], self.yr.at[k, s], self.me.yp)

    def x_copy(self, k, zz):
        u, me = self.units[k], self.me
        return self.remote(self.sub(u, self.A[k].at[2 * zz + 1 - me.x], me.y), self.RX[k].at[zz], self.xs.at[k, zz], self.xr.at[k, zz], me.xp)

    def z_copy(self, k, zz):
        u, me = self.units[k], self.me
        return self.remote(self.mine(k, zz), self.RZ[k].at[self.slot(me.z, zz)], self.zs.at[k, zz], self.zr.at[k, me.z], (2 * zz + me.x, me.batch))

    @staticmethod
    def slot(source, owner):
        return lax.rem(source - owner + NZ, NZ) - 1

    def z_recv(self, k, zz):
        u, me = self.units[k], self.me
        v = self.RZ[k].at[self.slot(zz, me.z)]
        return self.remote(v, v, self.zs.at[k, zz], self.zr.at[k, zz], (2 * zz + me.x, me.batch))

    def mine(self, k, zz):
        return self.sub(self.units[k], self.A[k].at[2 * zz + self.me.x], self.me.y)

    @staticmethod
    def add(dst, src):
        dst[...] = dst[...] + src[...]

    def begin(self, k, i):
        self.core_copy(k, i).start()
        self.local_copy(k, i).start()

    def core(self, k, i):
        u = self.units[k]; zz, xx, s = self.shard_at(i)
        self.local_copy(k, i).wait()
        self.core_copy(k, i).wait_recv()
        self.add(self.A[k].at[s], self.RC[k].at[s])
        if u.flow == "P":
            self.y_copy(k, i).start()
        else:
            pl.when(i < NZ)(lambda: self.x_copy(k, zz).start())

    def y(self, k, i):
        u = self.units[k]; zz, xx, s = self.shard_at(i)
        self.y_copy(k, i).wait_recv()
        self.add(self.sub(u, self.A[k].at[s], self.me.y), self.RY[k].at[s])
        pl.when(i < NZ)(lambda: self.x_copy(k, zz).start())

    def x(self, k, i):
        me = self.me
        zz = lax.rem(me.z + 1 + i, NZ)
        self.x_copy(k, zz).wait_recv()
        self.add(self.mine(k, zz), self.RX[k].at[zz])
        pl.when(zz != me.z)(lambda: self.z_copy(k, zz).start())

    def fin_y(self, k):
        u, me = self.units[k], self.me
        mine = self.mine(k, me.z)
        dst = rect(u, self.outs[u.arr], 2 * me.c + me.y, 4) if u.flow == "P" else self.RF[k]
        return self.remote(mine, dst, self.fs.at[k, 0], self.fr.at[k, 0], me.yp)

    def fin_c(self, k, w):
        u, me = self.units[k], self.me
        if u.flow == "P":
            if w == 0:
                return self.remote(self.mine(k, me.z), rect(u, self.outs[u.arr], 2 * me.c + me.y, 4), self.fs.at[k, 1], self.fr.at[k, 1], me.cp)
            v = rect(u, self.outs[u.arr], 2 * me.c + 1 - me.y, 4)
            return self.remote(v, v, self.fs.at[k, 2], self.fr.at[k, 2], me.cp)
        return self.remote(self.RF[k], rect(u, self.outs[u.arr], me.c, 2), self.fs.at[k, 1], self.fr.at[k, 1], me.cp)

    def out_copy(self, k):
        u, me = self.units[k], self.me
        if u.flow == "P":
            return pltpu.make_async_copy(self.mine(k, me.z), rect(u, self.outs[u.arr], 2 * me.c + me.y, 4), self.os_.at[k])
        return pltpu.make_async_copy(self.RF[k], rect(u, self.outs[u.arr], me.c, 2), self.os_.at[k])

    def own(self, k, i):
        me = self.me
        def body(i, c):
            zz = lax.rem(me.z + i, NZ)
            self.z_recv(k, zz).wait_recv()
            self.add(self.mine(k, me.z), self.RZ[k].at[self.slot(zz, me.z)])
            return c
        lax.fori_loop(1, NZ, body, 0)
        self.fin_y(k).start()
        if self.units[k].flow == "P":
            self.out_copy(k).start()
            self.fin_c(k, 0).start()

    def last(self, k, i):
        self.fin_y(k).wait_recv()
        if self.units[k].flow == "P":
            self.fin_c(k, 1).start()
        else:
            self.add(self.RF[k], self.mine(k, self.me.z))
            self.out_copy(k).start()
            self.fin_c(k, 0).start()

    def end(self, k, i):
        me = self.me
        flow = self.units[k].flow
        for w in range(2 if flow == "P" else 1):
            self.fin_c(k, w).wait_recv()
            self.fin_c(k, w).wait_send()
        self.out_copy(k).wait()
        self.fin_y(k).wait_send()
        def body(i, c):
            self.core_copy(k, i).wait_send()
            if flow == "P": self.y_copy(k, i).wait_send()
            return c
        lax.fori_loop(0, 8, body, 0)
        def body(zz, c):
            self.x_copy(k, zz).wait_send()
            pl.when(zz != me.z)(lambda: self.z_copy(k, zz).wait_send())
            return c
        lax.fori_loop(0, NZ, body, 0)

    def run(self, plan):
        for step, k, first, n in plan:
            fn = getattr(self, step)
            if n == 1:
                fn(k, first)
            else:
                def body(i, c):
                    fn(k, i)
                    return c
                lax.fori_loop(first, first + n, body, 0)

def reduce_kernel(units, narr, plan, *refs):
    me = Place()
    greet(me)
    red = Reduce(me, units, refs[:narr], refs[narr:2 * narr], refs[2 * narr:])
    red.run(plan)

def reduce_scratch(units):
    nu = len(units)
    DMA = pltpu.SemaphoreType.DMA
    bf = jnp.bfloat16
    V = pltpu.VMEM
    return ([V((8, *u.half), bf) for u in units] + [V((8, *u.half), bf) for u in units]
        + [V((8, *u.piece) if u.flow == "P" else (16, 128), bf) for u in units] + [V((4, *u.piece), bf) for u in units]
        + [V((3, *u.piece), bf) for u in units] + [V(u.piece if u.flow == "R" else (16, 128), bf) for u in units]
        + [DMA((nu, 8))] * 5 + [DMA((nu, 4))] * 4 + [DMA((nu, 3))] * 2 + [DMA((nu,))])

def reduce_weights(arrays, units, plan, cid):
    narr = len(arrays)
    return pl.pallas_call(
        functools.partial(reduce_kernel, units, narr, plan),
        out_shape=[jax.ShapeDtypeStruct(a.shape[1:], a.dtype) for a in arrays],
        in_specs=[pl.BlockSpec(memory_space=pl.ANY)] * narr,
        out_specs=[pl.BlockSpec(memory_space=pl.ANY)] * narr,
        scratch_shapes=reduce_scratch(units),
        compiler_params=pltpu.CompilerParams(collective_id=cid, has_side_effects=True, vmem_limit_bytes=58 << 20),
        name="reduce_weights",
    )(*arrays)

F32, BF16 = jnp.float32, jnp.bfloat16
NEG = -1e30

def nn(a, b):
    return lax.dot_general(a, b, (((1,), (0,)), ((), ())), preferred_element_type=F32)

def nt(a, b):
    return lax.dot_general(a, b, (((1,), (1,)), ((), ())), preferred_element_type=F32)

def expand(heads, dims, base):
    parts = []
    for h in range(2):
        parts.append((heads[base + h:base + h + 1] * dims[0] + heads[base + 2 + h:base + 3 + h] * dims[1]) * 0.5)
    return jnp.concatenate(parts, 0)

def queries(qh, qr):
    parts = []
    for h in range(2):
        total = qh[h:h + 1] * qr[0:64]
        for r in range(1, 6):
            total = total + qh[2 * r + h:2 * r + h + 1] * qr[64 * r:64 * r + 64]
        parts.append(total)
    return jnp.concatenate(parts, 0) / 6.0

def lanes_below(shape, n):
    return lax.broadcasted_iota(jnp.int32, shape, 1) < n

def stack_heads(part):
    first = lanes_below(part.shape, 64)
    zero = jnp.zeros_like(part)
    return jnp.concatenate([jnp.where(first, part, zero), jnp.where(first, zero, part)], 0)

def unstack_heads(part):
    n = part.shape[0] // 2
    return jnp.where(lanes_below((n, 128), 64), part[:n], part[n:])

def causal_bias(n2, span):
    row = lax.broadcasted_iota(jnp.int32, (n2, span), 0) % span
    col = lax.broadcasted_iota(jnp.int32, (n2, span), 1)
    return jnp.where(col <= row, 0.0, NEG)

def pair_factors(heads, dims, cond, base, at):
    hl, hs = heads
    dl, ds = dims
    low = expand(hl, (dl[at:at + 64].astype(F32), dl[at + 64:at + 128].astype(F32)), base).astype(BF16)
    sel = expand(hs, (ds[at:at + 64].astype(F32), ds[at + 64:at + 128].astype(F32)), base)
    left = jnp.where(cond > 0.5, sel, 0.0).astype(BF16)
    right = jnp.where(cond > 0.5, 0.0, sel).astype(BF16)
    return low, jnp.concatenate([left, right], 0)

def attend_kernel(span, chunk, qh_ref, qr_ref, hl_ref, hs_ref, dl_ref, ds_ref, cond_ref, bl_ref, bs_ref, o_ref, lse_ref, s1, s2):
    pair_forward(span, chunk, pl.program_id(1), qh_ref[0, 0], qr_ref[0], hl_ref[0, 0], hs_ref[0, 0], dl_ref, ds_ref, cond_ref, bl_ref, bs_ref, o_ref, lse_ref, s1, s2)

def pair_forward(span, chunk, p, qh, qr, hl, hs, dl_ref, ds_ref, cond_ref, bl_ref, bs_ref, o_ref, lse_ref, s1, s2):
    n2 = 2 * span
    nk = dl_ref.shape[-1]
    qt = queries(qh, qr)
    q = (qt.astype(BF16).astype(F32).T * 0.125).astype(BF16)
    qlo, qhi = stack_heads(q[:span]), stack_heads(q[span:])
    qboth = jnp.concatenate([qlo, qhi], 1)
    heads = (hl, hs)
    dims = (dl_ref[0], ds_ref[0])
    cond = cond_ref[...]
    klo, ksel = pair_factors(heads, dims, cond, 0, 0)
    vlo, vsel = pair_factors(heads, dims, cond, 4, 128)
    tri = causal_bias(n2, span)
    width = min(128, chunk)
    mlo = jnp.full((n2, width), NEG, F32)
    mhi = jnp.full((n2, width), NEG, F32)
    s3 = nn(qlo, klo[:, :span]) + bl_ref[0][:, :span] + tri
    m3 = jnp.max(s3, -1, keepdims=True)
    for c in range(0, nk, chunk):
        sl = slice(c, c + chunk)
        a = nn(qhi, klo[:, sl]) + bl_ref[0][:, sl]
        s1[:, sl] = a
        b = nn(qboth, ksel[:, sl]) + bs_ref[0][:, sl]
        if c == 0:
            b = jnp.concatenate([b[:, :span] + tri, b[:, span:]], 1)
        s2[:, sl] = b
        for i in range(0, chunk, width):
            on = cond[:, c + i:c + i + width] > 0.5
            ai, bi = a[:, i:i + width], b[:, i:i + width]
            mlo = jnp.maximum(mlo, jnp.where(on, bi, NEG))
            mhi = jnp.maximum(mhi, jnp.maximum(ai, jnp.where(on, NEG, bi)))
    mlo = jnp.maximum(jnp.max(mlo, -1, keepdims=True), m3)
    mhi = jnp.max(mhi, -1, keepdims=True)
    e3 = jnp.exp(s3 - mlo)
    tlo = jnp.zeros((n2, width), F32)
    thi = jnp.zeros((n2, width), F32)
    o3 = nt(e3.astype(BF16), vlo[:, :span])
    o1 = jnp.zeros((n2, 128), F32)
    o2 = jnp.zeros((n2, 256), F32)
    for c in range(0, nk, chunk):
        sl = slice(c, c + chunk)
        on = cond[:, sl] > 0.5
        a = jnp.exp(s1[:, sl] - mhi)
        b = jnp.exp(s2[:, sl] - jnp.where(on, mlo, mhi))
        blo = jnp.where(on, b, 0.0)
        bhi = a + jnp.where(on, 0.0, b)
        for i in range(0, chunk, width):
            tlo = tlo + blo[:, i:i + width]
            thi = thi + bhi[:, i:i + width]
        o1 = o1 + nt(a.astype(BF16), vlo[:, sl])
        o2 = o2 + nt(b.astype(BF16), vsel[:, sl])
    llo = jnp.sum(tlo, -1, keepdims=True) + jnp.sum(e3, -1, keepdims=True)
    lhi = jnp.sum(thi, -1, keepdims=True)
    olo = unstack_heads((o2[:, :128] + o3) / llo)
    ohi = unstack_heads((o2[:, 128:] + o1) / lhi)
    o_ref[0] = jnp.concatenate([olo, ohi], 0).astype(BF16)
    lane = lax.broadcasted_iota(jnp.int32, (span, 128), 1)
    tlo = mlo + jnp.log(llo)
    thi = mhi + jnp.log(lhi)
    old = jnp.where(p == 0, 0.0, lse_ref[0])
    new = []
    for k, t in enumerate((tlo, thi)):
        part = old[k * span:(k + 1) * span]
        part = jnp.where(lane == 2 * p, t[:span], part)
        new.append(jnp.where(lane == 2 * p + 1, t[span:], part))
    lse_ref[0] = jnp.concatenate(new, 0)

def attend(qh, qr, hl, hs, dl, ds, cond, bl, bs):
    rows, pairs, _, nq = qh.shape
    nk = dl.shape[-1]
    span = nq // 2
    chunk = min(512, nk)
    full = lambda *s: pl.BlockSpec((1, *s), lambda b, p: (b, *([0] * len(s))))
    pairb = lambda *s: pl.BlockSpec((1, 1, *s), lambda b, p: (b, p, *([0] * len(s))))
    return pl.pallas_call(
        functools.partial(attend_kernel, span, chunk),
        grid=(rows, pairs),
        out_shape=[jax.ShapeDtypeStruct((rows, nq, pairs * 128), BF16), jax.ShapeDtypeStruct((rows, nq, 128), F32)],
        in_specs=[pairb(12, nq), full(384, nq), pairb(8, nk), pairb(8, nk), full(256, nk), full(256, nk),
                  pl.BlockSpec((1, nk), lambda b, p: (0, 0)), full(1, nk), full(1, nk)],
        out_specs=[pl.BlockSpec((1, nq, 128), lambda b, p: (b, 0, p)), full(nq, 128)],
        scratch_shapes=[pltpu.VMEM((nq, nk), F32), pltpu.VMEM((nq, nk), F32)],
        compiler_params=pltpu.CompilerParams(vmem_limit_bytes=56 << 20),
        name="attend",
    )(qh, qr, hl, hs, dl, ds, cond, bl, bs)

def attend_back_kernel(span, chunk, qh_ref, qr_ref, hl_ref, hs_ref, dl_ref, ds_ref, cond_ref, bl_ref, bs_ref, lse_ref, o_ref, g_ref,
                       dqh_ref, dqr_ref, dhl_ref, dhs_ref, ddl_ref, dds_ref):
    p = pl.program_id(1)
    @pl.when(p == 0)
    def _():
        dqr_ref[...] = jnp.zeros_like(dqr_ref)
        ddl_ref[...] = jnp.zeros_like(ddl_ref)
        dds_ref[...] = jnp.zeros_like(dds_ref)
    pair_back(span, chunk, p, qh_ref, qr_ref, Pair(hl_ref, 0, 0), Pair(hs_ref, 0, 0), dl_ref, ds_ref, cond_ref, bl_ref, bs_ref, lse_ref, o_ref[0], g_ref[0],
              dqh_ref, dqr_ref, Pair(dhl_ref, 0, 0), Pair(dhs_ref, 0, 0), ddl_ref, dds_ref)

class Pair:
    def __init__(self, ref, *at):
        self.ref, self.at = ref, at

    def all(self):
        return self.ref[self.at]

    def row(self, j, sl):
        return self.ref[(*self.at, slice(j, j + 1), sl)]

    def put(self, j, sl, value):
        self.ref[(*self.at, slice(j, j + 1), sl)] = value

def pair_back(span, chunk, p, qh_ref, qr_ref, hl, hs, dl_ref, ds_ref, cond_ref, bl_ref, bs_ref, lse_ref, o, g,
              dqh_ref, dqr_ref, dhl, dhs, ddl_ref, dds_ref):
    n2 = 2 * span
    nk = dl_ref.shape[-1]
    qh, qr = qh_ref[0, 0], qr_ref[0]
    qt = (queries(qh, qr).astype(BF16).astype(F32)) * 0.125
    q = qt.T.astype(BF16)
    qlo, qhi = stack_heads(q[:span]), stack_heads(q[span:])
    qboth = jnp.concatenate([qlo, qhi], 1)
    glo, ghi = stack_heads(g[:span]), stack_heads(g[span:])
    gboth = jnp.concatenate([glo, ghi], 1)
    gt = g.astype(F32).T
    first = lax.broadcasted_iota(jnp.int32, (128, span), 0) < 64
    def stack_lanes(part):
        return jnp.concatenate([jnp.where(first, part, 0.0), jnp.where(first, 0.0, part)], 1).astype(BF16)
    qtlo, qthi = stack_lanes(qt[:, :span]), stack_lanes(qt[:, span:])
    gtlo, gthi = stack_lanes(gt[:, :span]), stack_lanes(gt[:, span:])
    qtboth = jnp.concatenate([qtlo, qthi], 0)
    gtboth = jnp.concatenate([gtlo, gthi], 0)
    prod = g.astype(F32) * o.astype(F32)
    flane = lanes_below((n2, 128), 64)
    d0 = jnp.sum(jnp.where(flane, prod, 0.0), -1, keepdims=True)
    d1 = jnp.sum(jnp.where(flane, 0.0, prod), -1, keepdims=True)
    lane = lax.broadcasted_iota(jnp.int32, (n2, 128), 1)
    lse = lse_ref[0]
    l0 = jnp.sum(jnp.where(lane == 2 * p, lse, 0.0), -1, keepdims=True)
    l1 = jnp.sum(jnp.where(lane == 2 * p + 1, lse, 0.0), -1, keepdims=True)
    dello, delhi = jnp.concatenate([d0[:span], d1[:span]], 0), jnp.concatenate([d0[span:], d1[span:]], 0)
    lselo, lsehi = jnp.concatenate([l0[:span], l1[:span]], 0), jnp.concatenate([l0[span:], l1[span:]], 0)
    heads = (hl.all(), hs.all())
    dims = (dl_ref[0], ds_ref[0])
    cond = cond_ref[...]
    klo, ksel = pair_factors(heads, dims, cond, 0, 0)
    vlo, vsel = pair_factors(heads, dims, cond, 4, 128)
    tri = causal_bias(n2, span)

    def put(dkt, h, d_ref, hd, dd_ref, base, at, sl):
        for r in range(2):
            dim = d_ref[0, at + 64 * r:at + 64 * r + 64, sl].astype(F32)
            total = None
            for k in range(2):
                part = dkt[64 * k:64 * k + 64]
                j = base + 2 * r + k
                hd.put(j, sl, jnp.sum(part * dim, 0, keepdims=True) * 0.5)
                term = part * h.row(j, sl)
                total = term if total is None else total + term
            dd_ref[0, at + 64 * r:at + 64 * r + 64, sl] += total * 0.5

    s3 = nn(qlo, klo[:, :span]) + bl_ref[0][:, :span] + tri
    p3 = jnp.exp(s3 - lselo)
    dp3 = nn(glo, vlo[:, :span])
    ds3 = (p3 * (dp3 - dello)).astype(BF16)
    p3 = p3.astype(BF16)
    dq3 = nt(ds3, klo[:, :span])
    dk3 = nn(qtlo, ds3)
    dv3 = nn(gtlo, p3)
    dq1 = jnp.zeros((n2, 128), F32)
    dq2 = jnp.zeros((n2, 256), F32)
    for c in range(0, nk, chunk):
        sl = slice(c, c + chunk)
        pa = jnp.exp(nn(qhi, klo[:, sl]) + bl_ref[0][:, sl] - lsehi)
        dpa = nn(ghi, vlo[:, sl])
        dsa = (pa * (dpa - delhi)).astype(BF16)
        pa = pa.astype(BF16)
        dq1 = dq1 + nt(dsa, klo[:, sl])
        dk = nn(qthi, dsa)
        dv = nn(gthi, pa)
        if c == 0:
            dk = jnp.concatenate([dk[:, :span] + dk3, dk[:, span:]], 1)
            dv = jnp.concatenate([dv[:, :span] + dv3, dv[:, span:]], 1)
        put(dk, hl, dl_ref, dhl, ddl_ref, 0, 0, sl)
        put(dv, hl, dl_ref, dhl, ddl_ref, 4, 128, sl)
    for c in range(0, nk, chunk):
        sl = slice(c, c + chunk)
        on = cond[:, sl] > 0.5
        s = nn(qboth, ksel[:, sl]) + bs_ref[0][:, sl]
        if c == 0:
            s = jnp.concatenate([s[:, :span] + tri, s[:, span:]], 1)
        pb = jnp.exp(s - jnp.where(on, lselo, lsehi))
        dpb = nn(gboth, vsel[:, sl])
        dsb = (pb * (dpb - jnp.where(on, dello, delhi))).astype(BF16)
        pb = pb.astype(BF16)
        dq2 = dq2 + nt(dsb, ksel[:, sl])
        dk = nn(qtboth, dsb)
        dv = nn(gtboth, pb)
        dk = jnp.where(on, dk[:128], dk[128:])
        dv = jnp.where(on, dv[:128], dv[128:])
        put(dk, hs, ds_ref, dhs, dds_ref, 0, 0, sl)
        put(dv, hs, ds_ref, dhs, dds_ref, 4, 128, sl)
    dqlo = unstack_heads(dq2[:, :128] + dq3)
    dqhi = unstack_heads(dq2[:, 128:] + dq1)
    dqt = (jnp.concatenate([dqlo, dqhi], 0) * (0.125 / 6.0)).T
    for r in range(6):
        total = None
        for h in range(2):
            part = dqt[64 * h:64 * h + 64]
            j = 2 * r + h
            dqh_ref[0, 0, j:j + 1, :] = jnp.sum(part * qr[64 * r:64 * r + 64], 0, keepdims=True)
            term = part * qh[j:j + 1]
            total = term if total is None else total + term
        dqr_ref[0, 64 * r:64 * r + 64, :] += total

def attend_back(qh, qr, hl, hs, dl, ds, cond, bl, bs, lse, o, g):
    rows, pairs, _, nq = qh.shape
    nk = dl.shape[-1]
    span = nq // 2
    chunk = min(512, nk)
    full = lambda *s: pl.BlockSpec((1, *s), lambda b, p: (b, *([0] * len(s))))
    pairb = lambda *s: pl.BlockSpec((1, 1, *s), lambda b, p: (b, p, *([0] * len(s))))
    tok = pl.BlockSpec((1, nq, 128), lambda b, p: (b, 0, p))
    sd = jax.ShapeDtypeStruct
    return pl.pallas_call(
        functools.partial(attend_back_kernel, span, chunk),
        grid=(rows, pairs),
        out_shape=[sd((rows, pairs, 12, nq), F32), sd((rows, 384, nq), F32), sd((rows, pairs, 8, nk), F32), sd((rows, pairs, 8, nk), F32),
                   sd((rows, 256, nk), F32), sd((rows, 256, nk), F32)],
        in_specs=[pairb(12, nq), full(384, nq), pairb(8, nk), pairb(8, nk), full(256, nk), full(256, nk),
                  pl.BlockSpec((1, nk), lambda b, p: (0, 0)), full(1, nk), full(1, nk), full(nq, 128), tok, tok],
        out_specs=[pairb(12, nq), full(384, nq), pairb(8, nk), pairb(8, nk), full(256, nk), full(256, nk)],
        compiler_params=pltpu.CompilerParams(vmem_limit_bytes=56 << 20),
        name="attend_back",
    )(qh, qr, hl, hs, dl, ds, cond, bl, bs, lse, o, g)

class Rows:
    def __init__(self, me, pack, out, RX, RZ, xs, xr, zs, zr):
        self.me, self.pack, self.out, self.RX, self.RZ = me, pack, out, RX, RZ
        self.xs, self.xr, self.zs, self.zr = xs, xr, zs, zr

    def remote(self, src, dst, ss, rs, dev):
        return pltpu.make_async_remote_copy(src_ref=src, dst_ref=dst, send_sem=ss, recv_sem=rs, device_id=dev, device_id_type=MESH)

    def x_copy(self, b, zz):
        return self.remote(self.pack.at[b, 2 * zz + 1 - self.me.x], self.RX.at[b, zz], self.xs.at[b, zz], self.xr.at[b, zz], self.me.xp)

    def z_copy(self, b, zz):
        me = self.me
        return self.remote(self.mine(b, zz), self.RZ.at[b, Reduce.slot(me.z, zz)], self.zs.at[b, zz], self.zr.at[b, me.z], (2 * zz + me.x, me.batch))

    def z_recv(self, b, zz):
        me = self.me
        v = self.RZ.at[b, Reduce.slot(zz, me.z)]
        return self.remote(v, v, self.zs.at[b, zz], self.zr.at[b, zz], (2 * zz + me.x, me.batch))

    def mine(self, b, zz):
        return self.pack.at[b, 2 * zz + self.me.x]

    @staticmethod
    def add(dst, src):
        dst[...] = dst[...] + src[...]

    def begin(self, b):
        def body(i, c):
            self.x_copy(b, lax.rem(self.me.z + 1 + i, NZ)).start()
            return c
        lax.fori_loop(0, NZ, body, 0)

    def x(self, b):
        me = self.me
        def body(i, c):
            zz = lax.rem(me.z + 1 + i, NZ)
            self.x_copy(b, zz).wait_recv()
            self.add(self.mine(b, zz), self.RX.at[b, zz])
            pl.when(zz != me.z)(lambda: self.z_copy(b, zz).start())
            return c
        lax.fori_loop(0, NZ, body, 0)

    def own(self, b):
        me = self.me
        def body(i, c):
            zz = lax.rem(me.z + i, NZ)
            self.z_recv(b, zz).wait_recv()
            self.add(self.mine(b, me.z), self.RZ.at[b, Reduce.slot(zz, me.z)])
            return c
        lax.fori_loop(1, NZ, body, 0)
        self.out[b] = self.pack[b, me.seq]

    def end(self, b):
        me = self.me
        def sent(zz, c):
            self.x_copy(b, zz).wait_send()
            pl.when(zz != me.z)(lambda: self.z_copy(b, zz).wait_send())
            return c
        lax.fori_loop(0, NZ, sent, 0)

def lay_out(me, block, n, span, cond_ref, dl, ds, hl, hs):
    for i in range(n):
        j = lax.rem(me.seq + i, n)
        sl = slice(i * span, (i + 1) * span)
        on = cond_ref[:, sl] > 0.5
        low = block(j)[:256, :span].astype(F32)
        high = block(j)[:256, span:].astype(F32)
        dl[0, :, sl] = low.astype(BF16)
        ds[0, :, sl] = jnp.where(on, low, high).astype(BF16)
        low = block(j)[256:, :span].astype(F32)
        high = block(j)[256:, span:].astype(F32)
        hl[:, :, sl] = low.reshape(PAIRS, 8, span)
        hs[:, :, sl] = jnp.where(on, low, high).reshape(PAIRS, 8, span)

def pack_up(me, b, span, cond_ref, pack, ddl, dds, dhl, dhs):
    n = pack.shape[1]
    for i in range(n):
        j = lax.rem(me.seq + i, n)
        sl = slice(i * span, (i + 1) * span)
        on = cond_ref[:, sl] > 0.5
        for at, lo, se in ((0, ddl[0, :, sl], dds[0, :, sl]), (256, dhl[:, :, sl].reshape(64, span), dhs[:, :, sl].reshape(64, span))):
            rows = slice(at, at + lo.shape[0])
            pack[b, j, rows, :span] = (lo + jnp.where(on, se, 0.0)).astype(BF16)
            pack[b, j, rows, span:] = jnp.where(on, 0.0, se).astype(BF16)

FFC = 256

class Feed:
    def __init__(self, hbm, outs, grads, buf):
        self.tok, self.heads_hbm, self.cot, self.w_out, self.w_gate, self.w_up, self.w_down, self.gain = hbm
        self.output, self.d_resid, self.gain_grad = outs
        self.g_out, self.g_gate, self.g_up, self.g_down = grads
        (self.xb, self.hb, self.gb, self.n2, self.n2t, self.resid, self.acc, self.dlo, self.dhi, self.wa, self.wd, self.sg, self.su, self.sd, self.dg, self.du, self.hidt,
         self.lsem, self.wsem, self.ssem) = buf
        self.rows, self.nq, self.width = self.tok.shape
        self.count = self.rows * self.nq

    def load(self):
        out = []
        for i, (src, dst) in enumerate(((self.tok, self.xb), (self.heads_hbm, self.hb), (self.cot, self.gb))):
            for r in range(self.rows):
                out.append(pltpu.make_async_copy(src.at[r], dst.at[pl.ds(r * self.nq, self.nq)], self.lsem.at[i, r]))
        return out

    def out_part(self, j):
        return pltpu.make_async_copy(self.w_out.at[:, pl.ds(j * FFC, FFC)], self.wa.at[j], self.wsem.at[0, j])

    def weights(self, c):
        k = lax.rem(c, 2)
        at = pl.ds(pl.multiple_of(c * FFC, FFC), FFC)
        return (pltpu.make_async_copy(self.w_gate.at[:, at], self.wa.at[k], self.wsem.at[1, k]),
                pltpu.make_async_copy(self.w_up.at[:, at], self.wa.at[2 + k], self.wsem.at[1, 2 + k]),
                pltpu.make_async_copy(self.w_down.at[at], self.wd.at[k], self.wsem.at[2, k]))

    def stores(self, c):
        at = pl.ds(pl.multiple_of(c * FFC, FFC), FFC)
        return (pltpu.make_async_copy(self.sg, self.g_gate.at[:, :, at], self.ssem.at[0]),
                pltpu.make_async_copy(self.su, self.g_up.at[:, :, at], self.ssem.at[1]),
                pltpu.make_async_copy(self.sd, self.g_down.at[at], self.ssem.at[2]))

    def out_store(self, j):
        return pltpu.make_async_copy((self.sg, self.su)[j % 2], self.g_out.at[:, :, pl.ds(j * FFC, FFC)], self.ssem.at[j % 2])

    def before(self):
        parts = self.width // FFC
        loads = self.load() + [self.out_part(j) for j in range(parts)]
        for cp in loads:
            cp.start()
        for cp in loads:
            cp.wait()
        for j in range(parts):
            sl = slice(j * FFC, (j + 1) * FFC)
            self.resid[:, sl] = self.xb[:, sl].astype(F32) + nn(self.hb[...], self.wa[j])
        for cp in self.weights(0):
            cp.start()
        gain = self.gain[...]
        for r in range(0, self.count, 128):
            sl = slice(r, r + 128)
            v = self.resid[sl, :]
            self.acc[sl, :] = v
            n2 = v * lax.rsqrt(jnp.mean(v * v, -1, keepdims=True) + 1e-6) * gain
            self.n2[sl, :] = n2.astype(BF16)
            self.n2t[:, sl] = n2.T.astype(BF16)
        self.dlo[...] = jnp.zeros_like(self.dlo)
        self.dhi[...] = jnp.zeros_like(self.dhi)

    def block(self, c, total):
        k = lax.rem(c, 2)
        for cp in self.weights(c):
            cp.wait()
        @pl.when(c + 1 < total)
        def _():
            for cp in self.weights(c + 1):
                cp.start()
        half = self.count // 2
        for r, dn in ((0, self.dlo), (half, self.dhi)):
            sl = slice(r, r + half)
            gate = nn(self.n2[sl, :], self.wa[k])
            up = nn(self.n2[sl, :], self.wa[2 + k])
            dh = nt(self.gb[sl, :], self.wd[k])
            sigma = 1.0 / (1.0 + jnp.exp(-gate))
            silu = gate * sigma
            hid = (silu * up).astype(BF16)
            d_gate = (dh * up * sigma * (1.0 + gate * (1.0 - sigma))).astype(BF16)
            d_up = (dh * silu).astype(BF16)
            self.dg[sl, :] = d_gate
            self.du[sl, :] = d_up
            self.hidt[:, sl] = hid.astype(F32).T.astype(BF16)
            self.acc[sl, :] += nn(hid, self.wd[k])
            dn[0] += nt(d_gate, self.wa[k]) + nt(d_up, self.wa[2 + k])
        @pl.when(c >= 1)
        def _():
            for cp in self.stores(c - 1):
                cp.wait()
        self.sg[...] = nn(self.n2t[...], self.dg[...]).astype(BF16).reshape(self.sg.shape)
        self.su[...] = nn(self.n2t[...], self.du[...]).astype(BF16).reshape(self.su.shape)
        self.sd[...] = nn(self.hidt[...], self.gb[...]).astype(BF16)
        for cp in self.stores(c):
            cp.start()

    def settle(self, c):
        for cp in self.stores(c):
            cp.wait()

    def after(self, total):
        parts = self.width // FFC
        for j in range(parts):
            self.out_part(j).start()
        gain = self.gain[...]
        sums = jnp.zeros((8, self.width), F32)
        half = self.count // 2
        for r in range(0, self.count, 128):
            sl = slice(r, r + 128)
            dn = self.dlo[0, r:r + 128] if r < half else self.dhi[0, r - half:r - half + 128]
            v = self.resid[sl, :]
            scale = lax.rsqrt(jnp.mean(v * v, -1, keepdims=True) + 1e-6)
            unit = v * scale
            prod = dn * unit
            sums = sums + jnp.sum(prod.reshape(16, 8, self.width), 0)
            e2 = dn * gain
            d = self.gb[sl, :].astype(F32) + scale * (e2 - unit * jnp.mean(e2 * unit, -1, keepdims=True))
            self.resid[sl, :] = d
            self.gb[sl, :] = d.astype(BF16)
            self.xb[sl, :] = self.acc[sl, :].astype(BF16)
            self.n2t[:, sl] = self.hb[sl, :].astype(F32).T.astype(BF16)
        self.gain_grad[...] = jnp.sum(sums, 0, keepdims=True)
        for cp in self.results():
            cp.start()
        for j in range(parts):
            self.out_part(j).wait()
        for j in range(parts):
            if j >= 2:
                self.out_store(j - 2).wait()
            (self.sg, self.su)[j % 2][...] = nn(self.n2t[...], self.gb[:, j * FFC:(j + 1) * FFC]).astype(BF16).reshape(self.sg.shape)
            self.out_store(j).start()
        for r in range(0, self.count, 128):
            total = None
            for j in range(parts):
                part = nt(self.gb[r:r + 128, j * FFC:(j + 1) * FFC], self.wa[j])
                total = part if total is None else total + part
            self.n2[r:r + 128, :] = total.astype(BF16)
        for j in range(parts - 2, parts):
            self.out_store(j).wait()

    def results(self):
        out = []
        for r in range(self.rows):
            at = pl.ds(r * self.nq, self.nq)
            out.append(pltpu.make_async_copy(self.xb.at[at], self.output.at[r], self.lsem.at[0, r]))
            out.append(pltpu.make_async_copy(self.resid.at[at], self.d_resid.at[r], self.lsem.at[1, r]))
        return out

def back_kernel(span, chunk, units, plan, blocks, qh_ref, qr_ref, shared_ref, cond_ref, bl_ref, bs_ref, lse_ref, *refs):
    feed_in, refs = refs[:8], refs[8:]
    dqh_ref, dqr_ref, mine_ref, output, d_resid, gain_grad = refs[:6]
    sums, grads, refs = refs[6:10], refs[10:14], refs[14:]
    dl, ds, hl, hs, ddl, dds, dhl, dhs, pack, RX, RZ, xs, xr, zs, zr, bsem = refs[:16]
    fb, refs = refs[16:34], refs[34:]
    me = Place()
    b, p = pl.program_id(0), pl.program_id(1)
    step = b * PAIRS + p
    nq = 2 * span
    red = Reduce(me, units, grads, sums, refs)
    row = Rows(me, pack, mine_ref, RX, RZ, xs, xr, zs, zr)
    feed = Feed(feed_in, (output, d_resid, gain_grad), grads, (*fb[:7], ddl, dds, *fb[7:]))

    def act(items):
        for it in items:
            if it[0] == "row":
                getattr(row, it[1])(it[2])
            elif it[0] == "settle":
                feed.settle(it[1])
            elif it[0] == "results":
                for cp in feed.results():
                    cp.wait()
            else:
                red.run([it])

    brought = [pltpu.make_async_copy(shared_ref.at[:, r], pack.at[r], bsem.at[r]) for r in range(pack.shape[0])]

    @pl.when(step == 0)
    def _():
        greet(me)
        for cp in brought:
            cp.start()
        feed.before()
        def body(c, carry):
            feed.block(c, blocks)
            for k, items in plan["feed"].items():
                pl.when(c == k)(functools.partial(act, items))
            return carry
        lax.fori_loop(0, blocks, body, 0)
        feed.settle(blocks - 1)
        act(plan["mid"])
        feed.after(blocks)
        act(plan["first"])
        for cp in brought:
            cp.wait()

    @pl.when(p == 0)
    def _():
        lay_out(me, lambda j: pack.at[b, j], 2 * NZ, span, cond_ref, dl, ds, hl, hs)
        dqr_ref[...] = jnp.zeros_like(dqr_ref)
        ddl[...] = jnp.zeros_like(ddl)
        dds[...] = jnp.zeros_like(dds)

    rows_at = pl.ds(pl.multiple_of(b * nq, nq), nq)
    lanes_at = pl.ds(pl.multiple_of(p * 128, 128), 128)
    pair_back(span, chunk, p, qh_ref, qr_ref, Pair(hl, p), Pair(hs, p), dl, ds, cond_ref, bl_ref, bs_ref, lse_ref,
              feed.hb[rows_at, lanes_at], feed.n2[rows_at, lanes_at], dqh_ref, dqr_ref, Pair(dhl, p), Pair(dhs, p), ddl, dds)

    @pl.when(p == PAIRS - 1)
    def _():
        pack_up(me, b, span, cond_ref, pack, ddl, dds, dhl, dhs)
        row.begin(b)

    for s, items in plan["steps"].items():
        pl.when(step == s)(functools.partial(act, items))

def backward(qh, qr, shared, cond, bl, bs, lse, tokens, heads_out, cotangent, w_out, w_gate, w_up, w_down, gain_two, units, plan, cid):
    rows, pairs, _, nq = qh.shape
    n = shared.shape[0]
    span = nq // 2
    nk = n * span
    width, ff = w_gate.shape
    count = rows * nq
    full = lambda *s: pl.BlockSpec((1, *s), lambda b, p: (b, *([0] * len(s))))
    pairb = lambda *s: pl.BlockSpec((1, 1, *s), lambda b, p: (b, p, *([0] * len(s))))
    sd = jax.ShapeDtypeStruct
    DMA = pltpu.SemaphoreType.DMA
    V = pltpu.VMEM
    whole = pl.BlockSpec(memory_space=pltpu.VMEM)
    far = pl.BlockSpec(memory_space=pl.ANY)
    part = shared.shape[2:]
    scratch = [V((1, 256, nk), BF16)] * 2 + [V((PAIRS, 8, nk), F32)] * 2 + [V((1, 256, nk), F32)] * 2 + [V((PAIRS, 8, nk), F32)] * 2
    scratch += [V((rows, n, *part), BF16), V((rows, NZ, *part), BF16), V((rows, NZ - 1, *part), BF16)] + [DMA((rows, NZ))] * 4 + [DMA((rows,))]
    scratch += [V((count, width), BF16)] * 4 + [V((width, count), BF16)] + [V((count, width), F32)] * 2
    scratch += [V((4, width, FFC), BF16), V((2, FFC, width), BF16)] + [V((n, width // n, FFC), BF16)] * 2 + [V((FFC, width), BF16)] + [V((count, FFC), BF16)] * 2 + [V((FFC, count), BF16)]
    scratch += [DMA((3, rows)), DMA((3, 4)), DMA((3,))]
    shard = (n, width // n)
    sums = [sd((width // n, width), BF16), sd((width // n, ff), BF16), sd((width // n, ff), BF16), sd((ff // n, width), BF16)]
    grads = [sd((*shard, width), BF16), sd((*shard, ff), BF16), sd((*shard, ff), BF16), sd((ff, width), BF16)]
    return pl.pallas_call(
        functools.partial(back_kernel, span, min(512, nk), units, plan, ff // FFC),
        grid=(rows, pairs),
        out_shape=[sd((rows, pairs, 12, nq), F32), sd((rows, 384, nq), F32), sd((rows, *part), BF16), sd((rows, nq, width), BF16),
                   sd((rows, nq, width), F32), sd((1, width), F32)] + sums + grads,
        in_specs=[pairb(12, nq), full(384, nq), far, pl.BlockSpec((1, nk), lambda b, p: (0, 0)), full(1, nk), full(1, nk), full(nq, 128)] + [far] * 7 + [whole],
        out_specs=[pairb(12, nq), full(384, nq), whole, far, far, whole] + [far] * 8,
        scratch_shapes=scratch + reduce_scratch(units),
        compiler_params=pltpu.CompilerParams(collective_id=cid, has_side_effects=True, vmem_limit_bytes=60 << 20),
        name="backward",
    )(qh, qr, shared, cond, bl, bs, lse, tokens, heads_out, cotangent, w_out, w_gate, w_up, w_down, gain_two)[:10]

class Gather:
    def __init__(self, me, units, ins, outs, sems):
        self.me, self.units, self.ins, self.outs = me, units, ins, outs
        self.zs, self.zr, self.xs, self.xr, self.ys, self.yr, self.cs, self.cr, self.ls = sems

    def remote(self, src, dst, ss, rs, dev):
        return pltpu.make_async_remote_copy(src_ref=src, dst_ref=dst, send_sem=ss, recv_sem=rs, device_id=dev, device_id_type=MESH)

    def view(self, k, shard, y, c):
        u = self.units[k]
        return self.part(u, self.outs[u.arr].at[shard], y, c)

    @staticmethod
    def part(u, ref, y, c):
        return rect(u, ref, 2 * c + y, 4) if u.flow == "P" else rect(u, ref, c, 2)

    def first(self, k, ss, rs, dev):
        u, me = self.units[k], self.me
        return self.remote(self.part(u, self.ins[u.arr], me.y, me.c), self.view(k, me.seq, me.y, me.c), ss, rs, dev)

    def onward(self, k, shard, y, ss, rs, dev):
        v = self.view(k, shard, y, self.me.c)
        return self.remote(v, v, ss, rs, dev)

    def zsend(self, k, zz):
        return self.first(k, self.zs.at[k, zz], self.zr.at[k, self.me.z], (2 * zz + self.me.x, self.me.batch))

    def zrecv(self, k, zz):
        me = self.me
        return self.onward(k, 2 * zz + me.x, me.y, self.zs.at[k, zz], self.zr.at[k, zz], (2 * zz + me.x, me.batch))

    def xown(self, k):
        return self.first(k, self.xs.at[k, self.me.z], self.xr.at[k, self.me.z], self.me.xp)

    def xsend(self, k, zz):
        return self.onward(k, 2 * zz + self.me.x, self.me.y, self.xs.at[k, zz], self.xr.at[k, zz], self.me.xp)

    def xrecv(self, k, zz):
        return self.onward(k, 2 * zz + 1 - self.me.x, self.me.y, self.xs.at[k, zz], self.xr.at[k, zz], self.me.xp)

    def ycopy(self, k, shard, mine):
        return self.onward(k, shard, self.me.y if mine else 1 - self.me.y, self.ys.at[k, shard], self.yr.at[k, shard], self.me.yp)

    def ccopy(self, k, w, shard):
        return self.onward(k, shard, self.me.y if w == 0 else 1 - self.me.y, self.cs.at[k, w, shard], self.cr.at[k, w, shard], self.me.cp)

    def crecv(self, k, w, shard):
        v = self.view(k, shard, self.me.y if w == 0 else 1 - self.me.y, 1 - self.me.c)
        return self.remote(v, v, self.cs.at[k, w, shard], self.cr.at[k, w, shard], self.me.cp)

    def local(self, a):
        return pltpu.make_async_copy(self.ins[a], self.outs[a].at[self.me.seq], self.ls.at[a])

    def other(self, i):
        return lax.rem(self.me.z + i, NZ)

    def begin(self, k, i):
        self.zsend(k, self.other(i)).start()
        pl.when(i == 1)(lambda: self.xown(k).start())

    def spread(self, k, shard):
        if self.units[k].flow == "P":
            self.ycopy(k, shard, True).start()
        self.ccopy(k, 0, shard).start()

    def z(self, k, i):
        zz = self.other(i)
        self.zrecv(k, zz).wait_recv()
        self.xsend(k, zz).start()
        self.spread(k, 2 * zz + self.me.x)

    def x(self, k, i):
        zz = self.other(i)
        self.xrecv(k, zz).wait_recv()
        self.spread(k, 2 * zz + 1 - self.me.x)

    def far(self, i):
        return 2 * self.other(i) + jnp.where(i < NZ, self.me.x, 1 - self.me.x)

    def y(self, k, i):
        shard = self.far(i)
        self.ycopy(k, shard, False).wait_recv()
        self.ccopy(k, 1, shard).start()

    def got(self, k, i):
        for w in range(2 if self.units[k].flow == "P" else 1):
            self.crecv(k, w, self.far(i)).wait_recv()

    def sent(self, k, i):
        me = self.me
        pl.when(i < NZ)(lambda: self.zsend(k, self.other(i)).wait_send())
        pl.when(i < NZ)(lambda: self.xsend(k, self.other(i)).wait_send())
        pl.when(i == NZ)(lambda: self.xown(k).wait_send())
        shard = self.far(i)
        self.ccopy(k, 0, shard).wait_send()
        if self.units[k].flow == "P":
            self.ycopy(k, shard, True).wait_send()
            self.ccopy(k, 1, shard).wait_send()

    def run(self, plan):
        for step, k, first, n in plan:
            fn = getattr(self, step)
            def body(i, c):
                fn(k, i)
                return c
            lax.fori_loop(first, first + n, body, 0)

class RowsGather:
    def __init__(self, me, shared, zs, zr, xs, xr):
        self.me, self.shared, self.zs, self.zr, self.xs, self.xr = me, shared, zs, zr, xs, xr

    def copy(self, b, shard, ss, rs, dev):
        v = self.shared.at[shard, b]
        return pltpu.make_async_remote_copy(src_ref=v, dst_ref=v, send_sem=ss, recv_sem=rs, device_id=dev, device_id_type=MESH)

    def zsend(self, b, zz):
        me = self.me
        return self.copy(b, me.seq, self.zs.at[b, zz], self.zr.at[b, me.z], (2 * zz + me.x, me.batch))

    def zrecv(self, b, zz):
        me = self.me
        return self.copy(b, 2 * zz + me.x, self.zs.at[b, zz], self.zr.at[b, zz], (2 * zz + me.x, me.batch))

    def xsend(self, b, zz):
        return self.copy(b, 2 * zz + self.me.x, self.xs.at[b, zz], self.xr.at[b, zz], self.me.xp)

    def xrecv(self, b, zz):
        return self.copy(b, 2 * zz + 1 - self.me.x, self.xs.at[b, zz], self.xr.at[b, zz], self.me.xp)

    def loop(self, first, fn):
        def body(i, c):
            fn(lax.rem(self.me.z + i, NZ))
            return c
        lax.fori_loop(first, NZ, body, 0)

    def begin(self, b):
        self.loop(1, lambda zz: self.zsend(b, zz).start())
        self.xsend(b, self.me.z).start()

    def z(self, b):
        def one(zz):
            self.zrecv(b, zz).wait_recv()
            self.xsend(b, zz).start()
        self.loop(1, one)

    def x(self, b):
        self.loop(0, lambda zz: self.xrecv(b, zz).wait_recv())

    def end(self, b):
        self.loop(1, lambda zz: self.zsend(b, zz).wait_send())
        self.loop(0, lambda zz: self.xsend(b, zz).wait_send())

def turn_rows(u, cosine, sine):
    out = []
    for r in range(0, u.shape[0], 64):
        a, b = u[r:r + 32], u[r + 32:r + 64]
        out += [a * cosine - b * sine, b * cosine + a * sine]
    return jnp.concatenate(out, 0)

def project(me, span, tok_ref, small_ref, cos_ref, sin_ref, normed_ref, qh_ref, qr_ref, shared_ref, b):
    nq = 2 * span
    d = tok_ref.shape[-1]
    gains = small_ref[:, :, 768:896].reshape(d, 128).astype(F32).T
    x = tok_ref[b].astype(F32)
    unit = x * lax.rsqrt(jnp.mean(x * x, -1, keepdims=True) + 1e-6)
    normed = (unit * gains[32:33]).astype(BF16)
    normed_ref[b] = normed
    w = small_ref[...].reshape(d, 896)
    f = nn(normed, w).T
    qh_ref[b] = f[:96].reshape(PAIRS, 12, nq)
    cosine, sine = cos_ref[...], sin_ref[...]
    qr_ref[b] = turn_rows(f[96:480], cosine, sine)
    own = jnp.concatenate([turn_rows(f[480:608], cosine, sine), f[608:800]], 0)
    shared_ref[me.seq, b] = own.astype(BF16)

def forward_kernel(span, chunk, units, narr, plan, tok_ref, cos_ref, sin_ref, cond_ref, bl_ref, bs_ref, *refs):
    ins = refs[:narr]
    normed_ref, qh_ref, qr_ref, shared_out, o_ref, lse_ref = refs[narr:narr + 6]
    outs = refs[narr + 6:2 * narr + 6]
    shared_ref, small, saved, dl, ds, hl, hs, s1, s2, rzs, rzr, rxs, rxr = refs[2 * narr + 6:2 * narr + 19]
    small_out, outs = outs[0], (small, *outs[1:])
    me = Place()
    b, p = pl.program_id(0), pl.program_id(1)
    step = b * PAIRS + p
    gat = Gather(me, units, ins, outs, refs[2 * narr + 19:])
    saves = (pltpu.make_async_copy(small, small_out, saved.at[0]), pltpu.make_async_copy(shared_ref, shared_out, saved.at[1]))
    row = RowsGather(me, shared_ref, rzs, rzr, rxs, rxr)

    def act(items):
        for it in items:
            if it[0] == "row":
                getattr(row, it[1])(it[2])
            elif it[0] == "project":
                for r in range(tok_ref.shape[0]):
                    project(me, span, tok_ref, small, cos_ref, sin_ref, normed_ref, qh_ref, qr_ref, shared_ref, r)
            elif it[0] == "local":
                for a in range(narr):
                    gat.local(a).start()
                gat.local(0).wait()
            elif it[0] == "locals":
                for a in range(1, narr):
                    gat.local(a).wait()
                for save in saves:
                    save.start()
                for save in saves:
                    save.wait()
            else:
                gat.run([it])

    @pl.when(step == 0)
    def _():
        greet(me)
        act(plan["first"])

    @pl.when(p == 0)
    def _():
        lay_out(me, lambda j: shared_ref.at[j, b], 2 * NZ, span, cond_ref, dl, ds, hl, hs)

    pair_forward(span, chunk, p, qh_ref[b, p], qr_ref[b], hl[p], hs[p], dl, ds, cond_ref, bl_ref, bs_ref, o_ref, lse_ref, s1, s2)

    for s, items in plan["steps"].items():
        pl.when(step == s)(functools.partial(act, items))

def forward(tokens, cosine, sine, cond, bl, bs, weights, units, plan, cid):
    rows, nq, width = tokens.shape
    span = nq // 2
    n = 2 * NZ
    nk = n * span
    narr, nu = len(weights), len(units)
    chunk = min(512, nk)
    whole = pl.BlockSpec(memory_space=pltpu.VMEM)
    far = pl.BlockSpec(memory_space=pl.ANY)
    full = lambda *s: pl.BlockSpec((1, *s), lambda b, p: (b, *([0] * len(s))))
    sd = jax.ShapeDtypeStruct
    DMA = pltpu.SemaphoreType.DMA
    V = pltpu.VMEM
    scratch = [V((n, rows, 320, nq), BF16), V((n, *weights[0].shape), BF16), DMA((2,))] + [V((1, 256, nk), BF16)] * 2 + [V((PAIRS, 8, nk), F32)] * 2 + [V((nq, nk), F32)] * 2 + [DMA((rows, NZ))] * 4
    scratch += [DMA((nu, NZ))] * 4 + [DMA((nu, n))] * 2 + [DMA((nu, 2, n))] * 2 + [DMA((narr,))]
    return pl.pallas_call(
        functools.partial(forward_kernel, span, chunk, units, narr, plan),
        grid=(rows, PAIRS),
        out_shape=[sd((rows, nq, width), BF16), sd((rows, PAIRS, 12, nq), F32), sd((rows, 384, nq), F32), sd((n, rows, 320, nq), BF16),
                   sd((rows, nq, width), BF16), sd((rows, nq, 128), F32)] + [sd((n, *a.shape), a.dtype) for a in weights],
        in_specs=[whole, whole, whole, pl.BlockSpec((1, nk), lambda b, p: (0, 0)), full(1, nk), full(1, nk)] + [far] * narr,
        out_specs=[whole, whole, whole, far, pl.BlockSpec((1, nq, 128), lambda b, p: (b, 0, p)), full(nq, 128)] + [far] * narr,
        scratch_shapes=scratch,
        compiler_params=pltpu.CompilerParams(collective_id=cid, has_side_effects=True, vmem_limit_bytes=56 << 20),
        name="forward",
    )(tokens, cosine, sine, cond, bl, bs, *weights)

HEADS, HDIM, QRANK, KVRANK = 16, 64, 6, 2
PAIRS = HEADS // 2
EPSILON = 1e-06


def rms_forward(values, gain):
    scale = lax.rsqrt(jnp.mean(values * values, -1, keepdims=True) + EPSILON)
    unit = values * scale
    return (unit * gain, unit, scale)


def rms_backward(grad_out, unit, scale, gain):
    scaled = grad_out * gain
    grad_in = scale * (scaled - unit * jnp.mean(scaled * unit, -1, keepdims=True))
    return (grad_in, jnp.sum(grad_out * unit, 0))


def rotation(positions):
    half = HDIM // 2
    index = jnp.arange(half).astype(F32)
    inverse = jnp.exp(index * (-math.log(10000.0) / half))
    angles = inverse[:, None] * positions.astype(F32)[None, :]
    return (jnp.cos(angles), jnp.sin(angles))


def rotate(u, cosine, sine):
    rows, depth, slots = u.shape
    v = u.reshape(rows, depth // HDIM, HDIM, slots)
    a, b = v[:, :, :HDIM // 2], v[:, :, HDIM // 2:]
    return jnp.concatenate([a * cosine - b * sine, b * cosine + a * sine], 2).reshape(u.shape)


def dot(a, b, ca, cb):
    return lax.dot_general(a, b, ((ca, cb), ((), ())), preferred_element_type=F32)


def pair_columns(a, ranks):
    return a.reshape(-1, ranks, PAIRS, 2).transpose(0, 2, 1, 3).reshape(a.shape)


def head_columns(a, ranks):
    return a.reshape(-1, PAIRS, ranks, 2).transpose(0, 2, 1, 3).reshape(a.shape)


GATHER_UNITS = [
    Unit(0, (0, 128), (0, 896), "P", 0), Unit(1, (0, 128), (0, 1024), "P", 0),
    Unit(2, (0, 128), (0, 1408), "P", 0), Unit(2, (0, 128), (1408, 1408), "P", 0),
    Unit(3, (0, 128), (0, 1408), "R", 0), Unit(3, (0, 128), (1408, 1408), "P", 0),
    Unit(4, (0, 176), (0, 1024), "P", 1), Unit(4, (176, 176), (0, 1024), "P", 1)]
GATHER_PLAN = {
    "first": [("local",), ("begin", 0, 1, 3), ("begin", 1, 1, 3), ("z", 0, 1, 3), ("x", 0, 0, 4), ("begin", 3, 1, 3), ("y", 0, 1, 7), ("begin", 7, 1, 3), ("begin", 2, 1, 3), ("z", 1, 1, 3), ("got", 0, 1, 7), ("x", 1, 0, 4), ("begin", 6, 1, 3), ("z", 3, 1, 3), ("project",), ("z", 2, 1, 3), ("x", 3, 0, 4), ("row", "begin", 0), ("row", "begin", 1), ("x", 2, 0, 4), ("z", 7, 1, 3), ("row", "z", 0), ("z", 6, 1, 3), ("row", "x", 0), ("y", 3, 4, 4), ("y", 2, 1, 3), ("begin", 5, 1, 3), ("begin", 4, 1, 3), ("y", 7, 1, 3)],
    "steps": {
        2: [("x", 6, 0, 4), ("y", 1, 1, 3), ("y", 3, 1, 3), ("row", "z", 1)],
        5: [("z", 5, 1, 3), ("y", 1, 4, 4)],
        6: [("x", 7, 0, 4)],
        7: [("y", 2, 4, 4), ("row", "x", 1)],
        10: [("z", 4, 1, 3), ("x", 5, 0, 4)],
        12: [("y", 7, 4, 4), ("y", 6, 1, 3)],
        13: [("y", 6, 4, 4), ("y", 5, 1, 3)],
        14: [("x", 4, 0, 4)],
        15: [("y", 5, 4, 4), ("got", 1, 1, 7), ("got", 2, 1, 7), ("got", 3, 1, 7), ("got", 4, 1, 7), ("got", 5, 1, 7), ("got", 6, 1, 7), ("got", 7, 1, 7), ("locals",), ("sent", 0, 1, 7), ("sent", 1, 1, 7), ("sent", 2, 1, 7), ("sent", 3, 1, 7), ("sent", 4, 1, 7), ("sent", 5, 1, 7), ("sent", 6, 1, 7), ("sent", 7, 1, 7), ("row", "end", 0), ("row", "end", 1)],
    },
}
REDUCE_UNITS = [
    Unit(1, (0, 128), (0, 1024), "P", 0), Unit(2, (0, 128), (0, 1024), "R", 0),
    Unit(1, (0, 128), (1024, 1024), "P", 0), Unit(2, (0, 128), (1024, 1024), "R", 0),
    Unit(1, (0, 128), (2048, 768), "P", 0), Unit(2, (0, 128), (2048, 768), "P", 0),
    Unit(3, (0, 176), (0, 1024), "P", 1), Unit(3, (176, 176), (0, 1024), "P", 1), Unit(0, (0, 128), (0, 1024), "P", 0)]
REDUCE_PLAN = {
    "feed": {
        4: [("begin", 0, 0, 8), ("begin", 1, 0, 8)],
        5: [("core", 0, 0, 4)],
        6: [("core", 1, 0, 4), ("core", 0, 4, 4)],
        7: [("y", 0, 0, 4)],
        8: [("begin", 2, 0, 8), ("begin", 3, 0, 8)],
        9: [("core", 2, 0, 4), ("y", 0, 4, 4), ("core", 1, 4, 4)],
    },
    "mid": [("begin", 5, 0, 8), ("begin", 7, 0, 8), ("x", 1, 0, 4), ("core", 2, 4, 4), ("core", 3, 0, 4), ("core", 5, 0, 4)],
    "first": [("begin", 4, 0, 8), ("core", 5, 4, 4), ("begin", 8, 0, 8), ("y", 2, 0, 4)],
    "steps": {
        0: [("y", 2, 4, 4), ("core", 4, 4, 4), ("core", 3, 4, 4), ("core", 7, 0, 4), ("x", 3, 0, 4), ("y", 5, 0, 4), ("core", 4, 0, 4)],
        2: [("core", 7, 4, 4), ("y", 5, 4, 4), ("x", 5, 0, 4)],
        4: [("y", 7, 0, 4), ("x", 0, 0, 4)],
        5: [("x", 2, 0, 4)],
        6: [("y", 4, 4, 4), ("y", 4, 0, 4), ("core", 8, 4, 4)],
        7: [("begin", 6, 0, 8), ("y", 7, 4, 4), ("x", 4, 0, 4), ("x", 7, 0, 4), ("core", 8, 0, 4)],
        8: [("core", 6, 0, 4)],
        10: [("y", 8, 0, 4), ("core", 6, 4, 4), ("row", "x", 0)],
        11: [("own", 5, 0, 1), ("own", 2, 0, 1), ("own", 7, 0, 1), ("y", 8, 4, 4), ("own", 4, 0, 1), ("y", 6, 0, 4)],
        12: [("x", 8, 0, 4)],
        13: [("y", 6, 4, 4)],
        14: [("last", 2, 0, 1), ("x", 6, 0, 4), ("last", 7, 0, 1)],
        15: [("own", 8, 0, 1), ("own", 1, 0, 1), ("row", "own", 0), ("own", 3, 0, 1), ("own", 0, 0, 1), ("row", "x", 1), ("last", 1, 0, 1), ("own", 6, 0, 1), ("last", 8, 0, 1), ("last", 0, 0, 1), ("last", 6, 0, 1), ("last", 4, 0, 1), ("last", 5, 0, 1), ("last", 3, 0, 1), ("row", "own", 1), ("end", 0, 0, 1), ("end", 1, 0, 1), ("end", 2, 0, 1), ("end", 3, 0, 1), ("end", 4, 0, 1), ("end", 5, 0, 1), ("end", 6, 0, 1), ("end", 7, 0, 1), ("end", 8, 0, 1), ("results",), ("row", "end", 0), ("row", "end", 1)],
    },
}
SMALL_UNITS = [Unit(0, (0, 128), (0, 896), "P", 0)]
SMALL_PLAN = [("begin", 0, 0, 8), ("core", 0, 0, 8), ("y", 0, 0, 8), ("x", 0, 0, 4), ("own", 0, 0, 1), ("last", 0, 0, 1), ("end", 0, 0, 1)]


def reduce_far(arrays):
    out = []
    for a in arrays:
        own = lax.psum_scatter(a.astype(F32), "seq", scatter_dimension=0, tiled=True)[0]
        out.append(lax.psum(own.astype(BF16), "batch"))
    return out


def per_device(near, tokens, cotangent, lengths, span_order, attn_gain, query_heads, query_dims, key_heads, key_dims,
               value_heads, value_dims, out_proj, ffn_gain, gate_proj, up_proj, down_proj):
    rows, slots, width = tokens.shape
    span = slots // 2
    count = rows * slots
    nseq = span_order.shape[0]
    nk = nseq * span
    me = lax.axis_index("seq")
    key_value_heads = pair_columns(jnp.concatenate([key_heads, value_heads], 1), 4)
    small = jnp.concatenate([pair_columns(query_heads, QRANK), query_dims, key_dims, value_dims, key_value_heads, attn_gain[:, None], ffn_gain[:, None]], 1)
    small = jnp.pad(small, ((0, 0), (0, 896 - small.shape[1])))
    offsets = jnp.arange(span, dtype=jnp.int32)
    spans = jnp.concatenate([span_order, span_order], 0)
    spans = lax.dynamic_slice_in_dim(spans, me, nseq, 0)
    local_pos = (spans[0][:, None] * span + offsets[None, :]).reshape(-1)
    cosine, sine = rotation(local_pos)
    chosen = spans[:, 0] < spans[0, 0]
    low_pos = (spans[:, 0][:, None] * span + offsets[None, :]).reshape(1, nk)
    sel_pos = (jnp.where(chosen, spans[:, 0], spans[:, 1])[:, None] * span + offsets[None, :]).reshape(1, nk)
    cond = jnp.repeat(chosen.astype(F32), span).reshape(1, nk)
    low_bias = jnp.where(low_pos < lengths[:, None], 0.0, NEG)[:, None, :]
    sel_bias = jnp.where(sel_pos < lengths[:, None], 0.0, NEG)[:, None, :]

    masks = (cond, low_bias, sel_bias)
    flat = tokens.reshape(count, width).astype(F32)
    weights = [small, out_proj, gate_proj, up_proj, down_proj]
    if near:
        by_row, qh, qr, shared, heads_out, lse, *parts = forward(tokens, cosine, sine, *masks, weights, GATHER_UNITS, GATHER_PLAN, 0)
    else:
        parts = [lax.all_gather(a, "seq", axis=0) for a in weights]
    small, w_out, w_gate, w_up, w_down = [p.reshape(-1, p.shape[-1]) for p in parts]
    w_qkv = small[:, :800]
    gain_one = small[:, 800].astype(F32)
    gain_two = small[:, 801].astype(F32)
    normed_full, unit_one, scale_one = rms_forward(flat, gain_one)
    if not near:
        by_row = normed_full.astype(BF16).reshape(rows, slots, width)
        factors = jnp.stack([dot(w_qkv, by_row[b], (0,), (1,)) for b in range(rows)])
        qh = factors[:, :96].reshape(rows, PAIRS, 12, slots)
        qr = rotate(factors[:, 96:480], cosine, sine)
        own = jnp.concatenate([rotate(factors[:, 480:608], cosine, sine), factors[:, 608:800]], 1).astype(BF16)
        shared = lax.all_gather(own, "seq", axis=0)
        turned = lax.dynamic_slice_in_dim(jnp.concatenate([shared, shared], 0), me, nseq, 0)
        low, high = turned[..., :span], turned[..., span:]
        sel = jnp.where(chosen[:, None, None, None], low, high)
        low = low.transpose(1, 2, 0, 3).reshape(rows, 320, nk)
        sel = sel.transpose(1, 2, 0, 3).reshape(rows, 320, nk)
        in_pairs = lambda a: a[:, 256:].astype(F32).reshape(rows, PAIRS, 8, nk)
        factors = (in_pairs(low), in_pairs(sel), low[:, :256], sel[:, :256])
        heads_out, lse = attend(qh, qr, *factors, *masks)
    if near:
        dqh, dqr, mine, output, d_resid, gain_two_grad, *sums = backward(
            qh, qr, shared, *masks, lse, tokens, heads_out, cotangent, w_out, w_gate, w_up, w_down, gain_two[None, :], REDUCE_UNITS, REDUCE_PLAN, 1)
        d_resid, gain_two_grad = d_resid.reshape(count, width), gain_two_grad[0]
    else:
        heads_flat = heads_out.reshape(count, width)

        resid = flat + dot(heads_flat, w_out, (1,), (0,))
        normed_two_full, unit_two, scale_two = rms_forward(resid, gain_two)
        normed_two = normed_two_full.astype(BF16)
        gate = dot(normed_two, w_gate, (1,), (0,))
        up_part = dot(normed_two, w_up, (1,), (0,))
        sigma = jax.nn.sigmoid(gate)
        hidden = (gate * sigma * up_part).astype(BF16)
        output = (resid + dot(hidden, w_down, (1,), (0,))).astype(BF16).reshape(rows, slots, width)

        grad_out = cotangent.reshape(count, width)
        down_grad = dot(hidden, grad_out, (0,), (0,)).astype(BF16)
        d_hidden = dot(grad_out, w_down, (1,), (1,))
        d_gate = (d_hidden * up_part * sigma * (1.0 + gate * (1.0 - sigma))).astype(BF16)
        d_up = (d_hidden * gate * sigma).astype(BF16)
        gate_grad = dot(normed_two, d_gate, (0,), (0,)).astype(BF16)
        up_grad = dot(normed_two, d_up, (0,), (0,)).astype(BF16)
        d_normed_two = dot(d_gate, w_gate, (1,), (1,)) + dot(d_up, w_up, (1,), (1,))
        d_mid, gain_two_grad = rms_backward(d_normed_two, unit_two, scale_two, gain_two)
        d_resid = grad_out.astype(F32) + d_mid
        d_attn = d_resid.astype(BF16)
        out_grad = dot(heads_flat, d_attn, (0,), (0,)).astype(BF16)
        d_heads = dot(d_attn, w_out, (1,), (1,)).astype(BF16).reshape(rows, slots, width)

        grads = [g.reshape(nseq, -1, g.shape[-1]) for g in (out_grad, gate_grad, up_grad, down_grad)]
        dqh, dqr, dhl, dhs, ddl, dds = attend_back(qh, qr, *factors, *masks, lse, heads_out, d_heads)
        from_low = jnp.concatenate([ddl, dhl.reshape(rows, 64, nk)], 1).reshape(rows, 320, nseq, span)
        from_sel = jnp.concatenate([dds, dhs.reshape(rows, 64, nk)], 1).reshape(rows, 320, nseq, span)
        pick = chosen[None, None, :, None]
        both = jnp.concatenate([from_low + jnp.where(pick, from_sel, 0.0), jnp.where(pick, 0.0, from_sel)], -1).transpose(2, 0, 1, 3)
        both = lax.dynamic_slice_in_dim(jnp.concatenate([both, both], 0), lax.rem(nseq - me, nseq), nseq, 0)
        mine = lax.psum_scatter(both, "seq", scatter_dimension=0, tiled=True)[0]
        sums = reduce_far(grads)
    mine = mine.astype(F32)
    turned = jnp.concatenate([dqh.reshape(rows, 96, slots), rotate(dqr, cosine, -sine), rotate(mine[:, :128], cosine, -sine), mine[:, 128:]], 1).astype(BF16)
    small_grad = dot(by_row, turned, (0, 1), (0, 2))
    d_normed = dot(turned, w_qkv, (1,), (1,)).reshape(count, width)
    d_first, gain_one_grad = rms_backward(d_normed, unit_one, scale_one, gain_one)
    input_grad = (d_resid + d_first).reshape(rows, slots, width)
    small_grad = jnp.concatenate([small_grad, gain_one_grad[:, None], gain_two_grad[:, None], jnp.zeros((width, 94), F32)], 1).astype(BF16)

    small_grad = small_grad.reshape(nseq, -1, 896)
    small_sum = reduce_weights([small_grad], SMALL_UNITS, SMALL_PLAN, 3)[0] if near else reduce_far([small_grad])[0]
    small_sum = small_sum.astype(F32)
    out_sum, gate_sum, up_sum, down_sum = [g.astype(F32) for g in sums]
    key_value = head_columns(small_sum[:, 736:800], 4)
    return (output, input_grad, small_sum[:, 800], head_columns(small_sum[:, :96], QRANK), small_sum[:, 96:480], key_value[:, :32], small_sum[:, 480:608],
            key_value[:, 32:], small_sum[:, 608:736], out_sum, small_sum[:, 801], gate_sum, up_sum, down_sum)


def solution(mesh):
    near = mesh.shape["seq"] == 8 and mesh.shape["batch"] == 4
    by_slot = P("batch", "seq", None)
    line, table = P("seq"), P("seq", None)
    return jax.shard_map(
        functools.partial(per_device, near),
        mesh=mesh,
        in_specs=(by_slot, by_slot, P("batch"), P(), line, *([table] * 7), line, *([table] * 3)),
        out_specs=(by_slot, by_slot, line, *([table] * 7), line, *([table] * 3)),
        check_vma=False,
    )
```

```python
import functools
import math

import jax
import jax.numpy as jnp
from jax import lax
from jax.experimental import pallas as pl
from jax.experimental.pallas import tpu as pltpu
from jax.sharding import PartitionSpec as P


MESH = pl.DeviceIdType.MESH
NZ, NX = 4, 2

class Place:
    def __init__(self):
        self.seq = lax.axis_index("seq")
        self.batch = lax.axis_index("batch")
        self.z = self.seq // 2
        self.x = lax.rem(self.seq, 2)
        self.y = self.batch // 2
        self.c = lax.rem(self.batch, 2)
        self.up = (jnp.minimum(self.seq + 2, 7), self.batch)
        self.down = (jnp.maximum(self.seq - 2, 0), self.batch)
        self.xp = (self.seq + 1 - 2 * self.x, self.batch)
        self.yp = (self.seq, lax.rem(self.batch + 2, 4))
        self.cp = (self.seq, self.batch + 1 - 2 * self.c)

    def along(self, k):
        return (2 * lax.rem(self.z + k, NZ) + self.x, self.batch)

def greet(me):
    bar = pltpu.get_barrier_semaphore()
    def sig(d):
        pl.semaphore_signal(bar, inc=1, device_id=d, device_id_type=MESH)
    for k in range(1, NZ):
        sig(me.along(k))
    sig(me.xp); sig(me.yp); sig(me.cp)
    pl.semaphore_wait(bar, NZ + 2)

class Unit:
    def __init__(self, arr, row, col, flow, axis):
        self.arr, self.row, self.col, self.flow, self.axis = arr, row, col, flow, axis
        self.shape = (row[1], col[1])
        h = list(self.shape); h[axis] //= 2
        self.half = tuple(h)
        q = list(h)
        if flow == "P": q[axis] //= 2
        self.piece = tuple(q)

def rect(unit, ref, part, nparts):
    start = [unit.row[0], unit.col[0]]
    size = list(unit.shape)
    size[unit.axis] //= nparts
    idx = []
    for d in range(2):
        if d == unit.axis:
            off = part * size[d] + start[d]
            idx.append(pl.ds(pl.multiple_of(off, 16 if d == 0 else 128), size[d]))
        else:
            idx.append(pl.ds(start[d], size[d]))
    return ref.at[tuple(idx)]

def shard_of(ref, s, n=8):
    if len(ref.shape) == 3:
        return ref.at[s]
    rows = ref.shape[0] // n
    return ref.at[pl.ds(pl.multiple_of(s * rows, 16), rows)]

class Reduce:
    def __init__(self, me, units, ins, outs, scratch):
        self.me, self.units, self.ins, self.outs = me, units, ins, outs
        nu = len(units)
        self.A, self.RC, self.RY, self.RX, self.RZ, self.RF = [scratch[i * nu:(i + 1) * nu] for i in range(6)]
        self.ls, self.cs, self.cr, self.ys, self.yr, self.xs, self.xr, self.zs, self.zr, self.fs, self.fr, self.os_ = scratch[6 * nu:]

    def shard_at(self, i):
        me = self.me
        zz = lax.rem(me.z + 1 + lax.rem(i, NZ), NZ)
        xx = jnp.where(i < NZ, 1 - me.x, me.x)
        return zz, xx, 2 * zz + xx

    def sub(self, u, ref, y):
        if u.flow == "R":
            return ref
        n = u.piece[u.axis]
        idx = [slice(None)] * 2
        idx[u.axis] = pl.ds(pl.multiple_of(y * n, n), n)
        return ref.at[tuple(idx)]

    def remote(self, src, dst, ss, rs, dev):
        return pltpu.make_async_remote_copy(src_ref=src, dst_ref=dst, send_sem=ss, recv_sem=rs, device_id=dev, device_id_type=MESH)

    def core_copy(self, k, i):
        u = self.units[k]; zz, xx, s = self.shard_at(i)
        return self.remote(rect(u, shard_of(self.ins[u.arr], s), 1 - self.me.c, 2), self.RC[k].at[s], self.cs.at[k, s], self.cr.at[k, s], self.me.cp)

    def local_copy(self, k, i):
        u = self.units[k]; zz, xx, s = self.shard_at(i)
        return pltpu.make_async_copy(rect(u, shard_of(self.ins[u.arr], s), self.me.c, 2), self.A[k].at[s], self.ls.at[k, s])

    def y_copy(self, k, i):
        u = self.units[k]; zz, xx, s = self.shard_at(i)
        return self.remote(self.sub(u, self.A[k].at[s], 1 - self.me.y), self.RY[k].at[s], self.ys.at[k, s], self.yr.at[k, s], self.me.yp)

    def x_copy(self, k, zz):
        u, me = self.units[k], self.me
        return self.remote(self.sub(u, self.A[k].at[2 * zz + 1 - me.x], me.y), self.RX[k].at[zz], self.xs.at[k, zz], self.xr.at[k, zz], me.xp)

    def z_copy(self, k, zz):
        u, me = self.units[k], self.me
        return self.remote(self.mine(k, zz), self.RZ[k].at[self.slot(me.z, zz)], self.zs.at[k, zz], self.zr.at[k, me.z], (2 * zz + me.x, me.batch))

    @staticmethod
    def slot(source, owner):
        return lax.rem(source - owner + NZ, NZ) - 1

    def z_recv(self, k, zz):
        u, me = self.units[k], self.me
        v = self.RZ[k].at[self.slot(zz, me.z)]
        return self.remote(v, v, self.zs.at[k, zz], self.zr.at[k, zz], (2 * zz + me.x, me.batch))

    def mine(self, k, zz):
        return self.sub(self.units[k], self.A[k].at[2 * zz + self.me.x], self.me.y)

    @staticmethod
    def add(dst, src):
        dst[...] = dst[...] + src[...]

    def begin(self, k, i):
        self.core_copy(k, i).start()
        self.local_copy(k, i).start()

    def core(self, k, i):
        u = self.units[k]; zz, xx, s = self.shard_at(i)
        self.local_copy(k, i).wait()
        self.core_copy(k, i).wait_recv()
        self.add(self.A[k].at[s], self.RC[k].at[s])
        if u.flow == "P":
            self.y_copy(k, i).start()
        else:
            pl.when(i < NZ)(lambda: self.x_copy(k, zz).start())

    def y(self, k, i):
        u = self.units[k]; zz, xx, s = self.shard_at(i)
        self.y_copy(k, i).wait_recv()
        self.add(self.sub(u, self.A[k].at[s], self.me.y), self.RY[k].at[s])
        pl.when(i < NZ)(lambda: self.x_copy(k, zz).start())

    def x(self, k, i):
        me = self.me
        zz = lax.rem(me.z + 1 + i, NZ)
        self.x_copy(k, zz).wait_recv()
        self.add(self.mine(k, zz), self.RX[k].at[zz])
        pl.when(zz != me.z)(lambda: self.z_copy(k, zz).start())

    def fin_y(self, k):
        u, me = self.units[k], self.me
        mine = self.mine(k, me.z)
        dst = rect(u, self.outs[u.arr], 2 * me.c + me.y, 4) if u.flow == "P" else self.RF[k]
        return self.remote(mine, dst, self.fs.at[k, 0], self.fr.at[k, 0], me.yp)

    def fin_c(self, k, w):
        u, me = self.units[k], self.me
        if u.flow == "P":
            if w == 0:
                return self.remote(self.mine(k, me.z), rect(u, self.outs[u.arr], 2 * me.c + me.y, 4), self.fs.at[k, 1], self.fr.at[k, 1], me.cp)
            v = rect(u, self.outs[u.arr], 2 * me.c + 1 - me.y, 4)
            return self.remote(v, v, self.fs.at[k, 2], self.fr.at[k, 2], me.cp)
        return self.remote(self.RF[k], rect(u, self.outs[u.arr], me.c, 2), self.fs.at[k, 1], self.fr.at[k, 1], me.cp)

    def out_copy(self, k):
        u, me = self.units[k], self.me
        if u.flow == "P":
            return pltpu.make_async_copy(self.mine(k, me.z), rect(u, self.outs[u.arr], 2 * me.c + me.y, 4), self.os_.at[k])
        return pltpu.make_async_copy(self.RF[k], rect(u, self.outs[u.arr], me.c, 2), self.os_.at[k])

    def own(self, k, i):
        me = self.me
        def body(i, c):
            zz = lax.rem(me.z + i, NZ)
            self.z_recv(k, zz).wait_recv()
            self.add(self.mine(k, me.z), self.RZ[k].at[self.slot(zz, me.z)])
            return c
        lax.fori_loop(1, NZ, body, 0)
        self.fin_y(k).start()
        if self.units[k].flow == "P":
            self.out_copy(k).start()
            self.fin_c(k, 0).start()

    def last(self, k, i):
        self.fin_y(k).wait_recv()
        if self.units[k].flow == "P":
            self.fin_c(k, 1).start()
        else:
            self.add(self.RF[k], self.mine(k, self.me.z))
            self.out_copy(k).start()
            self.fin_c(k, 0).start()

    def end(self, k, i):
        me = self.me
        flow = self.units[k].flow
        for w in range(2 if flow == "P" else 1):
            self.fin_c(k, w).wait_recv()
            self.fin_c(k, w).wait_send()
        self.out_copy(k).wait()
        self.fin_y(k).wait_send()
        def body(i, c):
            self.core_copy(k, i).wait_send()
            if flow == "P": self.y_copy(k, i).wait_send()
            return c
        lax.fori_loop(0, 8, body, 0)
        def body(zz, c):
            self.x_copy(k, zz).wait_send()
            pl.when(zz != me.z)(lambda: self.z_copy(k, zz).wait_send())
            return c
        lax.fori_loop(0, NZ, body, 0)

    def run(self, plan):
        for step, k, first, n in plan:
            fn = getattr(self, step)
            if n == 1:
                fn(k, first)
            else:
                def body(i, c):
                    fn(k, i)
                    return c
                lax.fori_loop(first, first + n, body, 0)

def reduce_kernel(units, narr, plan, *refs):
    me = Place()
    greet(me)
    red = Reduce(me, units, refs[:narr], refs[narr:2 * narr], refs[2 * narr:])
    red.run(plan)

def reduce_scratch(units):
    nu = len(units)
    DMA = pltpu.SemaphoreType.DMA
    bf = jnp.bfloat16
    V = pltpu.VMEM
    return ([V((8, *u.half), bf) for u in units] + [V((8, *u.half), bf) for u in units]
        + [V((8, *u.piece) if u.flow == "P" else (16, 128), bf) for u in units] + [V((4, *u.piece), bf) for u in units]
        + [V((3, *u.piece), bf) for u in units] + [V(u.piece if u.flow == "R" else (16, 128), bf) for u in units]
        + [DMA((nu, 8))] * 5 + [DMA((nu, 4))] * 4 + [DMA((nu, 3))] * 2 + [DMA((nu,))])

def reduce_weights(arrays, units, plan, cid):
    narr = len(arrays)
    return pl.pallas_call(
        functools.partial(reduce_kernel, units, narr, plan),
        out_shape=[jax.ShapeDtypeStruct(a.shape[1:], a.dtype) for a in arrays],
        in_specs=[pl.BlockSpec(memory_space=pl.ANY)] * narr,
        out_specs=[pl.BlockSpec(memory_space=pl.ANY)] * narr,
        scratch_shapes=reduce_scratch(units),
        compiler_params=pltpu.CompilerParams(collective_id=cid, has_side_effects=True, vmem_limit_bytes=58 << 20),
        name="reduce_weights",
    )(*arrays)

F32, BF16 = jnp.float32, jnp.bfloat16
NEG = -1e30

def nn(a, b):
    return lax.dot_general(a, b, (((1,), (0,)), ((), ())), preferred_element_type=F32)

def nt(a, b):
    return lax.dot_general(a, b, (((1,), (1,)), ((), ())), preferred_element_type=F32)

def expand(heads, dims, base):
    parts = []
    for h in range(2):
        parts.append((heads[base + h:base + h + 1] * dims[0] + heads[base + 2 + h:base + 3 + h] * dims[1]) * 0.5)
    return jnp.concatenate(parts, 0)

def queries(qh, qr):
    parts = []
    for h in range(2):
        total = qh[h:h + 1] * qr[0:64]
        for r in range(1, 6):
            total = total + qh[2 * r + h:2 * r + h + 1] * qr[64 * r:64 * r + 64]
        parts.append(total)
    return jnp.concatenate(parts, 0) / 6.0

def lanes_below(shape, n):
    return lax.broadcasted_iota(jnp.int32, shape, 1) < n

def stack_heads(part):
    first = lanes_below(part.shape, 64)
    zero = jnp.zeros_like(part)
    return jnp.concatenate([jnp.where(first, part, zero), jnp.where(first, zero, part)], 0)

def unstack_heads(part):
    n = part.shape[0] // 2
    return jnp.where(lanes_below((n, 128), 64), part[:n], part[n:])

def causal_bias(n2, span):
    row = lax.broadcasted_iota(jnp.int32, (n2, span), 0) % span
    col = lax.broadcasted_iota(jnp.int32, (n2, span), 1)
    return jnp.where(col <= row, 0.0, NEG)

def pair_factors(heads, dims, cond, base, at):
    hl, hs = heads
    dl, ds = dims
    low = expand(hl, (dl[at:at + 64].astype(F32), dl[at + 64:at + 128].astype(F32)), base).astype(BF16)
    sel = expand(hs, (ds[at:at + 64].astype(F32), ds[at + 64:at + 128].astype(F32)), base)
    left = jnp.where(cond > 0.5, sel, 0.0).astype(BF16)
    right = jnp.where(cond > 0.5, 0.0, sel).astype(BF16)
    return low, jnp.concatenate([left, right], 0)

def attend_kernel(span, chunk, qh_ref, qr_ref, hl_ref, hs_ref, dl_ref, ds_ref, cond_ref, bl_ref, bs_ref, o_ref, lse_ref, s1, s2):
    pair_forward(span, chunk, pl.program_id(1), qh_ref[0, 0], qr_ref[0], hl_ref[0, 0], hs_ref[0, 0], dl_ref, ds_ref, cond_ref, bl_ref, bs_ref, o_ref, lse_ref, s1, s2)

def pair_forward(span, chunk, p, qh, qr, hl, hs, dl_ref, ds_ref, cond_ref, bl_ref, bs_ref, o_ref, lse_ref, s1, s2):
    n2 = 2 * span
    nk = dl_ref.shape[-1]
    qt = queries(qh, qr)
    q = (qt.astype(BF16).astype(F32).T * 0.125).astype(BF16)
    qlo, qhi = stack_heads(q[:span]), stack_heads(q[span:])
    qboth = jnp.concatenate([qlo, qhi], 1)
    heads = (hl, hs)
    dims = (dl_ref[0], ds_ref[0])
    cond = cond_ref[...]
    klo, ksel = pair_factors(heads, dims, cond, 0, 0)
    vlo, vsel = pair_factors(heads, dims, cond, 4, 128)
    tri = causal_bias(n2, span)
    width = min(128, chunk)
    mlo = jnp.full((n2, width), NEG, F32)
    mhi = jnp.full((n2, width), NEG, F32)
    s3 = nn(qlo, klo[:, :span]) + bl_ref[0][:, :span] + tri
    m3 = jnp.max(s3, -1, keepdims=True)
    for c in range(0, nk, chunk):
        sl = slice(c, c + chunk)
        a = nn(qhi, klo[:, sl]) + bl_ref[0][:, sl]
        s1[:, sl] = a
        b = nn(qboth, ksel[:, sl]) + bs_ref[0][:, sl]
        if c == 0:
            b = jnp.concatenate([b[:, :span] + tri, b[:, span:]], 1)
        s2[:, sl] = b
        for i in range(0, chunk, width):
            on = cond[:, c + i:c + i + width] > 0.5
            ai, bi = a[:, i:i + width], b[:, i:i + width]
            mlo = jnp.maximum(mlo, jnp.where(on, bi, NEG))
            mhi = jnp.maximum(mhi, jnp.maximum(ai, jnp.where(on, NEG, bi)))
    mlo = jnp.maximum(jnp.max(mlo, -1, keepdims=True), m3)
    mhi = jnp.max(mhi, -1, keepdims=True)
    e3 = jnp.exp(s3 - mlo)
    tlo = jnp.zeros((n2, width), F32)
    thi = jnp.zeros((n2, width), F32)
    o3 = nt(e3.astype(BF16), vlo[:, :span])
    o1 = jnp.zeros((n2, 128), F32)
    o2 = jnp.zeros((n2, 256), F32)
    for c in range(0, nk, chunk):
        sl = slice(c, c + chunk)
        on = cond[:, sl] > 0.5
        a = jnp.exp(s1[:, sl] - mhi)
        b = jnp.exp(s2[:, sl] - jnp.where(on, mlo, mhi))
        blo = jnp.where(on, b, 0.0)
        bhi = a + jnp.where(on, 0.0, b)
        for i in range(0, chunk, width):
            tlo = tlo + blo[:, i:i + width]
            thi = thi + bhi[:, i:i + width]
        o1 = o1 + nt(a.astype(BF16), vlo[:, sl])
        o2 = o2 + nt(b.astype(BF16), vsel[:, sl])
    llo = jnp.sum(tlo, -1, keepdims=True) + jnp.sum(e3, -1, keepdims=True)
    lhi = jnp.sum(thi, -1, keepdims=True)
    olo = unstack_heads((o2[:, :128] + o3) / llo)
    ohi = unstack_heads((o2[:, 128:] + o1) / lhi)
    o_ref[0] = jnp.concatenate([olo, ohi], 0).astype(BF16)
    lane = lax.broadcasted_iota(jnp.int32, (span, 128), 1)
    tlo = mlo + jnp.log(llo)
    thi = mhi + jnp.log(lhi)
    old = jnp.where(p == 0, 0.0, lse_ref[0])
    new = []
    for k, t in enumerate((tlo, thi)):
        part = old[k * span:(k + 1) * span]
        part = jnp.where(lane == 2 * p, t[:span], part)
        new.append(jnp.where(lane == 2 * p + 1, t[span:], part))
    lse_ref[0] = jnp.concatenate(new, 0)

def attend(qh, qr, hl, hs, dl, ds, cond, bl, bs):
    rows, pairs, _, nq = qh.shape
    nk = dl.shape[-1]
    span = nq // 2
    chunk = min(512, nk)
    full = lambda *s: pl.BlockSpec((1, *s), lambda b, p: (b, *([0] * len(s))))
    pairb = lambda *s: pl.BlockSpec((1, 1, *s), lambda b, p: (b, p, *([0] * len(s))))
    return pl.pallas_call(
        functools.partial(attend_kernel, span, chunk),
        grid=(rows, pairs),
        out_shape=[jax.ShapeDtypeStruct((rows, nq, pairs * 128), BF16), jax.ShapeDtypeStruct((rows, nq, 128), F32)],
        in_specs=[pairb(12, nq), full(384, nq), pairb(8, nk), pairb(8, nk), full(256, nk), full(256, nk),
                  pl.BlockSpec((1, nk), lambda b, p: (0, 0)), full(1, nk), full(1, nk)],
        out_specs=[pl.BlockSpec((1, nq, 128), lambda b, p: (b, 0, p)), full(nq, 128)],
        scratch_shapes=[pltpu.VMEM((nq, nk), F32), pltpu.VMEM((nq, nk), F32)],
        compiler_params=pltpu.CompilerParams(vmem_limit_bytes=56 << 20),
        name="attend",
    )(qh, qr, hl, hs, dl, ds, cond, bl, bs)

def attend_back_kernel(span, chunk, qh_ref, qr_ref, hl_ref, hs_ref, dl_ref, ds_ref, cond_ref, bl_ref, bs_ref, lse_ref, o_ref, g_ref,
                       dqh_ref, dqr_ref, dhl_ref, dhs_ref, ddl_ref, dds_ref):
    p = pl.program_id(1)
    @pl.when(p == 0)
    def _():
        dqr_ref[...] = jnp.zeros_like(dqr_ref)
        ddl_ref[...] = jnp.zeros_like(ddl_ref)
        dds_ref[...] = jnp.zeros_like(dds_ref)
    pair_back(span, chunk, p, qh_ref, qr_ref, Pair(hl_ref, 0, 0), Pair(hs_ref, 0, 0), dl_ref, ds_ref, cond_ref, bl_ref, bs_ref, lse_ref, o_ref[0], g_ref[0],
              dqh_ref, dqr_ref, Pair(dhl_ref, 0, 0), Pair(dhs_ref, 0, 0), ddl_ref, dds_ref)

class Pair:
    def __init__(self, ref, *at):
        self.ref, self.at = ref, at

    def all(self):
        return self.ref[self.at]

    def row(self, j, sl):
        return self.ref[(*self.at, slice(j, j + 1), sl)]

    def put(self, j, sl, value):
        self.ref[(*self.at, slice(j, j + 1), sl)] = value

def pair_back(span, chunk, p, qh_ref, qr_ref, hl, hs, dl_ref, ds_ref, cond_ref, bl_ref, bs_ref, lse_ref, o, g,
              dqh_ref, dqr_ref, dhl, dhs, ddl_ref, dds_ref):
    n2 = 2 * span
    nk = dl_ref.shape[-1]
    qh, qr = qh_ref[0, 0], qr_ref[0]
    qt = (queries(qh, qr).astype(BF16).astype(F32)) * 0.125
    q = qt.T.astype(BF16)
    qlo, qhi = stack_heads(q[:span]), stack_heads(q[span:])
    qboth = jnp.concatenate([qlo, qhi], 1)
    glo, ghi = stack_heads(g[:span]), stack_heads(g[span:])
    gboth = jnp.concatenate([glo, ghi], 1)
    gt = g.astype(F32).T
    first = lax.broadcasted_iota(jnp.int32, (128, span), 0) < 64
    def stack_lanes(part):
        return jnp.concatenate([jnp.where(first, part, 0.0), jnp.where(first, 0.0, part)], 1).astype(BF16)
    qtlo, qthi = stack_lanes(qt[:, :span]), stack_lanes(qt[:, span:])
    gtlo, gthi = stack_lanes(gt[:, :span]), stack_lanes(gt[:, span:])
    qtboth = jnp.concatenate([qtlo, qthi], 0)
    gtboth = jnp.concatenate([gtlo, gthi], 0)
    prod = g.astype(F32) * o.astype(F32)
    flane = lanes_below((n2, 128), 64)
    d0 = jnp.sum(jnp.where(flane, prod, 0.0), -1, keepdims=True)
    d1 = jnp.sum(jnp.where(flane, 0.0, prod), -1, keepdims=True)
    lane = lax.broadcasted_iota(jnp.int32, (n2, 128), 1)
    lse = lse_ref[0]
    l0 = jnp.sum(jnp.where(lane == 2 * p, lse, 0.0), -1, keepdims=True)
    l1 = jnp.sum(jnp.where(lane == 2 * p + 1, lse, 0.0), -1, keepdims=True)
    dello, delhi = jnp.concatenate([d0[:span], d1[:span]], 0), jnp.concatenate([d0[span:], d1[span:]], 0)
    lselo, lsehi = jnp.concatenate([l0[:span], l1[:span]], 0), jnp.concatenate([l0[span:], l1[span:]], 0)
    heads = (hl.all(), hs.all())
    dims = (dl_ref[0], ds_ref[0])
    cond = cond_ref[...]
    klo, ksel = pair_factors(heads, dims, cond, 0, 0)
    vlo, vsel = pair_factors(heads, dims, cond, 4, 128)
    tri = causal_bias(n2, span)

    def put(dkt, h, d_ref, hd, dd_ref, base, at, sl):
        for r in range(2):
            dim = d_ref[0, at + 64 * r:at + 64 * r + 64, sl].astype(F32)
            total = None
            for k in range(2):
                part = dkt[64 * k:64 * k + 64]
                j = base + 2 * r + k
                hd.put(j, sl, jnp.sum(part * dim, 0, keepdims=True) * 0.5)
                term = part * h.row(j, sl)
                total = term if total is None else total + term
            dd_ref[0, at + 64 * r:at + 64 * r + 64, sl] += total * 0.5

    s3 = nn(qlo, klo[:, :span]) + bl_ref[0][:, :span] + tri
    p3 = jnp.exp(s3 - lselo)
    dp3 = nn(glo, vlo[:, :span])
    ds3 = (p3 * (dp3 - dello)).astype(BF16)
    p3 = p3.astype(BF16)
    dq3 = nt(ds3, klo[:, :span])
    dk3 = nn(qtlo, ds3)
    dv3 = nn(gtlo, p3)
    dq1 = jnp.zeros((n2, 128), F32)
    dq2 = jnp.zeros((n2, 256), F32)
    for c in range(0, nk, chunk):
        sl = slice(c, c + chunk)
        pa = jnp.exp(nn(qhi, klo[:, sl]) + bl_ref[0][:, sl] - lsehi)
        dpa = nn(ghi, vlo[:, sl])
        dsa = (pa * (dpa - delhi)).astype(BF16)
        pa = pa.astype(BF16)
        dq1 = dq1 + nt(dsa, klo[:, sl])
        dk = nn(qthi, dsa)
        dv = nn(gthi, pa)
        if c == 0:
            dk = jnp.concatenate([dk[:, :span] + dk3, dk[:, span:]], 1)
            dv = jnp.concatenate([dv[:, :span] + dv3, dv[:, span:]], 1)
        put(dk, hl, dl_ref, dhl, ddl_ref, 0, 0, sl)
        put(dv, hl, dl_ref, dhl, ddl_ref, 4, 128, sl)
    for c in range(0, nk, chunk):
        sl = slice(c, c + chunk)
        on = cond[:, sl] > 0.5
        s = nn(qboth, ksel[:, sl]) + bs_ref[0][:, sl]
        if c == 0:
            s = jnp.concatenate([s[:, :span] + tri, s[:, span:]], 1)
        pb = jnp.exp(s - jnp.where(on, lselo, lsehi))
        dpb = nn(gboth, vsel[:, sl])
        dsb = (pb * (dpb - jnp.where(on, dello, delhi))).astype(BF16)
        pb = pb.astype(BF16)
        dq2 = dq2 + nt(dsb, ksel[:, sl])
        dk = nn(qtboth, dsb)
        dv = nn(gtboth, pb)
        dk = jnp.where(on, dk[:128], dk[128:])
        dv = jnp.where(on, dv[:128], dv[128:])
        put(dk, hs, ds_ref, dhs, dds_ref, 0, 0, sl)
        put(dv, hs, ds_ref, dhs, dds_ref, 4, 128, sl)
    dqlo = unstack_heads(dq2[:, :128] + dq3)
    dqhi = unstack_heads(dq2[:, 128:] + dq1)
    dqt = (jnp.concatenate([dqlo, dqhi], 0) * (0.125 / 6.0)).T
    for r in range(6):
        total = None
        for h in range(2):
            part = dqt[64 * h:64 * h + 64]
            j = 2 * r + h
            dqh_ref[0, 0, j:j + 1, :] = jnp.sum(part * qr[64 * r:64 * r + 64], 0, keepdims=True)
            term = part * qh[j:j + 1]
            total = term if total is None else total + term
        dqr_ref[0, 64 * r:64 * r + 64, :] += total

def attend_back(qh, qr, hl, hs, dl, ds, cond, bl, bs, lse, o, g):
    rows, pairs, _, nq = qh.shape
    nk = dl.shape[-1]
    span = nq // 2
    chunk = min(512, nk)
    full = lambda *s: pl.BlockSpec((1, *s), lambda b, p: (b, *([0] * len(s))))
    pairb = lambda *s: pl.BlockSpec((1, 1, *s), lambda b, p: (b, p, *([0] * len(s))))
    tok = pl.BlockSpec((1, nq, 128), lambda b, p: (b, 0, p))
    sd = jax.ShapeDtypeStruct
    return pl.pallas_call(
        functools.partial(attend_back_kernel, span, chunk),
        grid=(rows, pairs),
        out_shape=[sd((rows, pairs, 12, nq), F32), sd((rows, 384, nq), F32), sd((rows, pairs, 8, nk), F32), sd((rows, pairs, 8, nk), F32),
                   sd((rows, 256, nk), F32), sd((rows, 256, nk), F32)],
        in_specs=[pairb(12, nq), full(384, nq), pairb(8, nk), pairb(8, nk), full(256, nk), full(256, nk),
                  pl.BlockSpec((1, nk), lambda b, p: (0, 0)), full(1, nk), full(1, nk), full(nq, 128), tok, tok],
        out_specs=[pairb(12, nq), full(384, nq), pairb(8, nk), pairb(8, nk), full(256, nk), full(256, nk)],
        compiler_params=pltpu.CompilerParams(vmem_limit_bytes=56 << 20),
        name="attend_back",
    )(qh, qr, hl, hs, dl, ds, cond, bl, bs, lse, o, g)

class Rows:
    def __init__(self, me, pack, out, RX, RZ, xs, xr, zs, zr):
        self.me, self.pack, self.out, self.RX, self.RZ = me, pack, out, RX, RZ
        self.xs, self.xr, self.zs, self.zr = xs, xr, zs, zr

    def remote(self, src, dst, ss, rs, dev):
        return pltpu.make_async_remote_copy(src_ref=src, dst_ref=dst, send_sem=ss, recv_sem=rs, device_id=dev, device_id_type=MESH)

    def x_copy(self, b, zz):
        return self.remote(self.pack.at[b, 2 * zz + 1 - self.me.x], self.RX.at[b, zz], self.xs.at[b, zz], self.xr.at[b, zz], self.me.xp)

    def z_copy(self, b, zz):
        me = self.me
        return self.remote(self.mine(b, zz), self.RZ.at[b, Reduce.slot(me.z, zz)], self.zs.at[b, zz], self.zr.at[b, me.z], (2 * zz + me.x, me.batch))

    def z_recv(self, b, zz):
        me = self.me
        v = self.RZ.at[b, Reduce.slot(zz, me.z)]
        return self.remote(v, v, self.zs.at[b, zz], self.zr.at[b, zz], (2 * zz + me.x, me.batch))

    def mine(self, b, zz):
        return self.pack.at[b, 2 * zz + self.me.x]

    @staticmethod
    def add(dst, src):
        dst[...] = dst[...] + src[...]

    def begin(self, b):
        def body(i, c):
            self.x_copy(b, lax.rem(self.me.z + 1 + i, NZ)).start()
            return c
        lax.fori_loop(0, NZ, body, 0)

    def x(self, b):
        me = self.me
        def body(i, c):
            zz = lax.rem(me.z + 1 + i, NZ)
            self.x_copy(b, zz).wait_recv()
            self.add(self.mine(b, zz), self.RX.at[b, zz])
            pl.when(zz != me.z)(lambda: self.z_copy(b, zz).start())
            return c
        lax.fori_loop(0, NZ, body, 0)

    def own(self, b):
        me = self.me
        def body(i, c):
            zz = lax.rem(me.z + i, NZ)
            self.z_recv(b, zz).wait_recv()
            self.add(self.mine(b, me.z), self.RZ.at[b, Reduce.slot(zz, me.z)])
            return c
        lax.fori_loop(1, NZ, body, 0)
        self.out[b] = self.pack[b, me.seq]

    def end(self, b):
        me = self.me
        def sent(zz, c):
            self.x_copy(b, zz).wait_send()
            pl.when(zz != me.z)(lambda: self.z_copy(b, zz).wait_send())
            return c
        lax.fori_loop(0, NZ, sent, 0)

def lay_out(me, block, n, span, cond_ref, dl, ds, hl, hs):
    for i in range(n):
        j = lax.rem(me.seq + i, n)
        sl = slice(i * span, (i + 1) * span)
        on = cond_ref[:, sl] > 0.5
        low = block(j)[:256, :span].astype(F32)
        high = block(j)[:256, span:].astype(F32)
        dl[0, :, sl] = low.astype(BF16)
        ds[0, :, sl] = jnp.where(on, low, high).astype(BF16)
        low = block(j)[256:, :span].astype(F32)
        high = block(j)[256:, span:].astype(F32)
        hl[:, :, sl] = low.reshape(PAIRS, 8, span)
        hs[:, :, sl] = jnp.where(on, low, high).reshape(PAIRS, 8, span)

def pack_up(me, b, span, cond_ref, pack, ddl, dds, dhl, dhs):
    n = pack.shape[1]
    for i in range(n):
        j = lax.rem(me.seq + i, n)
        sl = slice(i * span, (i + 1) * span)
        on = cond_ref[:, sl] > 0.5
        for at, lo, se in ((0, ddl[0, :, sl], dds[0, :, sl]), (256, dhl[:, :, sl].reshape(64, span), dhs[:, :, sl].reshape(64, span))):
            rows = slice(at, at + lo.shape[0])
            pack[b, j, rows, :span] = (lo + jnp.where(on, se, 0.0)).astype(BF16)
            pack[b, j, rows, span:] = jnp.where(on, 0.0, se).astype(BF16)

FFC = 256

class Feed:
    def __init__(self, hbm, outs, grads, buf):
        self.tok, self.heads_hbm, self.cot, self.w_out, self.w_gate, self.w_up, self.w_down, self.gain = hbm
        self.output, self.d_resid, self.gain_grad = outs
        self.g_out, self.g_gate, self.g_up, self.g_down = grads
        (self.xb, self.hb, self.gb, self.n2, self.n2t, self.resid, self.acc, self.dlo, self.dhi, self.wa, self.wd, self.sg, self.su, self.sd, self.dg, self.du, self.hidt,
         self.lsem, self.wsem, self.ssem) = buf
        self.rows, self.nq, self.width = self.tok.shape
        self.count = self.rows * self.nq

    def load(self):
        out = []
        for i, (src, dst) in enumerate(((self.tok, self.xb), (self.heads_hbm, self.hb), (self.cot, self.gb))):
            for r in range(self.rows):
                out.append(pltpu.make_async_copy(src.at[r], dst.at[pl.ds(r * self.nq, self.nq)], self.lsem.at[i, r]))
        return out

    def out_part(self, j):
        return pltpu.make_async_copy(self.w_out.at[:, pl.ds(j * FFC, FFC)], self.wa.at[j], self.wsem.at[0, j])

    def weights(self, c):
        k = lax.rem(c, 2)
        at = pl.ds(pl.multiple_of(c * FFC, FFC), FFC)
        return (pltpu.make_async_copy(self.w_gate.at[:, at], self.wa.at[k], self.wsem.at[1, k]),
                pltpu.make_async_copy(self.w_up.at[:, at], self.wa.at[2 + k], self.wsem.at[1, 2 + k]),
                pltpu.make_async_copy(self.w_down.at[at], self.wd.at[k], self.wsem.at[2, k]))

    def stores(self, c):
        at = pl.ds(pl.multiple_of(c * FFC, FFC), FFC)
        return (pltpu.make_async_copy(self.sg, self.g_gate.at[:, :, at], self.ssem.at[0]),
                pltpu.make_async_copy(self.su, self.g_up.at[:, :, at], self.ssem.at[1]),
                pltpu.make_async_copy(self.sd, self.g_down.at[at], self.ssem.at[2]))

    def out_store(self, j):
        return pltpu.make_async_copy((self.sg, self.su)[j % 2], self.g_out.at[:, :, pl.ds(j * FFC, FFC)], self.ssem.at[j % 2])

    def before(self):
        parts = self.width // FFC
        loads = self.load() + [self.out_part(j) for j in range(parts)]
        for cp in loads:
            cp.start()
        for cp in loads:
            cp.wait()
        for j in range(parts):
            sl = slice(j * FFC, (j + 1) * FFC)
            self.resid[:, sl] = self.xb[:, sl].astype(F32) + nn(self.hb[...], self.wa[j])
        for cp in self.weights(0):
            cp.start()
        gain = self.gain[...]
        for r in range(0, self.count, 128):
            sl = slice(r, r + 128)
            v = self.resid[sl, :]
            self.acc[sl, :] = v
            n2 = v * lax.rsqrt(jnp.mean(v * v, -1, keepdims=True) + 1e-6) * gain
            self.n2[sl, :] = n2.astype(BF16)
            self.n2t[:, sl] = n2.T.astype(BF16)
        self.dlo[...] = jnp.zeros_like(self.dlo)
        self.dhi[...] = jnp.zeros_like(self.dhi)

    def block(self, c, total):
        k = lax.rem(c, 2)
        for cp in self.weights(c):
            cp.wait()
        @pl.when(c + 1 < total)
        def _():
            for cp in self.weights(c + 1):
                cp.start()
        half = self.count // 2
        for r, dn in ((0, self.dlo), (half, self.dhi)):
            sl = slice(r, r + half)
            gate = nn(self.n2[sl, :], self.wa[k])
            up = nn(self.n2[sl, :], self.wa[2 + k])
            dh = nt(self.gb[sl, :], self.wd[k])
            sigma = 1.0 / (1.0 + jnp.exp(-gate))
            silu = gate * sigma
            hid = (silu * up).astype(BF16)
            d_gate = (dh * up * sigma * (1.0 + gate * (1.0 - sigma))).astype(BF16)
            d_up = (dh * silu).astype(BF16)
            self.dg[sl, :] = d_gate
            self.du[sl, :] = d_up
            self.hidt[:, sl] = hid.astype(F32).T.astype(BF16)
            self.acc[sl, :] += nn(hid, self.wd[k])
            dn[0] += nt(d_gate, self.wa[k]) + nt(d_up, self.wa[2 + k])
        @pl.when(c >= 1)
        def _():
            for cp in self.stores(c - 1):
                cp.wait()
        self.sg[...] = nn(self.n2t[...], self.dg[...]).astype(BF16).reshape(self.sg.shape)
        self.su[...] = nn(self.n2t[...], self.du[...]).astype(BF16).reshape(self.su.shape)
        self.sd[...] = nn(self.hidt[...], self.gb[...]).astype(BF16)
        for cp in self.stores(c):
            cp.start()

    def settle(self, c):
        for cp in self.stores(c):
            cp.wait()

    def after(self, total):
        parts = self.width // FFC
        for j in range(parts):
            self.out_part(j).start()
        gain = self.gain[...]
        sums = jnp.zeros((8, self.width), F32)
        half = self.count // 2
        for r in range(0, self.count, 128):
            sl = slice(r, r + 128)
            dn = self.dlo[0, r:r + 128] if r < half else self.dhi[0, r - half:r - half + 128]
            v = self.resid[sl, :]
            scale = lax.rsqrt(jnp.mean(v * v, -1, keepdims=True) + 1e-6)
            unit = v * scale
            prod = dn * unit
            sums = sums + jnp.sum(prod.reshape(16, 8, self.width), 0)
            e2 = dn * gain
            d = self.gb[sl, :].astype(F32) + scale * (e2 - unit * jnp.mean(e2 * unit, -1, keepdims=True))
            self.resid[sl, :] = d
            self.gb[sl, :] = d.astype(BF16)
            self.xb[sl, :] = self.acc[sl, :].astype(BF16)
            self.n2t[:, sl] = self.hb[sl, :].astype(F32).T.astype(BF16)
        self.gain_grad[...] = jnp.sum(sums, 0, keepdims=True)
        for cp in self.results():
            cp.start()
        for j in range(parts):
            self.out_part(j).wait()
        for j in range(parts):
            if j >= 2:
                self.out_store(j - 2).wait()
            (self.sg, self.su)[j % 2][...] = nn(self.n2t[...], self.gb[:, j * FFC:(j + 1) * FFC]).astype(BF16).reshape(self.sg.shape)
            self.out_store(j).start()
        for r in range(0, self.count, 128):
            total = None
            for j in range(parts):
                part = nt(self.gb[r:r + 128, j * FFC:(j + 1) * FFC], self.wa[j])
                total = part if total is None else total + part
            self.n2[r:r + 128, :] = total.astype(BF16)
        for j in range(parts - 2, parts):
            self.out_store(j).wait()

    def results(self):
        out = []
        for r in range(self.rows):
            at = pl.ds(r * self.nq, self.nq)
            out.append(pltpu.make_async_copy(self.xb.at[at], self.output.at[r], self.lsem.at[0, r]))
            out.append(pltpu.make_async_copy(self.resid.at[at], self.d_resid.at[r], self.lsem.at[1, r]))
        return out

def back_kernel(span, chunk, units, plan, blocks, qh_ref, qr_ref, shared_ref, cond_ref, bl_ref, bs_ref, lse_ref, *refs):
    feed_in, refs = refs[:8], refs[8:]
    dqh_ref, dqr_ref, mine_ref, output, d_resid, gain_grad = refs[:6]
    sums, grads, refs = refs[6:10], refs[10:14], refs[14:]
    dl, ds, hl, hs, ddl, dds, dhl, dhs, pack, RX, RZ, xs, xr, zs, zr, bsem = refs[:16]
    fb, refs = refs[16:34], refs[34:]
    me = Place()
    b, p = pl.program_id(0), pl.program_id(1)
    step = b * PAIRS + p
    nq = 2 * span
    red = Reduce(me, units, grads, sums, refs)
    row = Rows(me, pack, mine_ref, RX, RZ, xs, xr, zs, zr)
    feed = Feed(feed_in, (output, d_resid, gain_grad), grads, (*fb[:7], ddl, dds, *fb[7:]))

    def act(items):
        for it in items:
            if it[0] == "row":
                getattr(row, it[1])(it[2])
            elif it[0] == "settle":
                feed.settle(it[1])
            elif it[0] == "results":
                for cp in feed.results():
                    cp.wait()
            else:
                red.run([it])

    brought = [pltpu.make_async_copy(shared_ref.at[:, r], pack.at[r], bsem.at[r]) for r in range(pack.shape[0])]

    @pl.when(step == 0)
    def _():
        greet(me)
        for cp in brought:
            cp.start()
        feed.before()
        def body(c, carry):
            feed.block(c, blocks)
            for k, items in plan["feed"].items():
                pl.when(c == k)(functools.partial(act, items))
            return carry
        lax.fori_loop(0, blocks, body, 0)
        feed.settle(blocks - 1)
        act(plan["mid"])
        feed.after(blocks)
        act(plan["first"])
        for cp in brought:
            cp.wait()

    @pl.when(p == 0)
    def _():
        lay_out(me, lambda j: pack.at[b, j], 2 * NZ, span, cond_ref, dl, ds, hl, hs)
        dqr_ref[...] = jnp.zeros_like(dqr_ref)
        ddl[...] = jnp.zeros_like(ddl)
        dds[...] = jnp.zeros_like(dds)

    rows_at = pl.ds(pl.multiple_of(b * nq, nq), nq)
    lanes_at = pl.ds(pl.multiple_of(p * 128, 128), 128)
    pair_back(span, chunk, p, qh_ref, qr_ref, Pair(hl, p), Pair(hs, p), dl, ds, cond_ref, bl_ref, bs_ref, lse_ref,
              feed.hb[rows_at, lanes_at], feed.n2[rows_at, lanes_at], dqh_ref, dqr_ref, Pair(dhl, p), Pair(dhs, p), ddl, dds)

    @pl.when(p == PAIRS - 1)
    def _():
        pack_up(me, b, span, cond_ref, pack, ddl, dds, dhl, dhs)
        row.begin(b)

    for s, items in plan["steps"].items():
        pl.when(step == s)(functools.partial(act, items))

def backward(qh, qr, shared, cond, bl, bs, lse, tokens, heads_out, cotangent, w_out, w_gate, w_up, w_down, gain_two, units, plan, cid):
    rows, pairs, _, nq = qh.shape
    n = shared.shape[0]
    span = nq // 2
    nk = n * span
    width, ff = w_gate.shape
    count = rows * nq
    full = lambda *s: pl.BlockSpec((1, *s), lambda b, p: (b, *([0] * len(s))))
    pairb = lambda *s: pl.BlockSpec((1, 1, *s), lambda b, p: (b, p, *([0] * len(s))))
    sd = jax.ShapeDtypeStruct
    DMA = pltpu.SemaphoreType.DMA
    V = pltpu.VMEM
    whole = pl.BlockSpec(memory_space=pltpu.VMEM)
    far = pl.BlockSpec(memory_space=pl.ANY)
    part = shared.shape[2:]
    scratch = [V((1, 256, nk), BF16)] * 2 + [V((PAIRS, 8, nk), F32)] * 2 + [V((1, 256, nk), F32)] * 2 + [V((PAIRS, 8, nk), F32)] * 2
    scratch += [V((rows, n, *part), BF16), V((rows, NZ, *part), BF16), V((rows, NZ - 1, *part), BF16)] + [DMA((rows, NZ))] * 4 + [DMA((rows,))]
    scratch += [V((count, width), BF16)] * 4 + [V((width, count), BF16)] + [V((count, width), F32)] * 2
    scratch += [V((4, width, FFC), BF16), V((2, FFC, width), BF16)] + [V((n, width // n, FFC), BF16)] * 2 + [V((FFC, width), BF16)] + [V((count, FFC), BF16)] * 2 + [V((FFC, count), BF16)]
    scratch += [DMA((3, rows)), DMA((3, 4)), DMA((3,))]
    shard = (n, width // n)
    sums = [sd((width // n, width), BF16), sd((width // n, ff), BF16), sd((width // n, ff), BF16), sd((ff // n, width), BF16)]
    grads = [sd((*shard, width), BF16), sd((*shard, ff), BF16), sd((*shard, ff), BF16), sd((ff, width), BF16)]
    return pl.pallas_call(
        functools.partial(back_kernel, span, min(512, nk), units, plan, ff // FFC),
        grid=(rows, pairs),
        out_shape=[sd((rows, pairs, 12, nq), F32), sd((rows, 384, nq), F32), sd((rows, *part), BF16), sd((rows, nq, width), BF16),
                   sd((rows, nq, width), F32), sd((1, width), F32)] + sums + grads,
        in_specs=[pairb(12, nq), full(384, nq), far, pl.BlockSpec((1, nk), lambda b, p: (0, 0)), full(1, nk), full(1, nk), full(nq, 128)] + [far] * 7 + [whole],
        out_specs=[pairb(12, nq), full(384, nq), whole, far, far, whole] + [far] * 8,
        scratch_shapes=scratch + reduce_scratch(units),
        compiler_params=pltpu.CompilerParams(collective_id=cid, has_side_effects=True, vmem_limit_bytes=60 << 20),
        name="backward",
    )(qh, qr, shared, cond, bl, bs, lse, tokens, heads_out, cotangent, w_out, w_gate, w_up, w_down, gain_two)[:10]

class Gather:
    def __init__(self, me, units, ins, outs, sems):
        self.me, self.units, self.ins, self.outs = me, units, ins, outs
        self.zs, self.zr, self.xs, self.xr, self.ys, self.yr, self.cs, self.cr, self.ls = sems

    def remote(self, src, dst, ss, rs, dev):
        return pltpu.make_async_remote_copy(src_ref=src, dst_ref=dst, send_sem=ss, recv_sem=rs, device_id=dev, device_id_type=MESH)

    def view(self, k, shard, y, c):
        u = self.units[k]
        return self.part(u, self.outs[u.arr].at[shard], y, c)

    @staticmethod
    def part(u, ref, y, c):
        return rect(u, ref, 2 * c + y, 4) if u.flow == "P" else rect(u, ref, c, 2)

    def first(self, k, ss, rs, dev):
        u, me = self.units[k], self.me
        return self.remote(self.part(u, self.ins[u.arr], me.y, me.c), self.view(k, me.seq, me.y, me.c), ss, rs, dev)

    def onward(self, k, shard, y, ss, rs, dev):
        v = self.view(k, shard, y, self.me.c)
        return self.remote(v, v, ss, rs, dev)

    def zsend(self, k, zz):
        return self.first(k, self.zs.at[k, zz], self.zr.at[k, self.me.z], (2 * zz + self.me.x, self.me.batch))

    def zrecv(self, k, zz):
        me = self.me
        return self.onward(k, 2 * zz + me.x, me.y, self.zs.at[k, zz], self.zr.at[k, zz], (2 * zz + me.x, me.batch))

    def xown(self, k):
        return self.first(k, self.xs.at[k, self.me.z], self.xr.at[k, self.me.z], self.me.xp)

    def xsend(self, k, zz):
        return self.onward(k, 2 * zz + self.me.x, self.me.y, self.xs.at[k, zz], self.xr.at[k, zz], self.me.xp)

    def xrecv(self, k, zz):
        return self.onward(k, 2 * zz + 1 - self.me.x, self.me.y, self.xs.at[k, zz], self.xr.at[k, zz], self.me.xp)

    def ycopy(self, k, shard, mine):
        return self.onward(k, shard, self.me.y if mine else 1 - self.me.y, self.ys.at[k, shard], self.yr.at[k, shard], self.me.yp)

    def ccopy(self, k, w, shard):
        return self.onward(k, shard, self.me.y if w == 0 else 1 - self.me.y, self.cs.at[k, w, shard], self.cr.at[k, w, shard], self.me.cp)

    def crecv(self, k, w, shard):
        v = self.view(k, shard, self.me.y if w == 0 else 1 - self.me.y, 1 - self.me.c)
        return self.remote(v, v, self.cs.at[k, w, shard], self.cr.at[k, w, shard], self.me.cp)

    def local(self, a):
        return pltpu.make_async_copy(self.ins[a], self.outs[a].at[self.me.seq], self.ls.at[a])

    def other(self, i):
        return lax.rem(self.me.z + i, NZ)

    def begin(self, k, i):
        self.zsend(k, self.other(i)).start()
        pl.when(i == 1)(lambda: self.xown(k).start())

    def spread(self, k, shard):
        if self.units[k].flow == "P":
            self.ycopy(k, shard, True).start()
        self.ccopy(k, 0, shard).start()

    def z(self, k, i):
        zz = self.other(i)
        self.zrecv(k, zz).wait_recv()
        self.xsend(k, zz).start()
        self.spread(k, 2 * zz + self.me.x)

    def x(self, k, i):
        zz = self.other(i)
        self.xrecv(k, zz).wait_recv()
        self.spread(k, 2 * zz + 1 - self.me.x)

    def far(self, i):
        return 2 * self.other(i) + jnp.where(i < NZ, self.me.x, 1 - self.me.x)

    def y(self, k, i):
        shard = self.far(i)
        self.ycopy(k, shard, False).wait_recv()
        self.ccopy(k, 1, shard).start()

    def got(self, k, i):
        for w in range(2 if self.units[k].flow == "P" else 1):
            self.crecv(k, w, self.far(i)).wait_recv()

    def sent(self, k, i):
        me = self.me
        pl.when(i < NZ)(lambda: self.zsend(k, self.other(i)).wait_send())
        pl.when(i < NZ)(lambda: self.xsend(k, self.other(i)).wait_send())
        pl.when(i == NZ)(lambda: self.xown(k).wait_send())
        shard = self.far(i)
        self.ccopy(k, 0, shard).wait_send()
        if self.units[k].flow == "P":
            self.ycopy(k, shard, True).wait_send()
            self.ccopy(k, 1, shard).wait_send()

    def run(self, plan):
        for step, k, first, n in plan:
            fn = getattr(self, step)
            def body(i, c):
                fn(k, i)
                return c
            lax.fori_loop(first, first + n, body, 0)

class RowsGather:
    def __init__(self, me, shared, zs, zr, xs, xr):
        self.me, self.shared, self.zs, self.zr, self.xs, self.xr = me, shared, zs, zr, xs, xr

    def copy(self, b, shard, ss, rs, dev):
        v = self.shared.at[shard, b]
        return pltpu.make_async_remote_copy(src_ref=v, dst_ref=v, send_sem=ss, recv_sem=rs, device_id=dev, device_id_type=MESH)

    def zsend(self, b, zz):
        me = self.me
        return self.copy(b, me.seq, self.zs.at[b, zz], self.zr.at[b, me.z], (2 * zz + me.x, me.batch))

    def zrecv(self, b, zz):
        me = self.me
        return self.copy(b, 2 * zz + me.x, self.zs.at[b, zz], self.zr.at[b, zz], (2 * zz + me.x, me.batch))

    def xsend(self, b, zz):
        return self.copy(b, 2 * zz + self.me.x, self.xs.at[b, zz], self.xr.at[b, zz], self.me.xp)

    def xrecv(self, b, zz):
        return self.copy(b, 2 * zz + 1 - self.me.x, self.xs.at[b, zz], self.xr.at[b, zz], self.me.xp)

    def loop(self, first, fn):
        def body(i, c):
            fn(lax.rem(self.me.z + i, NZ))
            return c
        lax.fori_loop(first, NZ, body, 0)

    def begin(self, b):
        self.loop(1, lambda zz: self.zsend(b, zz).start())
        self.xsend(b, self.me.z).start()

    def z(self, b):
        def one(zz):
            self.zrecv(b, zz).wait_recv()
            self.xsend(b, zz).start()
        self.loop(1, one)

    def x(self, b):
        self.loop(0, lambda zz: self.xrecv(b, zz).wait_recv())

    def end(self, b):
        self.loop(1, lambda zz: self.zsend(b, zz).wait_send())
        self.loop(0, lambda zz: self.xsend(b, zz).wait_send())

def turn_rows(u, cosine, sine):
    out = []
    for r in range(0, u.shape[0], 64):
        a, b = u[r:r + 32], u[r + 32:r + 64]
        out += [a * cosine - b * sine, b * cosine + a * sine]
    return jnp.concatenate(out, 0)

def project(me, span, tok_ref, small_ref, cos_ref, sin_ref, normed_ref, qh_ref, qr_ref, shared_ref, b):
    nq = 2 * span
    d = tok_ref.shape[-1]
    gains = small_ref[:, :, 768:896].reshape(d, 128).astype(F32).T
    x = tok_ref[b].astype(F32)
    unit = x * lax.rsqrt(jnp.mean(x * x, -1, keepdims=True) + 1e-6)
    normed = (unit * gains[32:33]).astype(BF16)
    normed_ref[b] = normed
    w = small_ref[...].reshape(d, 896)
    f = nn(normed, w).T
    qh_ref[b] = f[:96].reshape(PAIRS, 12, nq)
    cosine, sine = cos_ref[...], sin_ref[...]
    qr_ref[b] = turn_rows(f[96:480], cosine, sine)
    own = jnp.concatenate([turn_rows(f[480:608], cosine, sine), f[608:800]], 0)
    shared_ref[me.seq, b] = own.astype(BF16)

def forward_kernel(span, chunk, units, narr, plan, tok_ref, cos_ref, sin_ref, cond_ref, bl_ref, bs_ref, *refs):
    ins = refs[:narr]
    normed_ref, qh_ref, qr_ref, shared_out, o_ref, lse_ref = refs[narr:narr + 6]
    outs = refs[narr + 6:2 * narr + 6]
    shared_ref, small, saved, dl, ds, hl, hs, s1, s2, rzs, rzr, rxs, rxr = refs[2 * narr + 6:2 * narr + 19]
    small_out, outs = outs[0], (small, *outs[1:])
    me = Place()
    b, p = pl.program_id(0), pl.program_id(1)
    step = b * PAIRS + p
    gat = Gather(me, units, ins, outs, refs[2 * narr + 19:])
    saves = (pltpu.make_async_copy(small, small_out, saved.at[0]), pltpu.make_async_copy(shared_ref, shared_out, saved.at[1]))
    row = RowsGather(me, shared_ref, rzs, rzr, rxs, rxr)

    def act(items):
        for it in items:
            if it[0] == "row":
                getattr(row, it[1])(it[2])
            elif it[0] == "project":
                for r in range(tok_ref.shape[0]):
                    project(me, span, tok_ref, small, cos_ref, sin_ref, normed_ref, qh_ref, qr_ref, shared_ref, r)
            elif it[0] == "local":
                for a in range(narr):
                    gat.local(a).start()
                gat.local(0).wait()
            elif it[0] == "locals":
                for a in range(1, narr):
                    gat.local(a).wait()
                for save in saves:
                    save.start()
                for save in saves:
                    save.wait()
            else:
                gat.run([it])

    @pl.when(step == 0)
    def _():
        greet(me)
        act(plan["first"])

    @pl.when(p == 0)
    def _():
        lay_out(me, lambda j: shared_ref.at[j, b], 2 * NZ, span, cond_ref, dl, ds, hl, hs)

    pair_forward(span, chunk, p, qh_ref[b, p], qr_ref[b], hl[p], hs[p], dl, ds, cond_ref, bl_ref, bs_ref, o_ref, lse_ref, s1, s2)

    for s, items in plan["steps"].items():
        pl.when(step == s)(functools.partial(act, items))

def forward(tokens, cosine, sine, cond, bl, bs, weights, units, plan, cid):
    rows, nq, width = tokens.shape
    span = nq // 2
    n = 2 * NZ
    nk = n * span
    narr, nu = len(weights), len(units)
    chunk = min(512, nk)
    whole = pl.BlockSpec(memory_space=pltpu.VMEM)
    far = pl.BlockSpec(memory_space=pl.ANY)
    full = lambda *s: pl.BlockSpec((1, *s), lambda b, p: (b, *([0] * len(s))))
    sd = jax.ShapeDtypeStruct
    DMA = pltpu.SemaphoreType.DMA
    V = pltpu.VMEM
    scratch = [V((n, rows, 320, nq), BF16), V((n, *weights[0].shape), BF16), DMA((2,))] + [V((1, 256, nk), BF16)] * 2 + [V((PAIRS, 8, nk), F32)] * 2 + [V((nq, nk), F32)] * 2 + [DMA((rows, NZ))] * 4
    scratch += [DMA((nu, NZ))] * 4 + [DMA((nu, n))] * 2 + [DMA((nu, 2, n))] * 2 + [DMA((narr,))]
    return pl.pallas_call(
        functools.partial(forward_kernel, span, chunk, units, narr, plan),
        grid=(rows, PAIRS),
        out_shape=[sd((rows, nq, width), BF16), sd((rows, PAIRS, 12, nq), F32), sd((rows, 384, nq), F32), sd((n, rows, 320, nq), BF16),
                   sd((rows, nq, width), BF16), sd((rows, nq, 128), F32)] + [sd((n, *a.shape), a.dtype) for a in weights],
        in_specs=[whole, whole, whole, pl.BlockSpec((1, nk), lambda b, p: (0, 0)), full(1, nk), full(1, nk)] + [far] * narr,
        out_specs=[whole, whole, whole, far, pl.BlockSpec((1, nq, 128), lambda b, p: (b, 0, p)), full(nq, 128)] + [far] * narr,
        scratch_shapes=scratch,
        compiler_params=pltpu.CompilerParams(collective_id=cid, has_side_effects=True, vmem_limit_bytes=56 << 20),
        name="forward",
    )(tokens, cosine, sine, cond, bl, bs, *weights)

def products_kernel(dqh_ref, dqr_ref, mine_ref, cos_ref, sin_ref, normed_ref, small_ref, tok_ref, res_ref, gain_two_ref, input_ref, out_ref, acc, sums):
    b = pl.program_id(0)
    d = tok_ref.shape[-1]
    nq = tok_ref.shape[1]
    @pl.when(b == 0)
    def _():
        acc[...] = jnp.zeros_like(acc)
        sums[...] = jnp.zeros_like(sums)
    cosine, sine = cos_ref[...], -sin_ref[...]
    mine = mine_ref[0].astype(F32)
    turned = jnp.concatenate([dqh_ref[0].reshape(96, nq), turn_rows(dqr_ref[0], cosine, sine), turn_rows(mine[:128], cosine, sine), mine[128:],
                              jnp.zeros((96, nq), F32)], 0)
    acc[...] += nn(turned.astype(BF16), normed_ref[0])
    w = small_ref[...].reshape(d, 896)
    gain = small_ref[:, :, 768:896].reshape(d, 128).astype(F32).T[32:33]
    back = nt(turned.T.astype(BF16), w)
    for r in range(0, nq, 128):
        sl = slice(r, r + 128)
        x = tok_ref[0, sl, :].astype(F32)
        scale = lax.rsqrt(jnp.mean(x * x, -1, keepdims=True) + 1e-6)
        unit = x * scale
        dn = back[sl]
        sums[...] += jnp.sum((dn * unit).reshape(16, 8, d), 0)
        e1 = dn * gain
        input_ref[0, sl, :] = res_ref[0, sl, :] + scale * (e1 - unit * jnp.mean(e1 * unit, -1, keepdims=True))
    @pl.when(b == pl.num_programs(0) - 1)
    def _():
        total = jnp.sum(sums[...], 0, keepdims=True)
        for s in range(out_ref.shape[0]):
            sl = slice(s * 128, s * 128 + 128)
            out_ref[s, :800, :] = acc[:800, sl].astype(BF16)
            out_ref[s, 800:, :] = jnp.concatenate([total[:, sl], gain_two_ref[:, sl], jnp.zeros((94, 128), F32)], 0).astype(BF16)

def products(dqh, dqr, mine, cosine, sine, normed, small, tokens, d_resid, gain_two):
    rows, nq, d = tokens.shape
    n = small.shape[0]
    row = lambda a: pl.BlockSpec((1, *a.shape[1:]), lambda b: (b, *([0] * (a.ndim - 1))))
    one = lambda a: pl.BlockSpec(a.shape, lambda b: (0,) * a.ndim)
    sd = jax.ShapeDtypeStruct
    return pl.pallas_call(
        products_kernel,
        grid=(rows,),
        out_shape=[sd(tokens.shape, F32), sd((n, 896, d // n), BF16)],
        in_specs=[row(dqh), row(dqr), row(mine), one(cosine), one(sine), row(normed), one(small), row(tokens), row(d_resid), one(gain_two)],
        out_specs=[row(tokens), pl.BlockSpec((n, 896, d // n), lambda b: (0, 0, 0))],
        scratch_shapes=[pltpu.VMEM((896, d), F32), pltpu.VMEM((8, d), F32)],
        compiler_params=pltpu.CompilerParams(vmem_limit_bytes=50 << 20),
        name="products",
    )(dqh, dqr, mine, cosine, sine, normed, small, tokens, d_resid, gain_two)

def results_kernel(small_ref, out_ref, gate_ref, up_ref, down_ref, qh_ref, qd_ref, kh_ref, kd_ref, vh_ref, vd_ref, g1_ref, g2_ref, o_ref, g_ref, u_ref, d_ref):
    for src, dst in ((out_ref, o_ref), (gate_ref, g_ref), (up_ref, u_ref), (down_ref, d_ref)):
        dst[...] = src[...].astype(F32)
    @pl.when(pl.program_id(0) == 0)
    def _():
        flat = small_ref[...].astype(F32)
        g1_ref[...] = flat[800:801]
        g2_ref[...] = flat[801:802]
        across = flat.T.astype(BF16)
        def pick(lo, hi, n, source):
            i = lax.broadcasted_iota(jnp.int32, (hi - lo, n), 0)
            j = lax.broadcasted_iota(jnp.int32, (hi - lo, n), 1)
            return nn(across[:, lo:hi], jnp.where(i == source(j), 1.0, 0.0).astype(BF16))
        pair = lambda j: (j & 15) >> 1
        rank = lambda j: j >> 4
        qh_ref[...] = pick(0, 128, 96, lambda j: pair(j) * 12 + rank(j) * 2 + (j & 1))
        qd_ref[...] = pick(0, 512, 384, lambda j: j + 96)
        kd_ref[...] = pick(384, 640, 128, lambda j: j + 96)
        vd_ref[...] = pick(512, 768, 128, lambda j: j + 96)
        kh_ref[...] = pick(640, 896, 32, lambda j: pair(j) * 8 + rank(j) * 2 + (j & 1) + 96)
        vh_ref[...] = pick(640, 896, 32, lambda j: pair(j) * 8 + rank(j) * 2 + (j & 1) + 100)

def results(small, out, gate, up, down):
    steps = 2
    n = small.shape[1]
    part = lambda a: pl.BlockSpec((a.shape[0] // steps, a.shape[1]), lambda i: (i, 0))
    one = lambda *s: pl.BlockSpec(s, lambda i: (0, 0))
    sd = lambda *s: jax.ShapeDtypeStruct(s, F32)
    shapes = [(n, 96), (n, 384), (n, 32), (n, 128), (n, 32), (n, 128), (1, n), (1, n)]
    big = (out, gate, up, down)
    return pl.pallas_call(
        results_kernel,
        grid=(steps,),
        out_shape=[sd(*s) for s in shapes] + [sd(*a.shape) for a in big],
        in_specs=[one(*small.shape)] + [part(a) for a in big],
        out_specs=[one(*s) for s in shapes] + [part(a) for a in big],
        compiler_params=pltpu.CompilerParams(vmem_limit_bytes=40 << 20),
        name="results",
    )(small, *big)

HEADS, HDIM, QRANK, KVRANK = 16, 64, 6, 2
PAIRS = HEADS // 2
EPSILON = 1e-06


def rms_forward(values, gain):
    scale = lax.rsqrt(jnp.mean(values * values, -1, keepdims=True) + EPSILON)
    unit = values * scale
    return (unit * gain, unit, scale)


def rms_backward(grad_out, unit, scale, gain):
    scaled = grad_out * gain
    grad_in = scale * (scaled - unit * jnp.mean(scaled * unit, -1, keepdims=True))
    return (grad_in, jnp.sum(grad_out * unit, 0))


def rotation(positions):
    half = HDIM // 2
    index = jnp.arange(half).astype(F32)
    inverse = jnp.exp(index * (-math.log(10000.0) / half))
    angles = inverse[:, None] * positions.astype(F32)[None, :]
    return (jnp.cos(angles), jnp.sin(angles))


def rotate(u, cosine, sine):
    rows, depth, slots = u.shape
    v = u.reshape(rows, depth // HDIM, HDIM, slots)
    a, b = v[:, :, :HDIM // 2], v[:, :, HDIM // 2:]
    return jnp.concatenate([a * cosine - b * sine, b * cosine + a * sine], 2).reshape(u.shape)


def dot(a, b, ca, cb):
    return lax.dot_general(a, b, ((ca, cb), ((), ())), preferred_element_type=F32)


def pair_columns(a, ranks):
    return a.reshape(-1, ranks, PAIRS, 2).transpose(0, 2, 1, 3).reshape(a.shape)


def head_columns(a, ranks):
    return a.reshape(-1, PAIRS, ranks, 2).transpose(0, 2, 1, 3).reshape(a.shape)


GATHER_UNITS = [
    Unit(0, (0, 128), (0, 896), "P", 0), Unit(1, (0, 128), (0, 1024), "P", 0),
    Unit(2, (0, 128), (0, 1408), "P", 0), Unit(2, (0, 128), (1408, 1408), "P", 0),
    Unit(3, (0, 128), (0, 1408), "R", 0), Unit(3, (0, 128), (1408, 1408), "P", 0),
    Unit(4, (0, 176), (0, 1024), "P", 1), Unit(4, (176, 176), (0, 1024), "P", 1)]
GATHER_PLAN = {
    "first": [("local",), ("begin", 0, 1, 3), ("begin", 1, 1, 3), ("z", 0, 1, 3), ("x", 0, 0, 4), ("begin", 3, 1, 3), ("y", 0, 1, 7), ("begin", 7, 1, 3), ("begin", 2, 1, 3), ("z", 1, 1, 3), ("got", 0, 1, 7), ("x", 1, 0, 4), ("begin", 6, 1, 3), ("z", 3, 1, 3), ("project",), ("z", 2, 1, 3), ("x", 3, 0, 4), ("row", "begin", 0), ("row", "begin", 1), ("x", 2, 0, 4), ("z", 7, 1, 3), ("row", "z", 0), ("z", 6, 1, 3), ("row", "x", 0), ("y", 3, 4, 4), ("y", 2, 1, 3), ("begin", 5, 1, 3), ("begin", 4, 1, 3), ("y", 7, 1, 3)],
    "steps": {
        2: [("x", 6, 0, 4), ("y", 1, 1, 3), ("y", 3, 1, 3), ("row", "z", 1)],
        5: [("z", 5, 1, 3), ("y", 1, 4, 4)],
        6: [("x", 7, 0, 4)],
        7: [("y", 2, 4, 4), ("row", "x", 1)],
        10: [("z", 4, 1, 3), ("x", 5, 0, 4)],
        12: [("y", 7, 4, 4), ("y", 6, 1, 3)],
        13: [("y", 6, 4, 4), ("y", 5, 1, 3)],
        14: [("x", 4, 0, 4)],
        15: [("y", 5, 4, 4), ("got", 1, 1, 7), ("got", 2, 1, 7), ("got", 3, 1, 7), ("got", 4, 1, 7), ("got", 5, 1, 7), ("got", 6, 1, 7), ("got", 7, 1, 7), ("locals",), ("sent", 0, 1, 7), ("sent", 1, 1, 7), ("sent", 2, 1, 7), ("sent", 3, 1, 7), ("sent", 4, 1, 7), ("sent", 5, 1, 7), ("sent", 6, 1, 7), ("sent", 7, 1, 7), ("row", "end", 0), ("row", "end", 1)],
    },
}
REDUCE_UNITS = [
    Unit(1, (0, 128), (0, 1024), "P", 0), Unit(2, (0, 128), (0, 1024), "R", 0),
    Unit(1, (0, 128), (1024, 1024), "P", 0), Unit(2, (0, 128), (1024, 1024), "R", 0),
    Unit(1, (0, 128), (2048, 768), "P", 0), Unit(2, (0, 128), (2048, 768), "P", 0),
    Unit(3, (0, 176), (0, 1024), "P", 1), Unit(3, (176, 176), (0, 1024), "P", 1), Unit(0, (0, 128), (0, 1024), "P", 0)]
REDUCE_PLAN = {
    "feed": {
        4: [("begin", 0, 0, 8), ("begin", 1, 0, 8)],
        5: [("core", 0, 0, 4)],
        6: [("core", 1, 0, 4), ("core", 0, 4, 4)],
        7: [("y", 0, 0, 4)],
        8: [("begin", 2, 0, 8), ("begin", 3, 0, 8)],
        9: [("core", 2, 0, 4), ("y", 0, 4, 4), ("core", 1, 4, 4)],
    },
    "mid": [("begin", 5, 0, 8), ("begin", 7, 0, 8), ("x", 1, 0, 4), ("core", 2, 4, 4), ("core", 3, 0, 4), ("core", 5, 0, 4)],
    "first": [("begin", 4, 0, 8), ("core", 5, 4, 4), ("begin", 8, 0, 8), ("y", 2, 0, 4)],
    "steps": {
        0: [("y", 2, 4, 4), ("core", 4, 4, 4), ("core", 3, 4, 4), ("core", 7, 0, 4), ("x", 3, 0, 4), ("y", 5, 0, 4), ("core", 4, 0, 4)],
        2: [("core", 7, 4, 4), ("y", 5, 4, 4), ("x", 5, 0, 4)],
        4: [("y", 7, 0, 4), ("x", 0, 0, 4)],
        5: [("x", 2, 0, 4)],
        6: [("y", 4, 4, 4), ("y", 4, 0, 4), ("core", 8, 4, 4)],
        7: [("begin", 6, 0, 8), ("y", 7, 4, 4), ("x", 4, 0, 4), ("x", 7, 0, 4), ("core", 8, 0, 4)],
        8: [("core", 6, 0, 4)],
        10: [("y", 8, 0, 4), ("core", 6, 4, 4), ("row", "x", 0)],
        11: [("own", 5, 0, 1), ("own", 2, 0, 1), ("own", 7, 0, 1), ("y", 8, 4, 4), ("own", 4, 0, 1), ("y", 6, 0, 4)],
        12: [("x", 8, 0, 4)],
        13: [("y", 6, 4, 4)],
        14: [("last", 2, 0, 1), ("x", 6, 0, 4), ("last", 7, 0, 1)],
        15: [("own", 8, 0, 1), ("own", 1, 0, 1), ("row", "own", 0), ("own", 3, 0, 1), ("own", 0, 0, 1), ("row", "x", 1), ("last", 1, 0, 1), ("own", 6, 0, 1), ("last", 8, 0, 1), ("last", 0, 0, 1), ("last", 6, 0, 1), ("last", 4, 0, 1), ("last", 5, 0, 1), ("last", 3, 0, 1), ("row", "own", 1), ("end", 0, 0, 1), ("end", 1, 0, 1), ("end", 2, 0, 1), ("end", 3, 0, 1), ("end", 4, 0, 1), ("end", 5, 0, 1), ("end", 6, 0, 1), ("end", 7, 0, 1), ("end", 8, 0, 1), ("results",), ("row", "end", 0), ("row", "end", 1)],
    },
}
SMALL_UNITS = [Unit(0, (0, 384), (0, 128), "R", 0), Unit(0, (384, 512), (0, 128), "P", 0)]
SMALL_PLAN = [("begin", 0, 0, 8), ("begin", 1, 0, 8), ("core", 1, 0, 8), ("core", 0, 0, 8), ("x", 0, 0, 4), ("y", 1, 0, 8), ("own", 0, 0, 1), ("x", 1, 0, 4),
              ("last", 0, 0, 1), ("own", 1, 0, 1), ("last", 1, 0, 1), ("end", 0, 0, 1), ("end", 1, 0, 1)]


def reduce_far(arrays):
    out = []
    for a in arrays:
        own = lax.psum_scatter(a.astype(F32), "seq", scatter_dimension=0, tiled=True)[0]
        out.append(lax.psum(own.astype(BF16), "batch"))
    return out


def per_device(near, tokens, cotangent, lengths, span_order, attn_gain, query_heads, query_dims, key_heads, key_dims,
               value_heads, value_dims, out_proj, ffn_gain, gate_proj, up_proj, down_proj):
    rows, slots, width = tokens.shape
    span = slots // 2
    count = rows * slots
    nseq = span_order.shape[0]
    nk = nseq * span
    me = lax.axis_index("seq")
    key_value_heads = pair_columns(jnp.concatenate([key_heads, value_heads], 1), 4)
    small = jnp.concatenate([pair_columns(query_heads, QRANK), query_dims, key_dims, value_dims, key_value_heads, attn_gain[:, None], ffn_gain[:, None]], 1)
    small = jnp.pad(small, ((0, 0), (0, 896 - small.shape[1])))
    offsets = jnp.arange(span, dtype=jnp.int32)
    spans = jnp.concatenate([span_order, span_order], 0)
    spans = lax.dynamic_slice_in_dim(spans, me, nseq, 0)
    local_pos = (spans[0][:, None] * span + offsets[None, :]).reshape(-1)
    cosine, sine = rotation(local_pos)
    chosen = spans[:, 0] < spans[0, 0]
    low_pos = (spans[:, 0][:, None] * span + offsets[None, :]).reshape(1, nk)
    sel_pos = (jnp.where(chosen, spans[:, 0], spans[:, 1])[:, None] * span + offsets[None, :]).reshape(1, nk)
    cond = jnp.repeat(chosen.astype(F32), span).reshape(1, nk)
    low_bias = jnp.where(low_pos < lengths[:, None], 0.0, NEG)[:, None, :]
    sel_bias = jnp.where(sel_pos < lengths[:, None], 0.0, NEG)[:, None, :]

    masks = (cond, low_bias, sel_bias)
    flat = tokens.reshape(count, width).astype(F32)
    weights = [small, out_proj, gate_proj, up_proj, down_proj]
    if near:
        by_row, qh, qr, shared, heads_out, lse, *parts = forward(tokens, cosine, sine, *masks, weights, GATHER_UNITS, GATHER_PLAN, 0)
    else:
        parts = [lax.all_gather(a, "seq", axis=0) for a in weights]
    small, w_out, w_gate, w_up, w_down = [p.reshape(-1, p.shape[-1]) for p in parts]
    w_qkv = small[:, :800]
    gain_one = small[:, 800].astype(F32)
    gain_two = small[:, 801].astype(F32)
    normed_full, unit_one, scale_one = rms_forward(flat, gain_one)
    if not near:
        by_row = normed_full.astype(BF16).reshape(rows, slots, width)
        factors = jnp.stack([dot(w_qkv, by_row[b], (0,), (1,)) for b in range(rows)])
        qh = factors[:, :96].reshape(rows, PAIRS, 12, slots)
        qr = rotate(factors[:, 96:480], cosine, sine)
        own = jnp.concatenate([rotate(factors[:, 480:608], cosine, sine), factors[:, 608:800]], 1).astype(BF16)
        shared = lax.all_gather(own, "seq", axis=0)
        turned = lax.dynamic_slice_in_dim(jnp.concatenate([shared, shared], 0), me, nseq, 0)
        low, high = turned[..., :span], turned[..., span:]
        sel = jnp.where(chosen[:, None, None, None], low, high)
        low = low.transpose(1, 2, 0, 3).reshape(rows, 320, nk)
        sel = sel.transpose(1, 2, 0, 3).reshape(rows, 320, nk)
        in_pairs = lambda a: a[:, 256:].astype(F32).reshape(rows, PAIRS, 8, nk)
        factors = (in_pairs(low), in_pairs(sel), low[:, :256], sel[:, :256])
        heads_out, lse = attend(qh, qr, *factors, *masks)
    if near:
        dqh, dqr, mine, output, d_resid, gain_two_grad, *sums = backward(
            qh, qr, shared, *masks, lse, tokens, heads_out, cotangent, w_out, w_gate, w_up, w_down, gain_two[None, :], REDUCE_UNITS, REDUCE_PLAN, 1)
        input_grad, small_grad = products(dqh, dqr, mine, cosine, sine, by_row, parts[0], tokens, d_resid, gain_two_grad)
        small_sum = reduce_weights([small_grad], SMALL_UNITS, SMALL_PLAN, 3)[0]
        d_qh, d_qd, d_kh, d_kd, d_vh, d_vd, d_g1, d_g2, d_out, d_gate, d_up, d_down = results(small_sum, *sums)
        return (output, input_grad, d_g1[0], d_qh, d_qd, d_kh, d_kd, d_vh, d_vd, d_out, d_g2[0], d_gate, d_up, d_down)
    else:
        heads_flat = heads_out.reshape(count, width)

        resid = flat + dot(heads_flat, w_out, (1,), (0,))
        normed_two_full, unit_two, scale_two = rms_forward(resid, gain_two)
        normed_two = normed_two_full.astype(BF16)
        gate = dot(normed_two, w_gate, (1,), (0,))
        up_part = dot(normed_two, w_up, (1,), (0,))
        sigma = jax.nn.sigmoid(gate)
        hidden = (gate * sigma * up_part).astype(BF16)
        output = (resid + dot(hidden, w_down, (1,), (0,))).astype(BF16).reshape(rows, slots, width)

        grad_out = cotangent.reshape(count, width)
        down_grad = dot(hidden, grad_out, (0,), (0,)).astype(BF16)
        d_hidden = dot(grad_out, w_down, (1,), (1,))
        d_gate = (d_hidden * up_part * sigma * (1.0 + gate * (1.0 - sigma))).astype(BF16)
        d_up = (d_hidden * gate * sigma).astype(BF16)
        gate_grad = dot(normed_two, d_gate, (0,), (0,)).astype(BF16)
        up_grad = dot(normed_two, d_up, (0,), (0,)).astype(BF16)
        d_normed_two = dot(d_gate, w_gate, (1,), (1,)) + dot(d_up, w_up, (1,), (1,))
        d_mid, gain_two_grad = rms_backward(d_normed_two, unit_two, scale_two, gain_two)
        d_resid = grad_out.astype(F32) + d_mid
        d_attn = d_resid.astype(BF16)
        out_grad = dot(heads_flat, d_attn, (0,), (0,)).astype(BF16)
        d_heads = dot(d_attn, w_out, (1,), (1,)).astype(BF16).reshape(rows, slots, width)

        grads = [g.reshape(nseq, -1, g.shape[-1]) for g in (out_grad, gate_grad, up_grad, down_grad)]
        dqh, dqr, dhl, dhs, ddl, dds = attend_back(qh, qr, *factors, *masks, lse, heads_out, d_heads)
        from_low = jnp.concatenate([ddl, dhl.reshape(rows, 64, nk)], 1).reshape(rows, 320, nseq, span)
        from_sel = jnp.concatenate([dds, dhs.reshape(rows, 64, nk)], 1).reshape(rows, 320, nseq, span)
        pick = chosen[None, None, :, None]
        both = jnp.concatenate([from_low + jnp.where(pick, from_sel, 0.0), jnp.where(pick, 0.0, from_sel)], -1).transpose(2, 0, 1, 3)
        both = lax.dynamic_slice_in_dim(jnp.concatenate([both, both], 0), lax.rem(nseq - me, nseq), nseq, 0)
        mine = lax.psum_scatter(both, "seq", scatter_dimension=0, tiled=True)[0]
        sums = reduce_far(grads)
    mine = mine.astype(F32)
    turned = jnp.concatenate([dqh.reshape(rows, 96, slots), rotate(dqr, cosine, -sine), rotate(mine[:, :128], cosine, -sine), mine[:, 128:]], 1).astype(BF16)
    small_grad = dot(by_row, turned, (0, 1), (0, 2))
    d_normed = dot(turned, w_qkv, (1,), (1,)).reshape(count, width)
    d_first, gain_one_grad = rms_backward(d_normed, unit_one, scale_one, gain_one)
    input_grad = (d_resid + d_first).reshape(rows, slots, width)
    small_grad = jnp.concatenate([small_grad, gain_one_grad[:, None], gain_two_grad[:, None], jnp.zeros((width, 94), F32)], 1).astype(BF16)

    small_grad = small_grad.reshape(nseq, -1, 896)
    small_sum = reduce_far([small_grad])[0]
    small_sum = small_sum.astype(F32)
    out_sum, gate_sum, up_sum, down_sum = [g.astype(F32) for g in sums]
    key_value = head_columns(small_sum[:, 736:800], 4)
    return (output, input_grad, small_sum[:, 800], head_columns(small_sum[:, :96], QRANK), small_sum[:, 96:480], key_value[:, :32], small_sum[:, 480:608],
            key_value[:, 32:], small_sum[:, 608:736], out_sum, small_sum[:, 801], gate_sum, up_sum, down_sum)


def solution(mesh):
    near = mesh.shape["seq"] == 8 and mesh.shape["batch"] == 4
    by_slot = P("batch", "seq", None)
    line, table = P("seq"), P("seq", None)
    return jax.shard_map(
        functools.partial(per_device, near),
        mesh=mesh,
        in_specs=(by_slot, by_slot, P("batch"), P(), line, *([table] * 7), line, *([table] * 3)),
        out_specs=(by_slot, by_slot, line, *([table] * 7), line, *([table] * 3)),
        check_vma=False,
    )
```

```python
import functools
import math

import jax
import jax.numpy as jnp
from jax import lax
from jax.experimental import pallas as pl
from jax.experimental.pallas import tpu as pltpu
from jax.sharding import PartitionSpec as P


MESH = pl.DeviceIdType.MESH
NZ, NX = 4, 2

class Place:
    def __init__(self):
        self.seq = lax.axis_index("seq")
        self.batch = lax.axis_index("batch")
        self.z = self.seq // 2
        self.x = lax.rem(self.seq, 2)
        self.y = self.batch // 2
        self.c = lax.rem(self.batch, 2)
        self.up = (jnp.minimum(self.seq + 2, 7), self.batch)
        self.down = (jnp.maximum(self.seq - 2, 0), self.batch)
        self.xp = (self.seq + 1 - 2 * self.x, self.batch)
        self.yp = (self.seq, lax.rem(self.batch + 2, 4))
        self.cp = (self.seq, self.batch + 1 - 2 * self.c)

    def along(self, k):
        return (2 * lax.rem(self.z + k, NZ) + self.x, self.batch)

def greet(me):
    bar = pltpu.get_barrier_semaphore()
    def sig(d):
        pl.semaphore_signal(bar, inc=1, device_id=d, device_id_type=MESH)
    for k in range(1, NZ):
        sig(me.along(k))
    sig(me.xp); sig(me.yp); sig(me.cp)
    pl.semaphore_wait(bar, NZ + 2)

class Unit:
    def __init__(self, arr, row, col, flow, axis):
        self.arr, self.row, self.col, self.flow, self.axis = arr, row, col, flow, axis
        self.shape = (row[1], col[1])
        h = list(self.shape); h[axis] //= 2
        self.half = tuple(h)
        q = list(h)
        if flow == "P": q[axis] //= 2
        self.piece = tuple(q)

def rect(unit, ref, part, nparts):
    start = [unit.row[0], unit.col[0]]
    size = list(unit.shape)
    size[unit.axis] //= nparts
    idx = []
    for d in range(2):
        if d == unit.axis:
            off = part * size[d] + start[d]
            idx.append(pl.ds(pl.multiple_of(off, 16 if d == 0 else 128), size[d]))
        else:
            idx.append(pl.ds(start[d], size[d]))
    return ref.at[tuple(idx)]

def shard_of(ref, s, n=8):
    if len(ref.shape) == 3:
        return ref.at[s]
    rows = ref.shape[0] // n
    return ref.at[pl.ds(pl.multiple_of(s * rows, 16), rows)]

class Reduce:
    def __init__(self, me, units, ins, outs, scratch):
        self.me, self.units, self.ins, self.outs = me, units, ins, outs
        nu = len(units)
        self.A, self.RC, self.RY, self.RX, self.RZ, self.RF = [scratch[i * nu:(i + 1) * nu] for i in range(6)]
        self.ls, self.cs, self.cr, self.ys, self.yr, self.xs, self.xr, self.zs, self.zr, self.fs, self.fr, self.os_ = scratch[6 * nu:]

    def shard_at(self, i):
        me = self.me
        zz = lax.rem(me.z + 1 + lax.rem(i, NZ), NZ)
        xx = jnp.where(i < NZ, 1 - me.x, me.x)
        return zz, xx, 2 * zz + xx

    def sub(self, u, ref, y):
        if u.flow == "R":
            return ref
        n = u.piece[u.axis]
        idx = [slice(None)] * 2
        idx[u.axis] = pl.ds(pl.multiple_of(y * n, n), n)
        return ref.at[tuple(idx)]

    def remote(self, src, dst, ss, rs, dev):
        return pltpu.make_async_remote_copy(src_ref=src, dst_ref=dst, send_sem=ss, recv_sem=rs, device_id=dev, device_id_type=MESH)

    def core_copy(self, k, i):
        u = self.units[k]; zz, xx, s = self.shard_at(i)
        return self.remote(rect(u, shard_of(self.ins[u.arr], s), 1 - self.me.c, 2), self.RC[k].at[s], self.cs.at[k, s], self.cr.at[k, s], self.me.cp)

    def local_copy(self, k, i):
        u = self.units[k]; zz, xx, s = self.shard_at(i)
        return pltpu.make_async_copy(rect(u, shard_of(self.ins[u.arr], s), self.me.c, 2), self.A[k].at[s], self.ls.at[k, s])

    def y_copy(self, k, i):
        u = self.units[k]; zz, xx, s = self.shard_at(i)
        return self.remote(self.sub(u, self.A[k].at[s], 1 - self.me.y), self.RY[k].at[s], self.ys.at[k, s], self.yr.at[k, s], self.me.yp)

    def x_copy(self, k, zz):
        u, me = self.units[k], self.me
        return self.remote(self.sub(u, self.A[k].at[2 * zz + 1 - me.x], me.y), self.RX[k].at[zz], self.xs.at[k, zz], self.xr.at[k, zz], me.xp)

    def z_copy(self, k, zz):
        u, me = self.units[k], self.me
        return self.remote(self.mine(k, zz), self.RZ[k].at[self.slot(me.z, zz)], self.zs.at[k, zz], self.zr.at[k, me.z], (2 * zz + me.x, me.batch))

    @staticmethod
    def slot(source, owner):
        return lax.rem(source - owner + NZ, NZ) - 1

    def z_recv(self, k, zz):
        u, me = self.units[k], self.me
        v = self.RZ[k].at[self.slot(zz, me.z)]
        return self.remote(v, v, self.zs.at[k, zz], self.zr.at[k, zz], (2 * zz + me.x, me.batch))

    def mine(self, k, zz):
        return self.sub(self.units[k], self.A[k].at[2 * zz + self.me.x], self.me.y)

    @staticmethod
    def add(dst, src):
        dst[...] = dst[...] + src[...]

    def begin(self, k, i):
        self.core_copy(k, i).start()
        self.local_copy(k, i).start()

    def core(self, k, i):
        u = self.units[k]; zz, xx, s = self.shard_at(i)
        self.local_copy(k, i).wait()
        self.core_copy(k, i).wait_recv()
        self.add(self.A[k].at[s], self.RC[k].at[s])
        if u.flow == "P":
            self.y_copy(k, i).start()
        else:
            pl.when(i < NZ)(lambda: self.x_copy(k, zz).start())

    def y(self, k, i):
        u = self.units[k]; zz, xx, s = self.shard_at(i)
        self.y_copy(k, i).wait_recv()
        self.add(self.sub(u, self.A[k].at[s], self.me.y), self.RY[k].at[s])
        pl.when(i < NZ)(lambda: self.x_copy(k, zz).start())

    def x(self, k, i):
        me = self.me
        zz = lax.rem(me.z + 1 + i, NZ)
        self.x_copy(k, zz).wait_recv()
        self.add(self.mine(k, zz), self.RX[k].at[zz])
        pl.when(zz != me.z)(lambda: self.z_copy(k, zz).start())

    def fin_y(self, k):
        u, me = self.units[k], self.me
        mine = self.mine(k, me.z)
        dst = rect(u, self.outs[u.arr], 2 * me.c + me.y, 4) if u.flow == "P" else self.RF[k]
        return self.remote(mine, dst, self.fs.at[k, 0], self.fr.at[k, 0], me.yp)

    def fin_c(self, k, w):
        u, me = self.units[k], self.me
        if u.flow == "P":
            if w == 0:
                return self.remote(self.mine(k, me.z), rect(u, self.outs[u.arr], 2 * me.c + me.y, 4), self.fs.at[k, 1], self.fr.at[k, 1], me.cp)
            v = rect(u, self.outs[u.arr], 2 * me.c + 1 - me.y, 4)
            return self.remote(v, v, self.fs.at[k, 2], self.fr.at[k, 2], me.cp)
        return self.remote(self.RF[k], rect(u, self.outs[u.arr], me.c, 2), self.fs.at[k, 1], self.fr.at[k, 1], me.cp)

    def out_copy(self, k):
        u, me = self.units[k], self.me
        if u.flow == "P":
            return pltpu.make_async_copy(self.mine(k, me.z), rect(u, self.outs[u.arr], 2 * me.c + me.y, 4), self.os_.at[k])
        return pltpu.make_async_copy(self.RF[k], rect(u, self.outs[u.arr], me.c, 2), self.os_.at[k])

    def own(self, k, i):
        me = self.me
        def body(i, c):
            zz = lax.rem(me.z + i, NZ)
            self.z_recv(k, zz).wait_recv()
            self.add(self.mine(k, me.z), self.RZ[k].at[self.slot(zz, me.z)])
            return c
        lax.fori_loop(1, NZ, body, 0)
        self.fin_y(k).start()
        if self.units[k].flow == "P":
            self.out_copy(k).start()
            self.fin_c(k, 0).start()

    def last(self, k, i):
        self.fin_y(k).wait_recv()
        if self.units[k].flow == "P":
            self.fin_c(k, 1).start()
        else:
            self.add(self.RF[k], self.mine(k, self.me.z))
            self.out_copy(k).start()
            self.fin_c(k, 0).start()

    def end(self, k, i):
        me = self.me
        flow = self.units[k].flow
        for w in range(2 if flow == "P" else 1):
            self.fin_c(k, w).wait_recv()
            self.fin_c(k, w).wait_send()
        self.out_copy(k).wait()
        self.fin_y(k).wait_send()
        def body(i, c):
            self.core_copy(k, i).wait_send()
            if flow == "P": self.y_copy(k, i).wait_send()
            return c
        lax.fori_loop(0, 8, body, 0)
        def body(zz, c):
            self.x_copy(k, zz).wait_send()
            pl.when(zz != me.z)(lambda: self.z_copy(k, zz).wait_send())
            return c
        lax.fori_loop(0, NZ, body, 0)

    def run(self, plan):
        for step, k, first, n in plan:
            fn = getattr(self, step)
            if n == 1:
                fn(k, first)
            else:
                def body(i, c):
                    fn(k, i)
                    return c
                lax.fori_loop(first, first + n, body, 0)

def reduce_kernel(units, narr, plan, *refs):
    me = Place()
    greet(me)
    red = Reduce(me, units, refs[:narr], refs[narr:2 * narr], refs[2 * narr:])
    red.run(plan)

def reduce_scratch(units):
    nu = len(units)
    DMA = pltpu.SemaphoreType.DMA
    bf = jnp.bfloat16
    V = pltpu.VMEM
    return ([V((8, *u.half), bf) for u in units] + [V((8, *u.half), bf) for u in units]
        + [V((8, *u.piece) if u.flow == "P" else (16, 128), bf) for u in units] + [V((4, *u.piece), bf) for u in units]
        + [V((3, *u.piece), bf) for u in units] + [V(u.piece if u.flow == "R" else (16, 128), bf) for u in units]
        + [DMA((nu, 8))] * 5 + [DMA((nu, 4))] * 4 + [DMA((nu, 3))] * 2 + [DMA((nu,))])

def reduce_weights(arrays, units, plan, cid):
    narr = len(arrays)
    return pl.pallas_call(
        functools.partial(reduce_kernel, units, narr, plan),
        out_shape=[jax.ShapeDtypeStruct(a.shape[1:], a.dtype) for a in arrays],
        in_specs=[pl.BlockSpec(memory_space=pl.ANY)] * narr,
        out_specs=[pl.BlockSpec(memory_space=pl.ANY)] * narr,
        scratch_shapes=reduce_scratch(units),
        compiler_params=pltpu.CompilerParams(collective_id=cid, has_side_effects=True, vmem_limit_bytes=58 << 20),
        name="reduce_weights",
    )(*arrays)

F32, BF16 = jnp.float32, jnp.bfloat16
NEG = -1e30

def nn(a, b):
    return lax.dot_general(a, b, (((1,), (0,)), ((), ())), preferred_element_type=F32)

def nt(a, b):
    return lax.dot_general(a, b, (((1,), (1,)), ((), ())), preferred_element_type=F32)

def expand(heads, dims, base):
    parts = []
    for h in range(2):
        parts.append((heads[base + h:base + h + 1] * dims[0] + heads[base + 2 + h:base + 3 + h] * dims[1]) * 0.5)
    return jnp.concatenate(parts, 0)

def queries(qh, qr):
    parts = []
    for h in range(2):
        total = qh[h:h + 1] * qr[0:64]
        for r in range(1, 6):
            total = total + qh[2 * r + h:2 * r + h + 1] * qr[64 * r:64 * r + 64]
        parts.append(total)
    return jnp.concatenate(parts, 0) / 6.0

def lanes_below(shape, n):
    return lax.broadcasted_iota(jnp.int32, shape, 1) < n

def stack_heads(part):
    first = lanes_below(part.shape, 64)
    zero = jnp.zeros_like(part)
    return jnp.concatenate([jnp.where(first, part, zero), jnp.where(first, zero, part)], 0)

def unstack_heads(part):
    n = part.shape[0] // 2
    return jnp.where(lanes_below((n, 128), 64), part[:n], part[n:])

def causal_bias(n2, span):
    row = lax.broadcasted_iota(jnp.int32, (n2, span), 0) % span
    col = lax.broadcasted_iota(jnp.int32, (n2, span), 1)
    return jnp.where(col <= row, 0.0, NEG)

def pair_factors(heads, dims, cond, base, at):
    hl, hs = heads
    dl, ds = dims
    low = expand(hl, (dl[at:at + 64].astype(F32), dl[at + 64:at + 128].astype(F32)), base).astype(BF16)
    sel = expand(hs, (ds[at:at + 64].astype(F32), ds[at + 64:at + 128].astype(F32)), base)
    left = jnp.where(cond > 0.5, sel, 0.0).astype(BF16)
    right = jnp.where(cond > 0.5, 0.0, sel).astype(BF16)
    return low, jnp.concatenate([left, right], 0)

def attend_kernel(span, chunk, qh_ref, qr_ref, hl_ref, hs_ref, dl_ref, ds_ref, cond_ref, bl_ref, bs_ref, o_ref, lse_ref, s1, s2):
    pair_forward(span, chunk, pl.program_id(1), qh_ref[0, 0], qr_ref[0], hl_ref[0, 0], hs_ref[0, 0], dl_ref, ds_ref, cond_ref, bl_ref, bs_ref, o_ref, lse_ref, s1, s2)

def pair_forward(span, chunk, p, qh, qr, hl, hs, dl_ref, ds_ref, cond_ref, bl_ref, bs_ref, o_ref, lse_ref, s1, s2):
    n2 = 2 * span
    nk = dl_ref.shape[-1]
    qt = queries(qh, qr)
    q = (qt.astype(BF16).astype(F32).T * 0.125).astype(BF16)
    qlo, qhi = stack_heads(q[:span]), stack_heads(q[span:])
    qboth = jnp.concatenate([qlo, qhi], 1)
    heads = (hl, hs)
    dims = (dl_ref[0], ds_ref[0])
    cond = cond_ref[...]
    klo, ksel = pair_factors(heads, dims, cond, 0, 0)
    vlo, vsel = pair_factors(heads, dims, cond, 4, 128)
    tri = causal_bias(n2, span)
    width = min(128, chunk)
    mlo = jnp.full((n2, width), NEG, F32)
    mhi = jnp.full((n2, width), NEG, F32)
    s3 = nn(qlo, klo[:, :span]) + bl_ref[0][:, :span] + tri
    m3 = jnp.max(s3, -1, keepdims=True)
    for c in range(0, nk, chunk):
        sl = slice(c, c + chunk)
        a = nn(qhi, klo[:, sl]) + bl_ref[0][:, sl]
        s1[:, sl] = a
        b = nn(qboth, ksel[:, sl]) + bs_ref[0][:, sl]
        if c == 0:
            b = jnp.concatenate([b[:, :span] + tri, b[:, span:]], 1)
        s2[:, sl] = b
        for i in range(0, chunk, width):
            on = cond[:, c + i:c + i + width] > 0.5
            ai, bi = a[:, i:i + width], b[:, i:i + width]
            mlo = jnp.maximum(mlo, jnp.where(on, bi, NEG))
            mhi = jnp.maximum(mhi, jnp.maximum(ai, jnp.where(on, NEG, bi)))
    mlo = jnp.maximum(jnp.max(mlo, -1, keepdims=True), m3)
    mhi = jnp.max(mhi, -1, keepdims=True)
    e3 = jnp.exp(s3 - mlo)
    tlo = jnp.zeros((n2, width), F32)
    thi = jnp.zeros((n2, width), F32)
    o3 = nt(e3.astype(BF16), vlo[:, :span])
    o1 = jnp.zeros((n2, 128), F32)
    o2 = jnp.zeros((n2, 256), F32)
    for c in range(0, nk, chunk):
        sl = slice(c, c + chunk)
        on = cond[:, sl] > 0.5
        a = jnp.exp(s1[:, sl] - mhi)
        b = jnp.exp(s2[:, sl] - jnp.where(on, mlo, mhi))
        blo = jnp.where(on, b, 0.0)
        bhi = a + jnp.where(on, 0.0, b)
        for i in range(0, chunk, width):
            tlo = tlo + blo[:, i:i + width]
            thi = thi + bhi[:, i:i + width]
        o1 = o1 + nt(a.astype(BF16), vlo[:, sl])
        o2 = o2 + nt(b.astype(BF16), vsel[:, sl])
    llo = jnp.sum(tlo, -1, keepdims=True) + jnp.sum(e3, -1, keepdims=True)
    lhi = jnp.sum(thi, -1, keepdims=True)
    olo = unstack_heads((o2[:, :128] + o3) / llo)
    ohi = unstack_heads((o2[:, 128:] + o1) / lhi)
    o_ref[0] = jnp.concatenate([olo, ohi], 0).astype(BF16)
    lane = lax.broadcasted_iota(jnp.int32, (span, 128), 1)
    tlo = mlo + jnp.log(llo)
    thi = mhi + jnp.log(lhi)
    old = jnp.where(p == 0, 0.0, lse_ref[0])
    new = []
    for k, t in enumerate((tlo, thi)):
        part = old[k * span:(k + 1) * span]
        part = jnp.where(lane == 2 * p, t[:span], part)
        new.append(jnp.where(lane == 2 * p + 1, t[span:], part))
    lse_ref[0] = jnp.concatenate(new, 0)

def attend(qh, qr, hl, hs, dl, ds, cond, bl, bs):
    rows, pairs, _, nq = qh.shape
    nk = dl.shape[-1]
    span = nq // 2
    chunk = min(512, nk)
    full = lambda *s: pl.BlockSpec((1, *s), lambda b, p: (b, *([0] * len(s))))
    pairb = lambda *s: pl.BlockSpec((1, 1, *s), lambda b, p: (b, p, *([0] * len(s))))
    return pl.pallas_call(
        functools.partial(attend_kernel, span, chunk),
        grid=(rows, pairs),
        out_shape=[jax.ShapeDtypeStruct((rows, nq, pairs * 128), BF16), jax.ShapeDtypeStruct((rows, nq, 128), F32)],
        in_specs=[pairb(12, nq), full(384, nq), pairb(8, nk), pairb(8, nk), full(256, nk), full(256, nk),
                  pl.BlockSpec((1, nk), lambda b, p: (0, 0)), full(1, nk), full(1, nk)],
        out_specs=[pl.BlockSpec((1, nq, 128), lambda b, p: (b, 0, p)), full(nq, 128)],
        scratch_shapes=[pltpu.VMEM((nq, nk), F32), pltpu.VMEM((nq, nk), F32)],
        compiler_params=pltpu.CompilerParams(vmem_limit_bytes=56 << 20),
        name="attend",
    )(qh, qr, hl, hs, dl, ds, cond, bl, bs)

def attend_back_kernel(span, chunk, qh_ref, qr_ref, hl_ref, hs_ref, dl_ref, ds_ref, cond_ref, bl_ref, bs_ref, lse_ref, o_ref, g_ref,
                       dqh_ref, dqr_ref, dhl_ref, dhs_ref, ddl_ref, dds_ref):
    p = pl.program_id(1)
    @pl.when(p == 0)
    def _():
        dqr_ref[...] = jnp.zeros_like(dqr_ref)
        ddl_ref[...] = jnp.zeros_like(ddl_ref)
        dds_ref[...] = jnp.zeros_like(dds_ref)
    pair_back(span, chunk, p, qh_ref, qr_ref, Pair(hl_ref, 0, 0), Pair(hs_ref, 0, 0), dl_ref, ds_ref, cond_ref, bl_ref, bs_ref, lse_ref, o_ref[0], g_ref[0],
              dqh_ref, dqr_ref, Pair(dhl_ref, 0, 0), Pair(dhs_ref, 0, 0), ddl_ref, dds_ref)

class Pair:
    def __init__(self, ref, *at):
        self.ref, self.at = ref, at

    def all(self):
        return self.ref[self.at]

    def row(self, j, sl):
        return self.ref[(*self.at, slice(j, j + 1), sl)]

    def put(self, j, sl, value):
        self.ref[(*self.at, slice(j, j + 1), sl)] = value

def pair_back(span, chunk, p, qh_ref, qr_ref, hl, hs, dl_ref, ds_ref, cond_ref, bl_ref, bs_ref, lse_ref, o, g,
              dqh_ref, dqr_ref, dhl, dhs, ddl_ref, dds_ref):
    n2 = 2 * span
    nk = dl_ref.shape[-1]
    qh, qr = qh_ref[0, 0], qr_ref[0]
    qt = (queries(qh, qr).astype(BF16).astype(F32)) * 0.125
    q = qt.T.astype(BF16)
    qlo, qhi = stack_heads(q[:span]), stack_heads(q[span:])
    qboth = jnp.concatenate([qlo, qhi], 1)
    glo, ghi = stack_heads(g[:span]), stack_heads(g[span:])
    gboth = jnp.concatenate([glo, ghi], 1)
    gt = g.astype(F32).T
    first = lax.broadcasted_iota(jnp.int32, (128, span), 0) < 64
    def stack_lanes(part):
        return jnp.concatenate([jnp.where(first, part, 0.0), jnp.where(first, 0.0, part)], 1).astype(BF16)
    qtlo, qthi = stack_lanes(qt[:, :span]), stack_lanes(qt[:, span:])
    gtlo, gthi = stack_lanes(gt[:, :span]), stack_lanes(gt[:, span:])
    qtboth = jnp.concatenate([qtlo, qthi], 0)
    gtboth = jnp.concatenate([gtlo, gthi], 0)
    prod = g.astype(F32) * o.astype(F32)
    flane = lanes_below((n2, 128), 64)
    d0 = jnp.sum(jnp.where(flane, prod, 0.0), -1, keepdims=True)
    d1 = jnp.sum(jnp.where(flane, 0.0, prod), -1, keepdims=True)
    lane = lax.broadcasted_iota(jnp.int32, (n2, 128), 1)
    lse = lse_ref[0]
    l0 = jnp.sum(jnp.where(lane == 2 * p, lse, 0.0), -1, keepdims=True)
    l1 = jnp.sum(jnp.where(lane == 2 * p + 1, lse, 0.0), -1, keepdims=True)
    dello, delhi = jnp.concatenate([d0[:span], d1[:span]], 0), jnp.concatenate([d0[span:], d1[span:]], 0)
    lselo, lsehi = jnp.concatenate([l0[:span], l1[:span]], 0), jnp.concatenate([l0[span:], l1[span:]], 0)
    heads = (hl.all(), hs.all())
    dims = (dl_ref[0], ds_ref[0])
    cond = cond_ref[...]
    klo, ksel = pair_factors(heads, dims, cond, 0, 0)
    vlo, vsel = pair_factors(heads, dims, cond, 4, 128)
    tri = causal_bias(n2, span)

    def put(dkt, h, d_ref, hd, dd_ref, base, at, sl):
        for r in range(2):
            dim = d_ref[0, at + 64 * r:at + 64 * r + 64, sl].astype(F32)
            total = None
            for k in range(2):
                part = dkt[64 * k:64 * k + 64]
                j = base + 2 * r + k
                hd.put(j, sl, jnp.sum(part * dim, 0, keepdims=True) * 0.5)
                term = part * h.row(j, sl)
                total = term if total is None else total + term
            dd_ref[0, at + 64 * r:at + 64 * r + 64, sl] += total * 0.5

    s3 = nn(qlo, klo[:, :span]) + bl_ref[0][:, :span] + tri
    p3 = jnp.exp(s3 - lselo)
    dp3 = nn(glo, vlo[:, :span])
    ds3 = (p3 * (dp3 - dello)).astype(BF16)
    p3 = p3.astype(BF16)
    dq3 = nt(ds3, klo[:, :span])
    dk3 = nn(qtlo, ds3)
    dv3 = nn(gtlo, p3)
    dq1 = jnp.zeros((n2, 128), F32)
    dq2 = jnp.zeros((n2, 256), F32)
    for c in range(0, nk, chunk):
        sl = slice(c, c + chunk)
        pa = jnp.exp(nn(qhi, klo[:, sl]) + bl_ref[0][:, sl] - lsehi)
        dpa = nn(ghi, vlo[:, sl])
        dsa = (pa * (dpa - delhi)).astype(BF16)
        pa = pa.astype(BF16)
        dq1 = dq1 + nt(dsa, klo[:, sl])
        dk = nn(qthi, dsa)
        dv = nn(gthi, pa)
        if c == 0:
            dk = jnp.concatenate([dk[:, :span] + dk3, dk[:, span:]], 1)
            dv = jnp.concatenate([dv[:, :span] + dv3, dv[:, span:]], 1)
        put(dk, hl, dl_ref, dhl, ddl_ref, 0, 0, sl)
        put(dv, hl, dl_ref, dhl, ddl_ref, 4, 128, sl)
    for c in range(0, nk, chunk):
        sl = slice(c, c + chunk)
        on = cond[:, sl] > 0.5
        s = nn(qboth, ksel[:, sl]) + bs_ref[0][:, sl]
        if c == 0:
            s = jnp.concatenate([s[:, :span] + tri, s[:, span:]], 1)
        pb = jnp.exp(s - jnp.where(on, lselo, lsehi))
        dpb = nn(gboth, vsel[:, sl])
        dsb = (pb * (dpb - jnp.where(on, dello, delhi))).astype(BF16)
        pb = pb.astype(BF16)
        dq2 = dq2 + nt(dsb, ksel[:, sl])
        dk = nn(qtboth, dsb)
        dv = nn(gtboth, pb)
        dk = jnp.where(on, dk[:128], dk[128:])
        dv = jnp.where(on, dv[:128], dv[128:])
        put(dk, hs, ds_ref, dhs, dds_ref, 0, 0, sl)
        put(dv, hs, ds_ref, dhs, dds_ref, 4, 128, sl)
    dqlo = unstack_heads(dq2[:, :128] + dq3)
    dqhi = unstack_heads(dq2[:, 128:] + dq1)
    dqt = (jnp.concatenate([dqlo, dqhi], 0) * (0.125 / 6.0)).T
    for r in range(6):
        total = None
        for h in range(2):
            part = dqt[64 * h:64 * h + 64]
            j = 2 * r + h
            dqh_ref[0, 0, j:j + 1, :] = jnp.sum(part * qr[64 * r:64 * r + 64], 0, keepdims=True)
            term = part * qh[j:j + 1]
            total = term if total is None else total + term
        dqr_ref[0, 64 * r:64 * r + 64, :] += total

def attend_back(qh, qr, hl, hs, dl, ds, cond, bl, bs, lse, o, g):
    rows, pairs, _, nq = qh.shape
    nk = dl.shape[-1]
    span = nq // 2
    chunk = min(512, nk)
    full = lambda *s: pl.BlockSpec((1, *s), lambda b, p: (b, *([0] * len(s))))
    pairb = lambda *s: pl.BlockSpec((1, 1, *s), lambda b, p: (b, p, *([0] * len(s))))
    tok = pl.BlockSpec((1, nq, 128), lambda b, p: (b, 0, p))
    sd = jax.ShapeDtypeStruct
    return pl.pallas_call(
        functools.partial(attend_back_kernel, span, chunk),
        grid=(rows, pairs),
        out_shape=[sd((rows, pairs, 12, nq), F32), sd((rows, 384, nq), F32), sd((rows, pairs, 8, nk), F32), sd((rows, pairs, 8, nk), F32),
                   sd((rows, 256, nk), F32), sd((rows, 256, nk), F32)],
        in_specs=[pairb(12, nq), full(384, nq), pairb(8, nk), pairb(8, nk), full(256, nk), full(256, nk),
                  pl.BlockSpec((1, nk), lambda b, p: (0, 0)), full(1, nk), full(1, nk), full(nq, 128), tok, tok],
        out_specs=[pairb(12, nq), full(384, nq), pairb(8, nk), pairb(8, nk), full(256, nk), full(256, nk)],
        compiler_params=pltpu.CompilerParams(vmem_limit_bytes=56 << 20),
        name="attend_back",
    )(qh, qr, hl, hs, dl, ds, cond, bl, bs, lse, o, g)

class Rows:
    def __init__(self, me, pack, out, RX, RZ, xs, xr, zs, zr):
        self.me, self.pack, self.out, self.RX, self.RZ = me, pack, out, RX, RZ
        self.xs, self.xr, self.zs, self.zr = xs, xr, zs, zr

    def remote(self, src, dst, ss, rs, dev):
        return pltpu.make_async_remote_copy(src_ref=src, dst_ref=dst, send_sem=ss, recv_sem=rs, device_id=dev, device_id_type=MESH)

    def x_copy(self, b, zz):
        return self.remote(self.pack.at[b, 2 * zz + 1 - self.me.x], self.RX.at[b, zz], self.xs.at[b, zz], self.xr.at[b, zz], self.me.xp)

    def z_copy(self, b, zz):
        me = self.me
        return self.remote(self.mine(b, zz), self.RZ.at[b, Reduce.slot(me.z, zz)], self.zs.at[b, zz], self.zr.at[b, me.z], (2 * zz + me.x, me.batch))

    def z_recv(self, b, zz):
        me = self.me
        v = self.RZ.at[b, Reduce.slot(zz, me.z)]
        return self.remote(v, v, self.zs.at[b, zz], self.zr.at[b, zz], (2 * zz + me.x, me.batch))

    def mine(self, b, zz):
        return self.pack.at[b, 2 * zz + self.me.x]

    @staticmethod
    def add(dst, src):
        dst[...] = dst[...] + src[...]

    def begin(self, b):
        def body(i, c):
            self.x_copy(b, lax.rem(self.me.z + 1 + i, NZ)).start()
            return c
        lax.fori_loop(0, NZ, body, 0)

    def x(self, b):
        me = self.me
        def body(i, c):
            zz = lax.rem(me.z + 1 + i, NZ)
            self.x_copy(b, zz).wait_recv()
            self.add(self.mine(b, zz), self.RX.at[b, zz])
            pl.when(zz != me.z)(lambda: self.z_copy(b, zz).start())
            return c
        lax.fori_loop(0, NZ, body, 0)

    def own(self, b):
        me = self.me
        def body(i, c):
            zz = lax.rem(me.z + i, NZ)
            self.z_recv(b, zz).wait_recv()
            self.add(self.mine(b, me.z), self.RZ.at[b, Reduce.slot(zz, me.z)])
            return c
        lax.fori_loop(1, NZ, body, 0)
        self.out[b] = self.pack[b, me.seq]

    def end(self, b):
        me = self.me
        def sent(zz, c):
            self.x_copy(b, zz).wait_send()
            pl.when(zz != me.z)(lambda: self.z_copy(b, zz).wait_send())
            return c
        lax.fori_loop(0, NZ, sent, 0)

def lay_out(me, block, n, span, cond_ref, dl, ds, hl, hs):
    for i in range(n):
        j = lax.rem(me.seq + i, n)
        sl = slice(i * span, (i + 1) * span)
        on = cond_ref[:, sl] > 0.5
        low = block(j)[:256, :span].astype(F32)
        high = block(j)[:256, span:].astype(F32)
        dl[0, :, sl] = low.astype(BF16)
        ds[0, :, sl] = jnp.where(on, low, high).astype(BF16)
        low = block(j)[256:, :span].astype(F32)
        high = block(j)[256:, span:].astype(F32)
        hl[:, :, sl] = low.reshape(PAIRS, 8, span)
        hs[:, :, sl] = jnp.where(on, low, high).reshape(PAIRS, 8, span)

def pack_up(me, b, span, cond_ref, pack, ddl, dds, dhl, dhs):
    n = pack.shape[1]
    for i in range(n):
        j = lax.rem(me.seq + i, n)
        sl = slice(i * span, (i + 1) * span)
        on = cond_ref[:, sl] > 0.5
        for at, lo, se in ((0, ddl[0, :, sl], dds[0, :, sl]), (256, dhl[:, :, sl].reshape(64, span), dhs[:, :, sl].reshape(64, span))):
            rows = slice(at, at + lo.shape[0])
            pack[b, j, rows, :span] = (lo + jnp.where(on, se, 0.0)).astype(BF16)
            pack[b, j, rows, span:] = jnp.where(on, 0.0, se).astype(BF16)

FFC = 256

class Feed:
    def __init__(self, hbm, outs, grads, buf):
        self.tok, self.heads_hbm, self.cot, self.w_out, self.w_gate, self.w_up, self.w_down, self.gain = hbm
        self.output, self.d_resid, self.gain_grad = outs
        self.g_out, self.g_gate, self.g_up, self.g_down = grads
        (self.xb, self.hb, self.gb, self.n2, self.n2t, self.resid, self.acc, self.dlo, self.dhi, self.wa, self.wd, self.sg, self.su, self.sd, self.dg, self.du, self.hidt,
         self.lsem, self.wsem, self.ssem) = buf
        self.rows, self.nq, self.width = self.tok.shape
        self.count = self.rows * self.nq

    def load(self):
        out = []
        for i, (src, dst) in enumerate(((self.tok, self.xb), (self.heads_hbm, self.hb), (self.cot, self.gb))):
            for r in range(self.rows):
                out.append(pltpu.make_async_copy(src.at[r], dst.at[pl.ds(r * self.nq, self.nq)], self.lsem.at[i, r]))
        return out

    def out_part(self, j):
        return pltpu.make_async_copy(self.w_out.at[:, pl.ds(j * FFC, FFC)], self.wa.at[j], self.wsem.at[0, j])

    def weights(self, c):
        k = lax.rem(c, 2)
        at = pl.ds(pl.multiple_of(c * FFC, FFC), FFC)
        return (pltpu.make_async_copy(self.w_gate.at[:, at], self.wa.at[k], self.wsem.at[1, k]),
                pltpu.make_async_copy(self.w_up.at[:, at], self.wa.at[2 + k], self.wsem.at[1, 2 + k]),
                pltpu.make_async_copy(self.w_down.at[at], self.wd.at[k], self.wsem.at[2, k]))

    def stores(self, c):
        at = pl.ds(pl.multiple_of(c * FFC, FFC), FFC)
        return (pltpu.make_async_copy(self.sg, self.g_gate.at[:, :, at], self.ssem.at[0]),
                pltpu.make_async_copy(self.su, self.g_up.at[:, :, at], self.ssem.at[1]),
                pltpu.make_async_copy(self.sd, self.g_down.at[at], self.ssem.at[2]))

    def out_store(self, j):
        return pltpu.make_async_copy((self.sg, self.su)[j % 2], self.g_out.at[:, :, pl.ds(j * FFC, FFC)], self.ssem.at[j % 2])

    def before(self):
        parts = self.width // FFC
        loads = self.load() + [self.out_part(j) for j in range(parts)]
        for cp in loads:
            cp.start()
        for cp in loads:
            cp.wait()
        for j in range(parts):
            sl = slice(j * FFC, (j + 1) * FFC)
            self.resid[:, sl] = self.xb[:, sl].astype(F32) + nn(self.hb[...], self.wa[j])
        for cp in self.weights(0):
            cp.start()
        gain = self.gain[...]
        for r in range(0, self.count, 128):
            sl = slice(r, r + 128)
            v = self.resid[sl, :]
            self.acc[sl, :] = v
            n2 = v * lax.rsqrt(jnp.mean(v * v, -1, keepdims=True) + 1e-6) * gain
            self.n2[sl, :] = n2.astype(BF16)
            self.n2t[:, sl] = n2.T.astype(BF16)
        self.dlo[...] = jnp.zeros_like(self.dlo)
        self.dhi[...] = jnp.zeros_like(self.dhi)

    def block(self, c, total):
        k = lax.rem(c, 2)
        for cp in self.weights(c):
            cp.wait()
        @pl.when(c + 1 < total)
        def _():
            for cp in self.weights(c + 1):
                cp.start()
        half = self.count // 2
        for r, dn in ((0, self.dlo), (half, self.dhi)):
            sl = slice(r, r + half)
            gate = nn(self.n2[sl, :], self.wa[k])
            up = nn(self.n2[sl, :], self.wa[2 + k])
            dh = nt(self.gb[sl, :], self.wd[k])
            sigma = 1.0 / (1.0 + jnp.exp(-gate))
            silu = gate * sigma
            hid = (silu * up).astype(BF16)
            d_gate = (dh * up * sigma * (1.0 + gate * (1.0 - sigma))).astype(BF16)
            d_up = (dh * silu).astype(BF16)
            self.dg[sl, :] = d_gate
            self.du[sl, :] = d_up
            self.hidt[:, sl] = hid.astype(F32).T.astype(BF16)
            self.acc[sl, :] += nn(hid, self.wd[k])
            dn[0] += nt(d_gate, self.wa[k]) + nt(d_up, self.wa[2 + k])
        @pl.when(c >= 1)
        def _():
            for cp in self.stores(c - 1):
                cp.wait()
        self.sg[...] = nn(self.n2t[...], self.dg[...]).astype(BF16).reshape(self.sg.shape)
        self.su[...] = nn(self.n2t[...], self.du[...]).astype(BF16).reshape(self.su.shape)
        self.sd[...] = nn(self.hidt[...], self.gb[...]).astype(BF16)
        for cp in self.stores(c):
            cp.start()

    def settle(self, c):
        for cp in self.stores(c):
            cp.wait()

    def after(self, total):
        parts = self.width // FFC
        for j in range(parts):
            self.out_part(j).start()
        gain = self.gain[...]
        sums = jnp.zeros((8, self.width), F32)
        half = self.count // 2
        for r in range(0, self.count, 128):
            sl = slice(r, r + 128)
            dn = self.dlo[0, r:r + 128] if r < half else self.dhi[0, r - half:r - half + 128]
            v = self.resid[sl, :]
            scale = lax.rsqrt(jnp.mean(v * v, -1, keepdims=True) + 1e-6)
            unit = v * scale
            prod = dn * unit
            sums = sums + jnp.sum(prod.reshape(16, 8, self.width), 0)
            e2 = dn * gain
            d = self.gb[sl, :].astype(F32) + scale * (e2 - unit * jnp.mean(e2 * unit, -1, keepdims=True))
            self.resid[sl, :] = d
            self.gb[sl, :] = d.astype(BF16)
            self.xb[sl, :] = self.acc[sl, :].astype(BF16)
            self.n2t[:, sl] = self.hb[sl, :].astype(F32).T.astype(BF16)
        self.gain_grad[...] = jnp.sum(sums, 0, keepdims=True)
        for cp in self.results():
            cp.start()
        for j in range(parts):
            self.out_part(j).wait()
        for j in range(parts):
            if j >= 2:
                self.out_store(j - 2).wait()
            (self.sg, self.su)[j % 2][...] = nn(self.n2t[...], self.gb[:, j * FFC:(j + 1) * FFC]).astype(BF16).reshape(self.sg.shape)
            self.out_store(j).start()
        for r in range(0, self.count, 128):
            total = None
            for j in range(parts):
                part = nt(self.gb[r:r + 128, j * FFC:(j + 1) * FFC], self.wa[j])
                total = part if total is None else total + part
            self.n2[r:r + 128, :] = total.astype(BF16)
        for j in range(parts - 2, parts):
            self.out_store(j).wait()

    def results(self):
        out = []
        for r in range(self.rows):
            at = pl.ds(r * self.nq, self.nq)
            out.append(pltpu.make_async_copy(self.xb.at[at], self.output.at[r], self.lsem.at[0, r]))
            out.append(pltpu.make_async_copy(self.resid.at[at], self.d_resid.at[r], self.lsem.at[1, r]))
        return out

def back_kernel(span, chunk, units, plan, blocks, qh_ref, qr_ref, shared_ref, cond_ref, bl_ref, bs_ref, lse_ref, *refs):
    feed_in, refs = refs[:8], refs[8:]
    dqh_ref, dqr_ref, mine_ref, output, d_resid, gain_grad = refs[:6]
    sums, grads, refs = refs[6:10], refs[10:14], refs[14:]
    dl, ds, hl, hs, ddl, dds, dhl, dhs, pack, RX, RZ, xs, xr, zs, zr, bsem = refs[:16]
    fb, refs = refs[16:34], refs[34:]
    me = Place()
    b, p = pl.program_id(0), pl.program_id(1)
    step = b * PAIRS + p
    nq = 2 * span
    red = Reduce(me, units, grads, sums, refs)
    row = Rows(me, pack, mine_ref, RX, RZ, xs, xr, zs, zr)
    feed = Feed(feed_in, (output, d_resid, gain_grad), grads, (*fb[:7], ddl, dds, *fb[7:]))

    def act(items):
        for it in items:
            if it[0] == "row":
                getattr(row, it[1])(it[2])
            elif it[0] == "settle":
                feed.settle(it[1])
            elif it[0] == "results":
                for cp in feed.results():
                    cp.wait()
            else:
                red.run([it])

    brought = [pltpu.make_async_copy(shared_ref.at[:, r], pack.at[r], bsem.at[r]) for r in range(pack.shape[0])]

    @pl.when(step == 0)
    def _():
        greet(me)
        for cp in brought:
            cp.start()
        feed.before()
        def body(c, carry):
            feed.block(c, blocks)
            for k, items in plan["feed"].items():
                pl.when(c == k)(functools.partial(act, items))
            return carry
        lax.fori_loop(0, blocks, body, 0)
        feed.settle(blocks - 1)
        act(plan["mid"])
        feed.after(blocks)
        act(plan["first"])
        for cp in brought:
            cp.wait()

    @pl.when(p == 0)
    def _():
        lay_out(me, lambda j: pack.at[b, j], 2 * NZ, span, cond_ref, dl, ds, hl, hs)
        dqr_ref[...] = jnp.zeros_like(dqr_ref)
        ddl[...] = jnp.zeros_like(ddl)
        dds[...] = jnp.zeros_like(dds)

    rows_at = pl.ds(pl.multiple_of(b * nq, nq), nq)
    lanes_at = pl.ds(pl.multiple_of(p * 128, 128), 128)
    pair_back(span, chunk, p, qh_ref, qr_ref, Pair(hl, p), Pair(hs, p), dl, ds, cond_ref, bl_ref, bs_ref, lse_ref,
              feed.hb[rows_at, lanes_at], feed.n2[rows_at, lanes_at], dqh_ref, dqr_ref, Pair(dhl, p), Pair(dhs, p), ddl, dds)

    @pl.when(p == PAIRS - 1)
    def _():
        pack_up(me, b, span, cond_ref, pack, ddl, dds, dhl, dhs)
        row.begin(b)

    for s, items in plan["steps"].items():
        pl.when(step == s)(functools.partial(act, items))

def backward(qh, qr, shared, cond, bl, bs, lse, tokens, heads_out, cotangent, w_out, w_gate, w_up, w_down, gain_two, units, plan, cid):
    rows, pairs, _, nq = qh.shape
    n = shared.shape[0]
    span = nq // 2
    nk = n * span
    width, ff = w_gate.shape
    count = rows * nq
    full = lambda *s: pl.BlockSpec((1, *s), lambda b, p: (b, *([0] * len(s))))
    pairb = lambda *s: pl.BlockSpec((1, 1, *s), lambda b, p: (b, p, *([0] * len(s))))
    sd = jax.ShapeDtypeStruct
    DMA = pltpu.SemaphoreType.DMA
    V = pltpu.VMEM
    whole = pl.BlockSpec(memory_space=pltpu.VMEM)
    far = pl.BlockSpec(memory_space=pl.ANY)
    part = shared.shape[2:]
    scratch = [V((1, 256, nk), BF16)] * 2 + [V((PAIRS, 8, nk), F32)] * 2 + [V((1, 256, nk), F32)] * 2 + [V((PAIRS, 8, nk), F32)] * 2
    scratch += [V((rows, n, *part), BF16), V((rows, NZ, *part), BF16), V((rows, NZ - 1, *part), BF16)] + [DMA((rows, NZ))] * 4 + [DMA((rows,))]
    scratch += [V((count, width), BF16)] * 4 + [V((width, count), BF16)] + [V((count, width), F32)] * 2
    scratch += [V((4, width, FFC), BF16), V((2, FFC, width), BF16)] + [V((n, width // n, FFC), BF16)] * 2 + [V((FFC, width), BF16)] + [V((count, FFC), BF16)] * 2 + [V((FFC, count), BF16)]
    scratch += [DMA((3, rows)), DMA((3, 4)), DMA((3,))]
    shard = (n, width // n)
    sums = [sd((width // n, width), BF16), sd((width // n, ff), BF16), sd((width // n, ff), BF16), sd((ff // n, width), BF16)]
    grads = [sd((*shard, width), BF16), sd((*shard, ff), BF16), sd((*shard, ff), BF16), sd((ff, width), BF16)]
    return pl.pallas_call(
        functools.partial(back_kernel, span, min(512, nk), units, plan, ff // FFC),
        grid=(rows, pairs),
        out_shape=[sd((rows, pairs, 12, nq), F32), sd((rows, 384, nq), F32), sd((rows, *part), BF16), sd((rows, nq, width), BF16),
                   sd((rows, nq, width), F32), sd((1, width), F32)] + sums + grads,
        in_specs=[pairb(12, nq), full(384, nq), far, pl.BlockSpec((1, nk), lambda b, p: (0, 0)), full(1, nk), full(1, nk), full(nq, 128)] + [far] * 7 + [whole],
        out_specs=[pairb(12, nq), full(384, nq), whole, far, far, whole] + [far] * 8,
        scratch_shapes=scratch + reduce_scratch(units),
        compiler_params=pltpu.CompilerParams(collective_id=cid, has_side_effects=True, vmem_limit_bytes=60 << 20),
        name="backward",
    )(qh, qr, shared, cond, bl, bs, lse, tokens, heads_out, cotangent, w_out, w_gate, w_up, w_down, gain_two)[:10]

class Gather:
    def __init__(self, me, units, ins, outs, sems):
        self.me, self.units, self.ins, self.outs = me, units, ins, outs
        self.zs, self.zr, self.xs, self.xr, self.ys, self.yr, self.cs, self.cr, self.ls = sems

    def remote(self, src, dst, ss, rs, dev):
        return pltpu.make_async_remote_copy(src_ref=src, dst_ref=dst, send_sem=ss, recv_sem=rs, device_id=dev, device_id_type=MESH)

    def view(self, k, shard, y, c):
        u = self.units[k]
        return self.part(u, self.outs[u.arr].at[shard], y, c)

    @staticmethod
    def part(u, ref, y, c):
        return rect(u, ref, 2 * c + y, 4) if u.flow == "P" else rect(u, ref, c, 2)

    def first(self, k, ss, rs, dev):
        u, me = self.units[k], self.me
        return self.remote(self.part(u, self.ins[u.arr], me.y, me.c), self.view(k, me.seq, me.y, me.c), ss, rs, dev)

    def onward(self, k, shard, y, ss, rs, dev):
        v = self.view(k, shard, y, self.me.c)
        return self.remote(v, v, ss, rs, dev)

    def zsend(self, k, zz):
        return self.first(k, self.zs.at[k, zz], self.zr.at[k, self.me.z], (2 * zz + self.me.x, self.me.batch))

    def zrecv(self, k, zz):
        me = self.me
        return self.onward(k, 2 * zz + me.x, me.y, self.zs.at[k, zz], self.zr.at[k, zz], (2 * zz + me.x, me.batch))

    def xown(self, k):
        return self.first(k, self.xs.at[k, self.me.z], self.xr.at[k, self.me.z], self.me.xp)

    def xsend(self, k, zz):
        return self.onward(k, 2 * zz + self.me.x, self.me.y, self.xs.at[k, zz], self.xr.at[k, zz], self.me.xp)

    def xrecv(self, k, zz):
        return self.onward(k, 2 * zz + 1 - self.me.x, self.me.y, self.xs.at[k, zz], self.xr.at[k, zz], self.me.xp)

    def ycopy(self, k, shard, mine):
        return self.onward(k, shard, self.me.y if mine else 1 - self.me.y, self.ys.at[k, shard], self.yr.at[k, shard], self.me.yp)

    def ccopy(self, k, w, shard):
        return self.onward(k, shard, self.me.y if w == 0 else 1 - self.me.y, self.cs.at[k, w, shard], self.cr.at[k, w, shard], self.me.cp)

    def crecv(self, k, w, shard):
        v = self.view(k, shard, self.me.y if w == 0 else 1 - self.me.y, 1 - self.me.c)
        return self.remote(v, v, self.cs.at[k, w, shard], self.cr.at[k, w, shard], self.me.cp)

    def local(self, a):
        return pltpu.make_async_copy(self.ins[a], self.outs[a].at[self.me.seq], self.ls.at[a])

    def other(self, i):
        return lax.rem(self.me.z + i, NZ)

    def begin(self, k, i):
        self.zsend(k, self.other(i)).start()
        pl.when(i == 1)(lambda: self.xown(k).start())

    def spread(self, k, shard):
        if self.units[k].flow == "P":
            self.ycopy(k, shard, True).start()
        self.ccopy(k, 0, shard).start()

    def z(self, k, i):
        zz = self.other(i)
        self.zrecv(k, zz).wait_recv()
        self.xsend(k, zz).start()
        self.spread(k, 2 * zz + self.me.x)

    def x(self, k, i):
        zz = self.other(i)
        self.xrecv(k, zz).wait_recv()
        self.spread(k, 2 * zz + 1 - self.me.x)

    def far(self, i):
        return 2 * self.other(i) + jnp.where(i < NZ, self.me.x, 1 - self.me.x)

    def y(self, k, i):
        shard = self.far(i)
        self.ycopy(k, shard, False).wait_recv()
        self.ccopy(k, 1, shard).start()

    def got(self, k, i):
        for w in range(2 if self.units[k].flow == "P" else 1):
            self.crecv(k, w, self.far(i)).wait_recv()

    def sent(self, k, i):
        me = self.me
        pl.when(i < NZ)(lambda: self.zsend(k, self.other(i)).wait_send())
        pl.when(i < NZ)(lambda: self.xsend(k, self.other(i)).wait_send())
        pl.when(i == NZ)(lambda: self.xown(k).wait_send())
        shard = self.far(i)
        self.ccopy(k, 0, shard).wait_send()
        if self.units[k].flow == "P":
            self.ycopy(k, shard, True).wait_send()
            self.ccopy(k, 1, shard).wait_send()

    def run(self, plan):
        for step, k, first, n in plan:
            fn = getattr(self, step)
            def body(i, c):
                fn(k, i)
                return c
            lax.fori_loop(first, first + n, body, 0)

class RowsGather:
    def __init__(self, me, shared, zs, zr, xs, xr):
        self.me, self.shared, self.zs, self.zr, self.xs, self.xr = me, shared, zs, zr, xs, xr

    def copy(self, b, shard, ss, rs, dev):
        v = self.shared.at[shard, b]
        return pltpu.make_async_remote_copy(src_ref=v, dst_ref=v, send_sem=ss, recv_sem=rs, device_id=dev, device_id_type=MESH)

    def zsend(self, b, zz):
        me = self.me
        return self.copy(b, me.seq, self.zs.at[b, zz], self.zr.at[b, me.z], (2 * zz + me.x, me.batch))

    def zrecv(self, b, zz):
        me = self.me
        return self.copy(b, 2 * zz + me.x, self.zs.at[b, zz], self.zr.at[b, zz], (2 * zz + me.x, me.batch))

    def xsend(self, b, zz):
        return self.copy(b, 2 * zz + self.me.x, self.xs.at[b, zz], self.xr.at[b, zz], self.me.xp)

    def xrecv(self, b, zz):
        return self.copy(b, 2 * zz + 1 - self.me.x, self.xs.at[b, zz], self.xr.at[b, zz], self.me.xp)

    def loop(self, first, fn):
        def body(i, c):
            fn(lax.rem(self.me.z + i, NZ))
            return c
        lax.fori_loop(first, NZ, body, 0)

    def begin(self, b):
        self.loop(1, lambda zz: self.zsend(b, zz).start())
        self.xsend(b, self.me.z).start()

    def z(self, b):
        def one(zz):
            self.zrecv(b, zz).wait_recv()
            self.xsend(b, zz).start()
        self.loop(1, one)

    def x(self, b):
        self.loop(0, lambda zz: self.xrecv(b, zz).wait_recv())

    def end(self, b):
        self.loop(1, lambda zz: self.zsend(b, zz).wait_send())
        self.loop(0, lambda zz: self.xsend(b, zz).wait_send())

def turn_rows(u, cosine, sine):
    out = []
    for r in range(0, u.shape[0], 64):
        a, b = u[r:r + 32], u[r + 32:r + 64]
        out += [a * cosine - b * sine, b * cosine + a * sine]
    return jnp.concatenate(out, 0)

def project(me, span, tok_ref, small_ref, cos_ref, sin_ref, normed_ref, qh_ref, qr_ref, shared_ref, gain_ref, b):
    nq = 2 * span
    d = tok_ref.shape[-1]
    gains = small_ref[:, :, 768:896].reshape(d, 128).astype(F32).T
    x = tok_ref[b].astype(F32)
    unit = x * lax.rsqrt(jnp.mean(x * x, -1, keepdims=True) + 1e-6)
    normed = (unit * gains[32:33]).astype(BF16)
    normed_ref[b] = normed
    gain_ref[...] = gains[33:34]
    w = small_ref[...].reshape(d, 896)
    f = nn(normed, w).T
    qh_ref[b] = f[:96].reshape(PAIRS, 12, nq)
    cosine, sine = cos_ref[...], sin_ref[...]
    qr_ref[b] = turn_rows(f[96:480], cosine, sine)
    own = jnp.concatenate([turn_rows(f[480:608], cosine, sine), f[608:800]], 0)
    shared_ref[me.seq, b] = own.astype(BF16)

def forward_kernel(span, chunk, units, narr, plan, tok_ref, cos_ref, sin_ref, cond_ref, bl_ref, bs_ref, *refs):
    ins = refs[:narr]
    normed_ref, qh_ref, qr_ref, shared_out, o_ref, lse_ref, gain_ref = refs[narr:narr + 7]
    outs = refs[narr + 7:2 * narr + 7]
    shared_ref, small, saved, dl, ds, hl, hs, s1, s2, rzs, rzr, rxs, rxr = refs[2 * narr + 7:2 * narr + 20]
    small_out, outs = outs[0], (small, *outs[1:])
    me = Place()
    b, p = pl.program_id(0), pl.program_id(1)
    step = b * PAIRS + p
    gat = Gather(me, units, ins, outs, refs[2 * narr + 20:])
    saves = (pltpu.make_async_copy(small, small_out, saved.at[0]), pltpu.make_async_copy(shared_ref, shared_out, saved.at[1]))
    row = RowsGather(me, shared_ref, rzs, rzr, rxs, rxr)

    def act(items):
        for it in items:
            if it[0] == "row":
                getattr(row, it[1])(it[2])
            elif it[0] == "project":
                for r in range(tok_ref.shape[0]):
                    project(me, span, tok_ref, small, cos_ref, sin_ref, normed_ref, qh_ref, qr_ref, shared_ref, gain_ref, r)
            elif it[0] == "local":
                for a in range(narr):
                    gat.local(a).start()
                gat.local(0).wait()
            elif it[0] == "locals":
                for a in range(1, narr):
                    gat.local(a).wait()
                for save in saves:
                    save.start()
                for save in saves:
                    save.wait()
            else:
                gat.run([it])

    @pl.when(step == 0)
    def _():
        greet(me)
        act(plan["first"])

    @pl.when(p == 0)
    def _():
        lay_out(me, lambda j: shared_ref.at[j, b], 2 * NZ, span, cond_ref, dl, ds, hl, hs)

    pair_forward(span, chunk, p, qh_ref[b, p], qr_ref[b], hl[p], hs[p], dl, ds, cond_ref, bl_ref, bs_ref, o_ref, lse_ref, s1, s2)

    for s, items in plan["steps"].items():
        pl.when(step == s)(functools.partial(act, items))

def forward(tokens, cosine, sine, cond, bl, bs, weights, units, plan, cid):
    rows, nq, width = tokens.shape
    span = nq // 2
    n = 2 * NZ
    nk = n * span
    narr, nu = len(weights), len(units)
    chunk = min(512, nk)
    whole = pl.BlockSpec(memory_space=pltpu.VMEM)
    far = pl.BlockSpec(memory_space=pl.ANY)
    full = lambda *s: pl.BlockSpec((1, *s), lambda b, p: (b, *([0] * len(s))))
    sd = jax.ShapeDtypeStruct
    DMA = pltpu.SemaphoreType.DMA
    V = pltpu.VMEM
    scratch = [V((n, rows, 320, nq), BF16), V((n, *weights[0].shape), BF16), DMA((2,))] + [V((1, 256, nk), BF16)] * 2 + [V((PAIRS, 8, nk), F32)] * 2 + [V((nq, nk), F32)] * 2 + [DMA((rows, NZ))] * 4
    scratch += [DMA((nu, NZ))] * 4 + [DMA((nu, n))] * 2 + [DMA((nu, 2, n))] * 2 + [DMA((narr,))]
    return pl.pallas_call(
        functools.partial(forward_kernel, span, chunk, units, narr, plan),
        grid=(rows, PAIRS),
        out_shape=[sd((rows, nq, width), BF16), sd((rows, PAIRS, 12, nq), F32), sd((rows, 384, nq), F32), sd((n, rows, 320, nq), BF16),
                   sd((rows, nq, width), BF16), sd((rows, nq, 128), F32), sd((1, width), F32)] + [sd((n, *a.shape), a.dtype) for a in weights],
        in_specs=[whole, whole, whole, pl.BlockSpec((1, nk), lambda b, p: (0, 0)), full(1, nk), full(1, nk)] + [far] * narr,
        out_specs=[whole, whole, whole, far, pl.BlockSpec((1, nq, 128), lambda b, p: (b, 0, p)), full(nq, 128), whole] + [far] * narr,
        scratch_shapes=scratch,
        compiler_params=pltpu.CompilerParams(collective_id=cid, has_side_effects=True, vmem_limit_bytes=62 << 20),
        name="forward",
    )(tokens, cosine, sine, cond, bl, bs, *weights)

def products_kernel(dqh_ref, dqr_ref, mine_ref, cos_ref, sin_ref, normed_ref, small_ref, tok_ref, res_ref, gain_two_ref, input_ref, out_ref, acc, sums):
    b = pl.program_id(0)
    d = tok_ref.shape[-1]
    nq = tok_ref.shape[1]
    @pl.when(b == 0)
    def _():
        acc[...] = jnp.zeros_like(acc)
        sums[...] = jnp.zeros_like(sums)
    cosine, sine = cos_ref[...], -sin_ref[...]
    mine = mine_ref[0].astype(F32)
    turned = jnp.concatenate([dqh_ref[0].reshape(96, nq), turn_rows(dqr_ref[0], cosine, sine), turn_rows(mine[:128], cosine, sine), mine[128:],
                              jnp.zeros((96, nq), F32)], 0)
    acc[...] += nn(turned.astype(BF16), normed_ref[0])
    w = small_ref[...].reshape(d, 896)
    gain = small_ref[:, :, 768:896].reshape(d, 128).astype(F32).T[32:33]
    back = nt(turned.T.astype(BF16), w)
    for r in range(0, nq, 128):
        sl = slice(r, r + 128)
        x = tok_ref[0, sl, :].astype(F32)
        scale = lax.rsqrt(jnp.mean(x * x, -1, keepdims=True) + 1e-6)
        unit = x * scale
        dn = back[sl]
        sums[...] += jnp.sum((dn * unit).reshape(16, 8, d), 0)
        e1 = dn * gain
        input_ref[0, sl, :] = res_ref[0, sl, :] + scale * (e1 - unit * jnp.mean(e1 * unit, -1, keepdims=True))
    @pl.when(b == pl.num_programs(0) - 1)
    def _():
        total = jnp.sum(sums[...], 0, keepdims=True)
        for s in range(out_ref.shape[0]):
            sl = slice(s * 128, s * 128 + 128)
            out_ref[s, :800, :] = acc[:800, sl].astype(BF16)
            out_ref[s, 800:, :] = jnp.concatenate([total[:, sl], gain_two_ref[:, sl], jnp.zeros((94, 128), F32)], 0).astype(BF16)

def products(dqh, dqr, mine, cosine, sine, normed, small, tokens, d_resid, gain_two):
    rows, nq, d = tokens.shape
    n = small.shape[0]
    row = lambda a: pl.BlockSpec((1, *a.shape[1:]), lambda b: (b, *([0] * (a.ndim - 1))))
    one = lambda a: pl.BlockSpec(a.shape, lambda b: (0,) * a.ndim)
    sd = jax.ShapeDtypeStruct
    return pl.pallas_call(
        products_kernel,
        grid=(rows,),
        out_shape=[sd(tokens.shape, F32), sd((n, 896, d // n), BF16)],
        in_specs=[row(dqh), row(dqr), row(mine), one(cosine), one(sine), row(normed), one(small), row(tokens), row(d_resid), one(gain_two)],
        out_specs=[row(tokens), pl.BlockSpec((n, 896, d // n), lambda b: (0, 0, 0))],
        scratch_shapes=[pltpu.VMEM((896, d), F32), pltpu.VMEM((8, d), F32)],
        compiler_params=pltpu.CompilerParams(vmem_limit_bytes=62 << 20),
        name="products",
    )(dqh, dqr, mine, cosine, sine, normed, small, tokens, d_resid, gain_two)

def results_kernel(small_ref, out_ref, gate_ref, up_ref, down_ref, qh_ref, qd_ref, kh_ref, kd_ref, vh_ref, vd_ref, g1_ref, g2_ref, o_ref, g_ref, u_ref, d_ref):
    for src, dst in ((out_ref, o_ref), (gate_ref, g_ref), (up_ref, u_ref), (down_ref, d_ref)):
        dst[...] = src[...].astype(F32)
    @pl.when(pl.program_id(0) == 0)
    def _():
        flat = small_ref[...].astype(F32)
        g1_ref[...] = flat[800:801]
        g2_ref[...] = flat[801:802]
        across = flat.T.astype(BF16)
        def pick(lo, hi, n, source):
            i = lax.broadcasted_iota(jnp.int32, (hi - lo, n), 0)
            j = lax.broadcasted_iota(jnp.int32, (hi - lo, n), 1)
            return nn(across[:, lo:hi], jnp.where(i == source(j), 1.0, 0.0).astype(BF16))
        pair = lambda j: (j & 15) >> 1
        rank = lambda j: j >> 4
        qh_ref[...] = pick(0, 128, 96, lambda j: pair(j) * 12 + rank(j) * 2 + (j & 1)).T
        qd_ref[...] = pick(0, 512, 384, lambda j: j + 96)
        kd_ref[...] = pick(384, 640, 128, lambda j: j + 96)
        vd_ref[...] = pick(512, 768, 128, lambda j: j + 96)
        kh_ref[...] = pick(640, 896, 32, lambda j: pair(j) * 8 + rank(j) * 2 + (j & 1) + 96).T
        vh_ref[...] = pick(640, 896, 32, lambda j: pair(j) * 8 + rank(j) * 2 + (j & 1) + 100).T

def results(small, out, gate, up, down):
    steps = 2
    n = small.shape[1]
    part = lambda a: pl.BlockSpec((a.shape[0] // steps, a.shape[1]), lambda i: (i, 0))
    one = lambda *s: pl.BlockSpec(s, lambda i: (0, 0))
    sd = lambda *s: jax.ShapeDtypeStruct(s, F32)
    shapes = [(96, n), (n, 384), (32, n), (n, 128), (32, n), (n, 128), (1, n), (1, n)]
    big = (out, gate, up, down)
    return pl.pallas_call(
        results_kernel,
        grid=(steps,),
        out_shape=[sd(*s) for s in shapes] + [sd(*a.shape) for a in big],
        in_specs=[one(*small.shape)] + [part(a) for a in big],
        out_specs=[one(*s) for s in shapes] + [part(a) for a in big],
        compiler_params=pltpu.CompilerParams(vmem_limit_bytes=62 << 20),
        name="results",
    )(small, *big)

def prepare_kernel(n, span, order, lengths, inverse, qh, qd, kh, kd, vh, vd, g1, g2, small_ref, cond_ref, bl_ref, bs_ref, cos_ref, sin_ref):
    me = lax.axis_index("seq")
    rows = bl_ref.shape[0]
    lane = lax.broadcasted_iota(jnp.int32, (1, span), 1)
    own = order[0, me]
    for i in range(n):
        j = lax.rem(me + i, n)
        sl = slice(i * span, (i + 1) * span)
        low = order[0, j]
        chosen = low < own
        sel = jnp.where(chosen, low, order[1, j])
        cond_ref[:, sl] = jnp.full((1, span), jnp.where(chosen, 1.0, 0.0), F32)
        for b in range(rows):
            bl_ref[b, :, sl] = jnp.where(lane + low * span < lengths[b], 0.0, NEG)
            bs_ref[b, :, sl] = jnp.where(lane + sel * span < lengths[b], 0.0, NEG)
    for k in range(2):
        angle = inverse[...] * (lane + order[k, me] * span).astype(F32)
        sl = slice(k * span, (k + 1) * span)
        cos_ref[:, sl] = jnp.cos(angle)
        sin_ref[:, sl] = jnp.sin(angle)
    def place(ref, target, turned=False):
        value = ref[...].astype(F32).T.astype(BF16) if turned else ref[...]
        i = lax.broadcasted_iota(jnp.int32, (value.shape[1], 896), 0)
        j = lax.broadcasted_iota(jnp.int32, (value.shape[1], 896), 1)
        return nn(value, jnp.where(j == target(i), 1.0, 0.0).astype(BF16))
    pair = lambda i: (i & 15) >> 1
    rank = lambda i: i >> 4
    out = place(qh, lambda i: pair(i) * 12 + rank(i) * 2 + (i & 1), True) + place(qd, lambda i: i + 96)
    out = out + place(kd, lambda i: i + 480) + place(vd, lambda i: i + 608)
    out = out + place(kh, lambda i: 736 + pair(i) * 8 + rank(i) * 2 + (i & 1), True)
    out = out + place(vh, lambda i: 740 + pair(i) * 8 + rank(i) * 2 + (i & 1), True)
    d = out.shape[0]
    eye = lax.broadcasted_iota(jnp.int32, (d, d), 0) == lax.broadcasted_iota(jnp.int32, (d, d), 1)
    at = lax.broadcasted_iota(jnp.int32, (d, 896), 1)
    for ref, column in ((g1, 800), (g2, 801)):
        gain = jnp.sum(jnp.where(eye, ref[...].astype(F32), 0.0), 1, keepdims=True)
        out = jnp.where(at == column, gain, out)
    small_ref[...] = out.astype(BF16)

def prepare(span_order, lengths, inverse, query_heads, query_dims, key_heads, key_dims, value_heads, value_dims, gain_one, gain_two, slots):
    n, rows = span_order.shape[0], lengths.shape[0]
    span = slots // 2
    d = query_heads.shape[0]
    smem = pl.BlockSpec(memory_space=pltpu.SMEM)
    whole = pl.BlockSpec(memory_space=pltpu.VMEM)
    sd = jax.ShapeDtypeStruct
    return pl.pallas_call(
        functools.partial(prepare_kernel, n, span),
        out_shape=[sd((d, 896), BF16), sd((1, n * span), F32), sd((rows, 1, n * span), F32), sd((rows, 1, n * span), F32), sd((32, slots), F32), sd((32, slots), F32)],
        in_specs=[smem, smem] + [whole] * 9,
        out_specs=[whole] * 6,
        compiler_params=pltpu.CompilerParams(vmem_limit_bytes=62 << 20),
        name="prepare",
    )(span_order.T, lengths, inverse, query_heads.T, query_dims, key_heads.T, key_dims, value_heads.T, value_dims, gain_one[None, :], gain_two[None, :])

HEADS, HDIM, QRANK, KVRANK = 16, 64, 6, 2
PAIRS = HEADS // 2
EPSILON = 1e-06


def rms_forward(values, gain):
    scale = lax.rsqrt(jnp.mean(values * values, -1, keepdims=True) + EPSILON)
    unit = values * scale
    return (unit * gain, unit, scale)


def rms_backward(grad_out, unit, scale, gain):
    scaled = grad_out * gain
    grad_in = scale * (scaled - unit * jnp.mean(scaled * unit, -1, keepdims=True))
    return (grad_in, jnp.sum(grad_out * unit, 0))


def rotation(positions):
    half = HDIM // 2
    index = jnp.arange(half).astype(F32)
    inverse = jnp.exp(index * (-math.log(10000.0) / half))
    angles = inverse[:, None] * positions.astype(F32)[None, :]
    return (jnp.cos(angles), jnp.sin(angles))


def rotate(u, cosine, sine):
    rows, depth, slots = u.shape
    v = u.reshape(rows, depth // HDIM, HDIM, slots)
    a, b = v[:, :, :HDIM // 2], v[:, :, HDIM // 2:]
    return jnp.concatenate([a * cosine - b * sine, b * cosine + a * sine], 2).reshape(u.shape)


def dot(a, b, ca, cb):
    return lax.dot_general(a, b, ((ca, cb), ((), ())), preferred_element_type=F32)


def pair_columns(a, ranks):
    return a.reshape(-1, ranks, PAIRS, 2).transpose(0, 2, 1, 3).reshape(a.shape)


def head_columns(a, ranks):
    return a.reshape(-1, PAIRS, ranks, 2).transpose(0, 2, 1, 3).reshape(a.shape)


GATHER_UNITS = [
    Unit(0, (0, 128), (0, 896), "P", 0), Unit(1, (0, 128), (0, 1024), "P", 0),
    Unit(2, (0, 128), (0, 1408), "P", 0), Unit(2, (0, 128), (1408, 1408), "P", 0),
    Unit(3, (0, 128), (0, 1408), "R", 0), Unit(3, (0, 128), (1408, 1408), "P", 0),
    Unit(4, (0, 176), (0, 1024), "P", 1), Unit(4, (176, 176), (0, 1024), "P", 1)]
GATHER_PLAN = {
    "first": [("local",), ("begin", 0, 1, 3), ("begin", 5, 1, 3), ("z", 0, 1, 3), ("x", 0, 0, 4), ("begin", 3, 1, 3), ("y", 0, 1, 7), ("begin", 2, 1, 3), ("got", 0, 1, 7), ("z", 5, 1, 3), ("begin", 7, 1, 3), ("project",), ("row", "begin", 0), ("z", 3, 1, 3), ("x", 5, 0, 4), ("z", 7, 1, 3), ("y", 5, 4, 4), ("z", 2, 1, 3), ("begin", 6, 1, 3), ("row", "z", 0), ("x", 3, 0, 4), ("row", "begin", 1), ("begin", 1, 1, 3), ("x", 7, 0, 4), ("row", "x", 0), ("z", 6, 1, 3), ("y", 7, 1, 3), ("y", 2, 1, 3)],
    "steps": {
        3: [("y", 3, 1, 3), ("y", 5, 1, 3), ("y", 7, 4, 4), ("row", "z", 1), ("x", 2, 0, 4)],
        4: [("begin", 4, 1, 3)],
        6: [("z", 1, 1, 3), ("y", 3, 4, 4)],
        7: [("row", "x", 1), ("x", 6, 0, 4)],
        11: [("y", 1, 1, 3), ("z", 4, 1, 3), ("x", 1, 0, 4), ("y", 6, 1, 3)],
        12: [("y", 2, 4, 4)],
        15: [("y", 1, 4, 4), ("x", 4, 0, 4), ("y", 6, 4, 4), ("got", 1, 1, 7), ("got", 2, 1, 7), ("got", 3, 1, 7), ("got", 4, 1, 7), ("got", 5, 1, 7), ("got", 6, 1, 7), ("got", 7, 1, 7), ("locals",), ("sent", 0, 1, 7), ("sent", 1, 1, 7), ("sent", 2, 1, 7), ("sent", 3, 1, 7), ("sent", 4, 1, 7), ("sent", 5, 1, 7), ("sent", 6, 1, 7), ("sent", 7, 1, 7), ("row", "end", 0), ("row", "end", 1)],
    },
}
REDUCE_UNITS = [
    Unit(1, (0, 128), (0, 1024), "P", 0), Unit(2, (0, 128), (0, 1024), "R", 0),
    Unit(1, (0, 128), (1024, 1024), "P", 0), Unit(2, (0, 128), (1024, 1024), "R", 0),
    Unit(1, (0, 128), (2048, 768), "P", 0), Unit(2, (0, 128), (2048, 768), "P", 0),
    Unit(3, (0, 176), (0, 1024), "P", 1), Unit(3, (176, 176), (0, 1024), "P", 1), Unit(0, (0, 128), (0, 1024), "P", 0)]
REDUCE_PLAN = {
    "feed": {
        4: [("begin", 0, 0, 8), ("begin", 1, 0, 8)],
        5: [("core", 0, 0, 4)],
        6: [("core", 1, 0, 4), ("core", 0, 4, 4)],
        7: [("y", 0, 0, 4)],
        8: [("begin", 2, 0, 8), ("begin", 3, 0, 8)],
        9: [("core", 2, 0, 4), ("y", 0, 4, 4), ("core", 1, 4, 4)],
    },
    "mid": [("begin", 5, 0, 8), ("begin", 7, 0, 8), ("x", 1, 0, 4), ("core", 2, 4, 4), ("core", 3, 0, 4), ("core", 5, 0, 4)],
    "first": [("begin", 4, 0, 8), ("core", 5, 4, 4), ("begin", 8, 0, 8), ("y", 2, 0, 4)],
    "steps": {
        0: [("y", 2, 4, 4), ("core", 4, 4, 4), ("core", 3, 4, 4), ("core", 7, 0, 4), ("x", 3, 0, 4), ("y", 5, 0, 4), ("core", 4, 0, 4)],
        2: [("core", 7, 4, 4), ("y", 5, 4, 4), ("x", 5, 0, 4)],
        4: [("y", 7, 0, 4), ("x", 0, 0, 4)],
        5: [("x", 2, 0, 4)],
        6: [("y", 4, 4, 4), ("y", 4, 0, 4), ("core", 8, 4, 4)],
        7: [("begin", 6, 0, 8), ("y", 7, 4, 4), ("x", 4, 0, 4), ("x", 7, 0, 4), ("core", 8, 0, 4)],
        8: [("core", 6, 0, 4)],
        10: [("y", 8, 0, 4), ("core", 6, 4, 4), ("row", "x", 0)],
        11: [("own", 5, 0, 1), ("own", 2, 0, 1), ("own", 7, 0, 1), ("y", 8, 4, 4), ("own", 4, 0, 1), ("y", 6, 0, 4)],
        12: [("x", 8, 0, 4)],
        13: [("y", 6, 4, 4)],
        14: [("last", 2, 0, 1), ("x", 6, 0, 4), ("last", 7, 0, 1)],
        15: [("own", 8, 0, 1), ("own", 1, 0, 1), ("row", "own", 0), ("own", 3, 0, 1), ("own", 0, 0, 1), ("row", "x", 1), ("last", 1, 0, 1), ("own", 6, 0, 1), ("last", 8, 0, 1), ("last", 0, 0, 1), ("last", 6, 0, 1), ("last", 4, 0, 1), ("last", 5, 0, 1), ("last", 3, 0, 1), ("row", "own", 1), ("end", 0, 0, 1), ("end", 1, 0, 1), ("end", 2, 0, 1), ("end", 3, 0, 1), ("end", 4, 0, 1), ("end", 5, 0, 1), ("end", 6, 0, 1), ("end", 7, 0, 1), ("end", 8, 0, 1), ("results",), ("row", "end", 0), ("row", "end", 1)],
    },
}
SMALL_UNITS = [Unit(0, (0, 384), (0, 128), "R", 0), Unit(0, (384, 512), (0, 128), "P", 0)]
SMALL_PLAN = [("begin", 0, 0, 8), ("begin", 1, 0, 8), ("core", 1, 0, 8), ("core", 0, 0, 8), ("x", 0, 0, 4), ("y", 1, 0, 8), ("own", 0, 0, 1), ("x", 1, 0, 4),
              ("last", 0, 0, 1), ("own", 1, 0, 1), ("last", 1, 0, 1), ("end", 0, 0, 1), ("end", 1, 0, 1)]


def reduce_far(arrays):
    out = []
    for a in arrays:
        own = lax.psum_scatter(a.astype(F32), "seq", scatter_dimension=0, tiled=True)[0]
        out.append(lax.psum(own.astype(BF16), "batch"))
    return out


def per_device(near, tokens, cotangent, lengths, span_order, attn_gain, query_heads, query_dims, key_heads, key_dims,
               value_heads, value_dims, out_proj, ffn_gain, gate_proj, up_proj, down_proj):
    rows, slots, width = tokens.shape
    span = slots // 2
    count = rows * slots
    nseq = span_order.shape[0]
    nk = nseq * span
    me = lax.axis_index("seq")
    flat = tokens.reshape(count, width).astype(F32)
    if near:
        inverse = jnp.exp(jnp.arange(HDIM // 2).astype(F32) * (-math.log(10000.0) / (HDIM // 2)))[:, None]
        small, cond, low_bias, sel_bias, cosine, sine = prepare(span_order, lengths, inverse, query_heads, query_dims, key_heads, key_dims,
                                                                value_heads, value_dims, attn_gain, ffn_gain, slots)
    else:
        key_value_heads = pair_columns(jnp.concatenate([key_heads, value_heads], 1), 4)
        small = jnp.concatenate([pair_columns(query_heads, QRANK), query_dims, key_dims, value_dims, key_value_heads, attn_gain[:, None], ffn_gain[:, None]], 1)
        small = jnp.pad(small, ((0, 0), (0, 896 - small.shape[1])))
        offsets = jnp.arange(span, dtype=jnp.int32)
        spans = jnp.concatenate([span_order, span_order], 0)
        spans = lax.dynamic_slice_in_dim(spans, me, nseq, 0)
        local_pos = (spans[0][:, None] * span + offsets[None, :]).reshape(-1)
        cosine, sine = rotation(local_pos)
        chosen = spans[:, 0] < spans[0, 0]
        low_pos = (spans[:, 0][:, None] * span + offsets[None, :]).reshape(1, nk)
        sel_pos = (jnp.where(chosen, spans[:, 0], spans[:, 1])[:, None] * span + offsets[None, :]).reshape(1, nk)
        cond = jnp.repeat(chosen.astype(F32), span).reshape(1, nk)
        low_bias = jnp.where(low_pos < lengths[:, None], 0.0, NEG)[:, None, :]
        sel_bias = jnp.where(sel_pos < lengths[:, None], 0.0, NEG)[:, None, :]
    masks = (cond, low_bias, sel_bias)
    weights = [small, out_proj, gate_proj, up_proj, down_proj]
    if near:
        by_row, qh, qr, shared, heads_out, lse, gain_two, *parts = forward(tokens, cosine, sine, *masks, weights, GATHER_UNITS, GATHER_PLAN, 0)
    else:
        parts = [lax.all_gather(a, "seq", axis=0) for a in weights]
    small, w_out, w_gate, w_up, w_down = [p.reshape(-1, p.shape[-1]) for p in parts]
    w_qkv = small[:, :800]
    gain_one = small[:, 800].astype(F32)
    normed_full, unit_one, scale_one = rms_forward(flat, gain_one)
    if not near:
        gain_two = small[:, 801].astype(F32)
        by_row = normed_full.astype(BF16).reshape(rows, slots, width)
        factors = jnp.stack([dot(w_qkv, by_row[b], (0,), (1,)) for b in range(rows)])
        qh = factors[:, :96].reshape(rows, PAIRS, 12, slots)
        qr = rotate(factors[:, 96:480], cosine, sine)
        own = jnp.concatenate([rotate(factors[:, 480:608], cosine, sine), factors[:, 608:800]], 1).astype(BF16)
        shared = lax.all_gather(own, "seq", axis=0)
        turned = lax.dynamic_slice_in_dim(jnp.concatenate([shared, shared], 0), me, nseq, 0)
        low, high = turned[..., :span], turned[..., span:]
        sel = jnp.where(chosen[:, None, None, None], low, high)
        low = low.transpose(1, 2, 0, 3).reshape(rows, 320, nk)
        sel = sel.transpose(1, 2, 0, 3).reshape(rows, 320, nk)
        in_pairs = lambda a: a[:, 256:].astype(F32).reshape(rows, PAIRS, 8, nk)
        factors = (in_pairs(low), in_pairs(sel), low[:, :256], sel[:, :256])
        heads_out, lse = attend(qh, qr, *factors, *masks)
    if near:
        dqh, dqr, mine, output, d_resid, gain_two_grad, *sums = backward(
            qh, qr, shared, *masks, lse, tokens, heads_out, cotangent, w_out, w_gate, w_up, w_down, gain_two, REDUCE_UNITS, REDUCE_PLAN, 1)
        input_grad, small_grad = products(dqh, dqr, mine, cosine, sine, by_row, parts[0], tokens, d_resid, gain_two_grad)
        small_sum = reduce_weights([small_grad], SMALL_UNITS, SMALL_PLAN, 3)[0]
        d_qh, d_qd, d_kh, d_kd, d_vh, d_vd, d_g1, d_g2, d_out, d_gate, d_up, d_down = results(small_sum, *sums)
        return (output, input_grad, d_g1[0], d_qh.T, d_qd, d_kh.T, d_kd, d_vh.T, d_vd, d_out, d_g2[0], d_gate, d_up, d_down)
    else:
        heads_flat = heads_out.reshape(count, width)

        resid = flat + dot(heads_flat, w_out, (1,), (0,))
        normed_two_full, unit_two, scale_two = rms_forward(resid, gain_two)
        normed_two = normed_two_full.astype(BF16)
        gate = dot(normed_two, w_gate, (1,), (0,))
        up_part = dot(normed_two, w_up, (1,), (0,))
        sigma = jax.nn.sigmoid(gate)
        hidden = (gate * sigma * up_part).astype(BF16)
        output = (resid + dot(hidden, w_down, (1,), (0,))).astype(BF16).reshape(rows, slots, width)

        grad_out = cotangent.reshape(count, width)
        down_grad = dot(hidden, grad_out, (0,), (0,)).astype(BF16)
        d_hidden = dot(grad_out, w_down, (1,), (1,))
        d_gate = (d_hidden * up_part * sigma * (1.0 + gate * (1.0 - sigma))).astype(BF16)
        d_up = (d_hidden * gate * sigma).astype(BF16)
        gate_grad = dot(normed_two, d_gate, (0,), (0,)).astype(BF16)
        up_grad = dot(normed_two, d_up, (0,), (0,)).astype(BF16)
        d_normed_two = dot(d_gate, w_gate, (1,), (1,)) + dot(d_up, w_up, (1,), (1,))
        d_mid, gain_two_grad = rms_backward(d_normed_two, unit_two, scale_two, gain_two)
        d_resid = grad_out.astype(F32) + d_mid
        d_attn = d_resid.astype(BF16)
        out_grad = dot(heads_flat, d_attn, (0,), (0,)).astype(BF16)
        d_heads = dot(d_attn, w_out, (1,), (1,)).astype(BF16).reshape(rows, slots, width)

        grads = [g.reshape(nseq, -1, g.shape[-1]) for g in (out_grad, gate_grad, up_grad, down_grad)]
        dqh, dqr, dhl, dhs, ddl, dds = attend_back(qh, qr, *factors, *masks, lse, heads_out, d_heads)
        from_low = jnp.concatenate([ddl, dhl.reshape(rows, 64, nk)], 1).reshape(rows, 320, nseq, span)
        from_sel = jnp.concatenate([dds, dhs.reshape(rows, 64, nk)], 1).reshape(rows, 320, nseq, span)
        pick = chosen[None, None, :, None]
        both = jnp.concatenate([from_low + jnp.where(pick, from_sel, 0.0), jnp.where(pick, 0.0, from_sel)], -1).transpose(2, 0, 1, 3)
        both = lax.dynamic_slice_in_dim(jnp.concatenate([both, both], 0), lax.rem(nseq - me, nseq), nseq, 0)
        mine = lax.psum_scatter(both, "seq", scatter_dimension=0, tiled=True)[0]
        sums = reduce_far(grads)
    mine = mine.astype(F32)
    turned = jnp.concatenate([dqh.reshape(rows, 96, slots), rotate(dqr, cosine, -sine), rotate(mine[:, :128], cosine, -sine), mine[:, 128:]], 1).astype(BF16)
    small_grad = dot(by_row, turned, (0, 1), (0, 2))
    d_normed = dot(turned, w_qkv, (1,), (1,)).reshape(count, width)
    d_first, gain_one_grad = rms_backward(d_normed, unit_one, scale_one, gain_one)
    input_grad = (d_resid + d_first).reshape(rows, slots, width)
    small_grad = jnp.concatenate([small_grad, gain_one_grad[:, None], gain_two_grad[:, None], jnp.zeros((width, 94), F32)], 1).astype(BF16)

    small_grad = small_grad.reshape(nseq, -1, 896)
    small_sum = reduce_far([small_grad])[0]
    small_sum = small_sum.astype(F32)
    out_sum, gate_sum, up_sum, down_sum = [g.astype(F32) for g in sums]
    key_value = head_columns(small_sum[:, 736:800], 4)
    return (output, input_grad, small_sum[:, 800], head_columns(small_sum[:, :96], QRANK), small_sum[:, 96:480], key_value[:, :32], small_sum[:, 480:608],
            key_value[:, 32:], small_sum[:, 608:736], out_sum, small_sum[:, 801], gate_sum, up_sum, down_sum)


def solution(mesh):
    near = mesh.shape["seq"] == 8 and mesh.shape["batch"] == 4
    by_slot = P("batch", "seq", None)
    line, table = P("seq"), P("seq", None)
    return jax.shard_map(
        functools.partial(per_device, near),
        mesh=mesh,
        in_specs=(by_slot, by_slot, P("batch"), P(), line, *([table] * 7), line, *([table] * 3)),
        out_specs=(by_slot, by_slot, line, *([table] * 7), line, *([table] * 3)),
        check_vma=False,
    )
```

```python
import functools
import math

import jax
import jax.numpy as jnp
from jax import lax
from jax.experimental import pallas as pl
from jax.experimental.pallas import tpu as pltpu
from jax.sharding import PartitionSpec as P


MESH = pl.DeviceIdType.MESH
NZ, NX = 4, 2

class Place:
    def __init__(self):
        self.seq = lax.axis_index("seq")
        self.batch = lax.axis_index("batch")
        self.z = self.seq // 2
        self.x = lax.rem(self.seq, 2)
        self.y = self.batch // 2
        self.c = lax.rem(self.batch, 2)
        self.up = (jnp.minimum(self.seq + 2, 7), self.batch)
        self.down = (jnp.maximum(self.seq - 2, 0), self.batch)
        self.xp = (self.seq + 1 - 2 * self.x, self.batch)
        self.yp = (self.seq, lax.rem(self.batch + 2, 4))
        self.cp = (self.seq, self.batch + 1 - 2 * self.c)

    def along(self, k):
        return (2 * lax.rem(self.z + k, NZ) + self.x, self.batch)

def greet(me):
    bar = pltpu.get_barrier_semaphore()
    def sig(d):
        pl.semaphore_signal(bar, inc=1, device_id=d, device_id_type=MESH)
    for k in range(1, NZ):
        sig(me.along(k))
    sig(me.xp); sig(me.yp); sig(me.cp)
    pl.semaphore_wait(bar, NZ + 2)

class Unit:
    def __init__(self, arr, row, col, flow, axis):
        self.arr, self.row, self.col, self.flow, self.axis = arr, row, col, flow, axis
        self.shape = (row[1], col[1])
        h = list(self.shape); h[axis] //= 2
        self.half = tuple(h)
        q = list(h)
        if flow == "P": q[axis] //= 2
        self.piece = tuple(q)

def rect(unit, ref, part, nparts):
    start = [unit.row[0], unit.col[0]]
    size = list(unit.shape)
    size[unit.axis] //= nparts
    idx = []
    for d in range(2):
        if d == unit.axis:
            off = part * size[d] + start[d]
            idx.append(pl.ds(pl.multiple_of(off, 16 if d == 0 else 128), size[d]))
        else:
            idx.append(pl.ds(start[d], size[d]))
    return ref.at[tuple(idx)]

def shard_of(ref, s, n=8):
    if len(ref.shape) == 3:
        return ref.at[s]
    rows = ref.shape[0] // n
    return ref.at[pl.ds(pl.multiple_of(s * rows, 16), rows)]

class Reduce:
    def __init__(self, me, units, ins, outs, scratch):
        self.me, self.units, self.ins, self.outs = me, units, ins, outs
        nu = len(units)
        self.A, self.RC, self.RY, self.RX, self.RZ, self.RF = [scratch[i * nu:(i + 1) * nu] for i in range(6)]
        self.ls, self.cs, self.cr, self.ys, self.yr, self.xs, self.xr, self.zs, self.zr, self.fs, self.fr, self.os_ = scratch[6 * nu:]

    def shard_at(self, i):
        me = self.me
        zz = lax.rem(me.z + 1 + lax.rem(i, NZ), NZ)
        xx = jnp.where(i < NZ, 1 - me.x, me.x)
        return zz, xx, 2 * zz + xx

    def sub(self, u, ref, y):
        if u.flow == "R":
            return ref
        n = u.piece[u.axis]
        idx = [slice(None)] * 2
        idx[u.axis] = pl.ds(pl.multiple_of(y * n, n), n)
        return ref.at[tuple(idx)]

    def remote(self, src, dst, ss, rs, dev):
        return pltpu.make_async_remote_copy(src_ref=src, dst_ref=dst, send_sem=ss, recv_sem=rs, device_id=dev, device_id_type=MESH)

    def core_copy(self, k, i):
        u = self.units[k]; zz, xx, s = self.shard_at(i)
        return self.remote(rect(u, shard_of(self.ins[u.arr], s), 1 - self.me.c, 2), self.RC[k].at[s], self.cs.at[k, s], self.cr.at[k, s], self.me.cp)

    def local_copy(self, k, i):
        u = self.units[k]; zz, xx, s = self.shard_at(i)
        return pltpu.make_async_copy(rect(u, shard_of(self.ins[u.arr], s), self.me.c, 2), self.A[k].at[s], self.ls.at[k, s])

    def y_copy(self, k, i):
        u = self.units[k]; zz, xx, s = self.shard_at(i)
        return self.remote(self.sub(u, self.A[k].at[s], 1 - self.me.y), self.RY[k].at[s], self.ys.at[k, s], self.yr.at[k, s], self.me.yp)

    def x_copy(self, k, zz):
        u, me = self.units[k], self.me
        return self.remote(self.sub(u, self.A[k].at[2 * zz + 1 - me.x], me.y), self.RX[k].at[zz], self.xs.at[k, zz], self.xr.at[k, zz], me.xp)

    def z_copy(self, k, zz):
        u, me = self.units[k], self.me
        return self.remote(self.mine(k, zz), self.RZ[k].at[self.slot(me.z, zz)], self.zs.at[k, zz], self.zr.at[k, me.z], (2 * zz + me.x, me.batch))

    @staticmethod
    def slot(source, owner):
        return lax.rem(source - owner + NZ, NZ) - 1

    def z_recv(self, k, zz):
        u, me = self.units[k], self.me
        v = self.RZ[k].at[self.slot(zz, me.z)]
        return self.remote(v, v, self.zs.at[k, zz], self.zr.at[k, zz], (2 * zz + me.x, me.batch))

    def mine(self, k, zz):
        return self.sub(self.units[k], self.A[k].at[2 * zz + self.me.x], self.me.y)

    @staticmethod
    def add(dst, src):
        dst[...] = dst[...] + src[...]

    def begin(self, k, i):
        self.core_copy(k, i).start()
        self.local_copy(k, i).start()

    def core(self, k, i):
        u = self.units[k]; zz, xx, s = self.shard_at(i)
        self.local_copy(k, i).wait()
        self.core_copy(k, i).wait_recv()
        self.add(self.A[k].at[s], self.RC[k].at[s])
        if u.flow == "P":
            self.y_copy(k, i).start()
        else:
            pl.when(i < NZ)(lambda: self.x_copy(k, zz).start())

    def y(self, k, i):
        u = self.units[k]; zz, xx, s = self.shard_at(i)
        self.y_copy(k, i).wait_recv()
        self.add(self.sub(u, self.A[k].at[s], self.me.y), self.RY[k].at[s])
        pl.when(i < NZ)(lambda: self.x_copy(k, zz).start())

    def x(self, k, i):
        me = self.me
        zz = lax.rem(me.z + 1 + i, NZ)
        self.x_copy(k, zz).wait_recv()
        self.add(self.mine(k, zz), self.RX[k].at[zz])
        pl.when(zz != me.z)(lambda: self.z_copy(k, zz).start())

    def fin_y(self, k):
        u, me = self.units[k], self.me
        mine = self.mine(k, me.z)
        dst = rect(u, self.outs[u.arr], 2 * me.c + me.y, 4) if u.flow == "P" else self.RF[k]
        return self.remote(mine, dst, self.fs.at[k, 0], self.fr.at[k, 0], me.yp)

    def fin_c(self, k, w):
        u, me = self.units[k], self.me
        if u.flow == "P":
            if w == 0:
                return self.remote(self.mine(k, me.z), rect(u, self.outs[u.arr], 2 * me.c + me.y, 4), self.fs.at[k, 1], self.fr.at[k, 1], me.cp)
            v = rect(u, self.outs[u.arr], 2 * me.c + 1 - me.y, 4)
            return self.remote(v, v, self.fs.at[k, 2], self.fr.at[k, 2], me.cp)
        return self.remote(self.RF[k], rect(u, self.outs[u.arr], me.c, 2), self.fs.at[k, 1], self.fr.at[k, 1], me.cp)

    def out_copy(self, k):
        u, me = self.units[k], self.me
        if u.flow == "P":
            return pltpu.make_async_copy(self.mine(k, me.z), rect(u, self.outs[u.arr], 2 * me.c + me.y, 4), self.os_.at[k])
        return pltpu.make_async_copy(self.RF[k], rect(u, self.outs[u.arr], me.c, 2), self.os_.at[k])

    def own(self, k, i):
        me = self.me
        def body(i, c):
            zz = lax.rem(me.z + i, NZ)
            self.z_recv(k, zz).wait_recv()
            self.add(self.mine(k, me.z), self.RZ[k].at[self.slot(zz, me.z)])
            return c
        lax.fori_loop(1, NZ, body, 0)
        self.fin_y(k).start()
        if self.units[k].flow == "P":
            self.out_copy(k).start()
            self.fin_c(k, 0).start()

    def last(self, k, i):
        self.fin_y(k).wait_recv()
        if self.units[k].flow == "P":
            self.fin_c(k, 1).start()
        else:
            self.add(self.RF[k], self.mine(k, self.me.z))
            self.out_copy(k).start()
            self.fin_c(k, 0).start()

    def end(self, k, i):
        me = self.me
        flow = self.units[k].flow
        for w in range(2 if flow == "P" else 1):
            self.fin_c(k, w).wait_recv()
            self.fin_c(k, w).wait_send()
        self.out_copy(k).wait()
        self.fin_y(k).wait_send()
        def body(i, c):
            self.core_copy(k, i).wait_send()
            if flow == "P": self.y_copy(k, i).wait_send()
            return c
        lax.fori_loop(0, 8, body, 0)
        def body(zz, c):
            self.x_copy(k, zz).wait_send()
            pl.when(zz != me.z)(lambda: self.z_copy(k, zz).wait_send())
            return c
        lax.fori_loop(0, NZ, body, 0)

    def run(self, plan):
        for step, k, first, n in plan:
            fn = getattr(self, step)
            if n == 1:
                fn(k, first)
            else:
                def body(i, c):
                    fn(k, i)
                    return c
                lax.fori_loop(first, first + n, body, 0)

def reduce_kernel(units, narr, plan, *refs):
    me = Place()
    greet(me)
    red = Reduce(me, units, refs[:narr], refs[narr:2 * narr], refs[2 * narr:])
    red.run(plan)

def reduce_scratch(units):
    nu = len(units)
    DMA = pltpu.SemaphoreType.DMA
    bf = jnp.bfloat16
    V = pltpu.VMEM
    return ([V((8, *u.half), bf) for u in units] + [V((8, *u.half), bf) for u in units]
        + [V((8, *u.piece) if u.flow == "P" else (16, 128), bf) for u in units] + [V((4, *u.piece), bf) for u in units]
        + [V((3, *u.piece), bf) for u in units] + [V(u.piece if u.flow == "R" else (16, 128), bf) for u in units]
        + [DMA((nu, 8))] * 5 + [DMA((nu, 4))] * 4 + [DMA((nu, 3))] * 2 + [DMA((nu,))])

def reduce_weights(arrays, units, plan, cid):
    narr = len(arrays)
    return pl.pallas_call(
        functools.partial(reduce_kernel, units, narr, plan),
        out_shape=[jax.ShapeDtypeStruct(a.shape[1:], a.dtype) for a in arrays],
        in_specs=[pl.BlockSpec(memory_space=pl.ANY)] * narr,
        out_specs=[pl.BlockSpec(memory_space=pl.ANY)] * narr,
        scratch_shapes=reduce_scratch(units),
        compiler_params=pltpu.CompilerParams(collective_id=cid, has_side_effects=True, vmem_limit_bytes=58 << 20),
        name="reduce_weights",
    )(*arrays)

F32, BF16 = jnp.float32, jnp.bfloat16
NEG = -1e30

def nn(a, b):
    return lax.dot_general(a, b, (((1,), (0,)), ((), ())), preferred_element_type=F32)

def nt(a, b):
    return lax.dot_general(a, b, (((1,), (1,)), ((), ())), preferred_element_type=F32)

def expand(heads, dims, base):
    parts = []
    for h in range(2):
        parts.append((heads[base + h:base + h + 1] * dims[0] + heads[base + 2 + h:base + 3 + h] * dims[1]) * 0.5)
    return jnp.concatenate(parts, 0)

def queries(qh, qr):
    parts = []
    for h in range(2):
        total = qh[h:h + 1] * qr[0:64]
        for r in range(1, 6):
            total = total + qh[2 * r + h:2 * r + h + 1] * qr[64 * r:64 * r + 64]
        parts.append(total)
    return jnp.concatenate(parts, 0) / 6.0

def lanes_below(shape, n):
    return lax.broadcasted_iota(jnp.int32, shape, 1) < n

def stack_heads(part):
    first = lanes_below(part.shape, 64)
    zero = jnp.zeros_like(part)
    return jnp.concatenate([jnp.where(first, part, zero), jnp.where(first, zero, part)], 0)

def unstack_heads(part):
    n = part.shape[0] // 2
    return jnp.where(lanes_below((n, 128), 64), part[:n], part[n:])

def causal_bias(n2, span):
    row = lax.broadcasted_iota(jnp.int32, (n2, span), 0) % span
    col = lax.broadcasted_iota(jnp.int32, (n2, span), 1)
    return jnp.where(col <= row, 0.0, NEG)

def pair_factors(heads, dims, cond, base, at):
    hl, hs = heads
    dl, ds = dims
    low = expand(hl, (dl[at:at + 64].astype(F32), dl[at + 64:at + 128].astype(F32)), base).astype(BF16)
    sel = expand(hs, (ds[at:at + 64].astype(F32), ds[at + 64:at + 128].astype(F32)), base)
    left = jnp.where(cond > 0.5, sel, 0.0).astype(BF16)
    right = jnp.where(cond > 0.5, 0.0, sel).astype(BF16)
    return low, jnp.concatenate([left, right], 0)

def attend_kernel(span, chunk, qh_ref, qr_ref, hl_ref, hs_ref, dl_ref, ds_ref, cond_ref, bl_ref, bs_ref, o_ref, lse_ref, s1, s2):
    pair_forward(span, chunk, pl.program_id(1), qh_ref[0, 0], qr_ref[0], hl_ref[0, 0], hs_ref[0, 0], dl_ref, ds_ref, cond_ref, bl_ref, bs_ref, o_ref, lse_ref, s1, s2)

def pair_forward(span, chunk, p, qh, qr, hl, hs, dl_ref, ds_ref, cond_ref, bl_ref, bs_ref, o_ref, lse_ref, s1, s2):
    n2 = 2 * span
    nk = dl_ref.shape[-1]
    qt = queries(qh, qr)
    q = (qt.astype(BF16).astype(F32).T * 0.125).astype(BF16)
    qlo, qhi = stack_heads(q[:span]), stack_heads(q[span:])
    qboth = jnp.concatenate([qlo, qhi], 1)
    heads = (hl, hs)
    dims = (dl_ref[0], ds_ref[0])
    cond = cond_ref[...]
    klo, ksel = pair_factors(heads, dims, cond, 0, 0)
    vlo, vsel = pair_factors(heads, dims, cond, 4, 128)
    tri = causal_bias(n2, span)
    width = min(128, chunk)
    mlo = jnp.full((n2, width), NEG, F32)
    mhi = jnp.full((n2, width), NEG, F32)
    s3 = nn(qlo, klo[:, :span]) + bl_ref[0][:, :span] + tri
    m3 = jnp.max(s3, -1, keepdims=True)
    for c in range(0, nk, chunk):
        sl = slice(c, c + chunk)
        a = nn(qhi, klo[:, sl]) + bl_ref[0][:, sl]
        s1[:, sl] = a
        b = nn(qboth, ksel[:, sl]) + bs_ref[0][:, sl]
        if c == 0:
            b = jnp.concatenate([b[:, :span] + tri, b[:, span:]], 1)
        s2[:, sl] = b
        for i in range(0, chunk, width):
            on = cond[:, c + i:c + i + width] > 0.5
            ai, bi = a[:, i:i + width], b[:, i:i + width]
            mlo = jnp.maximum(mlo, jnp.where(on, bi, NEG))
            mhi = jnp.maximum(mhi, jnp.maximum(ai, jnp.where(on, NEG, bi)))
    mlo = jnp.maximum(jnp.max(mlo, -1, keepdims=True), m3)
    mhi = jnp.max(mhi, -1, keepdims=True)
    e3 = jnp.exp(s3 - mlo)
    tlo = jnp.zeros((n2, width), F32)
    thi = jnp.zeros((n2, width), F32)
    o3 = nt(e3.astype(BF16), vlo[:, :span])
    o1 = jnp.zeros((n2, 128), F32)
    o2 = jnp.zeros((n2, 256), F32)
    for c in range(0, nk, chunk):
        sl = slice(c, c + chunk)
        on = cond[:, sl] > 0.5
        a = jnp.exp(s1[:, sl] - mhi)
        b = jnp.exp(s2[:, sl] - jnp.where(on, mlo, mhi))
        blo = jnp.where(on, b, 0.0)
        bhi = a + jnp.where(on, 0.0, b)
        for i in range(0, chunk, width):
            tlo = tlo + blo[:, i:i + width]
            thi = thi + bhi[:, i:i + width]
        o1 = o1 + nt(a.astype(BF16), vlo[:, sl])
        o2 = o2 + nt(b.astype(BF16), vsel[:, sl])
    llo = jnp.sum(tlo, -1, keepdims=True) + jnp.sum(e3, -1, keepdims=True)
    lhi = jnp.sum(thi, -1, keepdims=True)
    olo = unstack_heads((o2[:, :128] + o3) / llo)
    ohi = unstack_heads((o2[:, 128:] + o1) / lhi)
    o_ref[0] = jnp.concatenate([olo, ohi], 0).astype(BF16)
    lane = lax.broadcasted_iota(jnp.int32, (span, 128), 1)
    tlo = mlo + jnp.log(llo)
    thi = mhi + jnp.log(lhi)
    old = jnp.where(p == 0, 0.0, lse_ref[0])
    new = []
    for k, t in enumerate((tlo, thi)):
        part = old[k * span:(k + 1) * span]
        part = jnp.where(lane == 2 * p, t[:span], part)
        new.append(jnp.where(lane == 2 * p + 1, t[span:], part))
    lse_ref[0] = jnp.concatenate(new, 0)

def attend(qh, qr, hl, hs, dl, ds, cond, bl, bs):
    rows, pairs, _, nq = qh.shape
    nk = dl.shape[-1]
    span = nq // 2
    chunk = min(512, nk)
    full = lambda *s: pl.BlockSpec((1, *s), lambda b, p: (b, *([0] * len(s))))
    pairb = lambda *s: pl.BlockSpec((1, 1, *s), lambda b, p: (b, p, *([0] * len(s))))
    return pl.pallas_call(
        functools.partial(attend_kernel, span, chunk),
        grid=(rows, pairs),
        out_shape=[jax.ShapeDtypeStruct((rows, nq, pairs * 128), BF16), jax.ShapeDtypeStruct((rows, nq, 128), F32)],
        in_specs=[pairb(12, nq), full(384, nq), pairb(8, nk), pairb(8, nk), full(256, nk), full(256, nk),
                  pl.BlockSpec((1, nk), lambda b, p: (0, 0)), full(1, nk), full(1, nk)],
        out_specs=[pl.BlockSpec((1, nq, 128), lambda b, p: (b, 0, p)), full(nq, 128)],
        scratch_shapes=[pltpu.VMEM((nq, nk), F32), pltpu.VMEM((nq, nk), F32)],
        compiler_params=pltpu.CompilerParams(vmem_limit_bytes=56 << 20),
        name="attend",
    )(qh, qr, hl, hs, dl, ds, cond, bl, bs)

def attend_back_kernel(span, chunk, qh_ref, qr_ref, hl_ref, hs_ref, dl_ref, ds_ref, cond_ref, bl_ref, bs_ref, lse_ref, o_ref, g_ref,
                       dqh_ref, dqr_ref, dhl_ref, dhs_ref, ddl_ref, dds_ref):
    p = pl.program_id(1)
    @pl.when(p == 0)
    def _():
        dqr_ref[...] = jnp.zeros_like(dqr_ref)
        ddl_ref[...] = jnp.zeros_like(ddl_ref)
        dds_ref[...] = jnp.zeros_like(dds_ref)
    pair_back(span, chunk, p, qh_ref, qr_ref, Pair(hl_ref, 0, 0), Pair(hs_ref, 0, 0), dl_ref, ds_ref, cond_ref, bl_ref, bs_ref, lse_ref, o_ref[0], g_ref[0],
              dqh_ref, dqr_ref, Pair(dhl_ref, 0, 0), Pair(dhs_ref, 0, 0), ddl_ref, dds_ref)

class Pair:
    def __init__(self, ref, *at):
        self.ref, self.at = ref, at

    def all(self):
        return self.ref[self.at]

    def row(self, j, sl):
        return self.ref[(*self.at, slice(j, j + 1), sl)]

    def put(self, j, sl, value):
        self.ref[(*self.at, slice(j, j + 1), sl)] = value

def pair_back(span, chunk, p, qh_ref, qr_ref, hl, hs, dl_ref, ds_ref, cond_ref, bl_ref, bs_ref, lse_ref, o, g,
              dqh_ref, dqr_ref, dhl, dhs, ddl_ref, dds_ref):
    n2 = 2 * span
    nk = dl_ref.shape[-1]
    qh, qr = qh_ref[0, 0], qr_ref[0]
    qt = (queries(qh, qr).astype(BF16).astype(F32)) * 0.125
    q = qt.T.astype(BF16)
    qlo, qhi = stack_heads(q[:span]), stack_heads(q[span:])
    qboth = jnp.concatenate([qlo, qhi], 1)
    glo, ghi = stack_heads(g[:span]), stack_heads(g[span:])
    gboth = jnp.concatenate([glo, ghi], 1)
    gt = g.astype(F32).T
    first = lax.broadcasted_iota(jnp.int32, (128, span), 0) < 64
    def stack_lanes(part):
        return jnp.concatenate([jnp.where(first, part, 0.0), jnp.where(first, 0.0, part)], 1).astype(BF16)
    qtlo, qthi = stack_lanes(qt[:, :span]), stack_lanes(qt[:, span:])
    gtlo, gthi = stack_lanes(gt[:, :span]), stack_lanes(gt[:, span:])
    qtboth = jnp.concatenate([qtlo, qthi], 0)
    gtboth = jnp.concatenate([gtlo, gthi], 0)
    prod = g.astype(F32) * o.astype(F32)
    flane = lanes_below((n2, 128), 64)
    d0 = jnp.sum(jnp.where(flane, prod, 0.0), -1, keepdims=True)
    d1 = jnp.sum(jnp.where(flane, 0.0, prod), -1, keepdims=True)
    lane = lax.broadcasted_iota(jnp.int32, (n2, 128), 1)
    lse = lse_ref[0]
    l0 = jnp.sum(jnp.where(lane == 2 * p, lse, 0.0), -1, keepdims=True)
    l1 = jnp.sum(jnp.where(lane == 2 * p + 1, lse, 0.0), -1, keepdims=True)
    dello, delhi = jnp.concatenate([d0[:span], d1[:span]], 0), jnp.concatenate([d0[span:], d1[span:]], 0)
    lselo, lsehi = jnp.concatenate([l0[:span], l1[:span]], 0), jnp.concatenate([l0[span:], l1[span:]], 0)
    heads = (hl.all(), hs.all())
    dims = (dl_ref[0], ds_ref[0])
    cond = cond_ref[...]
    klo, ksel = pair_factors(heads, dims, cond, 0, 0)
    vlo, vsel = pair_factors(heads, dims, cond, 4, 128)
    tri = causal_bias(n2, span)

    def put(dkt, h, d_ref, hd, dd_ref, base, at, sl):
        for r in range(2):
            dim = d_ref[0, at + 64 * r:at + 64 * r + 64, sl].astype(F32)
            total = None
            for k in range(2):
                part = dkt[64 * k:64 * k + 64]
                j = base + 2 * r + k
                hd.put(j, sl, jnp.sum(part * dim, 0, keepdims=True) * 0.5)
                term = part * h.row(j, sl)
                total = term if total is None else total + term
            dd_ref[0, at + 64 * r:at + 64 * r + 64, sl] += total * 0.5

    s3 = nn(qlo, klo[:, :span]) + bl_ref[0][:, :span] + tri
    p3 = jnp.exp(s3 - lselo)
    dp3 = nn(glo, vlo[:, :span])
    ds3 = (p3 * (dp3 - dello)).astype(BF16)
    p3 = p3.astype(BF16)
    dq3 = nt(ds3, klo[:, :span])
    dk3 = nn(qtlo, ds3)
    dv3 = nn(gtlo, p3)
    dq1 = jnp.zeros((n2, 128), F32)
    dq2 = jnp.zeros((n2, 256), F32)
    for c in range(0, nk, chunk):
        sl = slice(c, c + chunk)
        pa = jnp.exp(nn(qhi, klo[:, sl]) + bl_ref[0][:, sl] - lsehi)
        dpa = nn(ghi, vlo[:, sl])
        dsa = (pa * (dpa - delhi)).astype(BF16)
        pa = pa.astype(BF16)
        dq1 = dq1 + nt(dsa, klo[:, sl])
        dk = nn(qthi, dsa)
        dv = nn(gthi, pa)
        if c == 0:
            dk = jnp.concatenate([dk[:, :span] + dk3, dk[:, span:]], 1)
            dv = jnp.concatenate([dv[:, :span] + dv3, dv[:, span:]], 1)
        put(dk, hl, dl_ref, dhl, ddl_ref, 0, 0, sl)
        put(dv, hl, dl_ref, dhl, ddl_ref, 4, 128, sl)
    for c in range(0, nk, chunk):
        sl = slice(c, c + chunk)
        on = cond[:, sl] > 0.5
        s = nn(qboth, ksel[:, sl]) + bs_ref[0][:, sl]
        if c == 0:
            s = jnp.concatenate([s[:, :span] + tri, s[:, span:]], 1)
        pb = jnp.exp(s - jnp.where(on, lselo, lsehi))
        dpb = nn(gboth, vsel[:, sl])
        dsb = (pb * (dpb - jnp.where(on, dello, delhi))).astype(BF16)
        pb = pb.astype(BF16)
        dq2 = dq2 + nt(dsb, ksel[:, sl])
        dk = nn(qtboth, dsb)
        dv = nn(gtboth, pb)
        dk = jnp.where(on, dk[:128], dk[128:])
        dv = jnp.where(on, dv[:128], dv[128:])
        put(dk, hs, ds_ref, dhs, dds_ref, 0, 0, sl)
        put(dv, hs, ds_ref, dhs, dds_ref, 4, 128, sl)
    dqlo = unstack_heads(dq2[:, :128] + dq3)
    dqhi = unstack_heads(dq2[:, 128:] + dq1)
    dqt = (jnp.concatenate([dqlo, dqhi], 0) * (0.125 / 6.0)).T
    for r in range(6):
        total = None
        for h in range(2):
            part = dqt[64 * h:64 * h + 64]
            j = 2 * r + h
            dqh_ref[0, 0, j:j + 1, :] = jnp.sum(part * qr[64 * r:64 * r + 64], 0, keepdims=True)
            term = part * qh[j:j + 1]
            total = term if total is None else total + term
        dqr_ref[0, 64 * r:64 * r + 64, :] += total

def attend_back(qh, qr, hl, hs, dl, ds, cond, bl, bs, lse, o, g):
    rows, pairs, _, nq = qh.shape
    nk = dl.shape[-1]
    span = nq // 2
    chunk = min(512, nk)
    full = lambda *s: pl.BlockSpec((1, *s), lambda b, p: (b, *([0] * len(s))))
    pairb = lambda *s: pl.BlockSpec((1, 1, *s), lambda b, p: (b, p, *([0] * len(s))))
    tok = pl.BlockSpec((1, nq, 128), lambda b, p: (b, 0, p))
    sd = jax.ShapeDtypeStruct
    return pl.pallas_call(
        functools.partial(attend_back_kernel, span, chunk),
        grid=(rows, pairs),
        out_shape=[sd((rows, pairs, 12, nq), F32), sd((rows, 384, nq), F32), sd((rows, pairs, 8, nk), F32), sd((rows, pairs, 8, nk), F32),
                   sd((rows, 256, nk), F32), sd((rows, 256, nk), F32)],
        in_specs=[pairb(12, nq), full(384, nq), pairb(8, nk), pairb(8, nk), full(256, nk), full(256, nk),
                  pl.BlockSpec((1, nk), lambda b, p: (0, 0)), full(1, nk), full(1, nk), full(nq, 128), tok, tok],
        out_specs=[pairb(12, nq), full(384, nq), pairb(8, nk), pairb(8, nk), full(256, nk), full(256, nk)],
        compiler_params=pltpu.CompilerParams(vmem_limit_bytes=56 << 20),
        name="attend_back",
    )(qh, qr, hl, hs, dl, ds, cond, bl, bs, lse, o, g)

class Rows:
    def __init__(self, me, pack, out, RX, RZ, xs, xr, zs, zr):
        self.me, self.pack, self.out, self.RX, self.RZ = me, pack, out, RX, RZ
        self.xs, self.xr, self.zs, self.zr = xs, xr, zs, zr

    def remote(self, src, dst, ss, rs, dev):
        return pltpu.make_async_remote_copy(src_ref=src, dst_ref=dst, send_sem=ss, recv_sem=rs, device_id=dev, device_id_type=MESH)

    def x_copy(self, b, zz):
        return self.remote(self.pack.at[b, 2 * zz + 1 - self.me.x], self.RX.at[b, zz], self.xs.at[b, zz], self.xr.at[b, zz], self.me.xp)

    def z_copy(self, b, zz):
        me = self.me
        return self.remote(self.mine(b, zz), self.RZ.at[b, Reduce.slot(me.z, zz)], self.zs.at[b, zz], self.zr.at[b, me.z], (2 * zz + me.x, me.batch))

    def z_recv(self, b, zz):
        me = self.me
        v = self.RZ.at[b, Reduce.slot(zz, me.z)]
        return self.remote(v, v, self.zs.at[b, zz], self.zr.at[b, zz], (2 * zz + me.x, me.batch))

    def mine(self, b, zz):
        return self.pack.at[b, 2 * zz + self.me.x]

    @staticmethod
    def add(dst, src):
        dst[...] = dst[...] + src[...]

    def begin(self, b):
        def body(i, c):
            self.x_copy(b, lax.rem(self.me.z + 1 + i, NZ)).start()
            return c
        lax.fori_loop(0, NZ, body, 0)

    def x(self, b):
        me = self.me
        def body(i, c):
            zz = lax.rem(me.z + 1 + i, NZ)
            self.x_copy(b, zz).wait_recv()
            self.add(self.mine(b, zz), self.RX.at[b, zz])
            pl.when(zz != me.z)(lambda: self.z_copy(b, zz).start())
            return c
        lax.fori_loop(0, NZ, body, 0)

    def own(self, b):
        me = self.me
        def body(i, c):
            zz = lax.rem(me.z + i, NZ)
            self.z_recv(b, zz).wait_recv()
            self.add(self.mine(b, me.z), self.RZ.at[b, Reduce.slot(zz, me.z)])
            return c
        lax.fori_loop(1, NZ, body, 0)
        self.out[b] = self.pack[b, me.seq]

    def end(self, b):
        me = self.me
        def sent(zz, c):
            self.x_copy(b, zz).wait_send()
            pl.when(zz != me.z)(lambda: self.z_copy(b, zz).wait_send())
            return c
        lax.fori_loop(0, NZ, sent, 0)

def lay_out(me, block, n, span, cond_ref, dl, ds, hl, hs):
    for i in range(n):
        j = lax.rem(me.seq + i, n)
        sl = slice(i * span, (i + 1) * span)
        on = cond_ref[:, sl] > 0.5
        low = block(j)[:256, :span].astype(F32)
        high = block(j)[:256, span:].astype(F32)
        dl[0, :, sl] = low.astype(BF16)
        ds[0, :, sl] = jnp.where(on, low, high).astype(BF16)
        low = block(j)[256:, :span].astype(F32)
        high = block(j)[256:, span:].astype(F32)
        hl[:, :, sl] = low.reshape(PAIRS, 8, span)
        hs[:, :, sl] = jnp.where(on, low, high).reshape(PAIRS, 8, span)

def pack_up(me, b, span, cond_ref, pack, ddl, dds, dhl, dhs):
    n = pack.shape[1]
    for i in range(n):
        j = lax.rem(me.seq + i, n)
        sl = slice(i * span, (i + 1) * span)
        on = cond_ref[:, sl] > 0.5
        for at, lo, se in ((0, ddl[0, :, sl], dds[0, :, sl]), (256, dhl[:, :, sl].reshape(64, span), dhs[:, :, sl].reshape(64, span))):
            rows = slice(at, at + lo.shape[0])
            pack[b, j, rows, :span] = (lo + jnp.where(on, se, 0.0)).astype(BF16)
            pack[b, j, rows, span:] = jnp.where(on, 0.0, se).astype(BF16)

FFC = 256

class Feed:
    def __init__(self, hbm, outs, grads, buf):
        self.tok, self.heads_hbm, self.cot, self.w_out, self.w_gate, self.w_up, self.w_down, self.gain = hbm
        self.output, self.d_resid, self.gain_grad = outs
        self.g_out, self.g_gate, self.g_up, self.g_down = grads
        (self.xb, self.hb, self.gb, self.n2, self.n2t, self.resid, self.acc, self.dlo, self.dhi, self.wa, self.wd, self.sg, self.su, self.sd, self.dg, self.du, self.hidt,
         self.lsem, self.wsem, self.ssem) = buf
        self.rows, self.nq, self.width = self.tok.shape
        self.count = self.rows * self.nq

    def load(self):
        out = []
        for i, (src, dst) in enumerate(((self.tok, self.xb), (self.heads_hbm, self.hb), (self.cot, self.gb))):
            for r in range(self.rows):
                out.append(pltpu.make_async_copy(src.at[r], dst.at[pl.ds(r * self.nq, self.nq)], self.lsem.at[i, r]))
        return out

    def out_part(self, j):
        return pltpu.make_async_copy(self.w_out.at[:, pl.ds(j * FFC, FFC)], self.wa.at[j], self.wsem.at[0, j])

    def weights(self, c):
        k = lax.rem(c, 2)
        at = pl.ds(pl.multiple_of(c * FFC, FFC), FFC)
        return (pltpu.make_async_copy(self.w_gate.at[:, at], self.wa.at[k], self.wsem.at[1, k]),
                pltpu.make_async_copy(self.w_up.at[:, at], self.wa.at[2 + k], self.wsem.at[1, 2 + k]),
                pltpu.make_async_copy(self.w_down.at[at], self.wd.at[k], self.wsem.at[2, k]))

    def stores(self, c):
        at = pl.ds(pl.multiple_of(c * FFC, FFC), FFC)
        return (pltpu.make_async_copy(self.sg, self.g_gate.at[:, :, at], self.ssem.at[0]),
                pltpu.make_async_copy(self.su, self.g_up.at[:, :, at], self.ssem.at[1]),
                pltpu.make_async_copy(self.sd, self.g_down.at[at], self.ssem.at[2]))

    def out_store(self, j):
        return pltpu.make_async_copy((self.sg, self.su)[j % 2], self.g_out.at[:, :, pl.ds(j * FFC, FFC)], self.ssem.at[j % 2])

    def before(self):
        parts = self.width // FFC
        loads = self.load() + [self.out_part(j) for j in range(parts)]
        for cp in loads:
            cp.start()
        for cp in loads:
            cp.wait()
        for j in range(parts):
            sl = slice(j * FFC, (j + 1) * FFC)
            self.resid[:, sl] = self.xb[:, sl].astype(F32) + nn(self.hb[...], self.wa[j])
        for cp in self.weights(0):
            cp.start()
        gain = self.gain[...]
        for r in range(0, self.count, 128):
            sl = slice(r, r + 128)
            v = self.resid[sl, :]
            self.acc[sl, :] = v
            n2 = v * lax.rsqrt(jnp.mean(v * v, -1, keepdims=True) + 1e-6) * gain
            self.n2[sl, :] = n2.astype(BF16)
            self.n2t[:, sl] = n2.T.astype(BF16)
        self.dlo[...] = jnp.zeros_like(self.dlo)
        self.dhi[...] = jnp.zeros_like(self.dhi)

    def block(self, c, total):
        k = lax.rem(c, 2)
        for cp in self.weights(c):
            cp.wait()
        @pl.when(c + 1 < total)
        def _():
            for cp in self.weights(c + 1):
                cp.start()
        half = self.count // 2
        for r, dn in ((0, self.dlo), (half, self.dhi)):
            sl = slice(r, r + half)
            gate = nn(self.n2[sl, :], self.wa[k])
            up = nn(self.n2[sl, :], self.wa[2 + k])
            dh = nt(self.gb[sl, :], self.wd[k])
            sigma = 1.0 / (1.0 + jnp.exp(-gate))
            silu = gate * sigma
            hid = (silu * up).astype(BF16)
            d_gate = (dh * up * sigma * (1.0 + gate * (1.0 - sigma))).astype(BF16)
            d_up = (dh * silu).astype(BF16)
            self.dg[sl, :] = d_gate
            self.du[sl, :] = d_up
            self.hidt[:, sl] = hid.astype(F32).T.astype(BF16)
            self.acc[sl, :] += nn(hid, self.wd[k])
            dn[0] += nt(d_gate, self.wa[k]) + nt(d_up, self.wa[2 + k])
        @pl.when(c >= 1)
        def _():
            for cp in self.stores(c - 1):
                cp.wait()
        self.sg[...] = nn(self.n2t[...], self.dg[...]).astype(BF16).reshape(self.sg.shape)
        self.su[...] = nn(self.n2t[...], self.du[...]).astype(BF16).reshape(self.su.shape)
        self.sd[...] = nn(self.hidt[...], self.gb[...]).astype(BF16)
        for cp in self.stores(c):
            cp.start()

    def settle(self, c):
        for cp in self.stores(c):
            cp.wait()

    def after(self, total):
        parts = self.width // FFC
        for j in range(parts):
            self.out_part(j).start()
        gain = self.gain[...]
        sums = jnp.zeros((8, self.width), F32)
        half = self.count // 2
        for r in range(0, self.count, 128):
            sl = slice(r, r + 128)
            dn = self.dlo[0, r:r + 128] if r < half else self.dhi[0, r - half:r - half + 128]
            v = self.resid[sl, :]
            scale = lax.rsqrt(jnp.mean(v * v, -1, keepdims=True) + 1e-6)
            unit = v * scale
            prod = dn * unit
            sums = sums + jnp.sum(prod.reshape(16, 8, self.width), 0)
            e2 = dn * gain
            d = self.gb[sl, :].astype(F32) + scale * (e2 - unit * jnp.mean(e2 * unit, -1, keepdims=True))
            self.resid[sl, :] = d
            self.gb[sl, :] = d.astype(BF16)
            self.xb[sl, :] = self.acc[sl, :].astype(BF16)
            self.n2t[:, sl] = self.hb[sl, :].astype(F32).T.astype(BF16)
        self.gain_grad[...] = jnp.sum(sums, 0, keepdims=True)
        for cp in self.results():
            cp.start()
        for j in range(parts):
            self.out_part(j).wait()
        for j in range(parts):
            if j >= 2:
                self.out_store(j - 2).wait()
            (self.sg, self.su)[j % 2][...] = nn(self.n2t[...], self.gb[:, j * FFC:(j + 1) * FFC]).astype(BF16).reshape(self.sg.shape)
            self.out_store(j).start()
        for r in range(0, self.count, 128):
            total = None
            for j in range(parts):
                part = nt(self.gb[r:r + 128, j * FFC:(j + 1) * FFC], self.wa[j])
                total = part if total is None else total + part
            self.n2[r:r + 128, :] = total.astype(BF16)
        for j in range(parts - 2, parts):
            self.out_store(j).wait()

    def results(self):
        out = []
        for r in range(self.rows):
            at = pl.ds(r * self.nq, self.nq)
            out.append(pltpu.make_async_copy(self.xb.at[at], self.output.at[r], self.lsem.at[0, r]))
            out.append(pltpu.make_async_copy(self.resid.at[at], self.d_resid.at[r], self.lsem.at[1, r]))
        return out

def back_kernel(span, chunk, units, plan, blocks, qh_ref, qr_ref, shared_ref, cond_ref, bl_ref, bs_ref, lse_ref, *refs):
    feed_in, refs = refs[:8], refs[8:]
    dqh_ref, dqr_ref, mine_ref, output, d_resid, gain_grad = refs[:6]
    sums, grads, refs = refs[6:10], refs[10:14], refs[14:]
    dl, ds, hl, hs, ddl, dds, dhl, dhs, pack, RX, RZ, xs, xr, zs, zr, bsem = refs[:16]
    fb, refs = refs[16:34], refs[34:]
    me = Place()
    b, p = pl.program_id(0), pl.program_id(1)
    step = b * PAIRS + p
    nq = 2 * span
    red = Reduce(me, units, grads, sums, refs)
    row = Rows(me, pack, mine_ref, RX, RZ, xs, xr, zs, zr)
    feed = Feed(feed_in, (output, d_resid, gain_grad), grads, (*fb[:7], ddl, dds, *fb[7:]))

    def act(items):
        for it in items:
            if it[0] == "row":
                getattr(row, it[1])(it[2])
            elif it[0] == "settle":
                feed.settle(it[1])
            elif it[0] == "results":
                for cp in feed.results():
                    cp.wait()
            else:
                red.run([it])

    brought = [pltpu.make_async_copy(shared_ref.at[:, r], pack.at[r], bsem.at[r]) for r in range(pack.shape[0])]

    @pl.when(step == 0)
    def _():
        greet(me)
        for cp in brought:
            cp.start()
        feed.before()
        def body(c, carry):
            feed.block(c, blocks)
            for k, items in plan["feed"].items():
                pl.when(c == k)(functools.partial(act, items))
            return carry
        lax.fori_loop(0, blocks, body, 0)
        feed.settle(blocks - 1)
        act(plan["mid"])
        feed.after(blocks)
        act(plan["first"])
        for cp in brought:
            cp.wait()

    @pl.when(p == 0)
    def _():
        lay_out(me, lambda j: pack.at[b, j], 2 * NZ, span, cond_ref, dl, ds, hl, hs)
        dqr_ref[...] = jnp.zeros_like(dqr_ref)
        ddl[...] = jnp.zeros_like(ddl)
        dds[...] = jnp.zeros_like(dds)

    rows_at = pl.ds(pl.multiple_of(b * nq, nq), nq)
    lanes_at = pl.ds(pl.multiple_of(p * 128, 128), 128)
    pair_back(span, chunk, p, qh_ref, qr_ref, Pair(hl, p), Pair(hs, p), dl, ds, cond_ref, bl_ref, bs_ref, lse_ref,
              feed.hb[rows_at, lanes_at], feed.n2[rows_at, lanes_at], dqh_ref, dqr_ref, Pair(dhl, p), Pair(dhs, p), ddl, dds)

    @pl.when(p == PAIRS - 1)
    def _():
        pack_up(me, b, span, cond_ref, pack, ddl, dds, dhl, dhs)
        row.begin(b)

    for s, items in plan["steps"].items():
        pl.when(step == s)(functools.partial(act, items))

def backward(qh, qr, shared, cond, bl, bs, lse, tokens, heads_out, cotangent, w_out, w_gate, w_up, w_down, gain_two, units, plan, cid):
    rows, pairs, _, nq = qh.shape
    n = shared.shape[0]
    span = nq // 2
    nk = n * span
    width, ff = w_gate.shape
    count = rows * nq
    full = lambda *s: pl.BlockSpec((1, *s), lambda b, p: (b, *([0] * len(s))))
    pairb = lambda *s: pl.BlockSpec((1, 1, *s), lambda b, p: (b, p, *([0] * len(s))))
    sd = jax.ShapeDtypeStruct
    DMA = pltpu.SemaphoreType.DMA
    V = pltpu.VMEM
    whole = pl.BlockSpec(memory_space=pltpu.VMEM)
    far = pl.BlockSpec(memory_space=pl.ANY)
    part = shared.shape[2:]
    scratch = [V((1, 256, nk), BF16)] * 2 + [V((PAIRS, 8, nk), F32)] * 2 + [V((1, 256, nk), F32)] * 2 + [V((PAIRS, 8, nk), F32)] * 2
    scratch += [V((rows, n, *part), BF16), V((rows, NZ, *part), BF16), V((rows, NZ - 1, *part), BF16)] + [DMA((rows, NZ))] * 4 + [DMA((rows,))]
    scratch += [V((count, width), BF16)] * 4 + [V((width, count), BF16)] + [V((count, width), F32)] * 2
    scratch += [V((4, width, FFC), BF16), V((2, FFC, width), BF16)] + [V((n, width // n, FFC), BF16)] * 2 + [V((FFC, width), BF16)] + [V((count, FFC), BF16)] * 2 + [V((FFC, count), BF16)]
    scratch += [DMA((3, rows)), DMA((3, 4)), DMA((3,))]
    shard = (n, width // n)
    sums = [sd((width // n, width), BF16), sd((width // n, ff), BF16), sd((width // n, ff), BF16), sd((ff // n, width), BF16)]
    grads = [sd((*shard, width), BF16), sd((*shard, ff), BF16), sd((*shard, ff), BF16), sd((ff, width), BF16)]
    return pl.pallas_call(
        functools.partial(back_kernel, span, min(512, nk), units, plan, ff // FFC),
        grid=(rows, pairs),
        out_shape=[sd((rows, pairs, 12, nq), F32), sd((rows, 384, nq), F32), sd((rows, *part), BF16), sd((rows, nq, width), BF16),
                   sd((rows, nq, width), F32), sd((1, width), F32)] + sums + grads,
        in_specs=[pairb(12, nq), full(384, nq), far, pl.BlockSpec((1, nk), lambda b, p: (0, 0)), full(1, nk), full(1, nk), full(nq, 128)] + [far] * 7 + [whole],
        out_specs=[pairb(12, nq), full(384, nq), whole, far, far, whole] + [far] * 8,
        scratch_shapes=scratch + reduce_scratch(units),
        compiler_params=pltpu.CompilerParams(collective_id=cid, has_side_effects=True, vmem_limit_bytes=60 << 20),
        name="backward",
    )(qh, qr, shared, cond, bl, bs, lse, tokens, heads_out, cotangent, w_out, w_gate, w_up, w_down, gain_two)[:10]

class Gather:
    def __init__(self, me, units, ins, outs, sems):
        self.me, self.units, self.ins, self.outs = me, units, ins, outs
        self.zs, self.zr, self.xs, self.xr, self.ys, self.yr, self.cs, self.cr, self.ls = sems

    def remote(self, src, dst, ss, rs, dev):
        return pltpu.make_async_remote_copy(src_ref=src, dst_ref=dst, send_sem=ss, recv_sem=rs, device_id=dev, device_id_type=MESH)

    def view(self, k, shard, y, c):
        u = self.units[k]
        return self.part(u, self.outs[u.arr].at[shard], y, c)

    @staticmethod
    def part(u, ref, y, c):
        return rect(u, ref, 2 * c + y, 4) if u.flow == "P" else rect(u, ref, c, 2)

    def first(self, k, ss, rs, dev):
        u, me = self.units[k], self.me
        return self.remote(self.part(u, self.ins[u.arr], me.y, me.c), self.view(k, me.seq, me.y, me.c), ss, rs, dev)

    def onward(self, k, shard, y, ss, rs, dev):
        v = self.view(k, shard, y, self.me.c)
        return self.remote(v, v, ss, rs, dev)

    def zsend(self, k, zz):
        return self.first(k, self.zs.at[k, zz], self.zr.at[k, self.me.z], (2 * zz + self.me.x, self.me.batch))

    def zrecv(self, k, zz):
        me = self.me
        return self.onward(k, 2 * zz + me.x, me.y, self.zs.at[k, zz], self.zr.at[k, zz], (2 * zz + me.x, me.batch))

    def xown(self, k):
        return self.first(k, self.xs.at[k, self.me.z], self.xr.at[k, self.me.z], self.me.xp)

    def xsend(self, k, zz):
        return self.onward(k, 2 * zz + self.me.x, self.me.y, self.xs.at[k, zz], self.xr.at[k, zz], self.me.xp)

    def xrecv(self, k, zz):
        return self.onward(k, 2 * zz + 1 - self.me.x, self.me.y, self.xs.at[k, zz], self.xr.at[k, zz], self.me.xp)

    def ycopy(self, k, shard, mine):
        return self.onward(k, shard, self.me.y if mine else 1 - self.me.y, self.ys.at[k, shard], self.yr.at[k, shard], self.me.yp)

    def ccopy(self, k, w, shard):
        return self.onward(k, shard, self.me.y if w == 0 else 1 - self.me.y, self.cs.at[k, w, shard], self.cr.at[k, w, shard], self.me.cp)

    def crecv(self, k, w, shard):
        v = self.view(k, shard, self.me.y if w == 0 else 1 - self.me.y, 1 - self.me.c)
        return self.remote(v, v, self.cs.at[k, w, shard], self.cr.at[k, w, shard], self.me.cp)

    def local(self, a):
        return pltpu.make_async_copy(self.ins[a], self.outs[a].at[self.me.seq], self.ls.at[a])

    def other(self, i):
        return lax.rem(self.me.z + i, NZ)

    def begin(self, k, i):
        self.zsend(k, self.other(i)).start()
        pl.when(i == 1)(lambda: self.xown(k).start())

    def spread(self, k, shard):
        if self.units[k].flow == "P":
            self.ycopy(k, shard, True).start()
        self.ccopy(k, 0, shard).start()

    def z(self, k, i):
        zz = self.other(i)
        self.zrecv(k, zz).wait_recv()
        self.xsend(k, zz).start()
        self.spread(k, 2 * zz + self.me.x)

    def x(self, k, i):
        zz = self.other(i)
        self.xrecv(k, zz).wait_recv()
        self.spread(k, 2 * zz + 1 - self.me.x)

    def far(self, i):
        return 2 * self.other(i) + jnp.where(i < NZ, self.me.x, 1 - self.me.x)

    def y(self, k, i):
        shard = self.far(i)
        self.ycopy(k, shard, False).wait_recv()
        self.ccopy(k, 1, shard).start()

    def got(self, k, i):
        for w in range(2 if self.units[k].flow == "P" else 1):
            self.crecv(k, w, self.far(i)).wait_recv()

    def sent(self, k, i):
        me = self.me
        pl.when(i < NZ)(lambda: self.zsend(k, self.other(i)).wait_send())
        pl.when(i < NZ)(lambda: self.xsend(k, self.other(i)).wait_send())
        pl.when(i == NZ)(lambda: self.xown(k).wait_send())
        shard = self.far(i)
        self.ccopy(k, 0, shard).wait_send()
        if self.units[k].flow == "P":
            self.ycopy(k, shard, True).wait_send()
            self.ccopy(k, 1, shard).wait_send()

    def run(self, plan):
        for step, k, first, n in plan:
            fn = getattr(self, step)
            def body(i, c):
                fn(k, i)
                return c
            lax.fori_loop(first, first + n, body, 0)

class RowsGather:
    def __init__(self, me, shared, zs, zr, xs, xr):
        self.me, self.shared, self.zs, self.zr, self.xs, self.xr = me, shared, zs, zr, xs, xr

    def copy(self, b, shard, ss, rs, dev):
        v = self.shared.at[shard, b]
        return pltpu.make_async_remote_copy(src_ref=v, dst_ref=v, send_sem=ss, recv_sem=rs, device_id=dev, device_id_type=MESH)

    def zsend(self, b, zz):
        me = self.me
        return self.copy(b, me.seq, self.zs.at[b, zz], self.zr.at[b, me.z], (2 * zz + me.x, me.batch))

    def zrecv(self, b, zz):
        me = self.me
        return self.copy(b, 2 * zz + me.x, self.zs.at[b, zz], self.zr.at[b, zz], (2 * zz + me.x, me.batch))

    def xsend(self, b, zz):
        return self.copy(b, 2 * zz + self.me.x, self.xs.at[b, zz], self.xr.at[b, zz], self.me.xp)

    def xrecv(self, b, zz):
        return self.copy(b, 2 * zz + 1 - self.me.x, self.xs.at[b, zz], self.xr.at[b, zz], self.me.xp)

    def loop(self, first, fn):
        def body(i, c):
            fn(lax.rem(self.me.z + i, NZ))
            return c
        lax.fori_loop(first, NZ, body, 0)

    def begin(self, b):
        self.loop(1, lambda zz: self.zsend(b, zz).start())
        self.xsend(b, self.me.z).start()

    def z(self, b):
        def one(zz):
            self.zrecv(b, zz).wait_recv()
            self.xsend(b, zz).start()
        self.loop(1, one)

    def x(self, b):
        self.loop(0, lambda zz: self.xrecv(b, zz).wait_recv())

    def end(self, b):
        self.loop(1, lambda zz: self.zsend(b, zz).wait_send())
        self.loop(0, lambda zz: self.xsend(b, zz).wait_send())

def turn_rows(u, cosine, sine):
    out = []
    for r in range(0, u.shape[0], 64):
        a, b = u[r:r + 32], u[r + 32:r + 64]
        out += [a * cosine - b * sine, b * cosine + a * sine]
    return jnp.concatenate(out, 0)

def project(me, span, tok_ref, small_ref, cos_ref, sin_ref, normed_ref, qh_ref, qr_ref, shared_ref, gain_ref, b):
    nq = 2 * span
    d = tok_ref.shape[-1]
    gains = small_ref[:, :, 768:896].reshape(d, 128).astype(F32).T
    x = tok_ref[b].astype(F32)
    unit = x * lax.rsqrt(jnp.mean(x * x, -1, keepdims=True) + 1e-6)
    normed = (unit * gains[32:33]).astype(BF16)
    normed_ref[b] = normed
    gain_ref[...] = gains[33:34]
    w = small_ref[...].reshape(d, 896)
    f = nn(normed, w).T
    qh_ref[b] = f[:96].reshape(PAIRS, 12, nq)
    cosine, sine = cos_ref[...], sin_ref[...]
    qr_ref[b] = turn_rows(f[96:480], cosine, sine)
    own = jnp.concatenate([turn_rows(f[480:608], cosine, sine), f[608:800]], 0)
    shared_ref[me.seq, b] = own.astype(BF16)

def forward_kernel(span, chunk, units, narr, plan, tok_ref, cos_ref, sin_ref, cond_ref, bl_ref, bs_ref, *refs):
    ins = refs[:narr]
    normed_ref, qh_ref, qr_ref, shared_out, o_ref, lse_ref, gain_ref = refs[narr:narr + 7]
    outs = refs[narr + 7:2 * narr + 7]
    shared_ref, small, saved, dl, ds, hl, hs, s1, s2, rzs, rzr, rxs, rxr = refs[2 * narr + 7:2 * narr + 20]
    small_out, outs = outs[0], (small, *outs[1:])
    me = Place()
    b, p = pl.program_id(0), pl.program_id(1)
    step = b * PAIRS + p
    gat = Gather(me, units, ins, outs, refs[2 * narr + 20:])
    saves = (pltpu.make_async_copy(small, small_out, saved.at[0]), pltpu.make_async_copy(shared_ref, shared_out, saved.at[1]))
    row = RowsGather(me, shared_ref, rzs, rzr, rxs, rxr)

    def act(items):
        for it in items:
            if it[0] == "row":
                getattr(row, it[1])(it[2])
            elif it[0] == "project":
                for r in range(tok_ref.shape[0]):
                    project(me, span, tok_ref, small, cos_ref, sin_ref, normed_ref, qh_ref, qr_ref, shared_ref, gain_ref, r)
            elif it[0] == "local":
                for a in range(narr):
                    gat.local(a).start()
                gat.local(0).wait()
            elif it[0] == "locals":
                for a in range(1, narr):
                    gat.local(a).wait()
                for save in saves:
                    save.start()
                for save in saves:
                    save.wait()
            else:
                gat.run([it])

    @pl.when(step == 0)
    def _():
        greet(me)
        act(plan["first"])

    @pl.when(p == 0)
    def _():
        lay_out(me, lambda j: shared_ref.at[j, b], 2 * NZ, span, cond_ref, dl, ds, hl, hs)

    pair_forward(span, chunk, p, qh_ref[b, p], qr_ref[b], hl[p], hs[p], dl, ds, cond_ref, bl_ref, bs_ref, o_ref, lse_ref, s1, s2)

    for s, items in plan["steps"].items():
        pl.when(step == s)(functools.partial(act, items))

def forward(tokens, cosine, sine, cond, bl, bs, weights, units, plan, cid):
    rows, nq, width = tokens.shape
    span = nq // 2
    n = 2 * NZ
    nk = n * span
    narr, nu = len(weights), len(units)
    chunk = min(512, nk)
    whole = pl.BlockSpec(memory_space=pltpu.VMEM)
    far = pl.BlockSpec(memory_space=pl.ANY)
    full = lambda *s: pl.BlockSpec((1, *s), lambda b, p: (b, *([0] * len(s))))
    sd = jax.ShapeDtypeStruct
    DMA = pltpu.SemaphoreType.DMA
    V = pltpu.VMEM
    scratch = [V((n, rows, 320, nq), BF16), V((n, *weights[0].shape), BF16), DMA((2,))] + [V((1, 256, nk), BF16)] * 2 + [V((PAIRS, 8, nk), F32)] * 2 + [V((nq, nk), F32)] * 2 + [DMA((rows, NZ))] * 4
    scratch += [DMA((nu, NZ))] * 4 + [DMA((nu, n))] * 2 + [DMA((nu, 2, n))] * 2 + [DMA((narr,))]
    return pl.pallas_call(
        functools.partial(forward_kernel, span, chunk, units, narr, plan),
        grid=(rows, PAIRS),
        out_shape=[sd((rows, nq, width), BF16), sd((rows, PAIRS, 12, nq), F32), sd((rows, 384, nq), F32), sd((n, rows, 320, nq), BF16),
                   sd((rows, nq, width), BF16), sd((rows, nq, 128), F32), sd((1, width), F32)] + [sd((n, *a.shape), a.dtype) for a in weights],
        in_specs=[whole, whole, whole, pl.BlockSpec((1, nk), lambda b, p: (0, 0)), full(1, nk), full(1, nk)] + [far] * narr,
        out_specs=[whole, whole, whole, far, pl.BlockSpec((1, nq, 128), lambda b, p: (b, 0, p)), full(nq, 128), whole] + [far] * narr,
        scratch_shapes=scratch,
        compiler_params=pltpu.CompilerParams(collective_id=cid, has_side_effects=True, vmem_limit_bytes=62 << 20),
        name="forward",
    )(tokens, cosine, sine, cond, bl, bs, *weights)

def products_kernel(dqh_ref, dqr_ref, mine_ref, cos_ref, sin_ref, normed_ref, small_ref, tok_ref, res_ref, gain_two_ref, input_ref, out_ref, acc, sums):
    b = pl.program_id(0)
    d = tok_ref.shape[-1]
    nq = tok_ref.shape[1]
    @pl.when(b == 0)
    def _():
        acc[...] = jnp.zeros_like(acc)
        sums[...] = jnp.zeros_like(sums)
    cosine, sine = cos_ref[...], -sin_ref[...]
    mine = mine_ref[0].astype(F32)
    turned = jnp.concatenate([dqh_ref[0].reshape(96, nq), turn_rows(dqr_ref[0], cosine, sine), turn_rows(mine[:128], cosine, sine), mine[128:],
                              jnp.zeros((96, nq), F32)], 0)
    acc[...] += nn(turned.astype(BF16), normed_ref[0])
    w = small_ref[...].reshape(d, 896)
    gain = small_ref[:, :, 768:896].reshape(d, 128).astype(F32).T[32:33]
    back = nt(turned.T.astype(BF16), w)
    for r in range(0, nq, 128):
        sl = slice(r, r + 128)
        x = tok_ref[0, sl, :].astype(F32)
        scale = lax.rsqrt(jnp.mean(x * x, -1, keepdims=True) + 1e-6)
        unit = x * scale
        dn = back[sl]
        sums[...] += jnp.sum((dn * unit).reshape(16, 8, d), 0)
        e1 = dn * gain
        input_ref[0, sl, :] = res_ref[0, sl, :] + scale * (e1 - unit * jnp.mean(e1 * unit, -1, keepdims=True))
    @pl.when(b == pl.num_programs(0) - 1)
    def _():
        total = jnp.sum(sums[...], 0, keepdims=True)
        for s in range(out_ref.shape[0]):
            sl = slice(s * 128, s * 128 + 128)
            out_ref[s, :800, :] = acc[:800, sl].astype(BF16)
            out_ref[s, 800:, :] = jnp.concatenate([total[:, sl], gain_two_ref[:, sl], jnp.zeros((94, 128), F32)], 0).astype(BF16)

def products(dqh, dqr, mine, cosine, sine, normed, small, tokens, d_resid, gain_two):
    rows, nq, d = tokens.shape
    n = small.shape[0]
    row = lambda a: pl.BlockSpec((1, *a.shape[1:]), lambda b: (b, *([0] * (a.ndim - 1))))
    one = lambda a: pl.BlockSpec(a.shape, lambda b: (0,) * a.ndim)
    sd = jax.ShapeDtypeStruct
    return pl.pallas_call(
        products_kernel,
        grid=(rows,),
        out_shape=[sd(tokens.shape, F32), sd((n, 896, d // n), BF16)],
        in_specs=[row(dqh), row(dqr), row(mine), one(cosine), one(sine), row(normed), one(small), row(tokens), row(d_resid), one(gain_two)],
        out_specs=[row(tokens), pl.BlockSpec((n, 896, d // n), lambda b: (0, 0, 0))],
        scratch_shapes=[pltpu.VMEM((896, d), F32), pltpu.VMEM((8, d), F32)],
        compiler_params=pltpu.CompilerParams(vmem_limit_bytes=62 << 20),
        name="products",
    )(dqh, dqr, mine, cosine, sine, normed, small, tokens, d_resid, gain_two)

def results_kernel(small_ref, out_ref, gate_ref, up_ref, down_ref, qh_ref, qd_ref, kh_ref, kd_ref, vh_ref, vd_ref, g1_ref, g2_ref, o_ref, g_ref, u_ref, d_ref):
    for src, dst in ((out_ref, o_ref), (gate_ref, g_ref), (up_ref, u_ref), (down_ref, d_ref)):
        dst[...] = src[...].astype(F32)
    @pl.when(pl.program_id(0) == 0)
    def _():
        flat = small_ref[...].astype(F32)
        g1_ref[...] = flat[800:801]
        g2_ref[...] = flat[801:802]
        across = flat.T.astype(BF16)
        def pick(lo, hi, n, source):
            i = lax.broadcasted_iota(jnp.int32, (hi - lo, n), 0)
            j = lax.broadcasted_iota(jnp.int32, (hi - lo, n), 1)
            return nn(across[:, lo:hi], jnp.where(i == source(j), 1.0, 0.0).astype(BF16))
        pair = lambda j: (j & 15) >> 1
        rank = lambda j: j >> 4
        qh_ref[...] = pick(0, 128, 96, lambda j: pair(j) * 12 + rank(j) * 2 + (j & 1)).T
        qd_ref[...] = pick(0, 512, 384, lambda j: j + 96)
        kd_ref[...] = pick(384, 640, 128, lambda j: j + 96)
        vd_ref[...] = pick(512, 768, 128, lambda j: j + 96)
        kh_ref[...] = pick(640, 896, 32, lambda j: pair(j) * 8 + rank(j) * 2 + (j & 1) + 96).T
        vh_ref[...] = pick(640, 896, 32, lambda j: pair(j) * 8 + rank(j) * 2 + (j & 1) + 100).T

def results(small, out, gate, up, down):
    steps = 2
    n = small.shape[1]
    part = lambda a: pl.BlockSpec((a.shape[0] // steps, a.shape[1]), lambda i: (i, 0))
    one = lambda *s: pl.BlockSpec(s, lambda i: (0, 0))
    sd = lambda *s: jax.ShapeDtypeStruct(s, F32)
    shapes = [(96, n), (n, 384), (32, n), (n, 128), (32, n), (n, 128), (1, n), (1, n)]
    big = (out, gate, up, down)
    return pl.pallas_call(
        results_kernel,
        grid=(steps,),
        out_shape=[sd(*s) for s in shapes] + [sd(*a.shape) for a in big],
        in_specs=[one(*small.shape)] + [part(a) for a in big],
        out_specs=[one(*s) for s in shapes] + [part(a) for a in big],
        compiler_params=pltpu.CompilerParams(vmem_limit_bytes=62 << 20),
        name="results",
    )(small, *big)

def prepare_kernel(n, span, order, lengths, inverse, qh, qd, kh, kd, vh, vd, g1, g2, small_ref, cond_ref, bl_ref, bs_ref, cos_ref, sin_ref):
    me = lax.axis_index("seq")
    rows = bl_ref.shape[0]
    lane = lax.broadcasted_iota(jnp.int32, (1, span), 1)
    own = order[0, me]
    for i in range(n):
        j = lax.rem(me + i, n)
        sl = slice(i * span, (i + 1) * span)
        low = order[0, j]
        chosen = low < own
        sel = jnp.where(chosen, low, order[1, j])
        cond_ref[:, sl] = jnp.full((1, span), jnp.where(chosen, 1.0, 0.0), F32)
        for b in range(rows):
            bl_ref[b, :, sl] = jnp.where(lane + low * span < lengths[b], 0.0, NEG)
            bs_ref[b, :, sl] = jnp.where(lane + sel * span < lengths[b], 0.0, NEG)
    for k in range(2):
        angle = inverse[...] * (lane + order[k, me] * span).astype(F32)
        sl = slice(k * span, (k + 1) * span)
        cos_ref[:, sl] = jnp.cos(angle)
        sin_ref[:, sl] = jnp.sin(angle)
    def place(ref, target, turned=False):
        value = ref[...].astype(F32).T.astype(BF16) if turned else ref[...]
        i = lax.broadcasted_iota(jnp.int32, (value.shape[1], 896), 0)
        j = lax.broadcasted_iota(jnp.int32, (value.shape[1], 896), 1)
        return nn(value, jnp.where(j == target(i), 1.0, 0.0).astype(BF16))
    pair = lambda i: (i & 15) >> 1
    rank = lambda i: i >> 4
    out = place(qh, lambda i: pair(i) * 12 + rank(i) * 2 + (i & 1), True) + place(qd, lambda i: i + 96)
    out = out + place(kd, lambda i: i + 480) + place(vd, lambda i: i + 608)
    out = out + place(kh, lambda i: 736 + pair(i) * 8 + rank(i) * 2 + (i & 1), True)
    out = out + place(vh, lambda i: 740 + pair(i) * 8 + rank(i) * 2 + (i & 1), True)
    d = out.shape[0]
    eye = lax.broadcasted_iota(jnp.int32, (d, d), 0) == lax.broadcasted_iota(jnp.int32, (d, d), 1)
    at = lax.broadcasted_iota(jnp.int32, (d, 896), 1)
    for ref, column in ((g1, 800), (g2, 801)):
        gain = jnp.sum(jnp.where(eye, ref[...].astype(F32), 0.0), 1, keepdims=True)
        out = jnp.where(at == column, gain, out)
    small_ref[...] = out.astype(BF16)

def prepare(span_order, lengths, inverse, query_heads, query_dims, key_heads, key_dims, value_heads, value_dims, gain_one, gain_two, slots):
    n, rows = span_order.shape[0], lengths.shape[0]
    span = slots // 2
    d = query_heads.shape[0]
    smem = pl.BlockSpec(memory_space=pltpu.SMEM)
    whole = pl.BlockSpec(memory_space=pltpu.VMEM)
    sd = jax.ShapeDtypeStruct
    return pl.pallas_call(
        functools.partial(prepare_kernel, n, span),
        out_shape=[sd((d, 896), BF16), sd((1, n * span), F32), sd((rows, 1, n * span), F32), sd((rows, 1, n * span), F32), sd((32, slots), F32), sd((32, slots), F32)],
        in_specs=[smem, smem] + [whole] * 9,
        out_specs=[whole] * 6,
        compiler_params=pltpu.CompilerParams(vmem_limit_bytes=62 << 20),
        name="prepare",
    )(span_order.T, lengths, inverse, query_heads.T, query_dims, key_heads.T, key_dims, value_heads.T, value_dims, gain_one[None, :], gain_two[None, :])

HEADS, HDIM, QRANK, KVRANK = 16, 64, 6, 2
PAIRS = HEADS // 2
EPSILON = 1e-06


def rms_forward(values, gain):
    scale = lax.rsqrt(jnp.mean(values * values, -1, keepdims=True) + EPSILON)
    unit = values * scale
    return (unit * gain, unit, scale)


def rms_backward(grad_out, unit, scale, gain):
    scaled = grad_out * gain
    grad_in = scale * (scaled - unit * jnp.mean(scaled * unit, -1, keepdims=True))
    return (grad_in, jnp.sum(grad_out * unit, 0))


def rotation(positions):
    half = HDIM // 2
    index = jnp.arange(half).astype(F32)
    inverse = jnp.exp(index * (-math.log(10000.0) / half))
    angles = inverse[:, None] * positions.astype(F32)[None, :]
    return (jnp.cos(angles), jnp.sin(angles))


def rotate(u, cosine, sine):
    rows, depth, slots = u.shape
    v = u.reshape(rows, depth // HDIM, HDIM, slots)
    a, b = v[:, :, :HDIM // 2], v[:, :, HDIM // 2:]
    return jnp.concatenate([a * cosine - b * sine, b * cosine + a * sine], 2).reshape(u.shape)


def dot(a, b, ca, cb):
    return lax.dot_general(a, b, ((ca, cb), ((), ())), preferred_element_type=F32)


def pair_columns(a, ranks):
    return a.reshape(-1, ranks, PAIRS, 2).transpose(0, 2, 1, 3).reshape(a.shape)


def head_columns(a, ranks):
    return a.reshape(-1, PAIRS, ranks, 2).transpose(0, 2, 1, 3).reshape(a.shape)


GATHER_UNITS = [
    Unit(0, (0, 128), (0, 896), "P", 0), Unit(1, (0, 128), (0, 1024), "P", 0),
    Unit(2, (0, 128), (0, 1408), "P", 0), Unit(2, (0, 128), (1408, 1408), "P", 0),
    Unit(3, (0, 128), (0, 1408), "R", 0), Unit(3, (0, 128), (1408, 1408), "P", 0),
    Unit(4, (0, 176), (0, 1024), "P", 1), Unit(4, (176, 176), (0, 1024), "P", 1)]
GATHER_PLAN = {
    "first": [("local",), ("begin", 0, 1, 3), ("begin", 5, 1, 3), ("z", 0, 1, 3), ("x", 0, 0, 4), ("begin", 3, 1, 3), ("y", 0, 1, 7), ("begin", 2, 1, 3), ("got", 0, 1, 7), ("z", 5, 1, 3), ("begin", 7, 1, 3), ("project",), ("row", "begin", 0), ("z", 3, 1, 3), ("x", 5, 0, 4), ("z", 7, 1, 3), ("y", 5, 4, 4), ("z", 2, 1, 3), ("begin", 6, 1, 3), ("row", "z", 0), ("x", 3, 0, 4), ("row", "begin", 1), ("begin", 1, 1, 3), ("x", 7, 0, 4), ("row", "x", 0), ("z", 6, 1, 3), ("y", 7, 1, 3), ("y", 2, 1, 3)],
    "steps": {
        3: [("y", 3, 1, 3), ("y", 5, 1, 3), ("y", 7, 4, 4), ("row", "z", 1), ("x", 2, 0, 4)],
        4: [("begin", 4, 1, 3)],
        6: [("z", 1, 1, 3), ("y", 3, 4, 4)],
        7: [("row", "x", 1), ("x", 6, 0, 4)],
        11: [("y", 1, 1, 3), ("z", 4, 1, 3), ("x", 1, 0, 4), ("y", 6, 1, 3)],
        12: [("y", 2, 4, 4)],
        15: [("y", 1, 4, 4), ("x", 4, 0, 4), ("y", 6, 4, 4), ("got", 1, 1, 7), ("got", 2, 1, 7), ("got", 3, 1, 7), ("got", 4, 1, 7), ("got", 5, 1, 7), ("got", 6, 1, 7), ("got", 7, 1, 7), ("locals",), ("sent", 0, 1, 7), ("sent", 1, 1, 7), ("sent", 2, 1, 7), ("sent", 3, 1, 7), ("sent", 4, 1, 7), ("sent", 5, 1, 7), ("sent", 6, 1, 7), ("sent", 7, 1, 7), ("row", "end", 0), ("row", "end", 1)],
    },
}
REDUCE_UNITS = [
    Unit(1, (0, 128), (0, 1024), "P", 0), Unit(2, (0, 128), (0, 1024), "R", 0),
    Unit(1, (0, 128), (1024, 1024), "P", 0), Unit(2, (0, 128), (1024, 1024), "R", 0),
    Unit(1, (0, 128), (2048, 768), "P", 0), Unit(2, (0, 128), (2048, 768), "P", 0),
    Unit(3, (0, 176), (0, 1024), "P", 1), Unit(3, (176, 176), (0, 1024), "P", 1), Unit(0, (0, 128), (0, 1024), "P", 0)]
REDUCE_PLAN = {
    "feed": {
        4: [("begin", 0, 0, 8), ("begin", 1, 0, 8)],
        5: [("core", 0, 0, 4)],
        6: [("core", 1, 0, 4), ("core", 0, 4, 4)],
        7: [("y", 0, 0, 4)],
        8: [("begin", 2, 0, 8), ("begin", 3, 0, 8)],
        9: [("core", 2, 0, 4), ("y", 0, 4, 4), ("core", 1, 4, 4)],
    },
    "mid": [("begin", 5, 0, 8), ("begin", 7, 0, 8), ("x", 1, 0, 4), ("core", 2, 4, 4), ("core", 3, 0, 4), ("core", 5, 0, 4)],
    "first": [("begin", 4, 0, 8), ("core", 5, 4, 4), ("begin", 8, 0, 8), ("y", 2, 0, 4)],
    "steps": {
        0: [("y", 2, 4, 4), ("core", 4, 4, 4), ("core", 3, 4, 4), ("core", 7, 0, 4), ("x", 3, 0, 4), ("y", 5, 0, 4), ("core", 4, 0, 4)],
        2: [("core", 7, 4, 4), ("y", 5, 4, 4), ("x", 5, 0, 4)],
        4: [("y", 7, 0, 4), ("x", 0, 0, 4)],
        5: [("x", 2, 0, 4)],
        6: [("y", 4, 4, 4), ("y", 4, 0, 4), ("core", 8, 4, 4)],
        7: [("begin", 6, 0, 8), ("y", 7, 4, 4), ("x", 4, 0, 4), ("x", 7, 0, 4), ("core", 8, 0, 4)],
        8: [("core", 6, 0, 4)],
        10: [("y", 8, 0, 4), ("core", 6, 4, 4), ("row", "x", 0)],
        11: [("own", 5, 0, 1), ("own", 2, 0, 1), ("own", 7, 0, 1), ("y", 8, 4, 4), ("own", 4, 0, 1), ("y", 6, 0, 4)],
        12: [("x", 8, 0, 4)],
        13: [("y", 6, 4, 4)],
        14: [("last", 2, 0, 1), ("x", 6, 0, 4), ("last", 7, 0, 1)],
        15: [("own", 8, 0, 1), ("own", 1, 0, 1), ("row", "own", 0), ("own", 3, 0, 1), ("own", 0, 0, 1), ("row", "x", 1), ("last", 1, 0, 1), ("own", 6, 0, 1), ("last", 8, 0, 1), ("last", 0, 0, 1), ("last", 6, 0, 1), ("last", 4, 0, 1), ("last", 5, 0, 1), ("last", 3, 0, 1), ("row", "own", 1), ("end", 0, 0, 1), ("end", 1, 0, 1), ("end", 2, 0, 1), ("end", 3, 0, 1), ("end", 4, 0, 1), ("end", 5, 0, 1), ("end", 6, 0, 1), ("end", 7, 0, 1), ("end", 8, 0, 1), ("results",), ("row", "end", 0), ("row", "end", 1)],
    },
}
SMALL_UNITS = [Unit(0, (0, 256), (0, 128), "R", 0), Unit(0, (256, 640), (0, 128), "P", 0)]
SMALL_PLAN = [("begin", 0, 0, 8), ("begin", 1, 0, 8), ("core", 1, 0, 4), ("core", 0, 0, 4), ("core", 1, 4, 4), ("core", 0, 4, 4), ("y", 1, 0, 4), ("x", 0, 0, 4), ("y", 1, 4, 4), ("x", 1, 0, 4), ("own", 0, 0, 1),
              ("last", 0, 0, 1), ("own", 1, 0, 1), ("last", 1, 0, 1), ("end", 0, 0, 1), ("end", 1, 0, 1)]


def reduce_far(arrays):
    out = []
    for a in arrays:
        own = lax.psum_scatter(a.astype(F32), "seq", scatter_dimension=0, tiled=True)[0]
        out.append(lax.psum(own.astype(BF16), "batch"))
    return out


def per_device(near, tokens, cotangent, lengths, span_order, attn_gain, query_heads, query_dims, key_heads, key_dims,
               value_heads, value_dims, out_proj, ffn_gain, gate_proj, up_proj, down_proj):
    rows, slots, width = tokens.shape
    span = slots // 2
    count = rows * slots
    nseq = span_order.shape[0]
    nk = nseq * span
    me = lax.axis_index("seq")
    flat = tokens.reshape(count, width).astype(F32)
    if near:
        inverse = jnp.exp(jnp.arange(HDIM // 2).astype(F32) * (-math.log(10000.0) / (HDIM // 2)))[:, None]
        small, cond, low_bias, sel_bias, cosine, sine = prepare(span_order, lengths, inverse, query_heads, query_dims, key_heads, key_dims,
                                                                value_heads, value_dims, attn_gain, ffn_gain, slots)
    else:
        key_value_heads = pair_columns(jnp.concatenate([key_heads, value_heads], 1), 4)
        small = jnp.concatenate([pair_columns(query_heads, QRANK), query_dims, key_dims, value_dims, key_value_heads, attn_gain[:, None], ffn_gain[:, None]], 1)
        small = jnp.pad(small, ((0, 0), (0, 896 - small.shape[1])))
        offsets = jnp.arange(span, dtype=jnp.int32)
        spans = jnp.concatenate([span_order, span_order], 0)
        spans = lax.dynamic_slice_in_dim(spans, me, nseq, 0)
        local_pos = (spans[0][:, None] * span + offsets[None, :]).reshape(-1)
        cosine, sine = rotation(local_pos)
        chosen = spans[:, 0] < spans[0, 0]
        low_pos = (spans[:, 0][:, None] * span + offsets[None, :]).reshape(1, nk)
        sel_pos = (jnp.where(chosen, spans[:, 0], spans[:, 1])[:, None] * span + offsets[None, :]).reshape(1, nk)
        cond = jnp.repeat(chosen.astype(F32), span).reshape(1, nk)
        low_bias = jnp.where(low_pos < lengths[:, None], 0.0, NEG)[:, None, :]
        sel_bias = jnp.where(sel_pos < lengths[:, None], 0.0, NEG)[:, None, :]
    masks = (cond, low_bias, sel_bias)
    weights = [small, out_proj, gate_proj, up_proj, down_proj]
    if near:
        by_row, qh, qr, shared, heads_out, lse, gain_two, *parts = forward(tokens, cosine, sine, *masks, weights, GATHER_UNITS, GATHER_PLAN, 0)
    else:
        parts = [lax.all_gather(a, "seq", axis=0) for a in weights]
    small, w_out, w_gate, w_up, w_down = [p.reshape(-1, p.shape[-1]) for p in parts]
    w_qkv = small[:, :800]
    gain_one = small[:, 800].astype(F32)
    normed_full, unit_one, scale_one = rms_forward(flat, gain_one)
    if not near:
        gain_two = small[:, 801].astype(F32)
        by_row = normed_full.astype(BF16).reshape(rows, slots, width)
        factors = jnp.stack([dot(w_qkv, by_row[b], (0,), (1,)) for b in range(rows)])
        qh = factors[:, :96].reshape(rows, PAIRS, 12, slots)
        qr = rotate(factors[:, 96:480], cosine, sine)
        own = jnp.concatenate([rotate(factors[:, 480:608], cosine, sine), factors[:, 608:800]], 1).astype(BF16)
        shared = lax.all_gather(own, "seq", axis=0)
        turned = lax.dynamic_slice_in_dim(jnp.concatenate([shared, shared], 0), me, nseq, 0)
        low, high = turned[..., :span], turned[..., span:]
        sel = jnp.where(chosen[:, None, None, None], low, high)
        low = low.transpose(1, 2, 0, 3).reshape(rows, 320, nk)
        sel = sel.transpose(1, 2, 0, 3).reshape(rows, 320, nk)
        in_pairs = lambda a: a[:, 256:].astype(F32).reshape(rows, PAIRS, 8, nk)
        factors = (in_pairs(low), in_pairs(sel), low[:, :256], sel[:, :256])
        heads_out, lse = attend(qh, qr, *factors, *masks)
    if near:
        dqh, dqr, mine, output, d_resid, gain_two_grad, *sums = backward(
            qh, qr, shared, *masks, lse, tokens, heads_out, cotangent, w_out, w_gate, w_up, w_down, gain_two, REDUCE_UNITS, REDUCE_PLAN, 1)
        input_grad, small_grad = products(dqh, dqr, mine, cosine, sine, by_row, parts[0], tokens, d_resid, gain_two_grad)
        small_sum = reduce_weights([small_grad], SMALL_UNITS, SMALL_PLAN, 3)[0]
        d_qh, d_qd, d_kh, d_kd, d_vh, d_vd, d_g1, d_g2, d_out, d_gate, d_up, d_down = results(small_sum, *sums)
        return (output, input_grad, d_g1[0], d_qh.T, d_qd, d_kh.T, d_kd, d_vh.T, d_vd, d_out, d_g2[0], d_gate, d_up, d_down)
    else:
        heads_flat = heads_out.reshape(count, width)

        resid = flat + dot(heads_flat, w_out, (1,), (0,))
        normed_two_full, unit_two, scale_two = rms_forward(resid, gain_two)
        normed_two = normed_two_full.astype(BF16)
        gate = dot(normed_two, w_gate, (1,), (0,))
        up_part = dot(normed_two, w_up, (1,), (0,))
        sigma = jax.nn.sigmoid(gate)
        hidden = (gate * sigma * up_part).astype(BF16)
        output = (resid + dot(hidden, w_down, (1,), (0,))).astype(BF16).reshape(rows, slots, width)

        grad_out = cotangent.reshape(count, width)
        down_grad = dot(hidden, grad_out, (0,), (0,)).astype(BF16)
        d_hidden = dot(grad_out, w_down, (1,), (1,))
        d_gate = (d_hidden * up_part * sigma * (1.0 + gate * (1.0 - sigma))).astype(BF16)
        d_up = (d_hidden * gate * sigma).astype(BF16)
        gate_grad = dot(normed_two, d_gate, (0,), (0,)).astype(BF16)
        up_grad = dot(normed_two, d_up, (0,), (0,)).astype(BF16)
        d_normed_two = dot(d_gate, w_gate, (1,), (1,)) + dot(d_up, w_up, (1,), (1,))
        d_mid, gain_two_grad = rms_backward(d_normed_two, unit_two, scale_two, gain_two)
        d_resid = grad_out.astype(F32) + d_mid
        d_attn = d_resid.astype(BF16)
        out_grad = dot(heads_flat, d_attn, (0,), (0,)).astype(BF16)
        d_heads = dot(d_attn, w_out, (1,), (1,)).astype(BF16).reshape(rows, slots, width)

        grads = [g.reshape(nseq, -1, g.shape[-1]) for g in (out_grad, gate_grad, up_grad, down_grad)]
        dqh, dqr, dhl, dhs, ddl, dds = attend_back(qh, qr, *factors, *masks, lse, heads_out, d_heads)
        from_low = jnp.concatenate([ddl, dhl.reshape(rows, 64, nk)], 1).reshape(rows, 320, nseq, span)
        from_sel = jnp.concatenate([dds, dhs.reshape(rows, 64, nk)], 1).reshape(rows, 320, nseq, span)
        pick = chosen[None, None, :, None]
        both = jnp.concatenate([from_low + jnp.where(pick, from_sel, 0.0), jnp.where(pick, 0.0, from_sel)], -1).transpose(2, 0, 1, 3)
        both = lax.dynamic_slice_in_dim(jnp.concatenate([both, both], 0), lax.rem(nseq - me, nseq), nseq, 0)
        mine = lax.psum_scatter(both, "seq", scatter_dimension=0, tiled=True)[0]
        sums = reduce_far(grads)
    mine = mine.astype(F32)
    turned = jnp.concatenate([dqh.reshape(rows, 96, slots), rotate(dqr, cosine, -sine), rotate(mine[:, :128], cosine, -sine), mine[:, 128:]], 1).astype(BF16)
    small_grad = dot(by_row, turned, (0, 1), (0, 2))
    d_normed = dot(turned, w_qkv, (1,), (1,)).reshape(count, width)
    d_first, gain_one_grad = rms_backward(d_normed, unit_one, scale_one, gain_one)
    input_grad = (d_resid + d_first).reshape(rows, slots, width)
    small_grad = jnp.concatenate([small_grad, gain_one_grad[:, None], gain_two_grad[:, None], jnp.zeros((width, 94), F32)], 1).astype(BF16)

    small_grad = small_grad.reshape(nseq, -1, 896)
    small_sum = reduce_far([small_grad])[0]
    small_sum = small_sum.astype(F32)
    out_sum, gate_sum, up_sum, down_sum = [g.astype(F32) for g in sums]
    key_value = head_columns(small_sum[:, 736:800], 4)
    return (output, input_grad, small_sum[:, 800], head_columns(small_sum[:, :96], QRANK), small_sum[:, 96:480], key_value[:, :32], small_sum[:, 480:608],
            key_value[:, 32:], small_sum[:, 608:736], out_sum, small_sum[:, 801], gate_sum, up_sum, down_sum)


def solution(mesh):
    near = mesh.shape["seq"] == 8 and mesh.shape["batch"] == 4
    by_slot = P("batch", "seq", None)
    line, table = P("seq"), P("seq", None)
    return jax.shard_map(
        functools.partial(per_device, near),
        mesh=mesh,
        in_specs=(by_slot, by_slot, P("batch"), P(), line, *([table] * 7), line, *([table] * 3)),
        out_specs=(by_slot, by_slot, line, *([table] * 7), line, *([table] * 3)),
        check_vma=False,
    )
```
